32 devices in a mesh: dp: 4 (over x, core), ctx: 8 (over z, y).
Axes of the slice: x: 2, y: 2, z: 4, core: 2. Of those that a mesh axis runs over, the one named last changes fastest.
Arguments:
- inputs: bfloat16 [4, 1024, 2048], P('dp', 'ctx'), may hold values from -6 to 6
- b_proj: bfloat16 [4, 1024, 64], P('dp', 'ctx'), may hold values from -0.75 to 0.75
- c_proj: bfloat16 [4, 1024, 64], P('dp', 'ctx'), may hold values from -6 to 6
- step_sizes: float32 [4, 32, 1024], P('dp', None, 'ctx'), may hold values from 0.0001 to 0.37
- a_log: float32 [32], replicated, may hold values from -8 to -1.7
- skip_gain: float32 [32], replicated, may hold values from 0.5 to 1.5
- doc_lengths: int32 [4, 16], P('dp'), may hold values from 1 to 256, 1024 in all within a row
- grad_out: bfloat16 [4, 1024, 2048], P('dp', 'ctx'), may hold values from -6 to 6
Outputs:
- input_grads: bfloat16 [4, 1024, 2048], P('dp', 'ctx')
- b_gradient: bfloat16 [4, 1024, 64], P('dp', 'ctx')
- c_gradient: bfloat16 [4, 1024, 64], P('dp', 'ctx')
- step_grads: float32 [4, 32, 1024], P('dp', None, 'ctx')
- alog_grads: float32 [32], replicated
- skip_grads: float32 [32], replicated
The draws below stay inside these ranges and needn't reach their ends.
Inputs may be any that keep to these rules, and one draw needn't show every extreme that they name: `doc_lengths`: each row holds the 16 document lengths of one packed sequence, in order, summing to 1024; the longest is exactly 256.
All inputs are finite; a program needn't handle non-finite values.
Results may differ from the reference program's by a relative error of at most 0.0012.
Values sent between devices are 32-bit elements; how exact they have to be, the bound alone decides.
No kernel may reach another device: no remote copies, remote signals or barrier semaphores. Data moves between devices by JAX's collectives and lax.ppermute only.
A program may use at most 256 MiB of HBM per device.

```python
import math
import jax
import jax.numpy as jnp
import numpy as np
from jax import lax

H = 32
P_SIZE = 64
N = 64
GROUP = 128
DOCS = 16
LENGTH = 1024
BATCH = 4
MOST_DOC = 256


def head_rates(key):
    base_key = jax.random.fold_in(key, 101)
    slow_share = 0.5
    chooser = jax.random.uniform(jax.random.fold_in(base_key, 1), (H,), jnp.float32)
    slow_rates = jnp.exp(jax.random.uniform(jax.random.fold_in(base_key, 2), (H,), jnp.float32, jnp.log(0.25), jnp.log(2.0))) / MOST_DOC
    fast_rates = jnp.exp(jax.random.uniform(jax.random.fold_in(base_key, 3), (H,), jnp.float32, jnp.log(1.0 / 50.0), jnp.log(1.0 / 30.0)))
    return jnp.where(chooser < slow_share, slow_rates, fast_rates)


def draw_a_log(key, part):
    return 0.5 * jnp.log(head_rates(key))


def draw_step_sizes(key, part):
    head_rate = head_rates(key)
    roughness = jnp.exp(jax.random.uniform(jax.random.fold_in(key, 202), (BATCH, H, LENGTH), jnp.float32, -0.6931, 0.6931))
    return jnp.sqrt(head_rate)[None, :, None] * roughness


def block_scale(rng, dims, cuts, low, largest):
    gain, own = 1.0, jax.random.fold_in(rng, 6)
    for position, blocks in cuts:
        heights = jnp.exp(jax.random.uniform(jax.random.fold_in(own, position), (blocks,), jnp.float32, low / len(cuts), largest / len(cuts)))
        gain = gain * jnp.repeat(heights, dims[position] // blocks).reshape([-1 if axis == position else 1 for axis in range(len(dims))])
    return gain


def length_profile(count, total, bound, lean):
    weights = [(1 << 20) // math.isqrt(grade ** lean) + 1 for grade in range(2, count + 1)]
    rest, given = total - bound - (count - 1), [1] * (count - 1)
    while rest > 0:
        free = [i for i in range(count - 1) if given[i] < bound]
        pool, left = sum([weights[i] for i in free]), rest
        for i in free:
            addition = min(bound - given[i], max(1, left * weights[i] // pool), rest)
            given[i] = given[i] + addition
            rest = rest - addition
    return np.array([bound] + given)


def uneven(key, count, total, most, slope):
    if count == 2:
        one = jax.random.randint(key, (), max(1, total - most), min(most, total - 1) + 1)
        return jnp.stack([one, total - one])
    sizes = jnp.asarray(length_profile(count, total, most, slope), jnp.int32)
    pairs = (count - 1) // 2
    giver, sink = sizes[1:1 + 2 * pairs:2], sizes[2:2 + 2 * pairs:2]
    margin = jnp.minimum(giver - 1, most - sink)
    passed = jax.random.randint(jax.random.fold_in(key, 1), (pairs,), 0, 1 << 20) % (margin + 1)
    sizes = sizes.at[1:1 + 2 * pairs:2].set(giver - passed).at[2:2 + 2 * pairs:2].set(sink + passed)
    return sizes[jax.random.permutation(jax.random.fold_in(key, 2), count)]


def normal_values(own_key, extent, deviation, reach, split=(), kind=jnp.bfloat16):
    entries = deviation * jax.random.normal(own_key, extent, jnp.float32)
    if split:
        entries = entries * block_scale(own_key, extent, split, -0.22, 0.18)
    return jnp.clip(entries, -reach, reach).astype(kind)


def setup_inputs(seed: int = 0) -> dict:
    keys = jax.random.split(jax.random.key(seed), 9)
    inputs = normal_values(keys[0], (BATCH, LENGTH, H * P_SIZE), 1.0, 6.0, ((0, 4), (1, 8)))
    b_proj = normal_values(keys[1], (BATCH, LENGTH, N), N ** -0.5, 0.75, ((0, 4), (1, 8)))
    c_proj = normal_values(keys[2], (BATCH, LENGTH, N), 1.0, 6.0, ((0, 4), (1, 8)))
    step_sizes = draw_step_sizes(jax.random.fold_in(keys[8], 71), 0)
    a_log = draw_a_log(jax.random.fold_in(keys[8], 71), 0)
    skip_gain = jnp.clip(jax.random.uniform(keys[5], (H,), jnp.float32, 0.5, 1.5), 0.5, 1.5)
    doc_lengths = jax.vmap(lambda own: uneven(own, DOCS, LENGTH, MOST_DOC, 2))(jax.random.split(keys[6], BATCH)).reshape((BATCH, DOCS)).astype(jnp.int32)
    grad_out = normal_values(keys[7], (BATCH, LENGTH, H * P_SIZE), 1.0, 6.0, ((0, 4), (1, 8)))
    return {"inputs": inputs, "b_proj": b_proj, "c_proj": c_proj, "step_sizes": step_sizes, "a_log": a_log, "skip_gain": skip_gain, "doc_lengths": doc_lengths, "grad_out": grad_out}


very_negative = -1e+30
highest = lax.Precision.HIGHEST

def segment_ids(lengths, offset, row_count):
    starts = jnp.cumsum(lengths) - lengths
    places = offset + jnp.arange(row_count, dtype=jnp.int32)
    return lax.optimization_barrier(jnp.sum((starts[None, :] <= places[:, None]).astype(jnp.int32), axis=1)) - 1

def decay_logs(deltas, rate_log):
    return deltas * (-jnp.exp(rate_log))[:, None]

def intra_group(values, bvectors, cvectors, deltas, rate_log, segment):
    cumulated = jnp.cumsum(decay_logs(deltas, rate_log), axis=1)
    spread = cumulated[:, :, None] - cumulated[:, None, :]
    places = jnp.arange(segment.shape[0])
    allowed = (places[:, None] >= places[None, :]) & (segment[:, None] == segment[None, :])
    kernel = jnp.exp(jnp.where(allowed[None], spread, very_negative))
    scores = jnp.dot(cvectors, bvectors.T, precision=highest)
    weights = kernel * scores[None] * deltas[:, None, :]
    return jnp.einsum('hts,shp->thp', weights, values, precision=highest)

def group_cross(values, bvectors, cvectors, deltas, rate_log, segment, before, incoming):
    cumulated = jnp.cumsum(decay_logs(deltas, rate_log), axis=1)
    living = (segment == before).astype(cumulated.dtype)
    carried = jnp.exp(cumulated) * living[None, :]
    readout = jnp.einsum('tn,hpn->thp', cvectors, incoming, precision=highest) * jnp.transpose(carried)[:, :, None]
    ending = (segment == segment[-1]).astype(cumulated.dtype)
    keeping = jnp.exp(cumulated[:, -1:] - cumulated) * deltas * ending[None, :]
    weighted = values * jnp.transpose(keeping)[:, :, None]
    fresh_part = jnp.einsum('shp,sn->hpn', weighted, bvectors, precision=highest)
    return (readout, carried[:, -1][:, None, None] * incoming + fresh_part)

def intra_run(values, bvectors, cvectors, deltas, rate_log, segment):
    row_count = values.shape[0]
    group_count = row_count // GROUP
    pieces = (values.reshape(group_count, GROUP, values.shape[1], values.shape[2]), bvectors.reshape(group_count, GROUP, bvectors.shape[1]), cvectors.reshape(group_count, GROUP, cvectors.shape[1]), jnp.transpose(deltas.reshape(deltas.shape[0], group_count, GROUP), (1, 0, 2)), segment.reshape(group_count, GROUP))

    def within(pieces_now):
        return intra_group(pieces_now[0], pieces_now[1], pieces_now[2], pieces_now[3], rate_log, pieces_now[4])
    outcome = lax.map(jax.checkpoint(within), pieces)
    return outcome.reshape(row_count, values.shape[1], values.shape[2])

def cross_run(values, bvectors, cvectors, deltas, rate_log, segment, before, incoming):
    row_count = values.shape[0]
    group_count = row_count // GROUP
    befores = jnp.concatenate([jnp.reshape(before, (1,)).astype(jnp.int32), segment[GROUP - 1::GROUP][:-1].astype(jnp.int32)])
    pieces = (values.reshape(group_count, GROUP, values.shape[1], values.shape[2]), bvectors.reshape(group_count, GROUP, bvectors.shape[1]), cvectors.reshape(group_count, GROUP, cvectors.shape[1]), jnp.transpose(deltas.reshape(deltas.shape[0], group_count, GROUP), (1, 0, 2)), segment.reshape(group_count, GROUP), befores)

    def advance(carried_state, pieces_now):
        readout, next_state = group_cross(pieces_now[0], pieces_now[1], pieces_now[2], pieces_now[3], rate_log, pieces_now[4], pieces_now[5], carried_state)
        return (next_state, readout)
    ending_state, readout = lax.scan(jax.checkpoint(advance), incoming, pieces)
    return (readout.reshape(row_count, values.shape[1], values.shape[2]), ending_state)

def reference(inputs, b_proj, c_proj, step_sizes, a_log, skip_gain, doc_lengths, grad_out):

    def one_sequence(pieces):
        row_count = pieces[0].shape[0]
        values = pieces[0].astype(jnp.float32).reshape(row_count, H, P_SIZE)
        bvectors = pieces[1].astype(jnp.float32)
        cvectors = pieces[2].astype(jnp.float32)
        deltas = pieces[3]
        segment = segment_ids(pieces[4], jnp.int32(0), row_count)
        upstream = pieces[5].astype(jnp.float32).reshape(row_count, H, P_SIZE)
        nothing = jnp.zeros((H, P_SIZE, N), jnp.float32)
        opening = jnp.int32(-1)

        def forward(value_in, bvec_in, cvec_in, delta_in, rate_in, skip_in):
            readout, ending_state = cross_run(value_in, bvec_in, cvec_in, delta_in, rate_in, segment, opening, nothing)
            return intra_run(value_in, bvec_in, cvec_in, delta_in, rate_in, segment) + readout + skip_in[None, :, None] * value_in
        outcome, pullback = jax.vjp(forward, values, bvectors, cvectors, deltas, a_log, skip_gain)
        grads = pullback(upstream)
        return (grads[0].reshape(row_count, H * P_SIZE), grads[1], grads[2], grads[3], grads[4], grads[5])
    gradients = lax.map(one_sequence, (inputs, b_proj, c_proj, step_sizes, doc_lengths, grad_out))
    return (gradients[0].astype(jnp.bfloat16), gradients[1].astype(jnp.bfloat16), gradients[2].astype(jnp.bfloat16), gradients[3], lax.optimization_barrier(jnp.sum(gradients[4], axis=0)), lax.optimization_barrier(jnp.sum(gradients[5], axis=0)))
```

```python
import functools

import jax
import jax.numpy as jnp
from jax import lax
from jax.experimental import pallas as pl
from jax.experimental.pallas import tpu as pltpu
from jax.sharding import PartitionSpec as P

F32 = jnp.float32
BF16 = jnp.bfloat16
HIGHEST = lax.Precision.HIGHEST
LANES = 128
WIDE = 256
PARTS = WIDE // LANES
FAR = 2**30
VMEM_LIMIT = 48 * 1024 * 1024


def dot(a, b, ca, cb, precision=None):
    return lax.dot_general(
        a, b, (((ca,), (cb,)), ((), ())), precision=precision, preferred_element_type=F32
    )


def iota(shape, dim):
    return lax.broadcasted_iota(jnp.int32, shape, dim)


def split2(a):
    high = a.astype(BF16)
    return high, (a - high.astype(F32)).astype(BF16)


def split3(a):
    high = a.astype(BF16)
    rest = a - high.astype(F32)
    middle = rest.astype(BF16)
    return high, middle, (rest - middle.astype(F32)).astype(BF16)


def dot_pairs(a, b, ca, cb):
    return dot(a[0], b[0], ca, cb) + (dot(a[0], b[1], ca, cb) + dot(a[1], b[0], ca, cb))


def document_places(lens_ref, rows):
    offset = lax.axis_index("ctx") * rows
    starts = [jnp.int32(0)]
    for d in range(lens_ref.shape[1] - 1):
        starts.append(starts[-1] + lens_ref[0, d])
    first = jnp.int32(FAR)
    last = jnp.int32(0)
    for start in starts:
        first = jnp.minimum(first, jnp.where(start >= offset, start, FAR))
        last = jnp.maximum(last, jnp.where(start < offset + rows, start, 0))
    return starts, offset, first, last


def rate_column(alog_ref):
    heads = alog_ref.shape[1]
    square = jnp.broadcast_to(alog_ref[...], (heads, heads))
    picked = jnp.where(iota((heads, heads), 0) == iota((heads, heads), 1), square, 0.0)
    return -jnp.exp(jnp.sum(picked, axis=1, keepdims=True))


def head_block(heads, head_width, block, copies):
    shape = (copies * heads, WIDE)
    row = lax.rem(iota(shape, 0), heads)
    column = lax.div(iota(shape, 1) + block * WIDE, head_width)
    return jnp.where(row == column, 1.0, 0.0).astype(BF16)


def head_sums(ones, a):
    total = None
    for part in split3(a):
        term = dot(ones, part, 1, 1)
        total = term if total is None else total + term
    return total


def message_block(ref, block, width):
    at = block * PARTS
    return jnp.concatenate(
        [ref[(at + i) * width : (at + i + 1) * width, :] for i in range(PARTS)], axis=1
    )


def message_tail(ref, block, width):
    tail = ref.shape[0] // (width + 1) * width + block * PARTS
    return jnp.concatenate([ref[tail + i : tail + i + 1, :] for i in range(PARTS)], axis=1)


def received(refs, block, width):
    total = message_block(refs[-1], block, width)
    for ref in refs[-2::-1]:
        total = message_block(ref, block, width) + message_tail(ref, block, width) * total
    return total


def masked_rows(a, mask):
    return jnp.where(mask, a.astype(F32), 0.0).astype(BF16)


def states_kernel(
    lens_ref, alog_ref, dt_ref, x_ref, b_ref, dy_ref, c_ref, fwd_ref, bwd_ref, u_ref, v_ref, l_ref
):
    rows, columns = x_ref.shape[1:]
    heads, width = dt_ref.shape[1], b_ref.shape[2]
    _, offset, first, last = document_places(lens_ref, rows)
    through = jnp.where(first >= offset + rows, 1.0, 0.0)
    dt = dt_ref[0]
    decay = dt * rate_column(alog_ref)
    square = (rows, rows)
    lower = jnp.where(iota(square, 0) >= iota(square, 1), 1.0, 0.0)
    eye = jnp.where(iota(square, 0) == iota(square, 1), 1.0, 0.0)
    logs = dot(lower, decay, 1, 1, HIGHEST)
    steps = dot(eye, dt, 1, 1, HIGHEST)
    u = jnp.concatenate(split3(jnp.exp(logs)), axis=1)
    v = jnp.concatenate(split3(jnp.exp(-logs) * steps), axis=1)
    u_ref[...] = u
    v_ref[...] = v
    l_ref[...] = jnp.concatenate(split3(logs), axis=1)
    place = iota((rows, width), 0) + offset
    b_end = masked_rows(b_ref[0], place >= last)
    c_live = masked_rows(c_ref[0], place < first)
    for block in range(columns // WIDE):
        at = slice(block * WIDE, (block + 1) * WIDE)
        spread = head_block(heads, columns // heads, block, 3)
        u_wide = dot(u, spread, 1, 0)
        v_wide = dot(v, spread, 1, 0)
        x_high, x_low = split2(x_ref[0, :, at].astype(F32) * v_wide)
        y_high, y_low = split2(dy_ref[0, :, at].astype(F32) * u_wide)
        ending = u_wide[rows - 1 : rows, :]
        state = (dot(b_end, x_high, 0, 0) + dot(b_end, x_low, 0, 0)) * ending
        pulled = dot(c_live, y_high, 0, 0) + dot(c_live, y_low, 0, 0)
        kept = ending * through
        for i in range(PARTS):
            one = block * PARTS + i
            part = slice(i * LANES, (i + 1) * LANES)
            tail = columns // LANES * width + one
            fwd_ref[one * width : (one + 1) * width, :] = state[:, part]
            bwd_ref[one * width : (one + 1) * width, :] = pulled[:, part]
            fwd_ref[tail : tail + 1, :] = kept[:, part]
            bwd_ref[tail : tail + 1, :] = kept[:, part]


def inside_kernel(
    lens_ref,
    alog_ref,
    skip_ref,
    dt_ref,
    x_ref,
    b_ref,
    dy_ref,
    c_ref,
    u_ref,
    v_ref,
    l_ref,
    xh_ref,
    xl_ref,
    yh_ref,
    yl_ref,
    v_wide_ref,
    dx_ref,
    db_ref,
    dc_ref,
    dl_ref,
    sums_ref,
    fwd_ref,
    bwd_ref,
    small_ref,
):
    rows, columns = x_ref.shape[1:]
    heads, width = dt_ref.shape[1], b_ref.shape[2]
    starts, offset, first, last = document_places(lens_ref, rows)
    square = (rows, rows)
    place0, place1 = iota(square, 0) + offset, iota(square, 1) + offset
    segment0, segment1 = jnp.zeros(square, jnp.int32), jnp.zeros(square, jnp.int32)
    for start in starts:
        segment0 += jnp.where(place0 >= start, 1, 0)
        segment1 += jnp.where(place1 >= start, 1, 0)
    same = segment0 == segment1
    down = same & (place0 >= place1)
    scores = jnp.where(down, dot(c_ref[0], b_ref[0], 1, 1), 0.0)
    flipped = jnp.where(same & (place1 >= place0), dot(b_ref[0], c_ref[0], 1, 1), 0.0)
    scores, flipped = split2(scores), split2(flipped)
    place = iota((rows, width), 0) + offset
    b_end = masked_rows(b_ref[0], place >= last)
    c_live = masked_rows(c_ref[0], place < first)
    skips = jnp.concatenate(split3(jnp.broadcast_to(skip_ref[...], (16, heads))), axis=1)
    d_scores = jnp.zeros(square, F32)
    dl = jnp.zeros((heads, rows), F32)
    sums = jnp.zeros((heads, rows), F32)
    small = jnp.zeros((heads, 8), F32)
    for block in range(columns // WIDE):
        at = slice(block * WIDE, (block + 1) * WIDE)
        spread = head_block(heads, columns // heads, block, 3)
        ones = spread[:heads]
        u_wide = dot(u_ref[...], spread, 1, 0)
        v_wide = dot(v_ref[...], spread, 1, 0)
        l_wide = dot(l_ref[...], spread, 1, 0)
        skip_wide = dot(skips, spread, 1, 0)[:1]
        x = x_ref[0, :, at].astype(F32)
        dy = dy_ref[0, :, at].astype(F32)
        xv = x * v_wide
        yu = dy * u_wide
        xs, ys = split2(xv), split2(yu)
        xh_ref[:, at], xl_ref[:, at] = xs
        yh_ref[:, at], yl_ref[:, at] = ys
        v_wide_ref[:, at] = v_wide
        out = dot_pairs(scores, xs, 1, 0)
        back = dot_pairs(flipped, ys, 1, 0)
        d_scores += dot_pairs(ys, xs, 1, 1)
        dx_ref[:, at] = v_wide * back + skip_wide * dy
        column_part = xv * back
        dl += head_sums(ones, yu * out - column_part)
        sums += head_sums(ones, column_part)
        small += head_sums(
            ones, jnp.broadcast_to(jnp.sum(x * dy, axis=0, keepdims=True), (8, WIDE))
        )
        ending = u_wide[rows - 1 : rows, :]
        end_log = l_wide[rows - 1 : rows, :]
        fwd_ref[:, at] = sum(dot(b_end, p, 0, 0) for p in split2(xv * (end_log - l_wide))) * ending
        bwd_ref[:, at] = sum(dot(c_live, p, 0, 0) for p in split2(yu * l_wide))
    d_scores = split2(jnp.where(down, d_scores, 0.0))
    dc_ref[...] = sum(dot(p, b_ref[0], 1, 0) for p in d_scores)
    db_ref[...] = sum(dot(p, c_ref[0], 0, 0) for p in d_scores)
    dl_ref[...] = dl
    sums_ref[...] = sums
    decay = dt_ref[0] * rate_column(alog_ref)
    lower = jnp.where(iota(square, 0) <= iota(square, 1), 1.0, 0.0)
    logs = dot(decay, lower, 1, 0, HIGHEST)
    rate_grad = jnp.sum(logs * dl, axis=1, keepdims=True)
    lane = iota((heads, LANES), 1)
    small_ref[...] = jnp.where(lane == 0, rate_grad, jnp.where(lane == 1, small[:, :1], 0.0))


def rates_kernel(reach, *refs):
    fwds, bwds = refs[:reach], refs[reach : 2 * reach]
    own_ref, u_ref, l_ref, fwd_ref, bwd_ref, small_ref, out_ref = refs[2 * reach :]
    width, columns = fwd_ref.shape
    heads = small_ref.shape[0]
    rows = u_ref.shape[0]
    total = jnp.zeros((heads, 8), F32)
    for block in range(columns // WIDE):
        at = slice(block * WIDE, (block + 1) * WIDE)
        spread = head_block(heads, columns // heads, block, 3)
        end_log = dot(l_ref[rows - 16 : rows, :], spread, 1, 0)[15:16]
        came = received(fwds, block, width)
        pull = received(bwds, block, width)
        kept = message_tail(own_ref, block, width) * end_log
        terms = came * bwd_ref[:, at] + pull * (fwd_ref[:, at] + kept * came)
        whole = jnp.sum(terms, axis=0, keepdims=True)
        total += head_sums(spread[:heads], jnp.broadcast_to(whole, (8, WIDE)))
    lane = iota((heads, LANES), 1)
    small = small_ref[...]
    small = small + jnp.where(lane == 0, total[:, :1], 0.0)
    shape = (heads, LANES)
    pick = iota(shape, 0) == lane
    shifted = iota(shape, 0) + heads == lane
    rate = jnp.sum(jnp.where(pick, small[:, 0:1], 0.0), axis=0, keepdims=True)
    skip = jnp.sum(jnp.where(shifted, small[:, 1:2], 0.0), axis=0, keepdims=True)
    out_ref[...] = rate + skip


def outputs_kernel(reach, *refs):
    fwds, bwds = refs[:reach], refs[reach : 2 * reach]
    (
        lens_ref,
        alog_ref,
        dt_ref,
        own_ref,
        b_ref,
        c_ref,
        u_ref,
        xh_ref,
        xl_ref,
        yh_ref,
        yl_ref,
        v_wide_ref,
        dx_ref,
        db_ref,
        dc_ref,
        dl_ref,
        sums_ref,
        dx_out,
        db_out,
        dc_out,
        dt_out,
    ) = refs[2 * reach :]
    rows, columns = dx_ref.shape
    heads, width = dt_ref.shape[1], b_ref.shape[2]
    _, offset, first, last = document_places(lens_ref, rows)
    place = iota((rows, width), 0) + offset
    ends, lives = place >= last, place < first
    b_end = masked_rows(b_ref[0], ends)
    c_live = masked_rows(c_ref[0], lives)
    dl = dl_ref[...]
    cross = jnp.zeros((heads, rows), F32)
    corner = jnp.zeros((heads, 8), F32)
    dc = jnp.zeros((rows, width), F32)
    db = jnp.zeros((rows, width), F32)
    for block in range(columns // WIDE):
        at = slice(block * WIDE, (block + 1) * WIDE)
        spread = head_block(heads, columns // heads, block, 3)
        ones = spread[:heads]
        ending = dot(u_ref[rows - 16 : rows, :], spread, 1, 0)[15:16]
        came = received(fwds, block, width)
        pull = received(bwds, block, width)
        kept = message_tail(own_ref, block, width)
        meet = jnp.sum(came * pull, axis=0, keepdims=True) * kept
        corner += head_sums(ones, jnp.broadcast_to(meet, (8, WIDE)))
        cames, pulls = split2(came), split2(pull * ending)
        xs = xh_ref[:, at], xl_ref[:, at]
        ys = yh_ref[:, at], yl_ref[:, at]
        out = sum(dot(c_live, p, 1, 0) for p in cames)
        back = sum(dot(b_end, p, 1, 0) for p in pulls)
        column_part = (xs[0].astype(F32) + xs[1].astype(F32)) * back
        row_part = (ys[0].astype(F32) + ys[1].astype(F32)) * out
        dl += head_sums(ones, row_part - column_part)
        cross += head_sums(ones, column_part)
        dc += dot_pairs(ys, cames, 1, 1)
        db += dot_pairs(xs, pulls, 1, 1)
        dx_out[0, :, at] = (dx_ref[:, at] + v_wide_ref[:, at] * back).astype(BF16)
    dc_out[0] = (dc_ref[...] + jnp.where(lives, dc, 0.0)).astype(BF16)
    db_out[0] = (db_ref[...] + jnp.where(ends, db, 0.0)).astype(BF16)
    square = (rows, rows)
    upper = jnp.where(iota(square, 0) >= iota(square, 1), 1.0, 0.0)
    at_end = jnp.sum(cross, axis=1, keepdims=True) + corner[:, :1]
    d_decay = dot(dl, upper, 1, 0, HIGHEST) + at_end
    dt_out[0] = (sums_ref[...] + cross) / dt_ref[0] + rate_column(alog_ref) * d_decay


def call(kernel, outs, kinds, flops, moved):
    specs = [
        pl.BlockSpec(memory_space=pltpu.SMEM if kind else pltpu.VMEM) for kind in kinds
    ]
    return pl.pallas_call(
        kernel,
        out_shape=[jax.ShapeDtypeStruct(*out) for out in outs],
        in_specs=specs,
        out_specs=[pl.BlockSpec(memory_space=pltpu.VMEM)] * len(outs),
        compiler_params=pltpu.CompilerParams(vmem_limit_bytes=VMEM_LIMIT),
        cost_estimate=pl.CostEstimate(flops=flops, bytes_accessed=moved, transcendentals=0),
    )


def shift(a, axis, by):
    count = lax.axis_size(axis)
    pairs = [(i, i + by) for i in range(count) if 0 <= i + by < count]
    return lax.ppermute(a, axis, pairs)


def sum_over(a, axis):
    count = lax.axis_size(axis)
    parts = [a] + [
        lax.ppermute(a, axis, [(i, i ^ other) for i in range(count)]) for other in range(1, count)
    ]
    while len(parts) > 1:
        parts = [parts[i] + parts[i + 1] for i in range(0, len(parts), 2)]
    return parts[0]


def per_device(inputs, b_proj, c_proj, step_sizes, a_log, skip_gain, doc_lengths, grad_out):
    rows, columns = inputs.shape[1:]
    heads, width = a_log.shape[0], b_proj.shape[2]
    reach = max(lax.axis_size("ctx") // 4, 1)
    alog, skip = a_log[None], skip_gain[None]
    message = ((columns // LANES * (width + 1), LANES), F32)
    table = ((rows, 3 * heads), BF16)
    state = ((width, columns), F32)
    wide16, wide32 = ((rows, columns), BF16), ((rows, columns), F32)
    narrow = ((rows, width), F32)
    per_head = ((heads, rows), F32)
    small = ((heads, LANES), F32)

    fwd, bwd, u, v, logs = call(
        states_kernel, [message, message, table, table, table], [1] + [0] * 6, 10**9, 4 * 2**20
    )(doc_lengths, alog, step_sizes, inputs, b_proj, grad_out, c_proj)
    fwds = [shift(fwd, "ctx", by) for by in range(1, reach + 1)]
    bwds = [shift(bwd, "ctx", -by) for by in range(1, reach + 1)]
    xh, xl, yh, yl, v_wide, dx, db, dc, dl, sums, fwd_logs, bwd_logs, parts = call(
        inside_kernel,
        [wide16] * 4 + [wide32] * 2 + [narrow] * 2 + [per_head] * 2 + [state] * 2 + [small],
        [1] + [0] * 10,
        4 * 10**9,
        12 * 2**20,
    )(doc_lengths, alog, skip, step_sizes, inputs, b_proj, grad_out, c_proj, u, v, logs)
    (partial,) = call(
        functools.partial(rates_kernel, reach),
        [((1, LANES), F32)],
        [0] * (2 * reach + 6),
        10**8,
        4 * 2**20,
    )(*fwds, *bwds, fwd, u, logs, fwd_logs, bwd_logs, parts)
    totals = sum_over(sum_over(partial[0], "dp"), "ctx")
    input_grads, b_gradient, c_gradient, step_grads = call(
        functools.partial(outputs_kernel, reach),
        [
            ((1, rows, columns), BF16),
            ((1, rows, width), BF16),
            ((1, rows, width), BF16),
            ((1, heads, rows), F32),
        ],
        [0] * (2 * reach) + [1] + [0] * 16,
        2 * 10**9,
        12 * 2**20,
    )(
        *fwds,
        *bwds,
        doc_lengths,
        alog,
        step_sizes,
        fwd,
        b_proj,
        c_proj,
        u,
        xh,
        xl,
        yh,
        yl,
        v_wide,
        dx,
        db,
        dc,
        dl,
        sums,
    )
    return (
        input_grads,
        b_gradient,
        c_gradient,
        step_grads,
        totals[:heads],
        totals[heads : 2 * heads],
    )


def solution(mesh):
    in_specs = (
        P("dp", "ctx", None),
        P("dp", "ctx", None),
        P("dp", "ctx", None),
        P("dp", None, "ctx"),
        P(),
        P(),
        P("dp", None),
        P("dp", "ctx", None),
    )
    out_specs = (
        P("dp", "ctx", None),
        P("dp", "ctx", None),
        P("dp", "ctx", None),
        P("dp", None, "ctx"),
        P(),
        P(),
    )
    return jax.shard_map(
        per_device, mesh=mesh, in_specs=in_specs, out_specs=out_specs, check_vma=False
    )
```

```python
import functools

import jax
import jax.numpy as jnp
from jax import lax
from jax.experimental import pallas as pl
from jax.experimental.pallas import tpu as pltpu
from jax.sharding import PartitionSpec as P

F32 = jnp.float32
BF16 = jnp.bfloat16
LANES = 128
WIDE = 256
PARTS = WIDE // LANES
FAR = 2**30


def dot(a, b, ca, cb):
    return lax.dot_general(a, b, (((ca,), (cb,)), ((), ())), preferred_element_type=F32)


def iota(shape, dim):
    return lax.broadcasted_iota(jnp.int32, shape, dim)


def split2(a):
    high = a.astype(BF16)
    return high, (a - high.astype(F32)).astype(BF16)


def split3(a):
    high = a.astype(BF16)
    rest = a - high.astype(F32)
    middle = rest.astype(BF16)
    return high, middle, (rest - middle.astype(F32)).astype(BF16)


def dot_pairs(a, b, ca, cb):
    return dot(a[0], b[0], ca, cb) + (dot(a[0], b[1], ca, cb) + dot(a[1], b[0], ca, cb))


def stack(parts, axis):
    return jnp.concatenate(parts, axis=axis)


def document_places(lens_ref, rows):
    offset = lax.axis_index("ctx") * rows
    starts = [jnp.int32(0)]
    for d in range(lens_ref.shape[1] - 1):
        starts.append(starts[-1] + lens_ref[0, d])
    first = jnp.int32(FAR)
    last = jnp.int32(0)
    for start in starts:
        first = jnp.minimum(first, jnp.where(start >= offset, start, FAR))
        last = jnp.maximum(last, jnp.where(start < offset + rows, start, 0))
    return starts, offset, first, last


def rate_column(alog_ref):
    heads = alog_ref.shape[1]
    square = jnp.broadcast_to(alog_ref[...], (heads, heads))
    picked = jnp.where(iota((heads, heads), 0) == iota((heads, heads), 1), square, 0.0)
    return -jnp.exp(jnp.sum(picked, axis=1, keepdims=True))


def log2(size):
    assert size & (size - 1) == 0
    return size.bit_length() - 1


def head_distance(heads, head_width):
    shape = (3 * heads, WIDE)
    return (iota(shape, 0) & (heads - 1)) - lax.shift_right_logical(
        iota(shape, 1), log2(head_width)
    )


def head_rows(distance, head_width, block):
    return jnp.where(distance == block * (WIDE // head_width), 1.0, 0.0).astype(BF16)


def head_columns(heads, head_width, block):
    shape = (WIDE, heads)
    column = lax.shift_right_logical(iota(shape, 0), log2(head_width))
    return jnp.where(iota(shape, 1) - column == block * (WIDE // head_width), 1.0, 0.0).astype(BF16)


def is_odd(distance):
    return lax.rem(lax.div(lax.axis_index("ctx"), distance), 2)


def message_block(ref, block, width):
    at = block * PARTS
    return stack([ref[(at + i) * width : (at + i + 1) * width, :] for i in range(PARTS)], 1)


def message_tail(ref, block, width):
    tail = ref.shape[0] // (width + 1) * width + block * PARTS
    return stack([ref[tail + i : tail + i + 1, :] for i in range(PARTS)], 1)


def received(refs, block, width):
    came = pull = None
    for j in range(len(refs) // 2, 0, -1):
        one, two = refs[2 * j - 2], refs[2 * j - 1]
        a, b = message_block(one, block, width), message_block(two, block, width)
        odd = jnp.broadcast_to(is_odd(j), a.shape) == 1
        near_came, near_pull = jnp.where(odd, a, b), jnp.where(odd, b, a)
        if came is None:
            came, pull = near_came, near_pull
        else:
            a, b = message_tail(one, block, width), message_tail(two, block, width)
            odd = jnp.broadcast_to(is_odd(j), a.shape) == 1
            came = near_came + jnp.where(odd, a, b) * came
            pull = near_pull + jnp.where(odd, b, a) * pull
    return came, pull


def masked(a, mask):
    return jnp.where(mask, a.astype(F32), 0.0).astype(BF16)


def states_kernel(
    reach, lens_ref, alog_ref, dt_hbm, x_hbm, b_hbm, dy_hbm, c_hbm, u_ref, v_ref, l_ref, *refs
):
    dt_ref, x_ref, b_ref, dy_ref, c_ref = refs[:5]
    payloads = refs[5 : 5 + 2 * reach]
    small_sems, sems = refs[5 + 2 * reach :]
    rows, columns = x_ref.shape
    heads, width = dt_ref.shape[0], b_ref.shape[0]
    pieces = sems.shape[1]
    piece = columns // pieces
    small = [
        pltpu.make_async_copy(source.at[0], target, small_sems.at[i])
        for i, (source, target) in enumerate(((dt_hbm, dt_ref), (b_hbm, b_ref), (c_hbm, c_ref)))
    ]
    for copy in small:
        copy.start()
    large = []
    for i in range(pieces):
        at = slice(i * piece, (i + 1) * piece)
        for side, (source, target) in enumerate(((x_hbm, x_ref), (dy_hbm, dy_ref))):
            copy = pltpu.make_async_copy(
                source.at[0, :, at], target.at[:, at], sems.at[side, i]
            )
            copy.start()
            large.append(copy)
    _, offset, first, last = document_places(lens_ref, rows)
    through = jnp.where(first >= offset + rows, 1.0, 0.0)
    rate = rate_column(alog_ref)
    square = (rows, rows)
    lower = jnp.where(iota(square, 0) >= iota(square, 1), 1.0, 0.0).astype(BF16)
    eye = jnp.where(iota(square, 0) == iota(square, 1), 1.0, 0.0).astype(BF16)
    distance = head_distance(heads, columns // heads)
    place = iota((width, rows), 1) + offset
    for copy in small:
        copy.wait()
    dt = dt_ref[...]
    logs = sum(dot(lower, part, 1, 1) for part in split3(dt * rate))
    steps = sum(dot(eye, part, 1, 1) for part in split3(dt))
    u = stack(split3(jnp.exp(logs)), 1)
    v = stack(split3(jnp.exp(-logs) * steps), 1)
    u_ref[...] = u
    v_ref[...] = v
    l_ref[...] = stack(split3(logs), 1)
    both = stack([u, v], 0)
    b_end = masked(b_ref[...], place >= last)
    c_live = masked(c_ref[...], place < first)
    b_end, c_live = stack([b_end, b_end], 1), stack([c_live, c_live], 1)
    for block in range(columns // WIDE):
        if block * WIDE % piece == 0:
            large[block * WIDE // piece * 2].wait()
            large[block * WIDE // piece * 2 + 1].wait()
        at = slice(block * WIDE, (block + 1) * WIDE)
        wide = dot(both, head_rows(distance, columns // heads, block), 1, 0)
        u_wide, v_wide = wide[:rows], wide[rows:]
        ending = u_wide[rows - 1 : rows, :]
        state = dot(b_end, stack(split2(x_ref[:, at].astype(F32) * v_wide), 0), 1, 0) * ending
        pulled = dot(c_live, stack(split2(dy_ref[:, at].astype(F32) * u_wide), 0), 1, 0)
        kept = ending * through
        for j in range(1, reach + 1):
            odd = jnp.broadcast_to(is_odd(j), state.shape) == 1
            for ref, value in zip(
                payloads[2 * j - 2 : 2 * j],
                (jnp.where(odd, pulled, state), jnp.where(odd, state, pulled)),
            ):
                for i in range(PARTS):
                    one = block * PARTS + i
                    part = slice(i * LANES, (i + 1) * LANES)
                    tail = columns // LANES * width + one
                    ref[one * width : (one + 1) * width, :] = value[:, part]
                    ref[tail : tail + 1, :] = kept[:, part]


def inside_kernel(
    lens_ref,
    alog_ref,
    skip_ref,
    dt_ref,
    x_ref,
    b_ref,
    dy_ref,
    c_ref,
    u_ref,
    v_ref,
    l_ref,
    xs_ref,
    ys_ref,
    v_wide_ref,
    dx_ref,
    b_end_ref,
    c_live_ref,
    db_ref,
    dc_ref,
    sums_ref,
    fwd_ref,
    bwd_ref,
    ends_ref,
    small_ref,
):
    rows, columns = x_ref.shape
    heads, width = dt_ref.shape[0], b_ref.shape[0]
    head_width = columns // heads
    starts, offset, first, last = document_places(lens_ref, rows)
    through = jnp.where(first >= offset + rows, 1.0, 0.0)
    square = (rows, rows)
    place0, place1 = iota(square, 0) + offset, iota(square, 1) + offset
    segment0, segment1 = jnp.zeros(square, jnp.int32), jnp.zeros(square, jnp.int32)
    for start in starts:
        segment0 += jnp.where(place0 >= start, 1, 0)
        segment1 += jnp.where(place1 >= start, 1, 0)
    same = segment0 == segment1
    down = same & (place0 >= place1)
    bt, ct = b_ref[...], c_ref[...]
    scores = split2(jnp.where(down, dot(ct, bt, 0, 0), 0.0))
    flipped = split2(jnp.where(same & (place1 >= place0), dot(bt, ct, 0, 0), 0.0))
    place = iota((width, rows), 1) + offset
    bt_end = masked(bt, place >= last)
    ct_live = masked(ct, place < first)
    b_end = jnp.transpose(bt_end.astype(F32)).astype(BF16)
    c_live = jnp.transpose(ct_live.astype(F32)).astype(BF16)
    b_end_ref[...] = stack([b_end, b_end], 1)
    c_live_ref[...] = stack([c_live, c_live], 1)
    bt_end, ct_live = stack([bt_end, bt_end], 1), stack([ct_live, ct_live], 1)
    skips = stack(split3(jnp.broadcast_to(skip_ref[...], (16, heads))), 1)
    tables = stack([u_ref[...], v_ref[...], l_ref[...], skips], 0)
    distance = head_distance(heads, head_width)
    d_scores = jnp.zeros(square, F32)
    sums = jnp.zeros((2 * rows, heads), F32)
    products = jnp.zeros((8, heads), F32)
    for block in range(columns // WIDE):
        at = slice(block * WIDE, (block + 1) * WIDE)
        wide = dot(tables, head_rows(distance, head_width, block), 1, 0)
        ones = head_columns(heads, head_width, block)
        u_wide, v_wide, l_wide = wide[:rows], wide[rows : 2 * rows], wide[2 * rows : 3 * rows]
        skip_wide = wide[3 * rows : 3 * rows + 1]
        x = x_ref[:, at].astype(F32)
        dy = dy_ref[:, at].astype(F32)
        xv = x * v_wide
        yu = dy * u_wide
        xs, ys = split2(xv), split2(yu)
        xs_ref[:, at] = stack(xs, 0)
        ys_ref[:, at] = stack(ys, 0)
        v_wide_ref[:, at] = v_wide
        out = dot_pairs(scores, xs, 1, 0)
        back = dot_pairs(flipped, ys, 1, 0)
        d_scores += dot_pairs(ys, xs, 1, 1)
        dx_ref[:, at] = v_wide * back + skip_wide * dy
        column_part = xv * back
        for part in split3(stack([yu * out - column_part, column_part], 0)):
            sums += dot(part, ones, 1, 0)
        product = jnp.broadcast_to(jnp.sum(x * dy, axis=0, keepdims=True), (8, WIDE))
        for part in split3(product):
            products += dot(part, ones, 1, 0)
        ending = u_wide[rows - 1 : rows]
        end_log = l_wide[rows - 1 : rows]
        fwd_ref[:, at] = (
            dot(bt_end, stack(split2(xv * (end_log - l_wide)), 0), 1, 0) * ending
        )
        bwd_ref[:, at] = dot(ct_live, stack(split2(yu * l_wide), 0), 1, 0)
        ends_ref[0:1, at] = ending
        ends_ref[1:2, at] = ending * through
        ends_ref[2:3, at] = ending * through * end_log
    d_scores = split2(jnp.where(down, d_scores, 0.0))
    dc_ref[...] = sum(dot(bt, p, 1, 1) for p in d_scores)
    db_ref[...] = sum(dot(ct, p, 1, 0) for p in d_scores)
    sums_ref[...] = sums
    logs = l_ref[...].astype(F32)
    logs = (logs[:, :heads] + logs[:, heads : 2 * heads]) + logs[:, 2 * heads :]
    rate_grads = jnp.sum(logs * sums[:rows], axis=0, keepdims=True)
    empty = jnp.zeros((1, LANES - 2 * heads), F32)
    small_ref[...] = stack([rate_grads, products[:1], empty], 1)


def rates_kernel(reach, head_width, *refs):
    messages = refs[: 2 * reach]
    ends_ref, fwd_ref, bwd_ref, small_ref, out_ref = refs[2 * reach :]
    width, columns = fwd_ref.shape
    blocks = columns // WIDE
    whole = []
    for block in range(blocks):
        at = slice(block * WIDE, (block + 1) * WIDE)
        came, pull = received(messages, block, width)
        terms = came * bwd_ref[:, at] + pull * (fwd_ref[:, at] + ends_ref[2:3, at] * came)
        whole.append(jnp.sum(terms, axis=0, keepdims=True))
    whole = stack(whole, 0)
    own = WIDE // (head_width)
    shape = (WIDE, LANES)
    column = lax.shift_right_logical(iota(shape, 0), log2(head_width))
    ones = jnp.where(column == (iota(shape, 1) & (own - 1)), 1.0, 0.0).astype(BF16)
    sums = sum(dot(part, ones, 1, 0) for part in split3(whole))
    lane = iota(sums.shape, 1)
    mine = lax.shift_right_logical(lane, log2(own)) == iota(sums.shape, 0)
    total = small_ref[...] + jnp.sum(jnp.where(mine, sums, 0.0), axis=0, keepdims=True)
    out_ref[...] = jnp.broadcast_to(total, out_ref.shape)


def outputs_kernel(reach, *refs):
    messages = refs[: 2 * reach]
    (
        alog_ref,
        lens_ref,
        dt_ref,
        ends_ref,
        xs_ref,
        ys_ref,
        v_wide_ref,
        dx_ref,
        b_end_ref,
        c_live_ref,
        db_ref,
        dc_ref,
        sums_ref,
        dx_out,
        db_out,
        dc_out,
        dt_out,
    ) = refs[2 * reach :]
    rows, columns = dx_ref.shape
    heads, width = dt_ref.shape[0], db_ref.shape[0]
    head_width = columns // heads
    _, offset, first, last = document_places(lens_ref, rows)
    b_end, c_live = b_end_ref[...], c_live_ref[...]
    sums = sums_ref[...]
    own_sums = sums[rows:]
    dc = jnp.zeros((2 * width, 2 * rows), F32)
    db = jnp.zeros((2 * width, 2 * rows), F32)
    at_last = iota((rows, WIDE), 0) == rows - 1
    for block in range(columns // WIDE):
        at = slice(block * WIDE, (block + 1) * WIDE)
        ones = head_columns(heads, head_width, block)
        came, pull = received(messages, block, width)
        meet = jnp.sum(came * pull, axis=0, keepdims=True) * ends_ref[1:2, at]
        cames = stack(split2(came), 0)
        pulls = stack(split2(pull * ends_ref[0:1, at]), 0)
        xs, ys = xs_ref[:, at], ys_ref[:, at]
        out = dot(c_live, cames, 1, 0)
        back = dot(b_end, pulls, 1, 0)
        column_part = (xs[:rows].astype(F32) + xs[rows:].astype(F32)) * back
        row_part = (ys[:rows].astype(F32) + ys[rows:].astype(F32)) * out
        row_part = jnp.where(at_last, row_part + meet, row_part)
        for part in split2(stack([row_part - column_part, column_part], 0)):
            sums += dot(part, ones, 1, 0)
        dc += dot(cames, ys, 1, 1)
        db += dot(pulls, xs, 1, 1)
        dx_out[0, :, at] = (dx_ref[:, at] + v_wide_ref[:, at] * back).astype(BF16)
    place = iota((width, rows), 1) + offset
    dc = (dc[:width, :rows] + dc[:width, rows:]) + dc[width:, :rows]
    db = (db[:width, :rows] + db[:width, rows:]) + db[width:, :rows]
    dc_out[0] = (dc_ref[...] + jnp.where(place < first, dc, 0.0)).astype(BF16)
    db_out[0] = (db_ref[...] + jnp.where(place >= last, db, 0.0)).astype(BF16)
    square = (rows, rows)
    upper = jnp.where(iota(square, 0) >= iota(square, 1), 1.0, 0.0).astype(BF16)
    eye = jnp.where(iota(square, 0) == iota(square, 1), 1.0, 0.0).astype(BF16)
    at_end = jnp.sum(sums[rows:] - own_sums, axis=0, keepdims=True)
    dl = sums[:rows] + jnp.where(iota((rows, heads), 0) == rows - 1, at_end, 0.0)
    d_decay = sum(dot(part, upper, 0, 0) for part in split3(dl))
    total = sum(dot(part, eye, 0, 0) for part in split3(sums[rows:]))
    dt_out[0] = total / dt_ref[...] + rate_column(alog_ref) * d_decay


def call(kernel, reach, outs, kinds, flops, moved, scratch=()):
    spaces = {"s": pltpu.SMEM, "v": pltpu.VMEM, "h": pltpu.HBM}
    return pl.pallas_call(
        kernel,
        out_shape=[jax.ShapeDtypeStruct(*out) for out in outs],
        in_specs=[pl.BlockSpec(memory_space=spaces[kind]) for kind in kinds],
        out_specs=[pl.BlockSpec(memory_space=pltpu.VMEM)] * len(outs),
        scratch_shapes=scratch,
        compiler_params=pltpu.CompilerParams(
            vmem_limit_bytes=min(14 + 2 * reach, 56) * 2**20
        ),
        cost_estimate=pl.CostEstimate(flops=flops, bytes_accessed=moved, transcendentals=0),
    )


def swap(a, by, second):
    count = lax.axis_size("ctx")
    pairs = []
    for i in range(count - by):
        if i // by % 2 == second:
            pairs += [(i, i + by), (i + by, i)]
    return lax.ppermute(a, "ctx", pairs)


def per_device(inputs, b_proj, c_proj, step_sizes, a_log, skip_gain, doc_lengths, grad_out):
    rows, columns = inputs.shape[1:]
    heads, width = a_log.shape[0], b_proj.shape[2]
    reach = max(lax.axis_size("ctx") // 4, 1)
    devices = lax.axis_size("ctx") * lax.axis_size("dp")
    alog, skip = a_log[None], skip_gain[None]
    bt, ct = jnp.swapaxes(b_proj, 1, 2), jnp.swapaxes(c_proj, 1, 2)
    message = ((columns // LANES * (width + 1), LANES), F32)
    table = ((rows, 3 * heads), BF16)
    state = ((width, columns), F32)
    wide = ((rows, columns), F32)
    doubled = ((2 * rows, columns), BF16)
    half = ((rows, columns), BF16)
    transposed = ((width, rows), F32)
    pieces = 4

    u, v, logs, dt, x, b, dy, c, *payloads = call(
        functools.partial(states_kernel, reach),
        reach,
        [table] * 3
        + [((heads, rows), F32), half, ((width, rows), BF16), half, ((width, rows), BF16)]
        + [message] * (2 * reach),
        "svhhhhh",
        10**9,
        4 * 2**20,
        [pltpu.SemaphoreType.DMA((3,)), pltpu.SemaphoreType.DMA((2, pieces))],
    )(
        doc_lengths,
        alog,
        *(
            pltpu.with_memory_space_constraint(a, pltpu.HBM)
            for a in (step_sizes, inputs, bt, grad_out, ct)
        ),
    )
    messages = [None] * (2 * reach)
    for j in range(reach, 0, -1):
        for second in (1, 0):
            at = 2 * j - 2 + second
            messages[at] = swap(payloads[at], j, second)
    xs, ys, v_wide, dx, b_end, c_live, db, dc, sums, fwd_logs, bwd_logs, ends, small = call(
        inside_kernel,
        reach,
        [doubled, doubled, wide, wide]
        + [((rows, 2 * width), BF16)] * 2
        + [transposed] * 2
        + [((2 * rows, heads), F32), state, state, ((8, columns), F32), ((1, LANES), F32)],
        "s" + "v" * 10,
        4 * 10**9,
        12 * 2**20,
    )(doc_lengths, alog, skip, dt, x, b, dy, c, u, v, logs)
    (partial,) = call(
        functools.partial(rates_kernel, reach, columns // heads),
        reach,
        [((devices, LANES), F32)],
        "v" * (2 * reach + 4),
        10**8,
        4 * 2**20,
    )(*messages, ends, fwd_logs, bwd_logs, small)
    gathered = lax.all_to_all(partial, ("dp", "ctx"), 0, 0, tiled=True)
    totals = jnp.sum(gathered, axis=0)
    input_grads, b_gradient, c_gradient, step_grads = call(
        functools.partial(outputs_kernel, reach),
        reach,
        [
            ((1, rows, columns), BF16),
            ((1, width, rows), BF16),
            ((1, width, rows), BF16),
            ((1, heads, rows), F32),
        ],
        "v" * (2 * reach) + "vs" + "v" * 11,
        2 * 10**9,
        12 * 2**20,
    )(
        *messages,
        alog,
        doc_lengths,
        dt,
        ends,
        xs,
        ys,
        v_wide,
        dx,
        b_end,
        c_live,
        db,
        dc,
        sums,
    )
    return (
        input_grads,
        jnp.swapaxes(b_gradient, 1, 2),
        jnp.swapaxes(c_gradient, 1, 2),
        step_grads,
        totals[:heads],
        totals[heads : 2 * heads],
    )


def solution(mesh):
    in_specs = (
        P("dp", "ctx", None),
        P("dp", "ctx", None),
        P("dp", "ctx", None),
        P("dp", None, "ctx"),
        P(),
        P(),
        P("dp", None),
        P("dp", "ctx", None),
    )
    out_specs = (
        P("dp", "ctx", None),
        P("dp", "ctx", None),
        P("dp", "ctx", None),
        P("dp", None, "ctx"),
        P(),
        P(),
    )
    return jax.shard_map(
        per_device, mesh=mesh, in_specs=in_specs, out_specs=out_specs, check_vma=False
    )
```

```python
import functools

import jax
import jax.numpy as jnp
from jax import lax
from jax.experimental import pallas as pl
from jax.experimental.pallas import tpu as pltpu
from jax.sharding import PartitionSpec as P

F32 = jnp.float32
BF16 = jnp.bfloat16
LANES = 128
WIDE = 256
PARTS = WIDE // LANES
FAR = 2**30


def dot(a, b, ca, cb):
    return lax.dot_general(a, b, (((ca,), (cb,)), ((), ())), preferred_element_type=F32)


def iota(shape, dim):
    return lax.broadcasted_iota(jnp.int32, shape, dim)


def split2(a):
    high = a.astype(BF16)
    return high, (a - high.astype(F32)).astype(BF16)


def split3(a):
    high = a.astype(BF16)
    rest = a - high.astype(F32)
    middle = rest.astype(BF16)
    return high, middle, (rest - middle.astype(F32)).astype(BF16)


def dot_pairs(a, b, ca, cb):
    return dot(a[0], b[0], ca, cb) + (dot(a[0], b[1], ca, cb) + dot(a[1], b[0], ca, cb))


def stack(parts, axis):
    return jnp.concatenate(parts, axis=axis)


def document_places(lens_ref, rows):
    offset = lax.axis_index("ctx") * rows
    starts = [jnp.int32(0)]
    for d in range(lens_ref.shape[1] - 1):
        starts.append(starts[-1] + lens_ref[0, d])
    first = jnp.int32(FAR)
    last = jnp.int32(0)
    for start in starts:
        first = jnp.minimum(first, jnp.where(start >= offset, start, FAR))
        last = jnp.maximum(last, jnp.where(start < offset + rows, start, 0))
    return starts, offset, first, last


def rate_column(alog_ref):
    heads = alog_ref.shape[1]
    square = jnp.broadcast_to(alog_ref[...], (heads, heads))
    picked = jnp.where(iota((heads, heads), 0) == iota((heads, heads), 1), square, 0.0)
    return -jnp.exp(jnp.sum(picked, axis=1, keepdims=True))


def log2(size):
    assert size & (size - 1) == 0
    return size.bit_length() - 1


def head_distance(heads, head_width):
    shape = (3 * heads, WIDE)
    return (iota(shape, 0) & (heads - 1)) - lax.shift_right_logical(
        iota(shape, 1), log2(head_width)
    )


def head_rows(distance, head_width, block):
    return jnp.where(distance == block * (WIDE // head_width), 1.0, 0.0).astype(BF16)


def head_columns(heads, head_width, block):
    shape = (WIDE, heads)
    column = lax.shift_right_logical(iota(shape, 0), log2(head_width))
    return jnp.where(iota(shape, 1) - column == block * (WIDE // head_width), 1.0, 0.0).astype(BF16)


def is_odd(distance):
    return lax.rem(lax.div(lax.axis_index("ctx"), distance), 2)


def message_block(ref, block, width):
    at = block * PARTS
    return stack([ref[(at + i) * width : (at + i + 1) * width, :] for i in range(PARTS)], 1)


def message_tail(ref, block, width):
    tail = ref.shape[0] // (width + 1) * width + block * PARTS
    return stack([ref[tail + i : tail + i + 1, :] for i in range(PARTS)], 1)


def received(refs, block, width):
    came = pull = None
    for j in range(len(refs) // 2, 0, -1):
        one, two = refs[2 * j - 2], refs[2 * j - 1]
        a, b = message_block(one, block, width), message_block(two, block, width)
        odd = jnp.broadcast_to(is_odd(j), a.shape) == 1
        near_came, near_pull = jnp.where(odd, a, b), jnp.where(odd, b, a)
        if came is None:
            came, pull = near_came, near_pull
        else:
            a, b = message_tail(one, block, width), message_tail(two, block, width)
            odd = jnp.broadcast_to(is_odd(j), a.shape) == 1
            came = near_came + jnp.where(odd, a, b) * came
            pull = near_pull + jnp.where(odd, b, a) * pull
    return came, pull


def states_kernel(
    reach,
    sets,
    lens_hbm,
    alog_hbm,
    dt_hbm,
    x_hbm,
    b_hbm,
    dy_hbm,
    c_hbm,
    dt_ref,
    x_ref,
    b_ref,
    dy_ref,
    c_ref,
    *refs,
):
    payloads, (lens_ref, alog_ref, small_sems, sems) = refs[:-4], refs[-4:]
    rows, columns = x_ref.shape
    heads, width = dt_ref.shape[0], b_ref.shape[0]
    head_width = columns // heads
    pieces = sems.shape[1]
    piece = columns // pieces
    small = [
        pltpu.make_async_copy(source, target, small_sems.at[i])
        for i, (source, target) in enumerate(
            (
                (lens_hbm, lens_ref),
                (alog_hbm, alog_ref),
                (dt_hbm.at[0], dt_ref),
                (b_hbm.at[0], b_ref),
                (c_hbm.at[0], c_ref),
            )
        )
    ]
    for copy in small:
        copy.start()
    large = []
    for i in range(pieces):
        at = slice(i * piece, (i + 1) * piece)
        for side, (source, target) in enumerate(((x_hbm, x_ref), (dy_hbm, dy_ref))):
            copy = pltpu.make_async_copy(
                source.at[0, :, at], target.at[:, at], sems.at[side, i]
            )
            copy.start()
            large.append(copy)
    square = (rows, rows)
    upper = jnp.where(iota(square, 0) <= iota(square, 1), 1.0, 0.0).astype(BF16)
    odds = [
        jnp.broadcast_to(is_odd(j), (width, LANES)) == 1 for j in range(1, reach + 1)
    ]
    left = iota((1, LANES), 1) < head_width
    for copy in small:
        copy.wait()
    _, offset, first, last = document_places(lens_ref, rows)
    through = jnp.where(first >= offset + rows, 1.0, 0.0)
    dt = dt_ref[...]
    logs = sum(dot(part, upper, 1, 0) for part in split3(dt * rate_column(alog_ref)))
    end_log = logs[:, rows - 1 : rows]
    place = iota((heads, rows), 1) + offset
    keeping = jnp.where(place >= last, jnp.exp(end_log - logs) * dt, 0.0)
    carried = jnp.where(place < first, jnp.exp(logs), 0.0)
    kept = jnp.broadcast_to(jnp.exp(end_log) * through, (heads, LANES))
    b, c = b_ref[...].astype(F32), c_ref[...].astype(F32)
    own = LANES // head_width

    def pair_states(vectors, weights, values, pair):
        parts = []
        for h in range(own):
            row = weights[pair * own + h : pair * own + h + 1, :]
            parts += split2(vectors * row)
        out = dot(stack(parts, 0), values, 1, 0)
        sides = [
            out[2 * h * width : (2 * h + 1) * width]
            + out[(2 * h + 1) * width : (2 * h + 2) * width]
            for h in range(own)
        ]
        return jnp.where(left, sides[0], sides[1])

    done = 0
    for one, size in enumerate(sets):
        messages = payloads[2 * reach * one : 2 * reach * (one + 1)]
        for i in range(size * PARTS):
            pair = done * PARTS + i
            if pair * LANES % piece == 0:
                large[pair * LANES // piece * 2].wait()
                large[pair * LANES // piece * 2 + 1].wait()
            at = slice(pair * LANES, (pair + 1) * LANES)
            state = pair_states(b, keeping, x_ref[:, at], pair)
            pulled = pair_states(c, carried, dy_ref[:, at], pair)
            here = kept[pair * own : (pair + 1) * own]
            tail = jnp.where(left, here[:1], here[1:])
            for j in range(reach):
                values = jnp.where(odds[j], pulled, state), jnp.where(odds[j], state, pulled)
                for ref, value in zip(messages[2 * j : 2 * j + 2], values):
                    ref[i * width : (i + 1) * width, :] = value
                    ref[size * PARTS * width + i : size * PARTS * width + i + 1, :] = tail
        done += size


def inside_kernel(
    lens_ref,
    alog_ref,
    skip_ref,
    dt_ref,
    x_ref,
    b_ref,
    dy_ref,
    c_ref,
    xs_ref,
    ys_ref,
    v_wide_ref,
    dx_ref,
    b_end_ref,
    c_live_ref,
    masks_ref,
    db_ref,
    dc_ref,
    sums_ref,
    logs_ref,
    ends_ref,
    small_ref,
):
    rows, columns = x_ref.shape
    heads, width = dt_ref.shape[0], b_ref.shape[0]
    head_width = columns // heads
    starts, offset, first, last = document_places(lens_ref, rows)
    through = jnp.where(first >= offset + rows, 1.0, 0.0)
    square = (rows, rows)
    place0, place1 = iota(square, 0) + offset, iota(square, 1) + offset
    segment0, segment1 = jnp.zeros(square, jnp.int32), jnp.zeros(square, jnp.int32)
    for start in starts:
        segment0 += jnp.where(place0 >= start, 1, 0)
        segment1 += jnp.where(place1 >= start, 1, 0)
    same = segment0 == segment1
    down = same & (place0 >= place1)
    lower = jnp.where(place0 >= place1, 1.0, 0.0).astype(BF16)
    eye = jnp.where(place0 == place1, 1.0, 0.0).astype(BF16)
    dt = dt_ref[...]
    logs = sum(dot(lower, part, 1, 1) for part in split3(dt * rate_column(alog_ref)))
    steps = sum(dot(eye, part, 1, 1) for part in split3(dt))
    logs_ref[...] = logs
    bt, ct = b_ref[...], c_ref[...]
    scores = split2(jnp.where(down, dot(ct, bt, 0, 0), 0.0))
    flipped = split2(jnp.where(same & (place1 >= place0), dot(bt, ct, 0, 0), 0.0))
    place = iota((width, rows), 1) + offset
    b_end = jnp.transpose(jnp.where(place >= last, bt.astype(F32), 0.0)).astype(BF16)
    c_live = jnp.transpose(jnp.where(place < first, ct.astype(F32), 0.0)).astype(BF16)
    b_end_ref[...] = stack([b_end, b_end], 1)
    c_live_ref[...] = stack([c_live, c_live], 1)
    masks_ref[0:width] = jnp.where(place >= last, 1.0, 0.0)
    masks_ref[width : 2 * width] = jnp.where(place < first, 1.0, 0.0)
    tables = stack(
        [
            stack(split3(a), 1)
            for a in (
                jnp.exp(logs),
                jnp.exp(-logs) * steps,
                jnp.broadcast_to(skip_ref[...], (16, heads)),
            )
        ],
        0,
    )
    distance = head_distance(heads, head_width)
    d_scores = jnp.zeros(square, F32)
    sums = jnp.zeros((2 * rows, heads), F32)
    products = jnp.zeros((8, heads), F32)
    for block in range(columns // WIDE):
        at = slice(block * WIDE, (block + 1) * WIDE)
        wide = dot(tables, head_rows(distance, head_width, block), 1, 0)
        ones = head_columns(heads, head_width, block)
        u_wide, v_wide = wide[:rows], wide[rows : 2 * rows]
        skip_wide = wide[2 * rows : 2 * rows + 1]
        x = x_ref[:, at].astype(F32)
        dy = dy_ref[:, at].astype(F32)
        xv = x * v_wide
        yu = dy * u_wide
        xs, ys = split2(xv), split2(yu)
        xs_ref[:, at] = stack(xs, 0)
        ys_ref[:, at] = stack(ys, 0)
        v_wide_ref[:, at] = v_wide
        out = dot_pairs(scores, xs, 1, 0)
        back = dot_pairs(flipped, ys, 1, 0)
        d_scores += dot_pairs(ys, xs, 1, 1)
        dx_ref[:, at] = v_wide * back + skip_wide * dy
        column_part = xv * back
        for part in split3(stack([yu * out - column_part, column_part], 0)):
            sums += dot(part, ones, 1, 0)
        product = jnp.broadcast_to(jnp.sum(x * dy, axis=0, keepdims=True), (8, WIDE))
        for part in split3(product):
            products += dot(part, ones, 1, 0)
        ending = u_wide[rows - 1 : rows]
        ends_ref[0:1, at] = ending
        ends_ref[1:2, at] = ending * through
    d_scores = split2(jnp.where(down, d_scores, 0.0))
    dc_ref[...] = sum(dot(bt, p, 1, 1) for p in d_scores)
    db_ref[...] = sum(dot(ct, p, 1, 0) for p in d_scores)
    sums_ref[...] = sums
    small_ref[...] = products


def cross_kernel(start, size, final, *refs):
    (
        ends_ref,
        xs_ref,
        ys_ref,
        v_wide_ref,
        dx_ref,
        b_end_ref,
        c_live_ref,
        masks_ref,
        db_ref,
        dc_ref,
        sums_ref,
    ) = refs[:11]
    own_ref, logs_ref, alog_ref, dt_ref, small_ref = refs[11:16] if final else [None] * 5
    rest = refs[16:] if final else refs[11:]
    outs = 5 if final else 4
    rest, (stage_ref, sems) = rest[:-2], rest[-2:]
    messages = rest[(1 if start else 0) * final : len(rest) - outs]
    dx_out, db_out, dc_out, last_out, *partial_out = rest[len(rest) - outs :]
    rows, columns = dx_ref.shape
    heads, width = sums_ref.shape[1], db_ref.shape[0]
    head_width = columns // heads
    b_end, c_live = b_end_ref[...], c_live_ref[...]
    sums = sums_ref[...]
    dc = jnp.zeros((2 * width, 2 * rows), F32)
    db = jnp.zeros((2 * width, 2 * rows), F32)
    at_last = iota((rows, WIDE), 0) == rows - 1
    copies = []
    for i in range(size):
        block = start + i
        at = slice(block * WIDE, (block + 1) * WIDE)
        own = slice(i * WIDE, (i + 1) * WIDE)
        ones = head_columns(heads, head_width, block)
        came, pull = received(messages, i, width)
        meet = jnp.sum(came * pull, axis=0, keepdims=True) * ends_ref[1:2, at]
        cames = stack(split2(came), 0)
        pulls = stack(split2(pull * ends_ref[0:1, at]), 0)
        xs, ys = xs_ref[:, at], ys_ref[:, at]
        out = dot(c_live, cames, 1, 0)
        back = dot(b_end, pulls, 1, 0)
        stage_ref[:, own] = (dx_ref[:, at] + v_wide_ref[:, at] * back).astype(BF16)
        copy = pltpu.make_async_copy(stage_ref.at[:, own], dx_out.at[0, :, at], sems.at[i])
        copy.start()
        copies.append(copy)
        column_part = (xs[:rows].astype(F32) + xs[rows:].astype(F32)) * back
        row_part = (ys[:rows].astype(F32) + ys[rows:].astype(F32)) * out
        row_part = jnp.where(at_last, row_part + meet, row_part)
        for part in split3(stack([row_part - column_part, column_part], 0)):
            sums += dot(part, ones, 1, 0)
        dc += dot(cames, ys, 1, 1)
        db += dot(pulls, xs, 1, 1)
    dc = (dc[:width, :rows] + dc[:width, rows:]) + dc[width:, :rows]
    db = (db[:width, :rows] + db[:width, rows:]) + db[width:, :rows]
    db = db_ref[...] + masks_ref[0:width] * db
    dc = dc_ref[...] + masks_ref[width : 2 * width] * dc
    if final:
        db_out[0] = db.astype(BF16)
        dc_out[0] = dc.astype(BF16)
        square = (rows, rows)
        upper = jnp.where(iota(square, 0) >= iota(square, 1), 1.0, 0.0).astype(BF16)
        eye = jnp.where(iota(square, 0) == iota(square, 1), 1.0, 0.0).astype(BF16)
        at_end = jnp.sum(sums[rows:] - own_ref[rows:], axis=0, keepdims=True)
        dl = sums[:rows] + jnp.where(iota((rows, heads), 0) == rows - 1, at_end, 0.0)
        d_decay = sum(dot(part, upper, 0, 0) for part in split3(dl))
        total = sum(dot(part, eye, 0, 0) for part in split3(sums[rows:]))
        last_out[0] = total / dt_ref[...] + rate_column(alog_ref) * d_decay
        rate_grads = jnp.sum(logs_ref[...] * dl, axis=0, keepdims=True)
        empty = jnp.zeros((1, LANES - 2 * heads), F32)
        row = stack([rate_grads, small_ref[:1], empty], 1)
        partial_out[0][...] = jnp.broadcast_to(row, partial_out[0].shape)
    else:
        db_out[...] = db
        dc_out[...] = dc
        last_out[...] = sums
    for copy in copies:
        copy.wait()


def call(kernel, reach, outs, ins, flops, moved, scratch=(), aliases=None):
    spaces = {"s": pltpu.SMEM, "v": pltpu.VMEM, "h": pltpu.HBM}
    return pl.pallas_call(
        kernel,
        out_shape=[jax.ShapeDtypeStruct(*out) for _, out in outs],
        in_specs=[pl.BlockSpec(memory_space=spaces[place]) for place, _ in ins],
        out_specs=[pl.BlockSpec(memory_space=spaces[place]) for place, _ in outs],
        scratch_shapes=scratch,
        input_output_aliases=aliases or {},
        compiler_params=pltpu.CompilerParams(vmem_limit_bytes=min(16 + 2 * reach, 56) * 2**20),
        cost_estimate=pl.CostEstimate(flops=flops, bytes_accessed=moved, transcendentals=0),
    )(*(a for _, a in ins))


def swap(a, by, second):
    count = lax.axis_size("ctx")
    pairs = []
    for i in range(count - by):
        if i // by % 2 == second:
            pairs += [(i, i + by), (i + by, i)]
    return lax.ppermute(a, "ctx", pairs)


def in_hbm(a):
    return "h", pltpu.with_memory_space_constraint(a, pltpu.HBM)


def per_device(inputs, b_proj, c_proj, step_sizes, a_log, skip_gain, doc_lengths, grad_out):
    rows, columns = inputs.shape[1:]
    heads, width = a_log.shape[0], b_proj.shape[2]
    reach = max(lax.axis_size("ctx") // 4, 1)
    devices = lax.axis_size("ctx") * lax.axis_size("dp")
    alog, skip = a_log[None], skip_gain[None]
    bt, ct = jnp.swapaxes(b_proj, 1, 2), jnp.swapaxes(c_proj, 1, 2)
    blocks = columns // WIDE
    sets = (blocks,)
    pieces = 4

    def v(shape, kind=F32):
        return "v", (shape, kind)

    transposed = v((width, rows))
    per_token = v((2 * rows, heads))

    dt, x, b, dy, c, *payloads = call(
        functools.partial(states_kernel, reach, sets),
        reach,
        [
            v((heads, rows)),
            v((rows, columns), BF16),
            v((width, rows), BF16),
            v((rows, columns), BF16),
            v((width, rows), BF16),
        ]
        + [v((size * PARTS * (width + 1), LANES)) for size in sets for _ in range(2 * reach)],
        [in_hbm(a) for a in (doc_lengths, alog, step_sizes, inputs, bt, grad_out, ct)],
        10**9,
        4 * 2**20,
        [
            pltpu.SMEM(doc_lengths.shape, jnp.int32),
            pltpu.VMEM(alog.shape, F32),
            pltpu.SemaphoreType.DMA((5,)),
            pltpu.SemaphoreType.DMA((2, pieces)),
        ],
    )
    messages = [None] * len(payloads)
    for at in range(len(payloads) - 1, -1, -1):
        messages[at] = swap(payloads[at], at % (2 * reach) // 2 + 1, at % 2)
    xs, ys, v_wide, dx, b_end, c_live, masks, db, dc, own_sums, logs, ends, small = call(
        inside_kernel,
        reach,
        [v((2 * rows, columns), BF16)] * 2
        + [v((rows, columns))] * 2
        + [v((rows, 2 * width), BF16)] * 2
        + [v((2 * width, rows)), transposed, transposed, per_token]
        + [v((rows, heads)), v((8, columns)), v((8, heads))],
        [("s", doc_lengths)] + [("v", a) for a in (alog, skip, dt, x, b, dy, c)],
        4 * 10**9,
        12 * 2**20,
    )
    whole = "h", ((1, rows, columns), BF16)
    sums, input_grads = own_sums, None
    start = 0
    for one, size in enumerate(sets):
        final = one == len(sets) - 1
        outs = [whole, transposed, transposed, per_token]
        ins = [ends, xs, ys, v_wide, dx, b_end, c_live, masks, db, dc, sums]
        if final:
            ins += [own_sums, logs, alog, dt, small] + [input_grads] * (one > 0)
            narrow = v((1, width, rows), BF16)
            outs = [whole, narrow, narrow, v((1, heads, rows)), v((devices, LANES))]
        ins = [("h" if a is input_grads else "v", a) for a in ins]
        ins += [("v", a) for a in messages[2 * reach * one : 2 * reach * (one + 1)]]
        results = call(
            functools.partial(cross_kernel, start, size, final),
            reach,
            outs,
            ins,
            10**9,
            8 * 2**20,
            [pltpu.VMEM((rows, size * WIDE), BF16), pltpu.SemaphoreType.DMA((size,))],
            {16: 0} if final and one else None,
        )
        start += size
        if not final:
            input_grads, db, dc, sums = results
    input_grads, b_gradient, c_gradient, step_grads, partial = results
    gathered = lax.all_to_all(partial, ("dp", "ctx"), 0, 0, tiled=True)
    totals = jnp.sum(gathered, axis=0)
    return (
        input_grads,
        jnp.swapaxes(b_gradient, 1, 2),
        jnp.swapaxes(c_gradient, 1, 2),
        step_grads,
        totals[:heads],
        totals[heads : 2 * heads],
    )


def solution(mesh):
    in_specs = (
        P("dp", "ctx", None),
        P("dp", "ctx", None),
        P("dp", "ctx", None),
        P("dp", None, "ctx"),
        P(),
        P(),
        P("dp", None),
        P("dp", "ctx", None),
    )
    out_specs = (
        P("dp", "ctx", None),
        P("dp", "ctx", None),
        P("dp", "ctx", None),
        P("dp", None, "ctx"),
        P(),
        P(),
    )
    return jax.shard_map(
        per_device, mesh=mesh, in_specs=in_specs, out_specs=out_specs, check_vma=False
    )
```

```python
import functools

import jax
import jax.numpy as jnp
from jax import lax
from jax.experimental import pallas as pl
from jax.experimental.pallas import tpu as pltpu
from jax.sharding import PartitionSpec as P

F32 = jnp.float32
BF16 = jnp.bfloat16
LANES = 128
WIDE = 256
PARTS = WIDE // LANES
FAR = 2**30


def dot(a, b, ca, cb):
    return lax.dot_general(a, b, (((ca,), (cb,)), ((), ())), preferred_element_type=F32)


def iota(shape, dim):
    return lax.broadcasted_iota(jnp.int32, shape, dim)


def split2(a):
    high = a.astype(BF16)
    return high, (a - high.astype(F32)).astype(BF16)


def split3(a):
    high = a.astype(BF16)
    rest = a - high.astype(F32)
    middle = rest.astype(BF16)
    return high, middle, (rest - middle.astype(F32)).astype(BF16)


def dot_pairs(a, b, ca, cb):
    return dot(a[0], b[0], ca, cb) + (dot(a[0], b[1], ca, cb) + dot(a[1], b[0], ca, cb))


def stack(parts, axis):
    return jnp.concatenate(parts, axis=axis)


def document_places(lens_ref, rows):
    offset = lax.axis_index("ctx") * rows
    starts = [jnp.int32(0)]
    for d in range(lens_ref.shape[1] - 1):
        starts.append(starts[-1] + lens_ref[0, d])
    first = jnp.int32(FAR)
    last = jnp.int32(0)
    for start in starts:
        first = jnp.minimum(first, jnp.where(start >= offset, start, FAR))
        last = jnp.maximum(last, jnp.where(start < offset + rows, start, 0))
    return starts, offset, first, last


def rate_column(alog_ref):
    heads = alog_ref.shape[1]
    square = jnp.broadcast_to(alog_ref[...], (heads, heads))
    picked = jnp.where(iota((heads, heads), 0) == iota((heads, heads), 1), square, 0.0)
    return -jnp.exp(jnp.sum(picked, axis=1, keepdims=True))


def log2(size):
    assert size & (size - 1) == 0
    return size.bit_length() - 1


def head_distance(heads, head_width):
    shape = (3 * heads, WIDE)
    return (iota(shape, 0) & (heads - 1)) - lax.shift_right_logical(
        iota(shape, 1), log2(head_width)
    )


def head_rows(distance, head_width, block):
    return jnp.where(distance == block * (WIDE // head_width), 1.0, 0.0).astype(BF16)


def head_columns(heads, head_width, block):
    shape = (WIDE, heads)
    column = lax.shift_right_logical(iota(shape, 0), log2(head_width))
    return jnp.where(iota(shape, 1) - column == block * (WIDE // head_width), 1.0, 0.0).astype(BF16)


def is_odd(distance):
    return lax.rem(lax.div(lax.axis_index("ctx"), distance), 2)


def message_block(ref, block, width):
    at = block * PARTS
    return stack([ref[(at + i) * width : (at + i + 1) * width, :] for i in range(PARTS)], 1)


def message_tail(ref, block, width):
    tail = ref.shape[0] // (width + 1) * width + block * PARTS
    return stack([ref[tail + i : tail + i + 1, :] for i in range(PARTS)], 1)


def received(refs, block, width):
    came = pull = None
    for j in range(len(refs) // 2, 0, -1):
        one, two = refs[2 * j - 2], refs[2 * j - 1]
        a, b = message_block(one, block, width), message_block(two, block, width)
        odd = jnp.broadcast_to(is_odd(j), a.shape) == 1
        near_came, near_pull = jnp.where(odd, a, b), jnp.where(odd, b, a)
        if came is None:
            came, pull = near_came, near_pull
        else:
            a, b = message_tail(one, block, width), message_tail(two, block, width)
            odd = jnp.broadcast_to(is_odd(j), a.shape) == 1
            came = near_came + jnp.where(odd, a, b) * came
            pull = near_pull + jnp.where(odd, b, a) * pull
    return came, pull


def states_kernel(
    reach,
    lens_hbm,
    alog_hbm,
    dt_hbm,
    x_hbm,
    b_hbm,
    dy_hbm,
    c_hbm,
    dt_ref,
    x_ref,
    b_ref,
    dy_ref,
    c_ref,
    *refs,
):
    payloads, (lens_ref, alog_ref, small_sems, sems) = refs[:-4], refs[-4:]
    rows, columns = x_ref.shape
    heads, width = dt_ref.shape[0], b_ref.shape[0]
    head_width = columns // heads
    pieces = sems.shape[1]
    piece = columns // pieces
    small = [
        pltpu.make_async_copy(source, target, small_sems.at[i])
        for i, (source, target) in enumerate(
            (
                (lens_hbm, lens_ref),
                (alog_hbm, alog_ref),
                (dt_hbm.at[0], dt_ref),
                (b_hbm.at[0], b_ref),
                (c_hbm.at[0], c_ref),
            )
        )
    ]
    for copy in small:
        copy.start()
    large = []
    for i in range(pieces):
        at = slice(i * piece, (i + 1) * piece)
        for side, (source, target) in enumerate(((x_hbm, x_ref), (dy_hbm, dy_ref))):
            copy = pltpu.make_async_copy(
                source.at[0, :, at], target.at[:, at], sems.at[side, i]
            )
            copy.start()
            large.append(copy)
    square = (rows, rows)
    upper = jnp.where(iota(square, 0) <= iota(square, 1), 1.0, 0.0).astype(BF16)
    odds = [
        jnp.broadcast_to(is_odd(j), (width, LANES)) == 1 for j in range(1, reach + 1)
    ]
    left = iota((1, LANES), 1) < head_width
    for copy in small:
        copy.wait()
    _, offset, first, last = document_places(lens_ref, rows)
    through = jnp.where(first >= offset + rows, 1.0, 0.0)
    dt = dt_ref[...]
    logs = sum(dot(part, upper, 1, 0) for part in split3(dt * rate_column(alog_ref)))
    end_log = logs[:, rows - 1 : rows]
    place = iota((heads, rows), 1) + offset
    keeping = jnp.where(place >= last, jnp.exp(end_log - logs) * dt, 0.0)
    carried = jnp.where(place < first, jnp.exp(logs), 0.0)
    kept = jnp.broadcast_to(jnp.exp(end_log) * through, (heads, LANES))
    b, c = b_ref[...].astype(F32), c_ref[...].astype(F32)
    own = LANES // head_width

    def pair_states(vectors, weights, values, pair):
        parts = []
        for h in range(own):
            row = weights[pair * own + h : pair * own + h + 1, :]
            parts += split2(vectors * row)
        out = dot(stack(parts, 0), values, 1, 0)
        sides = [
            out[2 * h * width : (2 * h + 1) * width]
            + out[(2 * h + 1) * width : (2 * h + 2) * width]
            for h in range(own)
        ]
        return jnp.where(left, sides[0], sides[1])

    for pair in range(columns // LANES):
        if pair * LANES % piece == 0:
            large[pair * LANES // piece * 2].wait()
            large[pair * LANES // piece * 2 + 1].wait()
        at = slice(pair * LANES, (pair + 1) * LANES)
        state = pair_states(b, keeping, x_ref[:, at], pair)
        pulled = pair_states(c, carried, dy_ref[:, at], pair)
        here = kept[pair * own : (pair + 1) * own]
        tail = columns // LANES * width + pair
        for j in range(reach):
            values = jnp.where(odds[j], pulled, state), jnp.where(odds[j], state, pulled)
            for ref, value in zip(payloads[2 * j : 2 * j + 2], values):
                ref[pair * width : (pair + 1) * width, :] = value
                ref[tail : tail + 1, :] = jnp.where(left, here[:1], here[1:])


def inside_kernel(
    lens_ref,
    alog_ref,
    skip_ref,
    dt_ref,
    x_ref,
    b_ref,
    dy_ref,
    c_ref,
    xs_ref,
    ys_ref,
    v_wide_hbm,
    dx_hbm,
    b_end_ref,
    c_live_ref,
    masks_ref,
    db_ref,
    dc_ref,
    sums_ref,
    fwd_ref,
    bwd_ref,
    ends_ref,
    small_ref,
    v_stage,
    dx_stage,
    sems,
):
    rows, columns = x_ref.shape
    heads, width = dt_ref.shape[0], b_ref.shape[0]
    head_width = columns // heads
    starts, offset, first, last = document_places(lens_ref, rows)
    through = jnp.where(first >= offset + rows, 1.0, 0.0)
    square = (rows, rows)
    place0, place1 = iota(square, 0) + offset, iota(square, 1) + offset
    segment0, segment1 = jnp.zeros(square, jnp.int32), jnp.zeros(square, jnp.int32)
    for start in starts:
        segment0 += jnp.where(place0 >= start, 1, 0)
        segment1 += jnp.where(place1 >= start, 1, 0)
    same = segment0 == segment1
    down = same & (place0 >= place1)
    lower = jnp.where(place0 >= place1, 1.0, 0.0).astype(BF16)
    eye = jnp.where(place0 == place1, 1.0, 0.0).astype(BF16)
    dt = dt_ref[...]
    logs = sum(dot(lower, part, 1, 1) for part in split3(dt * rate_column(alog_ref)))
    steps = sum(dot(eye, part, 1, 1) for part in split3(dt))
    bt, ct = b_ref[...], c_ref[...]
    scores = split2(jnp.where(down, dot(ct, bt, 0, 0), 0.0))
    flipped = split2(jnp.where(same & (place1 >= place0), dot(bt, ct, 0, 0), 0.0))
    place = iota((width, rows), 1) + offset
    bt_end = jnp.where(place >= last, bt.astype(F32), 0.0)
    ct_live = jnp.where(place < first, ct.astype(F32), 0.0)
    b_end, c_live = jnp.transpose(bt_end).astype(BF16), jnp.transpose(ct_live).astype(BF16)
    bt_end, ct_live = bt_end.astype(BF16), ct_live.astype(BF16)
    b_end_ref[...] = stack([b_end, b_end], 1)
    c_live_ref[...] = stack([c_live, c_live], 1)
    bt_end, ct_live = stack([bt_end, bt_end], 1), stack([ct_live, ct_live], 1)
    masks_ref[0:1] = jnp.where(place[:1] >= last, 1.0, 0.0)
    masks_ref[1:2] = jnp.where(place[:1] < first, 1.0, 0.0)
    tables = stack(
        [
            stack(split3(a), 1)
            for a in (
                jnp.exp(logs),
                jnp.exp(-logs) * steps,
                logs,
                jnp.broadcast_to(skip_ref[...], (16, heads)),
            )
        ],
        0,
    )
    distance = head_distance(heads, head_width)
    d_scores = jnp.zeros(square, F32)
    sums = jnp.zeros((2 * rows, heads), F32)
    products = jnp.zeros((8, heads), F32)
    copies = []
    for block in range(columns // WIDE):
        at = slice(block * WIDE, (block + 1) * WIDE)
        wide = dot(tables, head_rows(distance, head_width, block), 1, 0)
        ones = head_columns(heads, head_width, block)
        u_wide, v_wide, l_wide = wide[:rows], wide[rows : 2 * rows], wide[2 * rows : 3 * rows]
        skip_wide = wide[3 * rows : 3 * rows + 1]
        x = x_ref[:, at].astype(F32)
        dy = dy_ref[:, at].astype(F32)
        xv = x * v_wide
        yu = dy * u_wide
        xs, ys = split2(xv), split2(yu)
        xs_ref[:, at] = stack(xs, 0)
        ys_ref[:, at] = stack(ys, 0)
        v_stage[:, at] = v_wide
        out = dot_pairs(scores, xs, 1, 0)
        back = dot_pairs(flipped, ys, 1, 0)
        d_scores += dot_pairs(ys, xs, 1, 1)
        dx_stage[:, at] = v_wide * back + skip_wide * dy
        for i, (stage, target) in enumerate(((v_stage, v_wide_hbm), (dx_stage, dx_hbm))):
            copy = pltpu.make_async_copy(stage.at[:, at], target.at[:, at], sems.at[i, block])
            copy.start()
            copies.append(copy)
        column_part = xv * back
        for part in split3(stack([yu * out - column_part, column_part], 0)):
            sums += dot(part, ones, 1, 0)
        product = jnp.broadcast_to(jnp.sum(x * dy, axis=0, keepdims=True), (8, WIDE))
        for part in split3(product):
            products += dot(part, ones, 1, 0)
        ending = u_wide[rows - 1 : rows]
        end_log = l_wide[rows - 1 : rows]
        gap = end_log - l_wide
        fwd_ref[:, at] = dot(bt_end, stack(split2(xv * gap), 0), 1, 0) * ending
        bwd_ref[:, at] = dot(ct_live, stack(split2(yu * l_wide), 0), 1, 0)
        ends_ref[0:1, at] = ending
        ends_ref[1:2, at] = ending * through
        ends_ref[2:3, at] = ending * through * end_log
    d_scores = split2(jnp.where(down, d_scores, 0.0))
    dc_ref[...] = sum(dot(bt, p, 1, 1) for p in d_scores)
    db_ref[...] = sum(dot(ct, p, 1, 0) for p in d_scores)
    sums_ref[...] = sums
    rate_grads = jnp.sum(logs * sums[:rows], axis=0, keepdims=True)
    empty = jnp.zeros((1, LANES - 2 * heads), F32)
    small_ref[...] = stack([rate_grads, products[:1], empty], 1)
    for copy in copies:
        copy.wait()


def swap_order(reach):
    return [0, *range(2, 2 * reach), 1]


def rates_kernel(reach, head_width, *refs):
    messages = [ref for _, ref in sorted(zip(swap_order(reach), refs), key=lambda pair: pair[0])]
    ends_ref, fwd_ref, bwd_ref, small_ref, out_ref, came_ref, pull_ref = refs[2 * reach :]
    width, columns = fwd_ref.shape
    blocks = columns // WIDE
    whole = []
    for block in range(blocks):
        at = slice(block * WIDE, (block + 1) * WIDE)
        came, pull = received(messages, block, width)
        came_ref[:, at] = came
        pull_ref[:, at] = pull
        terms = came * bwd_ref[:, at] + pull * (fwd_ref[:, at] + ends_ref[2:3, at] * came)
        whole.append(jnp.sum(terms, axis=0, keepdims=True))
    own = WIDE // head_width
    shape = (WIDE, LANES)
    column = lax.shift_right_logical(iota(shape, 0), log2(head_width))
    ones = jnp.where(column == (iota(shape, 1) & (own - 1)), 1.0, 0.0).astype(BF16)
    sums = sum(dot(part, ones, 1, 0) for part in split3(stack(whole, 0)))
    lane = iota(sums.shape, 1)
    mine = lax.shift_right_logical(lane, log2(own)) == iota(sums.shape, 0)
    total = small_ref[...] + jnp.sum(jnp.where(mine, sums, 0.0), axis=0, keepdims=True)
    out_ref[...] = jnp.broadcast_to(total, out_ref.shape)


def outputs_kernel(
    came_ref,
    pull_ref,
    ends_ref,
    xs_ref,
    ys_ref,
    v_wide_hbm,
    dx_hbm,
    b_end_ref,
    c_live_ref,
    masks_ref,
    db_ref,
    dc_ref,
    sums_ref,
    alog_ref,
    dt_ref,
    dx_out,
    db_out,
    dc_out,
    dt_out,
    v_stage,
    dx_stage,
    stage,
    in_sems,
    out_sems,
):
    rows, columns = dx_hbm.shape
    heads, width = dt_ref.shape[0], db_ref.shape[0]
    blocks = columns // WIDE
    copies = []
    for block in range(blocks):
        at = slice(block * WIDE, (block + 1) * WIDE)
        for i, (source, target) in enumerate(((v_wide_hbm, v_stage), (dx_hbm, dx_stage))):
            copy = pltpu.make_async_copy(
                source.at[:, at], target.at[:, at], in_sems.at[i, block]
            )
            copy.start()
            copies.append(copy)
    b_end, c_live = b_end_ref[...], c_live_ref[...]
    own_sums = sums_ref[...]
    sums = own_sums
    dc = jnp.zeros((2 * width, 2 * rows), F32)
    db = jnp.zeros((2 * width, 2 * rows), F32)
    at_last = iota((rows, WIDE), 0) == rows - 1
    sent = []
    for block in range(blocks):
        at = slice(block * WIDE, (block + 1) * WIDE)
        ones = head_columns(heads, columns // heads, block)
        came, pull = came_ref[:, at], pull_ref[:, at]
        meet = jnp.sum(came * pull, axis=0, keepdims=True) * ends_ref[1:2, at]
        cames = stack(split2(came), 0)
        pulls = stack(split2(pull * ends_ref[0:1, at]), 0)
        xs, ys = xs_ref[:, at], ys_ref[:, at]
        out = dot(c_live, cames, 1, 0)
        back = dot(b_end, pulls, 1, 0)
        column_part = (xs[:rows].astype(F32) + xs[rows:].astype(F32)) * back
        row_part = (ys[:rows].astype(F32) + ys[rows:].astype(F32)) * out
        row_part = jnp.where(at_last, row_part + meet, row_part)
        for part in split2(stack([row_part - column_part, column_part], 0)):
            sums += dot(part, ones, 1, 0)
        dc += dot(cames, ys, 1, 1)
        db += dot(pulls, xs, 1, 1)
        copies[2 * block].wait()
        copies[2 * block + 1].wait()
        stage[:, at] = (dx_stage[:, at] + v_stage[:, at] * back).astype(BF16)
        copy = pltpu.make_async_copy(stage.at[:, at], dx_out.at[0, :, at], out_sems.at[block])
        copy.start()
        sent.append(copy)
    dc = (dc[:width, :rows] + dc[:width, rows:]) + dc[width:, :rows]
    db = (db[:width, :rows] + db[:width, rows:]) + db[width:, :rows]
    db_out[0] = (db_ref[...] + masks_ref[0:1] * db).astype(BF16)
    dc_out[0] = (dc_ref[...] + masks_ref[1:2] * dc).astype(BF16)
    square = (rows, rows)
    upper = jnp.where(iota(square, 0) >= iota(square, 1), 1.0, 0.0).astype(BF16)
    eye = jnp.where(iota(square, 0) == iota(square, 1), 1.0, 0.0).astype(BF16)
    at_end = jnp.sum(sums[rows:] - own_sums[rows:], axis=0, keepdims=True)
    dl = sums[:rows] + jnp.where(iota((rows, heads), 0) == rows - 1, at_end, 0.0)
    d_decay = sum(dot(part, upper, 0, 0) for part in split3(dl))
    total = sum(dot(part, eye, 0, 0) for part in split3(sums[rows:]))
    dt_out[0] = total / dt_ref[...] + rate_column(alog_ref) * d_decay
    for copy in sent:
        copy.wait()


def call(kernel, reach, outs, ins, flops, moved, scratch=()):
    spaces = {"s": pltpu.SMEM, "v": pltpu.VMEM, "h": pltpu.HBM}
    return pl.pallas_call(
        kernel,
        out_shape=[
            pltpu.HBM(*out) if place == "h" else jax.ShapeDtypeStruct(*out) for place, out in outs
        ],
        in_specs=[pl.BlockSpec(memory_space=spaces[place]) for place, _ in ins],
        out_specs=[pl.BlockSpec(memory_space=spaces[place]) for place, _ in outs],
        scratch_shapes=scratch,
        compiler_params=pltpu.CompilerParams(vmem_limit_bytes=min(16 + 2 * reach, 56) * 2**20),
        cost_estimate=pl.CostEstimate(flops=flops, bytes_accessed=moved, transcendentals=0),
    )(*(a for _, a in ins))


def swap(a, by, second):
    count = lax.axis_size("ctx")
    pairs = []
    for i in range(count - by):
        if i // by % 2 == second:
            pairs += [(i, i + by), (i + by, i)]
    return lax.ppermute(a, "ctx", pairs)


def in_hbm(a):
    return "h", pltpu.with_memory_space_constraint(a, pltpu.HBM)


def per_device(inputs, b_proj, c_proj, step_sizes, a_log, skip_gain, doc_lengths, grad_out):
    rows, columns = inputs.shape[1:]
    heads, width = a_log.shape[0], b_proj.shape[2]
    reach = max(lax.axis_size("ctx") // 4, 1)
    devices = lax.axis_size("ctx") * lax.axis_size("dp")
    alog, skip = a_log[None], skip_gain[None]
    bt, ct = jnp.swapaxes(b_proj, 1, 2), jnp.swapaxes(c_proj, 1, 2)
    blocks = columns // WIDE
    pieces = 4

    def v(shape, kind=F32):
        return "v", (shape, kind)

    dt, x, b, dy, c, *payloads = call(
        functools.partial(states_kernel, reach),
        reach,
        [
            v((heads, rows)),
            v((rows, columns), BF16),
            v((width, rows), BF16),
            v((rows, columns), BF16),
            v((width, rows), BF16),
        ]
        + [v((columns // LANES * (width + 1), LANES))] * (2 * reach),
        [in_hbm(a) for a in (doc_lengths, alog, step_sizes, inputs, bt, grad_out, ct)],
        10**9,
        4 * 2**20,
        [
            pltpu.SMEM(doc_lengths.shape, jnp.int32),
            pltpu.VMEM(alog.shape, F32),
            pltpu.SemaphoreType.DMA((5,)),
            pltpu.SemaphoreType.DMA((2, pieces)),
        ],
    )
    messages = [swap(payloads[at], at // 2 + 1, at % 2) for at in swap_order(reach)]
    whole = "h", ((rows, columns), F32)
    state = v((width, columns))
    stage = pltpu.VMEM((rows, columns), F32)
    transposed = v((width, rows))
    xs, ys, v_wide, dx, b_end, c_live, masks, db, dc, sums, fwd_logs, bwd_logs, ends, small = call(
        inside_kernel,
        reach,
        [v((2 * rows, columns), BF16)] * 2
        + [whole] * 2
        + [v((rows, 2 * width), BF16)] * 2
        + [v((8, rows)), transposed, transposed, v((2 * rows, heads))]
        + [state, state, v((8, columns)), v((1, LANES))],
        [("s", doc_lengths)] + [("v", a) for a in (alog, skip, dt, x, b, dy, c)],
        4 * 10**9,
        12 * 2**20,
        [stage, stage, pltpu.SemaphoreType.DMA((2, blocks))],
    )
    partial, came, pull = call(
        functools.partial(rates_kernel, reach, columns // heads),
        reach,
        [v((devices, LANES)), state, state],
        [("v", a) for a in (*messages, ends, fwd_logs, bwd_logs, small)],
        10**8,
        4 * 2**20,
    )
    input_grads, b_gradient, c_gradient, step_grads = call(
        outputs_kernel,
        reach,
        [("h", ((1, rows, columns), BF16))]
        + [v((1, width, rows), BF16)] * 2
        + [v((1, heads, rows))],
        [("v", a) for a in (came, pull, ends, xs, ys)]
        + [in_hbm(v_wide), in_hbm(dx)]
        + [("v", a) for a in (b_end, c_live, masks, db, dc, sums, alog, dt)],
        2 * 10**9,
        12 * 2**20,
        [
            stage,
            stage,
            pltpu.VMEM((rows, columns), BF16),
            pltpu.SemaphoreType.DMA((2, blocks)),
            pltpu.SemaphoreType.DMA((blocks,)),
        ],
    )
    gathered = lax.all_to_all(partial, ("dp", "ctx"), 0, 0, tiled=True)
    totals = jnp.sum(gathered, axis=0)
    return (
        input_grads,
        jnp.swapaxes(b_gradient, 1, 2),
        jnp.swapaxes(c_gradient, 1, 2),
        step_grads,
        totals[:heads],
        totals[heads : 2 * heads],
    )


def solution(mesh):
    in_specs = (
        P("dp", "ctx", None),
        P("dp", "ctx", None),
        P("dp", "ctx", None),
        P("dp", None, "ctx"),
        P(),
        P(),
        P("dp", None),
        P("dp", "ctx", None),
    )
    out_specs = (
        P("dp", "ctx", None),
        P("dp", "ctx", None),
        P("dp", "ctx", None),
        P("dp", None, "ctx"),
        P(),
        P(),
    )
    return jax.shard_map(
        per_device, mesh=mesh, in_specs=in_specs, out_specs=out_specs, check_vma=False
    )
```

```python
import functools

import jax
import jax.numpy as jnp
from jax import lax
from jax.experimental import pallas as pl
from jax.experimental.pallas import tpu as pltpu
from jax.sharding import PartitionSpec as P

F32 = jnp.float32
BF16 = jnp.bfloat16
LANES = 128
WIDE = 256
PARTS = WIDE // LANES
FAR = 2**30
PIECES = 4


def dot(a, b, ca, cb):
    return lax.dot_general(a, b, (((ca,), (cb,)), ((), ())), preferred_element_type=F32)


def iota(shape, dim):
    return lax.broadcasted_iota(jnp.int32, shape, dim)


def split2(a):
    high = a.astype(BF16)
    return high, (a - high.astype(F32)).astype(BF16)


def split3(a):
    high = a.astype(BF16)
    rest = a - high.astype(F32)
    middle = rest.astype(BF16)
    return high, middle, (rest - middle.astype(F32)).astype(BF16)


def dot_pairs(a, b, ca, cb):
    return dot(a[0], b[0], ca, cb) + (dot(a[0], b[1], ca, cb) + dot(a[1], b[0], ca, cb))


def stack(parts, axis):
    return jnp.concatenate(parts, axis=axis)


def document_places(lens_ref, rows):
    offset = shard() * rows
    starts = [jnp.int32(0)]
    for d in range(lens_ref.shape[1] - 1):
        starts.append(starts[-1] + lens_ref[0, d])
    first = jnp.int32(FAR)
    last = jnp.int32(0)
    for start in starts:
        first = jnp.minimum(first, jnp.where(start >= offset, start, FAR))
        last = jnp.maximum(last, jnp.where(start < offset + rows, start, 0))
    return starts, offset, first, last


def rate_column(alog_ref):
    heads = alog_ref.shape[1]
    square = jnp.broadcast_to(alog_ref[...], (heads, heads))
    picked = jnp.where(iota((heads, heads), 0) == iota((heads, heads), 1), square, 0.0)
    return -jnp.exp(jnp.sum(picked, axis=1, keepdims=True))


def log2(size):
    assert size & (size - 1) == 0
    return size.bit_length() - 1


def head_distance(heads, head_width):
    shape = (3 * heads, WIDE)
    return (iota(shape, 0) & (heads - 1)) - lax.shift_right_logical(
        iota(shape, 1), log2(head_width)
    )


def head_rows(distance, head_width, block):
    return jnp.where(distance == block * (WIDE // head_width), 1.0, 0.0).astype(BF16)


def head_columns(heads, head_width, block):
    shape = (WIDE, heads)
    column = lax.shift_right_logical(iota(shape, 0), log2(head_width))
    return jnp.where(iota(shape, 1) - column == block * (WIDE // head_width), 1.0, 0.0).astype(BF16)


def shard():
    return lax.axis_index("ctx")


def message_block(ref, block, width):
    at = block * PARTS
    return stack([ref[(at + i) * width : (at + i + 1) * width, :] for i in range(PARTS)], 1)


def message_tail(ref, block, width):
    tail = ref.shape[0] // (width + 1) * width + block * PARTS
    return stack([ref[tail + i : tail + i + 1, :] for i in range(PARTS)], 1)


def received(refs, block, width):
    came = pull = None
    for j in range(len(refs) // 2, 0, -1):
        one, two = refs[2 * j - 2], refs[2 * j - 1]
        a, b = message_block(one, block, width), message_block(two, block, width)
        first = jnp.broadcast_to(lax.rem(shard() + j, 2), a.shape) == 0
        near_came, near_pull = jnp.where(first, a, b), jnp.where(first, b, a)
        if came is None:
            came, pull = near_came, near_pull
        else:
            a, b = message_tail(one, block, width), message_tail(two, block, width)
            first = jnp.broadcast_to(lax.rem(shard() + j, 2), a.shape) == 0
            came = near_came + jnp.where(first, a, b) * came
            pull = near_pull + jnp.where(first, b, a) * pull
    return came, pull


def states_kernel(
    lens_hbm,
    alog_hbm,
    dt_hbm,
    x_hbm,
    b_hbm,
    dy_hbm,
    c_hbm,
    dt_ref,
    x_ref,
    b_ref,
    dy_ref,
    c_ref,
    one_ref,
    two_ref,
    lens_ref,
    alog_ref,
    small_sems,
    sems,
):
    rows, columns = x_ref.shape
    heads, width = dt_ref.shape[0], b_ref.shape[0]
    head_width = columns // heads
    piece = columns // PIECES
    small = [
        pltpu.make_async_copy(source, target, small_sems.at[i])
        for i, (source, target) in enumerate(
            (
                (lens_hbm, lens_ref),
                (alog_hbm, alog_ref),
                (dt_hbm.at[0], dt_ref),
                (b_hbm.at[0], b_ref),
                (c_hbm.at[0], c_ref),
            )
        )
    ]
    for copy in small:
        copy.start()
    large = []
    for i in range(PIECES):
        at = slice(i * piece, (i + 1) * piece)
        for side, (source, target) in enumerate(((x_hbm, x_ref), (dy_hbm, dy_ref))):
            copy = pltpu.make_async_copy(
                source.at[0, :, at], target.at[:, at], sems.at[side, i]
            )
            copy.start()
            large.append(copy)
    square = (rows, rows)
    upper = jnp.where(iota(square, 0) <= iota(square, 1), 1.0, 0.0).astype(BF16)
    even = jnp.broadcast_to(lax.rem(shard(), 2), (width, LANES)) == 0
    left = iota((1, LANES), 1) < head_width
    for copy in small:
        copy.wait()
    _, offset, first, last = document_places(lens_ref, rows)
    through = jnp.where(first >= offset + rows, 1.0, 0.0)
    dt = dt_ref[...]
    logs = sum(dot(part, upper, 1, 0) for part in split3(dt * rate_column(alog_ref)))
    end_log = logs[:, rows - 1 : rows]
    place = iota((heads, rows), 1) + offset
    keeping = jnp.where(place >= last, jnp.exp(end_log - logs) * dt, 0.0)
    carried = jnp.where(place < first, jnp.exp(logs), 0.0)
    kept = jnp.broadcast_to(jnp.exp(end_log) * through, (heads, LANES))
    b, c = b_ref[...].astype(F32), c_ref[...].astype(F32)
    own = LANES // head_width

    def pair_states(vectors, weights, values):
        parts = []
        for h in range(own):
            parts += split2(vectors * weights[h : h + 1, :])
        out = dot(stack(parts, 0), values, 1, 0)
        sides = [
            out[2 * h * width : (2 * h + 1) * width]
            + out[(2 * h + 1) * width : (2 * h + 2) * width]
            for h in range(own)
        ]
        return jnp.where(left, sides[0], sides[1])

    for pair in range(columns // LANES):
        if pair * LANES % piece == 0:
            large[pair * LANES // piece * 2].wait()
            large[pair * LANES // piece * 2 + 1].wait()
        at = slice(pair * LANES, (pair + 1) * LANES)
        here = slice(pair * own, (pair + 1) * own)
        state = pair_states(b, keeping[here], x_ref[:, at])
        pulled = pair_states(c, carried[here], dy_ref[:, at])
        tail = columns // LANES * width + pair
        one_ref[pair * width : (pair + 1) * width, :] = jnp.where(even, state, pulled)
        two_ref[pair * width : (pair + 1) * width, :] = jnp.where(even, pulled, state)
        one_ref[tail : tail + 1, :] = jnp.where(left, kept[here][:1], kept[here][1:])
        two_ref[tail : tail + 1, :] = jnp.where(left, kept[here][:1], kept[here][1:])


def inside_kernel(
    lens_ref,
    alog_ref,
    skip_ref,
    dt_ref,
    x_ref,
    b_ref,
    dy_ref,
    c_ref,
    xs_ref,
    ys_ref,
    v_wide_hbm,
    dx_hbm,
    b_end_ref,
    c_live_ref,
    masks_ref,
    db_ref,
    dc_ref,
    sums_ref,
    fwd_ref,
    bwd_ref,
    ends_ref,
    small_ref,
    v_stage,
    dx_stage,
    sems,
):
    rows, columns = x_ref.shape
    heads, width = dt_ref.shape[0], b_ref.shape[0]
    head_width = columns // heads
    starts, offset, first, last = document_places(lens_ref, rows)
    through = jnp.where(first >= offset + rows, 1.0, 0.0)
    square = (rows, rows)
    place0, place1 = iota(square, 0) + offset, iota(square, 1) + offset
    segment0, segment1 = jnp.zeros(square, jnp.int32), jnp.zeros(square, jnp.int32)
    for start in starts:
        segment0 += jnp.where(place0 >= start, 1, 0)
        segment1 += jnp.where(place1 >= start, 1, 0)
    same = segment0 == segment1
    down = same & (place0 >= place1)
    lower = jnp.where(place0 >= place1, 1.0, 0.0).astype(BF16)
    eye = jnp.where(place0 == place1, 1.0, 0.0).astype(BF16)
    dt = dt_ref[...]
    logs = sum(dot(lower, part, 1, 1) for part in split3(dt * rate_column(alog_ref)))
    steps = sum(dot(eye, part, 1, 1) for part in split3(dt))
    bt, ct = b_ref[...], c_ref[...]
    scores = split2(jnp.where(down, dot(ct, bt, 0, 0), 0.0))
    flipped = split2(jnp.where(same & (place1 >= place0), dot(bt, ct, 0, 0), 0.0))
    place = iota((width, rows), 1) + offset
    bt_end = jnp.where(place >= last, bt.astype(F32), 0.0)
    ct_live = jnp.where(place < first, ct.astype(F32), 0.0)
    b_end, c_live = jnp.transpose(bt_end).astype(BF16), jnp.transpose(ct_live).astype(BF16)
    bt_end, ct_live = bt_end.astype(BF16), ct_live.astype(BF16)
    b_end_ref[...] = stack([b_end, b_end], 1)
    c_live_ref[...] = stack([c_live, c_live], 1)
    bt_end, ct_live = stack([bt_end, bt_end], 1), stack([ct_live, ct_live], 1)
    masks_ref[0:1] = jnp.where(place[:1] >= last, 1.0, 0.0)
    masks_ref[1:2] = jnp.where(place[:1] < first, 1.0, 0.0)
    tables = stack(
        [
            stack(split3(a), 1)
            for a in (
                jnp.exp(logs),
                jnp.exp(-logs) * steps,
                logs,
                jnp.broadcast_to(skip_ref[...], (16, heads)),
            )
        ],
        0,
    )
    distance = head_distance(heads, head_width)
    d_scores = jnp.zeros(square, F32)
    sums = jnp.zeros((2 * rows, heads), F32)
    products = jnp.zeros((8, heads), F32)
    copies = []
    for block in range(columns // WIDE):
        at = slice(block * WIDE, (block + 1) * WIDE)
        wide = dot(tables, head_rows(distance, head_width, block), 1, 0)
        ones = head_columns(heads, head_width, block)
        u_wide, v_wide, l_wide = wide[:rows], wide[rows : 2 * rows], wide[2 * rows : 3 * rows]
        skip_wide = wide[3 * rows : 3 * rows + 1]
        x = x_ref[:, at].astype(F32)
        dy = dy_ref[:, at].astype(F32)
        xv = x * v_wide
        yu = dy * u_wide
        xs, ys = split2(xv), split2(yu)
        xs_ref[:, at] = stack(xs, 0)
        ys_ref[:, at] = stack(ys, 0)
        v_stage[:, at] = v_wide
        out = dot_pairs(scores, xs, 1, 0)
        back = dot_pairs(flipped, ys, 1, 0)
        d_scores += dot_pairs(ys, xs, 1, 1)
        dx_stage[:, at] = v_wide * back + skip_wide * dy
        for i, (stage, target) in enumerate(((v_stage, v_wide_hbm), (dx_stage, dx_hbm))):
            copy = pltpu.make_async_copy(stage.at[:, at], target.at[:, at], sems.at[i, block])
            copy.start()
            copies.append(copy)
        column_part = xv * back
        for part in split3(stack([yu * out - column_part, column_part], 0)):
            sums += dot(part, ones, 1, 0)
        product = jnp.broadcast_to(jnp.sum(x * dy, axis=0, keepdims=True), (8, WIDE))
        for part in split3(product):
            products += dot(part, ones, 1, 0)
        ending = u_wide[rows - 1 : rows]
        end_log = l_wide[rows - 1 : rows]
        gap = end_log - l_wide
        fwd_ref[:, at] = dot(bt_end, stack(split2(xv * gap), 0), 1, 0) * ending
        bwd_ref[:, at] = dot(ct_live, stack(split2(yu * l_wide), 0), 1, 0)
        ends_ref[0:1, at] = ending
        ends_ref[1:2, at] = ending * through
        ends_ref[2:3, at] = ending * through * end_log
    d_scores = split2(jnp.where(down, d_scores, 0.0))
    dc_ref[...] = sum(dot(bt, p, 1, 1) for p in d_scores)
    db_ref[...] = sum(dot(ct, p, 1, 0) for p in d_scores)
    sums_ref[...] = sums
    rate_grads = jnp.sum(logs * sums[:rows], axis=0, keepdims=True)
    empty = jnp.zeros((1, LANES - 2 * heads), F32)
    small_ref[...] = stack([rate_grads, products[:1], empty], 1)
    for copy in copies:
        copy.wait()


def send_order(reach):
    return [*range(0, 2 * reach, 2), *range(1, 2 * reach, 2)]


def rates_kernel(reach, head_width, *refs):
    messages = [ref for _, ref in sorted(zip(send_order(reach), refs), key=lambda pair: pair[0])]
    ends_ref, fwd_ref, bwd_ref, small_ref, out_ref, came_ref, pull_ref = refs[2 * reach :]
    width, columns = fwd_ref.shape
    blocks = columns // WIDE
    whole = []
    for block in range(blocks):
        at = slice(block * WIDE, (block + 1) * WIDE)
        came, pull = received(messages, block, width)
        came_ref[:, at] = came
        pull_ref[:, at] = pull
        terms = came * bwd_ref[:, at] + pull * (fwd_ref[:, at] + ends_ref[2:3, at] * came)
        whole.append(jnp.sum(terms, axis=0, keepdims=True))
    own = WIDE // head_width
    shape = (WIDE, LANES)
    column = lax.shift_right_logical(iota(shape, 0), log2(head_width))
    ones = jnp.where(column == (iota(shape, 1) & (own - 1)), 1.0, 0.0).astype(BF16)
    sums = sum(dot(part, ones, 1, 0) for part in split3(stack(whole, 0)))
    lane = iota(sums.shape, 1)
    mine = lax.shift_right_logical(lane, log2(own)) == iota(sums.shape, 0)
    total = small_ref[...] + jnp.sum(jnp.where(mine, sums, 0.0), axis=0, keepdims=True)
    out_ref[...] = jnp.broadcast_to(total, out_ref.shape)


def outputs_kernel(
    came_ref,
    pull_ref,
    ends_ref,
    xs_ref,
    ys_ref,
    v_wide_hbm,
    dx_hbm,
    b_end_ref,
    c_live_ref,
    masks_ref,
    db_ref,
    dc_ref,
    sums_ref,
    alog_ref,
    dt_ref,
    dx_out,
    db_out,
    dc_out,
    dt_out,
    v_stage,
    dx_stage,
    stage,
    in_sems,
    out_sems,
):
    rows, columns = dx_hbm.shape
    heads, width = dt_ref.shape[0], db_ref.shape[0]
    blocks = columns // WIDE
    copies = []
    for block in range(blocks):
        at = slice(block * WIDE, (block + 1) * WIDE)
        for i, (source, target) in enumerate(((v_wide_hbm, v_stage), (dx_hbm, dx_stage))):
            copy = pltpu.make_async_copy(
                source.at[:, at], target.at[:, at], in_sems.at[i, block]
            )
            copy.start()
            copies.append(copy)
    b_end, c_live = b_end_ref[...], c_live_ref[...]
    own_sums = sums_ref[...]
    sums = own_sums
    dc = jnp.zeros((2 * width, 2 * rows), F32)
    db = jnp.zeros((2 * width, 2 * rows), F32)
    at_last = iota((rows, WIDE), 0) == rows - 1
    sent = []
    for block in range(blocks):
        at = slice(block * WIDE, (block + 1) * WIDE)
        ones = head_columns(heads, columns // heads, block)
        came, pull = came_ref[:, at], pull_ref[:, at]
        meet = jnp.sum(came * pull, axis=0, keepdims=True) * ends_ref[1:2, at]
        cames = stack(split2(came), 0)
        pulls = stack(split2(pull * ends_ref[0:1, at]), 0)
        xs, ys = xs_ref[:, at], ys_ref[:, at]
        out = dot(c_live, cames, 1, 0)
        back = dot(b_end, pulls, 1, 0)
        column_part = (xs[:rows].astype(F32) + xs[rows:].astype(F32)) * back
        row_part = (ys[:rows].astype(F32) + ys[rows:].astype(F32)) * out
        row_part = jnp.where(at_last, row_part + meet, row_part)
        for part in split2(stack([row_part - column_part, column_part], 0)):
            sums += dot(part, ones, 1, 0)
        dc += dot(cames, ys, 1, 1)
        db += dot(pulls, xs, 1, 1)
        copies[2 * block].wait()
        copies[2 * block + 1].wait()
        stage[:, at] = (dx_stage[:, at] + v_stage[:, at] * back).astype(BF16)
        copy = pltpu.make_async_copy(stage.at[:, at], dx_out.at[0, :, at], out_sems.at[block])
        copy.start()
        sent.append(copy)
    dc = (dc[:width, :rows] + dc[:width, rows:]) + dc[width:, :rows]
    db = (db[:width, :rows] + db[:width, rows:]) + db[width:, :rows]
    db_out[0] = (db_ref[...] + masks_ref[0:1] * db).astype(BF16)
    dc_out[0] = (dc_ref[...] + masks_ref[1:2] * dc).astype(BF16)
    square = (rows, rows)
    upper = jnp.where(iota(square, 0) >= iota(square, 1), 1.0, 0.0).astype(BF16)
    eye = jnp.where(iota(square, 0) == iota(square, 1), 1.0, 0.0).astype(BF16)
    at_end = jnp.sum(sums[rows:] - own_sums[rows:], axis=0, keepdims=True)
    dl = sums[:rows] + jnp.where(iota((rows, heads), 0) == rows - 1, at_end, 0.0)
    d_decay = sum(dot(part, upper, 0, 0) for part in split3(dl))
    total = sum(dot(part, eye, 0, 0) for part in split3(sums[rows:]))
    dt_out[0] = total / dt_ref[...] + rate_column(alog_ref) * d_decay
    for copy in sent:
        copy.wait()


def call(kernel, reach, outs, ins, flops, moved, scratch=()):
    spaces = {"s": pltpu.SMEM, "v": pltpu.VMEM, "h": pltpu.HBM}
    return pl.pallas_call(
        kernel,
        out_shape=[
            pltpu.HBM(*out) if place == "h" else jax.ShapeDtypeStruct(*out) for place, out in outs
        ],
        in_specs=[pl.BlockSpec(memory_space=spaces[place]) for place, _ in ins],
        out_specs=[pl.BlockSpec(memory_space=spaces[place]) for place, _ in outs],
        scratch_shapes=scratch,
        compiler_params=pltpu.CompilerParams(vmem_limit_bytes=min(16 + 2 * reach, 56) * 2**20),
        cost_estimate=pl.CostEstimate(flops=flops, bytes_accessed=moved, transcendentals=0),
    )(*(a for _, a in ins))


def send(a, by, second):
    count = lax.axis_size("ctx")
    pairs = [(i, i + by if (i + second) % 2 == 0 else i - by) for i in range(count)]
    return lax.ppermute(a, "ctx", [(i, j) for i, j in pairs if 0 <= j < count])


def in_hbm(a):
    return "h", pltpu.with_memory_space_constraint(a, pltpu.HBM)


def per_device(inputs, b_proj, c_proj, step_sizes, a_log, skip_gain, doc_lengths, grad_out):
    rows, columns = inputs.shape[1:]
    heads, width = a_log.shape[0], b_proj.shape[2]
    reach = max(lax.axis_size("ctx") // 4, 1)
    devices = lax.axis_size("ctx") * lax.axis_size("dp")
    alog, skip = a_log[None], skip_gain[None]
    bt, ct = jnp.swapaxes(b_proj, 1, 2), jnp.swapaxes(c_proj, 1, 2)
    blocks = columns // WIDE

    def v(shape, kind=F32):
        return "v", (shape, kind)

    dt, x, b, dy, c, *payloads = call(
        states_kernel,
        reach,
        [
            v((heads, rows)),
            v((rows, columns), BF16),
            v((width, rows), BF16),
            v((rows, columns), BF16),
            v((width, rows), BF16),
        ]
        + [v((columns // LANES * (width + 1), LANES))] * 2,
        [in_hbm(a) for a in (doc_lengths, alog, step_sizes, inputs, bt, grad_out, ct)],
        10**9,
        4 * 2**20,
        [
            pltpu.SMEM(doc_lengths.shape, jnp.int32),
            pltpu.VMEM(alog.shape, F32),
            pltpu.SemaphoreType.DMA((5,)),
            pltpu.SemaphoreType.DMA((2, PIECES)),
        ],
    )
    messages = [send(payloads[at % 2], at // 2 + 1, at % 2) for at in send_order(reach)]
    whole = "h", ((rows, columns), F32)
    state = v((width, columns))
    stage = pltpu.VMEM((rows, columns), F32)
    transposed = v((width, rows))
    xs, ys, v_wide, dx, b_end, c_live, masks, db, dc, sums, fwd_logs, bwd_logs, ends, small = call(
        inside_kernel,
        reach,
        [v((2 * rows, columns), BF16)] * 2
        + [whole] * 2
        + [v((rows, 2 * width), BF16)] * 2
        + [v((8, rows)), transposed, transposed, v((2 * rows, heads))]
        + [state, state, v((8, columns)), v((1, LANES))],
        [("s", doc_lengths)] + [("v", a) for a in (alog, skip, dt, x, b, dy, c)],
        4 * 10**9,
        12 * 2**20,
        [stage, stage, pltpu.SemaphoreType.DMA((2, blocks))],
    )
    partial, came, pull = call(
        functools.partial(rates_kernel, reach, columns // heads),
        reach,
        [v((devices, LANES)), state, state],
        [("v", a) for a in (*messages, ends, fwd_logs, bwd_logs, small)],
        10**8,
        4 * 2**20,
    )
    input_grads, b_gradient, c_gradient, step_grads = call(
        outputs_kernel,
        reach,
        [("h", ((1, rows, columns), BF16))]
        + [v((1, width, rows), BF16)] * 2
        + [v((1, heads, rows))],
        [("v", a) for a in (came, pull, ends, xs, ys)]
        + [in_hbm(v_wide), in_hbm(dx)]
        + [("v", a) for a in (b_end, c_live, masks, db, dc, sums, alog, dt)],
        2 * 10**9,
        12 * 2**20,
        [
            stage,
            stage,
            pltpu.VMEM((rows, columns), BF16),
            pltpu.SemaphoreType.DMA((2, blocks)),
            pltpu.SemaphoreType.DMA((blocks,)),
        ],
    )
    gathered = lax.all_to_all(partial, ("dp", "ctx"), 0, 0, tiled=True)
    totals = jnp.sum(gathered, axis=0)
    return (
        input_grads,
        jnp.swapaxes(b_gradient, 1, 2),
        jnp.swapaxes(c_gradient, 1, 2),
        step_grads,
        totals[:heads],
        totals[heads : 2 * heads],
    )


def solution(mesh):
    in_specs = (
        P("dp", "ctx", None),
        P("dp", "ctx", None),
        P("dp", "ctx", None),
        P("dp", None, "ctx"),
        P(),
        P(),
        P("dp", None),
        P("dp", "ctx", None),
    )
    out_specs = (
        P("dp", "ctx", None),
        P("dp", "ctx", None),
        P("dp", "ctx", None),
        P("dp", None, "ctx"),
        P(),
        P(),
    )
    return jax.shard_map(
        per_device, mesh=mesh, in_specs=in_specs, out_specs=out_specs, check_vma=False
    )
```

```python
import functools

import jax
import jax.numpy as jnp
from jax import lax
from jax.experimental import pallas as pl
from jax.experimental.pallas import tpu as pltpu
from jax.sharding import PartitionSpec as P

F32 = jnp.float32
BF16 = jnp.bfloat16
LANES = 128
WIDE = 256
PARTS = WIDE // LANES
FAR = 2**30
PIECES = 4


def dot(a, b, ca, cb):
    return lax.dot_general(a, b, (((ca,), (cb,)), ((), ())), preferred_element_type=F32)


def iota(shape, dim):
    return lax.broadcasted_iota(jnp.int32, shape, dim)


def split2(a):
    high = a.astype(BF16)
    return high, (a - high.astype(F32)).astype(BF16)


def split3(a):
    high = a.astype(BF16)
    rest = a - high.astype(F32)
    middle = rest.astype(BF16)
    return high, middle, (rest - middle.astype(F32)).astype(BF16)


def dot_pairs(a, b, ca, cb):
    return dot(a[0], b[0], ca, cb) + (dot(a[0], b[1], ca, cb) + dot(a[1], b[0], ca, cb))


def stack(parts, axis):
    return jnp.concatenate(parts, axis=axis)


def document_places(lens_ref, rows):
    offset = shard() * rows
    starts = [jnp.int32(0)]
    for d in range(lens_ref.shape[1] - 1):
        starts.append(starts[-1] + lens_ref[0, d])
    first = jnp.int32(FAR)
    last = jnp.int32(0)
    for start in starts:
        first = jnp.minimum(first, jnp.where(start >= offset, start, FAR))
        last = jnp.maximum(last, jnp.where(start < offset + rows, start, 0))
    return starts, offset, first, last


def rate_column(alog_ref):
    heads = alog_ref.shape[1]
    square = jnp.broadcast_to(alog_ref[...], (heads, heads))
    picked = jnp.where(iota((heads, heads), 0) == iota((heads, heads), 1), square, 0.0)
    return -jnp.exp(jnp.sum(picked, axis=1, keepdims=True))


def log2(size):
    assert size & (size - 1) == 0
    return size.bit_length() - 1


def head_distance(heads, head_width):
    shape = (3 * heads, WIDE)
    return (iota(shape, 0) & (heads - 1)) - lax.shift_right_logical(
        iota(shape, 1), log2(head_width)
    )


def head_rows(distance, head_width, block):
    return jnp.where(distance == block * (WIDE // head_width), 1.0, 0.0).astype(BF16)


def head_columns(heads, head_width, block):
    shape = (WIDE, heads)
    column = lax.shift_right_logical(iota(shape, 0), log2(head_width))
    return jnp.where(iota(shape, 1) - column == block * (WIDE // head_width), 1.0, 0.0).astype(BF16)


def shard():
    return lax.axis_index("ctx")


def message_block(ref, block, width):
    at = block * PARTS
    return stack([ref[(at + i) * width : (at + i + 1) * width, :] for i in range(PARTS)], 1)


def message_tail(ref, block, width):
    tail = ref.shape[0] // (width + 1) * width + block * PARTS
    return stack([ref[tail + i : tail + i + 1, :] for i in range(PARTS)], 1)


def received(refs, block, width):
    came = pull = None
    for j in range(len(refs) // 2, 0, -1):
        one, two = refs[2 * j - 2], refs[2 * j - 1]
        a, b = message_block(one, block, width), message_block(two, block, width)
        first = jnp.broadcast_to(lax.rem(shard() + j, 2), a.shape) == 0
        near_came, near_pull = jnp.where(first, a, b), jnp.where(first, b, a)
        if came is None:
            came, pull = near_came, near_pull
        else:
            a, b = message_tail(one, block, width), message_tail(two, block, width)
            first = jnp.broadcast_to(lax.rem(shard() + j, 2), a.shape) == 0
            came = near_came + jnp.where(first, a, b) * came
            pull = near_pull + jnp.where(first, b, a) * pull
    return came, pull


def states_kernel(
    lens_hbm,
    alog_hbm,
    dt_hbm,
    x_hbm,
    b_hbm,
    dy_hbm,
    c_hbm,
    dt_ref,
    x_ref,
    b_ref,
    dy_ref,
    c_ref,
    one_ref,
    two_ref,
    lens_ref,
    alog_ref,
    small_sems,
    sems,
):
    rows, columns = x_ref.shape
    heads, width = dt_ref.shape[0], b_ref.shape[0]
    head_width = columns // heads
    piece = columns // PIECES
    small = [
        pltpu.make_async_copy(source, target, small_sems.at[i])
        for i, (source, target) in enumerate(
            (
                (lens_hbm, lens_ref),
                (alog_hbm, alog_ref),
                (dt_hbm.at[0], dt_ref),
                (b_hbm.at[0], b_ref),
                (c_hbm.at[0], c_ref),
            )
        )
    ]
    for copy in small:
        copy.start()
    large = []
    for i in range(PIECES):
        at = slice(i * piece, (i + 1) * piece)
        for side, (source, target) in enumerate(((x_hbm, x_ref), (dy_hbm, dy_ref))):
            copy = pltpu.make_async_copy(
                source.at[0, :, at], target.at[:, at], sems.at[side, i]
            )
            copy.start()
            large.append(copy)
    square = (rows, rows)
    upper = jnp.where(iota(square, 0) <= iota(square, 1), 1.0, 0.0).astype(BF16)
    even = jnp.broadcast_to(lax.rem(shard(), 2), (width, LANES)) == 0
    left = iota((1, LANES), 1) < head_width
    for copy in small:
        copy.wait()
    _, offset, first, last = document_places(lens_ref, rows)
    through = jnp.where(first >= offset + rows, 1.0, 0.0)
    dt = dt_ref[...]
    logs = sum(dot(part, upper, 1, 0) for part in split3(dt * rate_column(alog_ref)))
    end_log = logs[:, rows - 1 : rows]
    place = iota((heads, rows), 1) + offset
    keeping = jnp.where(place >= last, jnp.exp(end_log - logs) * dt, 0.0)
    carried = jnp.where(place < first, jnp.exp(logs), 0.0)
    kept = jnp.broadcast_to(jnp.exp(end_log) * through, (heads, LANES))
    b, c = b_ref[...].astype(F32), c_ref[...].astype(F32)
    own = LANES // head_width

    def pair_states(vectors, weights, values):
        parts = []
        for h in range(own):
            parts += split2(vectors * weights[h : h + 1, :])
        out = dot(stack(parts, 0), values, 1, 0)
        sides = [
            out[2 * h * width : (2 * h + 1) * width]
            + out[(2 * h + 1) * width : (2 * h + 2) * width]
            for h in range(own)
        ]
        return jnp.where(left, sides[0], sides[1])

    for pair in range(columns // LANES):
        if pair * LANES % piece == 0:
            large[pair * LANES // piece * 2].wait()
            large[pair * LANES // piece * 2 + 1].wait()
        at = slice(pair * LANES, (pair + 1) * LANES)
        here = slice(pair * own, (pair + 1) * own)
        state = pair_states(b, keeping[here], x_ref[:, at])
        pulled = pair_states(c, carried[here], dy_ref[:, at])
        tail = columns // LANES * width + pair
        one_ref[pair * width : (pair + 1) * width, :] = jnp.where(even, state, pulled)
        two_ref[pair * width : (pair + 1) * width, :] = jnp.where(even, pulled, state)
        one_ref[tail : tail + 1, :] = jnp.where(left, kept[here][:1], kept[here][1:])
        two_ref[tail : tail + 1, :] = jnp.where(left, kept[here][:1], kept[here][1:])


def inside_kernel(
    lens_ref,
    alog_ref,
    skip_ref,
    dt_ref,
    x_ref,
    b_ref,
    dy_ref,
    c_ref,
    xs_ref,
    ys_ref,
    v_wide_hbm,
    dx_hbm,
    b_end_ref,
    c_live_ref,
    masks_ref,
    db_ref,
    dc_ref,
    sums_ref,
    fwd_ref,
    bwd_ref,
    ends_ref,
    small_ref,
    v_stage,
    dx_stage,
    sems,
):
    rows, columns = x_ref.shape
    heads, width = dt_ref.shape[0], b_ref.shape[0]
    head_width = columns // heads
    starts, offset, first, last = document_places(lens_ref, rows)
    through = jnp.where(first >= offset + rows, 1.0, 0.0)
    square = (rows, rows)
    place0, place1 = iota(square, 0) + offset, iota(square, 1) + offset
    segment0, segment1 = jnp.zeros(square, jnp.int32), jnp.zeros(square, jnp.int32)
    for start in starts:
        segment0 += jnp.where(place0 >= start, 1, 0)
        segment1 += jnp.where(place1 >= start, 1, 0)
    same = segment0 == segment1
    down = same & (place0 >= place1)
    lower = jnp.where(place0 >= place1, 1.0, 0.0).astype(BF16)
    eye = jnp.where(place0 == place1, 1.0, 0.0).astype(BF16)
    dt = dt_ref[...]
    logs = sum(dot(lower, part, 1, 1) for part in split3(dt * rate_column(alog_ref)))
    steps = sum(dot(eye, part, 1, 1) for part in split3(dt))
    bt, ct = b_ref[...], c_ref[...]
    scores = split2(jnp.where(down, dot(ct, bt, 0, 0), 0.0))
    flipped = split2(jnp.where(same & (place1 >= place0), dot(bt, ct, 0, 0), 0.0))
    place = iota((width, rows), 1) + offset
    bt_end = jnp.where(place >= last, bt.astype(F32), 0.0)
    ct_live = jnp.where(place < first, ct.astype(F32), 0.0)
    b_end, c_live = jnp.transpose(bt_end).astype(BF16), jnp.transpose(ct_live).astype(BF16)
    bt_end, ct_live = bt_end.astype(BF16), ct_live.astype(BF16)
    b_end_ref[...] = stack([b_end, b_end], 1)
    c_live_ref[...] = stack([c_live, c_live], 1)
    bt_end, ct_live = stack([bt_end, bt_end], 1), stack([ct_live, ct_live], 1)
    masks_ref[0:1] = jnp.where(place[:1] >= last, 1.0, 0.0)
    masks_ref[1:2] = jnp.where(place[:1] < first, 1.0, 0.0)
    tables = stack(
        [
            stack(split3(a), 1)
            for a in (
                jnp.exp(logs),
                jnp.exp(-logs) * steps,
                logs,
                jnp.broadcast_to(skip_ref[...], (16, heads)),
            )
        ],
        0,
    )
    distance = head_distance(heads, head_width)
    d_scores = jnp.zeros(square, F32)
    sums = jnp.zeros((2 * rows, heads), F32)
    products = jnp.zeros((8, heads), F32)
    copies = []
    for block in range(columns // WIDE):
        at = slice(block * WIDE, (block + 1) * WIDE)
        wide = dot(tables, head_rows(distance, head_width, block), 1, 0)
        ones = head_columns(heads, head_width, block)
        u_wide, v_wide, l_wide = wide[:rows], wide[rows : 2 * rows], wide[2 * rows : 3 * rows]
        skip_wide = wide[3 * rows : 3 * rows + 1]
        x = x_ref[:, at].astype(F32)
        dy = dy_ref[:, at].astype(F32)
        xv = x * v_wide
        yu = dy * u_wide
        xs, ys = split2(xv), split2(yu)
        xs_ref[:, at] = stack(xs, 0)
        ys_ref[:, at] = stack(ys, 0)
        v_stage[:, at] = v_wide
        out = dot_pairs(scores, xs, 1, 0)
        back = dot_pairs(flipped, ys, 1, 0)
        d_scores += dot_pairs(ys, xs, 1, 1)
        dx_stage[:, at] = v_wide * back + skip_wide * dy
        for i, (stage, target) in enumerate(((v_stage, v_wide_hbm), (dx_stage, dx_hbm))):
            copy = pltpu.make_async_copy(stage.at[:, at], target.at[:, at], sems.at[i, block])
            copy.start()
            copies.append(copy)
        column_part = xv * back
        for part in split3(stack([yu * out - column_part, column_part], 0)):
            sums += dot(part, ones, 1, 0)
        product = jnp.broadcast_to(jnp.sum(x * dy, axis=0, keepdims=True), (8, WIDE))
        for part in split3(product):
            products += dot(part, ones, 1, 0)
        ending = u_wide[rows - 1 : rows]
        end_log = l_wide[rows - 1 : rows]
        gap = end_log - l_wide
        fwd_ref[:, at] = dot(bt_end, stack(split2(xv * gap), 0), 1, 0) * ending
        bwd_ref[:, at] = dot(ct_live, stack(split2(yu * l_wide), 0), 1, 0)
        ends_ref[0:1, at] = ending
        ends_ref[1:2, at] = ending * through
        ends_ref[2:3, at] = ending * through * end_log
    d_scores = split2(jnp.where(down, d_scores, 0.0))
    dc_ref[...] = sum(dot(bt, p, 1, 1) for p in d_scores)
    db_ref[...] = sum(dot(ct, p, 1, 0) for p in d_scores)
    sums_ref[...] = sums
    rate_grads = jnp.sum(logs * sums[:rows], axis=0, keepdims=True)
    empty = jnp.zeros((1, LANES - 2 * heads), F32)
    small_ref[...] = stack([rate_grads, products[:1], empty], 1)
    for copy in copies:
        copy.wait()


def send_order(reach):
    return [at for j in range(reach) for at in (2 * j + 1, 2 * j)]


def rates_kernel(reach, head_width, *refs):
    messages = [ref for _, ref in sorted(zip(send_order(reach), refs), key=lambda pair: pair[0])]
    ends_ref, fwd_ref, bwd_ref, small_ref, out_ref, came_ref, pull_ref = refs[2 * reach :]
    width, columns = fwd_ref.shape
    blocks = columns // WIDE
    whole = []
    for block in range(blocks):
        at = slice(block * WIDE, (block + 1) * WIDE)
        came, pull = received(messages, block, width)
        came_ref[:, at] = came
        pull_ref[:, at] = pull
        terms = came * bwd_ref[:, at] + pull * (fwd_ref[:, at] + ends_ref[2:3, at] * came)
        whole.append(jnp.sum(terms, axis=0, keepdims=True))
    own = WIDE // head_width
    shape = (WIDE, LANES)
    column = lax.shift_right_logical(iota(shape, 0), log2(head_width))
    ones = jnp.where(column == (iota(shape, 1) & (own - 1)), 1.0, 0.0).astype(BF16)
    sums = sum(dot(part, ones, 1, 0) for part in split3(stack(whole, 0)))
    lane = iota(sums.shape, 1)
    mine = lax.shift_right_logical(lane, log2(own)) == iota(sums.shape, 0)
    total = small_ref[...] + jnp.sum(jnp.where(mine, sums, 0.0), axis=0, keepdims=True)
    out_ref[...] = jnp.broadcast_to(total, out_ref.shape)


def outputs_kernel(
    came_ref,
    pull_ref,
    ends_ref,
    xs_ref,
    ys_ref,
    v_wide_hbm,
    dx_hbm,
    b_end_ref,
    c_live_ref,
    masks_ref,
    db_ref,
    dc_ref,
    sums_ref,
    alog_ref,
    dt_ref,
    dx_out,
    db_out,
    dc_out,
    dt_out,
    v_stage,
    dx_stage,
    stage,
    in_sems,
    out_sems,
):
    rows, columns = dx_hbm.shape
    heads, width = dt_ref.shape[0], db_ref.shape[0]
    blocks = columns // WIDE
    copies = []
    for block in range(blocks):
        at = slice(block * WIDE, (block + 1) * WIDE)
        for i, (source, target) in enumerate(((v_wide_hbm, v_stage), (dx_hbm, dx_stage))):
            copy = pltpu.make_async_copy(
                source.at[:, at], target.at[:, at], in_sems.at[i, block]
            )
            copy.start()
            copies.append(copy)
    b_end, c_live = b_end_ref[...], c_live_ref[...]
    own_sums = sums_ref[...]
    sums = own_sums
    dc = jnp.zeros((2 * width, 2 * rows), F32)
    db = jnp.zeros((2 * width, 2 * rows), F32)
    at_last = iota((rows, WIDE), 0) == rows - 1
    sent = []
    for block in range(blocks):
        at = slice(block * WIDE, (block + 1) * WIDE)
        ones = head_columns(heads, columns // heads, block)
        came, pull = came_ref[:, at], pull_ref[:, at]
        meet = jnp.sum(came * pull, axis=0, keepdims=True) * ends_ref[1:2, at]
        cames = stack(split2(came), 0)
        pulls = stack(split2(pull * ends_ref[0:1, at]), 0)
        xs, ys = xs_ref[:, at], ys_ref[:, at]
        out = dot(c_live, cames, 1, 0)
        back = dot(b_end, pulls, 1, 0)
        column_part = (xs[:rows].astype(F32) + xs[rows:].astype(F32)) * back
        row_part = (ys[:rows].astype(F32) + ys[rows:].astype(F32)) * out
        row_part = jnp.where(at_last, row_part + meet, row_part)
        for part in split2(stack([row_part - column_part, column_part], 0)):
            sums += dot(part, ones, 1, 0)
        dc += dot(cames, ys, 1, 1)
        db += dot(pulls, xs, 1, 1)
        copies[2 * block].wait()
        copies[2 * block + 1].wait()
        stage[:, at] = (dx_stage[:, at] + v_stage[:, at] * back).astype(BF16)
        copy = pltpu.make_async_copy(stage.at[:, at], dx_out.at[0, :, at], out_sems.at[block])
        copy.start()
        sent.append(copy)
    dc = (dc[:width, :rows] + dc[:width, rows:]) + dc[width:, :rows]
    db = (db[:width, :rows] + db[:width, rows:]) + db[width:, :rows]
    db_out[0] = (db_ref[...] + masks_ref[0:1] * db).astype(BF16)
    dc_out[0] = (dc_ref[...] + masks_ref[1:2] * dc).astype(BF16)
    square = (rows, rows)
    upper = jnp.where(iota(square, 0) >= iota(square, 1), 1.0, 0.0).astype(BF16)
    eye = jnp.where(iota(square, 0) == iota(square, 1), 1.0, 0.0).astype(BF16)
    at_end = jnp.sum(sums[rows:] - own_sums[rows:], axis=0, keepdims=True)
    dl = sums[:rows] + jnp.where(iota((rows, heads), 0) == rows - 1, at_end, 0.0)
    d_decay = sum(dot(part, upper, 0, 0) for part in split3(dl))
    total = sum(dot(part, eye, 0, 0) for part in split3(sums[rows:]))
    dt_out[0] = total / dt_ref[...] + rate_column(alog_ref) * d_decay
    for copy in sent:
        copy.wait()


def call(kernel, reach, outs, ins, flops, moved, scratch=()):
    spaces = {"s": pltpu.SMEM, "v": pltpu.VMEM, "h": pltpu.HBM}
    return pl.pallas_call(
        kernel,
        out_shape=[
            pltpu.HBM(*out) if place == "h" else jax.ShapeDtypeStruct(*out) for place, out in outs
        ],
        in_specs=[pl.BlockSpec(memory_space=spaces[place]) for place, _ in ins],
        out_specs=[pl.BlockSpec(memory_space=spaces[place]) for place, _ in outs],
        scratch_shapes=scratch,
        compiler_params=pltpu.CompilerParams(vmem_limit_bytes=min(16 + 2 * reach, 56) * 2**20),
        cost_estimate=pl.CostEstimate(flops=flops, bytes_accessed=moved, transcendentals=0),
    )(*(a for _, a in ins))


def send(a, by, second):
    count = lax.axis_size("ctx")
    pairs = [(i, i + by if (i + second) % 2 == 0 else i - by) for i in range(count)]
    return lax.ppermute(a, "ctx", [(i, j) for i, j in pairs if 0 <= j < count])


def in_hbm(a):
    return "h", pltpu.with_memory_space_constraint(a, pltpu.HBM)


def per_device(inputs, b_proj, c_proj, step_sizes, a_log, skip_gain, doc_lengths, grad_out):
    rows, columns = inputs.shape[1:]
    heads, width = a_log.shape[0], b_proj.shape[2]
    reach = max(lax.axis_size("ctx") // 4, 1)
    devices = lax.axis_size("ctx") * lax.axis_size("dp")
    alog, skip = a_log[None], skip_gain[None]
    bt, ct = jnp.swapaxes(b_proj, 1, 2), jnp.swapaxes(c_proj, 1, 2)
    blocks = columns // WIDE

    def v(shape, kind=F32):
        return "v", (shape, kind)

    dt, x, b, dy, c, *payloads = call(
        states_kernel,
        reach,
        [
            v((heads, rows)),
            v((rows, columns), BF16),
            v((width, rows), BF16),
            v((rows, columns), BF16),
            v((width, rows), BF16),
        ]
        + [v((columns // LANES * (width + 1), LANES))] * 2,
        [in_hbm(a) for a in (doc_lengths, alog, step_sizes, inputs, bt, grad_out, ct)],
        10**9,
        4 * 2**20,
        [
            pltpu.SMEM(doc_lengths.shape, jnp.int32),
            pltpu.VMEM(alog.shape, F32),
            pltpu.SemaphoreType.DMA((5,)),
            pltpu.SemaphoreType.DMA((2, PIECES)),
        ],
    )
    messages = [send(payloads[at % 2], at // 2 + 1, at % 2) for at in send_order(reach)]
    whole = "h", ((rows, columns), F32)
    state = v((width, columns))
    stage = pltpu.VMEM((rows, columns), F32)
    transposed = v((width, rows))
    xs, ys, v_wide, dx, b_end, c_live, masks, db, dc, sums, fwd_logs, bwd_logs, ends, small = call(
        inside_kernel,
        reach,
        [v((2 * rows, columns), BF16)] * 2
        + [whole] * 2
        + [v((rows, 2 * width), BF16)] * 2
        + [v((8, rows)), transposed, transposed, v((2 * rows, heads))]
        + [state, state, v((8, columns)), v((1, LANES))],
        [("s", doc_lengths)] + [("v", a) for a in (alog, skip, dt, x, b, dy, c)],
        4 * 10**9,
        12 * 2**20,
        [stage, stage, pltpu.SemaphoreType.DMA((2, blocks))],
    )
    partial, came, pull = call(
        functools.partial(rates_kernel, reach, columns // heads),
        reach,
        [v((devices, LANES)), state, state],
        [("v", a) for a in (*messages, ends, fwd_logs, bwd_logs, small)],
        10**8,
        4 * 2**20,
    )
    input_grads, b_gradient, c_gradient, step_grads = call(
        outputs_kernel,
        reach,
        [("h", ((1, rows, columns), BF16))]
        + [v((1, width, rows), BF16)] * 2
        + [v((1, heads, rows))],
        [("v", a) for a in (came, pull, ends, xs, ys)]
        + [in_hbm(v_wide), in_hbm(dx)]
        + [("v", a) for a in (b_end, c_live, masks, db, dc, sums, alog, dt)],
        2 * 10**9,
        12 * 2**20,
        [
            stage,
            stage,
            pltpu.VMEM((rows, columns), BF16),
            pltpu.SemaphoreType.DMA((2, blocks)),
            pltpu.SemaphoreType.DMA((blocks,)),
        ],
    )
    gathered = lax.all_to_all(partial, ("dp", "ctx"), 0, 0, tiled=True)
    totals = jnp.sum(gathered, axis=0)
    return (
        input_grads,
        jnp.swapaxes(b_gradient, 1, 2),
        jnp.swapaxes(c_gradient, 1, 2),
        step_grads,
        totals[:heads],
        totals[heads : 2 * heads],
    )


def solution(mesh):
    in_specs = (
        P("dp", "ctx", None),
        P("dp", "ctx", None),
        P("dp", "ctx", None),
        P("dp", None, "ctx"),
        P(),
        P(),
        P("dp", None),
        P("dp", "ctx", None),
    )
    out_specs = (
        P("dp", "ctx", None),
        P("dp", "ctx", None),
        P("dp", "ctx", None),
        P("dp", None, "ctx"),
        P(),
        P(),
    )
    return jax.shard_map(
        per_device, mesh=mesh, in_specs=in_specs, out_specs=out_specs, check_vma=False
    )
```

```python
import functools

import jax
import jax.numpy as jnp
from jax import lax
from jax.experimental import pallas as pl
from jax.experimental.pallas import tpu as pltpu
from jax.sharding import PartitionSpec as P

F32 = jnp.float32
BF16 = jnp.bfloat16
LANES = 128
WIDE = 256
PARTS = WIDE // LANES
FAR = 2**30
PIECES = 4


def dot(a, b, ca, cb):
    return lax.dot_general(a, b, (((ca,), (cb,)), ((), ())), preferred_element_type=F32)


def iota(shape, dim):
    return lax.broadcasted_iota(jnp.int32, shape, dim)


def split2(a):
    high = a.astype(BF16)
    return high, (a - high.astype(F32)).astype(BF16)


def split3(a):
    high = a.astype(BF16)
    rest = a - high.astype(F32)
    middle = rest.astype(BF16)
    return high, middle, (rest - middle.astype(F32)).astype(BF16)


def dot_pairs(a, b, ca, cb):
    return dot(a[0], b[0], ca, cb) + (dot(a[0], b[1], ca, cb) + dot(a[1], b[0], ca, cb))


def stack(parts, axis):
    return jnp.concatenate(parts, axis=axis)


def document_places(lens_ref, rows):
    offset = shard() * rows
    starts = [jnp.int32(0)]
    for d in range(lens_ref.shape[1] - 1):
        starts.append(starts[-1] + lens_ref[0, d])
    first = jnp.int32(FAR)
    last = jnp.int32(0)
    for start in starts:
        first = jnp.minimum(first, jnp.where(start >= offset, start, FAR))
        last = jnp.maximum(last, jnp.where(start < offset + rows, start, 0))
    return starts, offset, first, last


def rate_column(alog_ref):
    heads = alog_ref.shape[1]
    square = jnp.broadcast_to(alog_ref[...], (heads, heads))
    picked = jnp.where(iota((heads, heads), 0) == iota((heads, heads), 1), square, 0.0)
    return -jnp.exp(jnp.sum(picked, axis=1, keepdims=True))


def log2(size):
    assert size & (size - 1) == 0
    return size.bit_length() - 1


def head_distance(heads, head_width):
    shape = (3 * heads, WIDE)
    return (iota(shape, 0) & (heads - 1)) - lax.shift_right_logical(
        iota(shape, 1), log2(head_width)
    )


def head_rows(distance, head_width, block):
    return jnp.where(distance == block * (WIDE // head_width), 1.0, 0.0).astype(BF16)


def head_columns(heads, head_width, block):
    shape = (WIDE, heads)
    column = lax.shift_right_logical(iota(shape, 0), log2(head_width))
    return jnp.where(iota(shape, 1) - column == block * (WIDE // head_width), 1.0, 0.0).astype(BF16)


def shard():
    return lax.axis_index("ctx")


def message_block(ref, block, width):
    at = block * PARTS
    return stack([ref[(at + i) * width : (at + i + 1) * width, :] for i in range(PARTS)], 1)


def message_tail(ref, block, width):
    tail = ref.shape[0] // (width + 1) * width + block * PARTS
    return stack([ref[tail + i : tail + i + 1, :] for i in range(PARTS)], 1)


def received(refs, block, width):
    came = pull = None
    for j in range(len(refs) // 2, 0, -1):
        one, two = refs[2 * j - 2], refs[2 * j - 1]
        a, b = message_block(one, block, width), message_block(two, block, width)
        first = jnp.broadcast_to(lax.rem(shard() + j, 2), a.shape) == 0
        near_came, near_pull = jnp.where(first, a, b), jnp.where(first, b, a)
        if came is None:
            came, pull = near_came, near_pull
        else:
            a, b = message_tail(one, block, width), message_tail(two, block, width)
            first = jnp.broadcast_to(lax.rem(shard() + j, 2), a.shape) == 0
            came = near_came + jnp.where(first, a, b) * came
            pull = near_pull + jnp.where(first, b, a) * pull
    return came, pull


def states_kernel(
    lens_hbm,
    alog_hbm,
    dt_hbm,
    x_hbm,
    b_hbm,
    dy_hbm,
    c_hbm,
    dt_ref,
    x_ref,
    b_ref,
    dy_ref,
    c_ref,
    one_ref,
    two_ref,
    lens_ref,
    alog_ref,
    small_sems,
    sems,
):
    rows, columns = x_ref.shape
    heads, width = dt_ref.shape[0], b_ref.shape[0]
    head_width = columns // heads
    piece = columns // PIECES
    small = [
        pltpu.make_async_copy(source, target, small_sems.at[i])
        for i, (source, target) in enumerate(
            (
                (lens_hbm, lens_ref),
                (alog_hbm, alog_ref),
                (dt_hbm.at[0], dt_ref),
                (b_hbm.at[0], b_ref),
                (c_hbm.at[0], c_ref),
            )
        )
    ]
    for copy in small:
        copy.start()
    large = []
    for i in range(PIECES):
        at = slice(i * piece, (i + 1) * piece)
        for side, (source, target) in enumerate(((x_hbm, x_ref), (dy_hbm, dy_ref))):
            copy = pltpu.make_async_copy(
                source.at[0, :, at], target.at[:, at], sems.at[side, i]
            )
            copy.start()
            large.append(copy)
    square = (rows, rows)
    upper = jnp.where(iota(square, 0) <= iota(square, 1), 1.0, 0.0).astype(BF16)
    even = jnp.broadcast_to(lax.rem(shard(), 2), (width, LANES)) == 0
    left = iota((1, LANES), 1) < head_width
    for copy in small:
        copy.wait()
    _, offset, first, last = document_places(lens_ref, rows)
    through = jnp.where(first >= offset + rows, 1.0, 0.0)
    dt = dt_ref[...]
    logs = sum(dot(part, upper, 1, 0) for part in split3(dt * rate_column(alog_ref)))
    end_log = logs[:, rows - 1 : rows]
    place = iota((heads, rows), 1) + offset
    keeping = jnp.where(place >= last, jnp.exp(end_log - logs) * dt, 0.0)
    carried = jnp.where(place < first, jnp.exp(logs), 0.0)
    kept = jnp.broadcast_to(jnp.exp(end_log) * through, (heads, LANES))
    b, c = b_ref[...].astype(F32), c_ref[...].astype(F32)
    own = LANES // head_width

    def pair_states(vectors, weights, values):
        parts = []
        for h in range(own):
            parts += split2(vectors * weights[h : h + 1, :])
        out = dot(stack(parts, 0), values, 1, 0)
        sides = [
            out[2 * h * width : (2 * h + 1) * width]
            + out[(2 * h + 1) * width : (2 * h + 2) * width]
            for h in range(own)
        ]
        return jnp.where(left, sides[0], sides[1])

    for pair in range(columns // LANES):
        if pair * LANES % piece == 0:
            large[pair * LANES // piece * 2].wait()
            large[pair * LANES // piece * 2 + 1].wait()
        at = slice(pair * LANES, (pair + 1) * LANES)
        here = slice(pair * own, (pair + 1) * own)
        state = pair_states(b, keeping[here], x_ref[:, at])
        pulled = pair_states(c, carried[here], dy_ref[:, at])
        tail = columns // LANES * width + pair
        one_ref[pair * width : (pair + 1) * width, :] = jnp.where(even, state, pulled)
        two_ref[pair * width : (pair + 1) * width, :] = jnp.where(even, pulled, state)
        one_ref[tail : tail + 1, :] = jnp.where(left, kept[here][:1], kept[here][1:])
        two_ref[tail : tail + 1, :] = jnp.where(left, kept[here][:1], kept[here][1:])


def inside_kernel(
    lens_ref,
    alog_ref,
    skip_ref,
    dt_ref,
    x_ref,
    b_ref,
    dy_ref,
    c_ref,
    xs_ref,
    ys_ref,
    v_wide_hbm,
    dx_hbm,
    b_end_ref,
    c_live_ref,
    masks_ref,
    db_ref,
    dc_ref,
    sums_ref,
    fwd_ref,
    bwd_ref,
    ends_ref,
    small_ref,
    v_stage,
    dx_stage,
    sems,
):
    rows, columns = x_ref.shape
    heads, width = dt_ref.shape[0], b_ref.shape[0]
    head_width = columns // heads
    starts, offset, first, last = document_places(lens_ref, rows)
    through = jnp.where(first >= offset + rows, 1.0, 0.0)
    square = (rows, rows)
    place0, place1 = iota(square, 0) + offset, iota(square, 1) + offset
    segment0, segment1 = jnp.zeros(square, jnp.int32), jnp.zeros(square, jnp.int32)
    for start in starts:
        segment0 += jnp.where(place0 >= start, 1, 0)
        segment1 += jnp.where(place1 >= start, 1, 0)
    same = segment0 == segment1
    down = same & (place0 >= place1)
    lower = jnp.where(place0 >= place1, 1.0, 0.0).astype(BF16)
    eye = jnp.where(place0 == place1, 1.0, 0.0).astype(BF16)
    dt = dt_ref[...]
    logs = sum(dot(lower, part, 1, 1) for part in split3(dt * rate_column(alog_ref)))
    steps = sum(dot(eye, part, 1, 1) for part in split3(dt))
    bt, ct = b_ref[...], c_ref[...]
    scores = split2(jnp.where(down, dot(ct, bt, 0, 0), 0.0))
    flipped = split2(jnp.where(same & (place1 >= place0), dot(bt, ct, 0, 0), 0.0))
    place = iota((width, rows), 1) + offset
    bt_end = jnp.where(place >= last, bt.astype(F32), 0.0)
    ct_live = jnp.where(place < first, ct.astype(F32), 0.0)
    b_end, c_live = jnp.transpose(bt_end).astype(BF16), jnp.transpose(ct_live).astype(BF16)
    bt_end, ct_live = bt_end.astype(BF16), ct_live.astype(BF16)
    b_end_ref[...] = stack([b_end, b_end], 1)
    c_live_ref[...] = stack([c_live, c_live], 1)
    bt_end, ct_live = stack([bt_end, bt_end], 1), stack([ct_live, ct_live], 1)
    masks_ref[0:1] = jnp.where(place[:1] >= last, 1.0, 0.0)
    masks_ref[1:2] = jnp.where(place[:1] < first, 1.0, 0.0)
    tables = stack(
        [
            stack(split3(a), 1)
            for a in (
                jnp.exp(logs),
                jnp.exp(-logs) * steps,
                logs,
                jnp.broadcast_to(skip_ref[...], (16, heads)),
            )
        ],
        0,
    )
    distance = head_distance(heads, head_width)
    d_scores = jnp.zeros(square, F32)
    sums = jnp.zeros((2 * rows, heads), F32)
    products = jnp.zeros((8, heads), F32)
    copies = []
    for block in range(columns // WIDE):
        at = slice(block * WIDE, (block + 1) * WIDE)
        wide = dot(tables, head_rows(distance, head_width, block), 1, 0)
        ones = head_columns(heads, head_width, block)
        u_wide, v_wide, l_wide = wide[:rows], wide[rows : 2 * rows], wide[2 * rows : 3 * rows]
        skip_wide = wide[3 * rows : 3 * rows + 1]
        x = x_ref[:, at].astype(F32)
        dy = dy_ref[:, at].astype(F32)
        xv = x * v_wide
        yu = dy * u_wide
        xs, ys = split2(xv), split2(yu)
        xs_ref[:, at] = stack(xs, 0)
        ys_ref[:, at] = stack(ys, 0)
        v_stage[:, at] = v_wide
        out = dot_pairs(scores, xs, 1, 0)
        back = dot_pairs(flipped, ys, 1, 0)
        d_scores += dot_pairs(ys, xs, 1, 1)
        dx_stage[:, at] = v_wide * back + skip_wide * dy
        for i, (stage, target) in enumerate(((v_stage, v_wide_hbm), (dx_stage, dx_hbm))):
            copy = pltpu.make_async_copy(stage.at[:, at], target.at[:, at], sems.at[i, block])
            copy.start()
            copies.append(copy)
        column_part = xv * back
        for part in split3(stack([yu * out - column_part, column_part], 0)):
            sums += dot(part, ones, 1, 0)
        product = jnp.broadcast_to(jnp.sum(x * dy, axis=0, keepdims=True), (8, WIDE))
        for part in split3(product):
            products += dot(part, ones, 1, 0)
        ending = u_wide[rows - 1 : rows]
        end_log = l_wide[rows - 1 : rows]
        gap = end_log - l_wide
        fwd_ref[:, at] = dot(bt_end, stack(split2(xv * gap), 0), 1, 0) * ending
        bwd_ref[:, at] = dot(ct_live, stack(split2(yu * l_wide), 0), 1, 0)
        ends_ref[0:1, at] = ending
        ends_ref[1:2, at] = ending * through
        ends_ref[2:3, at] = ending * through * end_log
    d_scores = split2(jnp.where(down, d_scores, 0.0))
    dc_ref[...] = sum(dot(bt, p, 1, 1) for p in d_scores)
    db_ref[...] = sum(dot(ct, p, 1, 0) for p in d_scores)
    sums_ref[...] = sums
    rate_grads = jnp.sum(logs * sums[:rows], axis=0, keepdims=True)
    empty = jnp.zeros((1, LANES - 2 * heads), F32)
    small_ref[...] = stack([rate_grads, products[:1], empty], 1)
    for copy in copies:
        copy.wait()


def send_order(reach):
    return [at for j in range(reach) for at in (2 * j + 1, 2 * j)]


def rates_kernel(reach, head_width, *refs):
    messages = [ref for _, ref in sorted(zip(send_order(reach), refs), key=lambda pair: pair[0])]
    ends_ref, fwd_ref, bwd_ref, small_ref, out_ref, came_ref, pull_ref = refs[2 * reach :]
    width, columns = fwd_ref.shape
    blocks = columns // WIDE
    whole = []
    for block in range(blocks):
        at = slice(block * WIDE, (block + 1) * WIDE)
        came, pull = received(messages, block, width)
        came_ref[:, at] = came
        pull_ref[:, at] = pull
        terms = came * bwd_ref[:, at] + pull * (fwd_ref[:, at] + ends_ref[2:3, at] * came)
        whole.append(jnp.sum(terms, axis=0, keepdims=True))
    own = WIDE // head_width
    shape = (WIDE, LANES)
    column = lax.shift_right_logical(iota(shape, 0), log2(head_width))
    ones = jnp.where(column == (iota(shape, 1) & (own - 1)), 1.0, 0.0).astype(BF16)
    sums = sum(dot(part, ones, 1, 0) for part in split3(stack(whole, 0)))
    lane = iota(sums.shape, 1)
    mine = lax.shift_right_logical(lane, log2(own)) == iota(sums.shape, 0)
    total = small_ref[...] + jnp.sum(jnp.where(mine, sums, 0.0), axis=0, keepdims=True)
    out_ref[...] = jnp.broadcast_to(total, out_ref.shape)


def outputs_kernel(start, size, final, *refs):
    (
        came_ref,
        pull_ref,
        ends_ref,
        xs_ref,
        ys_ref,
        v_wide_hbm,
        dx_hbm,
        b_end_ref,
        c_live_ref,
        masks_ref,
        db_ref,
        dc_ref,
        sums_ref,
        own_ref,
        alog_ref,
        dt_ref,
        *refs,
    ) = refs
    if start:
        refs = refs[2:]
    dx_out, db_out, dc_out, last_out = refs[:4]
    v_stage, dx_stage, back_stage, stage, in_sems, out_sems = refs[4:]
    rows, columns = dx_hbm.shape
    heads, width = dt_ref.shape[0], db_ref.shape[0]
    copies = []
    for i in range(size):
        own = slice(i * WIDE, (i + 1) * WIDE)
        at = slice((start + i) * WIDE, (start + i + 1) * WIDE)
        for side, (source, target) in enumerate(((v_wide_hbm, v_stage), (dx_hbm, dx_stage))):
            copy = pltpu.make_async_copy(
                source.at[:, at], target.at[:, own], in_sems.at[side, i]
            )
            copy.start()
            copies.append(copy)
    b_end, c_live = b_end_ref[...], c_live_ref[...]
    sums = sums_ref[...]
    dc = jnp.zeros((2 * width, 2 * rows), F32)
    db = jnp.zeros((2 * width, 2 * rows), F32)
    at_last = iota((rows, WIDE), 0) == rows - 1
    for i in range(size):
        own = slice(i * WIDE, (i + 1) * WIDE)
        at = slice((start + i) * WIDE, (start + i + 1) * WIDE)
        ones = head_columns(heads, columns // heads, start + i)
        came, pull = came_ref[:, at], pull_ref[:, at]
        meet = jnp.sum(came * pull, axis=0, keepdims=True) * ends_ref[1:2, at]
        cames = stack(split2(came), 0)
        pulls = stack(split2(pull * ends_ref[0:1, at]), 0)
        xs, ys = xs_ref[:, at], ys_ref[:, at]
        out = dot(c_live, cames, 1, 0)
        back = dot(b_end, pulls, 1, 0)
        back_stage[:, own] = back
        column_part = (xs[:rows].astype(F32) + xs[rows:].astype(F32)) * back
        row_part = (ys[:rows].astype(F32) + ys[rows:].astype(F32)) * out
        row_part = jnp.where(at_last, row_part + meet, row_part)
        for part in split2(stack([row_part - column_part, column_part], 0)):
            sums += dot(part, ones, 1, 0)
        dc += dot(cames, ys, 1, 1)
        db += dot(pulls, xs, 1, 1)
    sent = []
    for i in range(size):
        own = slice(i * WIDE, (i + 1) * WIDE)
        at = slice((start + i) * WIDE, (start + i + 1) * WIDE)
        copies[2 * i].wait()
        copies[2 * i + 1].wait()
        total = dx_stage[:, own] + v_stage[:, own] * back_stage[:, own]
        stage[:, own] = total.astype(BF16)
        copy = pltpu.make_async_copy(stage.at[:, own], dx_out.at[0, :, at], out_sems.at[i])
        copy.start()
        sent.append(copy)
    dc = (dc[:width, :rows] + dc[:width, rows:]) + dc[width:, :rows]
    db = (db[:width, :rows] + db[:width, rows:]) + db[width:, :rows]
    db = db_ref[...] + masks_ref[0:1] * db
    dc = dc_ref[...] + masks_ref[1:2] * dc
    if final:
        db_out[0] = db.astype(BF16)
        dc_out[0] = dc.astype(BF16)
        square = (rows, rows)
        upper = jnp.where(iota(square, 0) >= iota(square, 1), 1.0, 0.0).astype(BF16)
        eye = jnp.where(iota(square, 0) == iota(square, 1), 1.0, 0.0).astype(BF16)
        at_end = jnp.sum(sums[rows:] - own_ref[rows:], axis=0, keepdims=True)
        dl = sums[:rows] + jnp.where(iota((rows, heads), 0) == rows - 1, at_end, 0.0)
        d_decay = sum(dot(part, upper, 0, 0) for part in split3(dl))
        total = sum(dot(part, eye, 0, 0) for part in split3(sums[rows:]))
        last_out[0] = total / dt_ref[...] + rate_column(alog_ref) * d_decay
    else:
        db_out[...] = db
        dc_out[...] = dc
        last_out[...] = sums
    for copy in sent:
        copy.wait()


def call(kernel, reach, outs, ins, flops, moved, scratch=(), aliases=None):
    spaces = {"s": pltpu.SMEM, "v": pltpu.VMEM, "h": pltpu.HBM}
    return pl.pallas_call(
        kernel,
        out_shape=[
            pltpu.HBM(*out) if place == "h" else jax.ShapeDtypeStruct(*out) for place, out in outs
        ],
        in_specs=[pl.BlockSpec(memory_space=spaces[place]) for place, _ in ins],
        out_specs=[pl.BlockSpec(memory_space=spaces[place]) for place, _ in outs],
        scratch_shapes=scratch,
        input_output_aliases=aliases or {},
        compiler_params=pltpu.CompilerParams(vmem_limit_bytes=min(16 + 2 * reach, 56) * 2**20),
        cost_estimate=pl.CostEstimate(flops=flops, bytes_accessed=moved, transcendentals=0),
    )(*(a for _, a in ins))


def send(a, by, second):
    count = lax.axis_size("ctx")
    pairs = [(i, i + by if (i + second) % 2 == 0 else i - by) for i in range(count)]
    return lax.ppermute(a, "ctx", [(i, j) for i, j in pairs if 0 <= j < count])


def in_hbm(a):
    return "h", pltpu.with_memory_space_constraint(a, pltpu.HBM)


def per_device(inputs, b_proj, c_proj, step_sizes, a_log, skip_gain, doc_lengths, grad_out):
    rows, columns = inputs.shape[1:]
    heads, width = a_log.shape[0], b_proj.shape[2]
    reach = max(lax.axis_size("ctx") // 4, 1)
    alog, skip = a_log[None], skip_gain[None]
    bt, ct = jnp.swapaxes(b_proj, 1, 2), jnp.swapaxes(c_proj, 1, 2)
    blocks = columns // WIDE

    def v(shape, kind=F32):
        return "v", (shape, kind)

    dt, x, b, dy, c, *payloads = call(
        states_kernel,
        reach,
        [
            v((heads, rows)),
            v((rows, columns), BF16),
            v((width, rows), BF16),
            v((rows, columns), BF16),
            v((width, rows), BF16),
        ]
        + [v((columns // LANES * (width + 1), LANES))] * 2,
        [in_hbm(a) for a in (doc_lengths, alog, step_sizes, inputs, bt, grad_out, ct)],
        10**9,
        4 * 2**20,
        [
            pltpu.SMEM(doc_lengths.shape, jnp.int32),
            pltpu.VMEM(alog.shape, F32),
            pltpu.SemaphoreType.DMA((5,)),
            pltpu.SemaphoreType.DMA((2, PIECES)),
        ],
    )
    messages = [send(payloads[at % 2], at // 2 + 1, at % 2) for at in send_order(reach)]
    whole = "h", ((rows, columns), F32)
    state = v((width, columns))
    stage = pltpu.VMEM((rows, columns), F32)
    transposed = v((width, rows))
    xs, ys, v_wide, dx, b_end, c_live, masks, db, dc, own_sums, *rest = call(
        inside_kernel,
        reach,
        [v((2 * rows, columns), BF16)] * 2
        + [whole] * 2
        + [v((rows, 2 * width), BF16)] * 2
        + [v((8, rows)), transposed, transposed, v((2 * rows, heads))]
        + [state, state, v((8, columns)), v((1, LANES))],
        [("s", doc_lengths)] + [("v", a) for a in (alog, skip, dt, x, b, dy, c)],
        4 * 10**9,
        12 * 2**20,
        [stage, stage, pltpu.SemaphoreType.DMA((2, blocks))],
    )
    fwd_logs, bwd_logs, ends, small = rest
    partial, came, pull = call(
        functools.partial(rates_kernel, reach, columns // heads),
        reach,
        [v((lax.axis_size("ctx"), LANES)), state, state],
        [("v", a) for a in (*messages, ends, fwd_logs, bwd_logs, small)],
        10**8,
        4 * 2**20,
    )
    half = blocks // 2
    wide = (rows, half * WIDE)
    sums, previous = own_sums, []
    for start in (0, half):
        final = start > 0
        outs = [("h", ((1, rows, columns), BF16))]
        if final:
            outs += [v((1, width, rows), BF16)] * 2 + [v((1, heads, rows))]
        else:
            outs += [transposed, transposed, v((2 * rows, heads))]
            gathered = lax.all_to_all(partial, "ctx", 0, 0, tiled=True)
            own = jnp.broadcast_to(
                jnp.sum(gathered, axis=0, keepdims=True), (lax.axis_size("dp"), LANES)
            )
        results = call(
            functools.partial(outputs_kernel, start, half, final),
            reach,
            outs,
            [("v", a) for a in (came, pull, ends, xs, ys)]
            + [in_hbm(v_wide), in_hbm(dx)]
            + [("v", a) for a in (b_end, c_live, masks, db, dc, sums, own_sums, alog, dt)]
            + previous,
            10**9,
            6 * 2**20,
            [pltpu.VMEM(wide, F32)] * 3
            + [
                pltpu.VMEM(wide, BF16),
                pltpu.SemaphoreType.DMA((2, half)),
                pltpu.SemaphoreType.DMA((half,)),
            ],
            {16: 0} if final else None,
        )
        if not final:
            previous = [("h", results[0]), ("v", own)]
            _, db, dc, sums = results
    input_grads, b_gradient, c_gradient, step_grads = results
    totals = jnp.sum(lax.all_to_all(own, "dp", 0, 0, tiled=True), axis=0)
    return (
        input_grads,
        jnp.swapaxes(b_gradient, 1, 2),
        jnp.swapaxes(c_gradient, 1, 2),
        step_grads,
        totals[:heads],
        totals[heads : 2 * heads],
    )


def solution(mesh):
    in_specs = (
        P("dp", "ctx", None),
        P("dp", "ctx", None),
        P("dp", "ctx", None),
        P("dp", None, "ctx"),
        P(),
        P(),
        P("dp", None),
        P("dp", "ctx", None),
    )
    out_specs = (
        P("dp", "ctx", None),
        P("dp", "ctx", None),
        P("dp", "ctx", None),
        P("dp", None, "ctx"),
        P(),
        P(),
    )
    return jax.shard_map(
        per_device, mesh=mesh, in_specs=in_specs, out_specs=out_specs, check_vma=False
    )
```

```python
import functools

import jax
import jax.numpy as jnp
from jax import lax
from jax.experimental import pallas as pl
from jax.experimental.pallas import tpu as pltpu
from jax.sharding import PartitionSpec as P

F32 = jnp.float32
BF16 = jnp.bfloat16
LANES = 128
WIDE = 256
PARTS = WIDE // LANES
FAR = 2**30
PIECES = 4


def dot(a, b, ca, cb):
    return lax.dot_general(a, b, (((ca,), (cb,)), ((), ())), preferred_element_type=F32)


def iota(shape, dim):
    return lax.broadcasted_iota(jnp.int32, shape, dim)


def split2(a):
    high = a.astype(BF16)
    return high, (a - high.astype(F32)).astype(BF16)


def split3(a):
    high = a.astype(BF16)
    rest = a - high.astype(F32)
    middle = rest.astype(BF16)
    return high, middle, (rest - middle.astype(F32)).astype(BF16)


def dot_pairs(a, b, ca, cb):
    return dot(a[0], b[0], ca, cb) + (dot(a[0], b[1], ca, cb) + dot(a[1], b[0], ca, cb))


def stack(parts, axis):
    return jnp.concatenate(parts, axis=axis)


def document_places(lens_ref, rows):
    offset = shard() * rows
    starts = [jnp.int32(0)]
    for d in range(lens_ref.shape[1] - 1):
        starts.append(starts[-1] + lens_ref[0, d])
    first = jnp.int32(FAR)
    last = jnp.int32(0)
    for start in starts:
        first = jnp.minimum(first, jnp.where(start >= offset, start, FAR))
        last = jnp.maximum(last, jnp.where(start < offset + rows, start, 0))
    return starts, offset, first, last


def rate_column(alog_ref):
    heads = alog_ref.shape[1]
    square = jnp.broadcast_to(alog_ref[...], (heads, heads))
    picked = jnp.where(iota((heads, heads), 0) == iota((heads, heads), 1), square, 0.0)
    return -jnp.exp(jnp.sum(picked, axis=1, keepdims=True))


def log2(size):
    assert size & (size - 1) == 0
    return size.bit_length() - 1


def head_distance(heads, head_width):
    shape = (3 * heads, WIDE)
    return (iota(shape, 0) & (heads - 1)) - lax.shift_right_logical(
        iota(shape, 1), log2(head_width)
    )


def head_rows(distance, head_width, block):
    return jnp.where(distance == block * (WIDE // head_width), 1.0, 0.0).astype(BF16)


def head_columns(heads, head_width, block):
    shape = (WIDE, heads)
    column = lax.shift_right_logical(iota(shape, 0), log2(head_width))
    return jnp.where(iota(shape, 1) - column == block * (WIDE // head_width), 1.0, 0.0).astype(BF16)


def shard():
    return lax.axis_index("ctx")


def message_block(ref, block, width):
    at = block * PARTS
    return stack([ref[(at + i) * width : (at + i + 1) * width, :] for i in range(PARTS)], 1)


def message_tail(ref, block, width):
    tail = ref.shape[0] // (width + 1) * width + block * PARTS
    return stack([ref[tail + i : tail + i + 1, :] for i in range(PARTS)], 1)


def message_plan(reach):
    near = [(1, 0, 0)]
    relayed = [(1, 1, 0), (1, 1, 1)]
    far = [(2, 1, 0), (2, 1, 1), (2, 0, 0)] if reach > 1 else []
    rest = [(j, *one) for j in range(3, reach + 1) for one in ((0, 0), (1, 0), (1, 1))]
    return near + far + relayed + rest


def received(messages, reach, block, blocks, width):
    came = pull = None
    half, inner = divmod(block, blocks // 2)
    for j in range(reach, 0, -1):
        one, two = messages[j, 0, 0], messages[j, 1, half]
        a, b = message_block(one, block, width), message_block(two, inner, width)
        first = jnp.broadcast_to(lax.rem(shard() + j, 2), a.shape) == 0
        near_came, near_pull = jnp.where(first, a, b), jnp.where(first, b, a)
        if came is None:
            came, pull = near_came, near_pull
        else:
            a, b = message_tail(one, block, width), message_tail(two, inner, width)
            first = jnp.broadcast_to(lax.rem(shard() + j, 2), a.shape) == 0
            came = near_came + jnp.where(first, a, b) * came
            pull = near_pull + jnp.where(first, b, a) * pull
    return came, pull


def states_kernel(
    lens_hbm,
    alog_hbm,
    dt_hbm,
    x_hbm,
    b_hbm,
    dy_hbm,
    c_hbm,
    dt_ref,
    x_ref,
    b_ref,
    dy_ref,
    c_ref,
    one_ref,
    two_ref,
    three_ref,
    lens_ref,
    alog_ref,
    small_sems,
    sems,
):
    rows, columns = x_ref.shape
    heads, width = dt_ref.shape[0], b_ref.shape[0]
    head_width = columns // heads
    piece = columns // PIECES
    small = [
        pltpu.make_async_copy(source, target, small_sems.at[i])
        for i, (source, target) in enumerate(
            (
                (lens_hbm, lens_ref),
                (alog_hbm, alog_ref),
                (dt_hbm.at[0], dt_ref),
                (b_hbm.at[0], b_ref),
                (c_hbm.at[0], c_ref),
            )
        )
    ]
    for copy in small:
        copy.start()
    large = []
    for i in range(PIECES):
        at = slice(i * piece, (i + 1) * piece)
        for side, (source, target) in enumerate(((x_hbm, x_ref), (dy_hbm, dy_ref))):
            copy = pltpu.make_async_copy(
                source.at[0, :, at], target.at[:, at], sems.at[side, i]
            )
            copy.start()
            large.append(copy)
    square = (rows, rows)
    upper = jnp.where(iota(square, 0) <= iota(square, 1), 1.0, 0.0).astype(BF16)
    even = jnp.broadcast_to(lax.rem(shard(), 2), (width, LANES)) == 0
    left = iota((1, LANES), 1) < head_width
    for copy in small:
        copy.wait()
    _, offset, first, last = document_places(lens_ref, rows)
    through = jnp.where(first >= offset + rows, 1.0, 0.0)
    dt = dt_ref[...]
    logs = sum(dot(part, upper, 1, 0) for part in split3(dt * rate_column(alog_ref)))
    end_log = logs[:, rows - 1 : rows]
    place = iota((heads, rows), 1) + offset
    keeping = jnp.where(place >= last, jnp.exp(end_log - logs) * dt, 0.0)
    carried = jnp.where(place < first, jnp.exp(logs), 0.0)
    kept = jnp.broadcast_to(jnp.exp(end_log) * through, (heads, LANES))
    b, c = b_ref[...].astype(F32), c_ref[...].astype(F32)
    own = LANES // head_width

    def pair_states(vectors, weights, values):
        parts = []
        for h in range(own):
            parts += split2(vectors * weights[h : h + 1, :])
        out = dot(stack(parts, 0), values, 1, 0)
        sides = [
            out[2 * h * width : (2 * h + 1) * width]
            + out[(2 * h + 1) * width : (2 * h + 2) * width]
            for h in range(own)
        ]
        return jnp.where(left, sides[0], sides[1])

    for pair in range(columns // LANES):
        if pair * LANES % piece == 0:
            large[pair * LANES // piece * 2].wait()
            large[pair * LANES // piece * 2 + 1].wait()
        at = slice(pair * LANES, (pair + 1) * LANES)
        here = slice(pair * own, (pair + 1) * own)
        state = pair_states(b, keeping[here], x_ref[:, at])
        pulled = pair_states(c, carried[here], dy_ref[:, at])
        kept_row = jnp.where(left, kept[here][:1], kept[here][1:])
        first, second = jnp.where(even, state, pulled), jnp.where(even, pulled, state)
        pairs = columns // LANES
        half, inner = divmod(pair, pairs // 2)
        for ref, at, whole, value in (
            (one_ref, pair, pairs, first),
            ((two_ref, three_ref)[half], inner, pairs // 2, second),
        ):
            ref[at * width : (at + 1) * width, :] = value
            ref[whole * width + at : whole * width + at + 1, :] = kept_row


def inside_kernel(
    lens_ref,
    alog_ref,
    skip_ref,
    dt_ref,
    x_ref,
    b_ref,
    dy_ref,
    c_ref,
    _,
    xs_ref,
    ys_ref,
    v_wide_hbm,
    dx_hbm,
    b_end_ref,
    c_live_ref,
    masks_ref,
    db_ref,
    dc_ref,
    sums_ref,
    fwd_ref,
    bwd_ref,
    ends_ref,
    small_ref,
    v_stage,
    dx_stage,
    sems,
):
    rows, columns = x_ref.shape
    heads, width = dt_ref.shape[0], b_ref.shape[0]
    head_width = columns // heads
    starts, offset, first, last = document_places(lens_ref, rows)
    through = jnp.where(first >= offset + rows, 1.0, 0.0)
    square = (rows, rows)
    place0, place1 = iota(square, 0) + offset, iota(square, 1) + offset
    segment0, segment1 = jnp.zeros(square, jnp.int32), jnp.zeros(square, jnp.int32)
    for start in starts:
        segment0 += jnp.where(place0 >= start, 1, 0)
        segment1 += jnp.where(place1 >= start, 1, 0)
    same = segment0 == segment1
    down = same & (place0 >= place1)
    lower = jnp.where(place0 >= place1, 1.0, 0.0).astype(BF16)
    eye = jnp.where(place0 == place1, 1.0, 0.0).astype(BF16)
    dt = dt_ref[...]
    logs = sum(dot(lower, part, 1, 1) for part in split3(dt * rate_column(alog_ref)))
    steps = sum(dot(eye, part, 1, 1) for part in split3(dt))
    bt, ct = b_ref[...], c_ref[...]
    scores = split2(jnp.where(down, dot(ct, bt, 0, 0), 0.0))
    flipped = split2(jnp.where(same & (place1 >= place0), dot(bt, ct, 0, 0), 0.0))
    place = iota((width, rows), 1) + offset
    bt_end = jnp.where(place >= last, bt.astype(F32), 0.0)
    ct_live = jnp.where(place < first, ct.astype(F32), 0.0)
    b_end, c_live = jnp.transpose(bt_end).astype(BF16), jnp.transpose(ct_live).astype(BF16)
    bt_end, ct_live = bt_end.astype(BF16), ct_live.astype(BF16)
    b_end_ref[...] = stack([b_end, b_end], 1)
    c_live_ref[...] = stack([c_live, c_live], 1)
    bt_end, ct_live = stack([bt_end, bt_end], 1), stack([ct_live, ct_live], 1)
    masks_ref[0:1] = jnp.where(place[:1] >= last, 1.0, 0.0)
    masks_ref[1:2] = jnp.where(place[:1] < first, 1.0, 0.0)
    tables = stack(
        [
            stack(split3(a), 1)
            for a in (
                jnp.exp(logs),
                jnp.exp(-logs) * steps,
                logs,
                jnp.broadcast_to(skip_ref[...], (16, heads)),
            )
        ],
        0,
    )
    distance = head_distance(heads, head_width)
    d_scores = jnp.zeros(square, F32)
    sums = jnp.zeros((2 * rows, heads), F32)
    products = jnp.zeros((8, heads), F32)
    copies = []
    for block in range(columns // WIDE):
        at = slice(block * WIDE, (block + 1) * WIDE)
        wide = dot(tables, head_rows(distance, head_width, block), 1, 0)
        ones = head_columns(heads, head_width, block)
        u_wide, v_wide, l_wide = wide[:rows], wide[rows : 2 * rows], wide[2 * rows : 3 * rows]
        skip_wide = wide[3 * rows : 3 * rows + 1]
        x = x_ref[:, at].astype(F32)
        dy = dy_ref[:, at].astype(F32)
        xv = x * v_wide
        yu = dy * u_wide
        xs, ys = split2(xv), split2(yu)
        xs_ref[:, at] = stack(xs, 0)
        ys_ref[:, at] = stack(ys, 0)
        v_stage[:, at] = v_wide
        out = dot_pairs(scores, xs, 1, 0)
        back = dot_pairs(flipped, ys, 1, 0)
        d_scores += dot_pairs(ys, xs, 1, 1)
        dx_stage[:, at] = v_wide * back + skip_wide * dy
        for i, (stage, target) in enumerate(((v_stage, v_wide_hbm), (dx_stage, dx_hbm))):
            copy = pltpu.make_async_copy(stage.at[:, at], target.at[:, at], sems.at[i, block])
            copy.start()
            copies.append(copy)
        column_part = xv * back
        for part in split3(stack([yu * out - column_part, column_part], 0)):
            sums += dot(part, ones, 1, 0)
        product = jnp.broadcast_to(jnp.sum(x * dy, axis=0, keepdims=True), (8, WIDE))
        for part in split3(product):
            products += dot(part, ones, 1, 0)
        ending = u_wide[rows - 1 : rows]
        end_log = l_wide[rows - 1 : rows]
        gap = end_log - l_wide
        fwd_ref[:, at] = dot(bt_end, stack(split2(xv * gap), 0), 1, 0) * ending
        bwd_ref[:, at] = dot(ct_live, stack(split2(yu * l_wide), 0), 1, 0)
        ends_ref[0:1, at] = ending
        ends_ref[1:2, at] = ending * through
        ends_ref[2:3, at] = ending * through * end_log
    d_scores = split2(jnp.where(down, d_scores, 0.0))
    dc_ref[...] = sum(dot(bt, p, 1, 1) for p in d_scores)
    db_ref[...] = sum(dot(ct, p, 1, 0) for p in d_scores)
    sums_ref[...] = sums
    rate_grads = jnp.sum(logs * sums[:rows], axis=0, keepdims=True)
    empty = jnp.zeros((1, LANES - 2 * heads), F32)
    small_ref[...] = stack([rate_grads, products[:1], empty], 1)
    for copy in copies:
        copy.wait()


def rates_kernel(reach, head_width, *refs):
    plan = message_plan(reach)
    messages = dict(zip(plan, refs))
    ends_ref, fwd_ref, bwd_ref, small_ref, out_ref, came_ref, pull_ref = refs[len(plan) :]
    width, columns = fwd_ref.shape
    blocks = columns // WIDE
    whole = []
    for block in range(blocks):
        at = slice(block * WIDE, (block + 1) * WIDE)
        came, pull = received(messages, reach, block, blocks, width)
        came_ref[:, at] = came
        pull_ref[:, at] = pull
        terms = came * bwd_ref[:, at] + pull * (fwd_ref[:, at] + ends_ref[2:3, at] * came)
        whole.append(jnp.sum(terms, axis=0, keepdims=True))
    own = WIDE // head_width
    shape = (WIDE, LANES)
    column = lax.shift_right_logical(iota(shape, 0), log2(head_width))
    ones = jnp.where(column == (iota(shape, 1) & (own - 1)), 1.0, 0.0).astype(BF16)
    sums = sum(dot(part, ones, 1, 0) for part in split3(stack(whole, 0)))
    lane = iota(sums.shape, 1)
    mine = lax.shift_right_logical(lane, log2(own)) == iota(sums.shape, 0)
    total = small_ref[...] + jnp.sum(jnp.where(mine, sums, 0.0), axis=0, keepdims=True)
    out_ref[...] = jnp.broadcast_to(total, out_ref.shape)


def outputs_kernel(
    came_ref,
    pull_ref,
    ends_ref,
    xs_ref,
    ys_ref,
    v_wide_hbm,
    dx_hbm,
    b_end_ref,
    c_live_ref,
    masks_ref,
    db_ref,
    dc_ref,
    sums_ref,
    alog_ref,
    dt_ref,
    dx_out,
    db_out,
    dc_out,
    dt_out,
    v_stage,
    dx_stage,
    stage,
    in_sems,
    out_sems,
):
    rows, columns = dx_hbm.shape
    heads, width = dt_ref.shape[0], db_ref.shape[0]
    blocks = columns // WIDE
    copies = []
    for block in range(blocks):
        at = slice(block * WIDE, (block + 1) * WIDE)
        for i, (source, target) in enumerate(((v_wide_hbm, v_stage), (dx_hbm, dx_stage))):
            copy = pltpu.make_async_copy(
                source.at[:, at], target.at[:, at], in_sems.at[i, block]
            )
            copy.start()
            copies.append(copy)
    b_end, c_live = b_end_ref[...], c_live_ref[...]
    own_sums = sums_ref[...]
    sums = own_sums
    dc = jnp.zeros((2 * width, 2 * rows), F32)
    db = jnp.zeros((2 * width, 2 * rows), F32)
    at_last = iota((rows, WIDE), 0) == rows - 1
    sent = []
    for block in range(blocks):
        at = slice(block * WIDE, (block + 1) * WIDE)
        ones = head_columns(heads, columns // heads, block)
        came, pull = came_ref[:, at], pull_ref[:, at]
        meet = jnp.sum(came * pull, axis=0, keepdims=True) * ends_ref[1:2, at]
        cames = stack(split2(came), 0)
        pulls = stack(split2(pull * ends_ref[0:1, at]), 0)
        xs, ys = xs_ref[:, at], ys_ref[:, at]
        out = dot(c_live, cames, 1, 0)
        back = dot(b_end, pulls, 1, 0)
        column_part = (xs[:rows].astype(F32) + xs[rows:].astype(F32)) * back
        row_part = (ys[:rows].astype(F32) + ys[rows:].astype(F32)) * out
        row_part = jnp.where(at_last, row_part + meet, row_part)
        for part in split2(stack([row_part - column_part, column_part], 0)):
            sums += dot(part, ones, 1, 0)
        dc += dot(cames, ys, 1, 1)
        db += dot(pulls, xs, 1, 1)
        copies[2 * block].wait()
        copies[2 * block + 1].wait()
        stage[:, at] = (dx_stage[:, at] + v_stage[:, at] * back).astype(BF16)
        copy = pltpu.make_async_copy(stage.at[:, at], dx_out.at[0, :, at], out_sems.at[block])
        copy.start()
        sent.append(copy)
    dc = (dc[:width, :rows] + dc[:width, rows:]) + dc[width:, :rows]
    db = (db[:width, :rows] + db[:width, rows:]) + db[width:, :rows]
    db_out[0] = (db_ref[...] + masks_ref[0:1] * db).astype(BF16)
    dc_out[0] = (dc_ref[...] + masks_ref[1:2] * dc).astype(BF16)
    square = (rows, rows)
    upper = jnp.where(iota(square, 0) >= iota(square, 1), 1.0, 0.0).astype(BF16)
    eye = jnp.where(iota(square, 0) == iota(square, 1), 1.0, 0.0).astype(BF16)
    at_end = jnp.sum(sums[rows:] - own_sums[rows:], axis=0, keepdims=True)
    dl = sums[:rows] + jnp.where(iota((rows, heads), 0) == rows - 1, at_end, 0.0)
    d_decay = sum(dot(part, upper, 0, 0) for part in split3(dl))
    total = sum(dot(part, eye, 0, 0) for part in split3(sums[rows:]))
    dt_out[0] = total / dt_ref[...] + rate_column(alog_ref) * d_decay
    for copy in sent:
        copy.wait()


def call(kernel, reach, outs, ins, flops, moved, scratch=()):
    spaces = {"s": pltpu.SMEM, "v": pltpu.VMEM, "h": pltpu.HBM, "any": pl.ANY}
    return pl.pallas_call(
        kernel,
        out_shape=[
            pltpu.HBM(*out) if place == "h" else jax.ShapeDtypeStruct(*out) for place, out in outs
        ],
        in_specs=[pl.BlockSpec(memory_space=spaces[place]) for place, _ in ins],
        out_specs=[pl.BlockSpec(memory_space=spaces[place]) for place, _ in outs],
        scratch_shapes=scratch,
        compiler_params=pltpu.CompilerParams(vmem_limit_bytes=min(16 + 2 * reach, 56) * 2**20),
        cost_estimate=pl.CostEstimate(flops=flops, bytes_accessed=moved, transcendentals=0),
    )(*(a for _, a in ins))


def send(a, by, second):
    count = lax.axis_size("ctx")
    pairs = [(i, i + by if (i + second) % 2 == 0 else i - by) for i in range(count)]
    return lax.ppermute(a, "ctx", [(i, j) for i, j in pairs if 0 <= j < count])


def hand_on(a):
    count = lax.axis_size("ctx")
    return lax.ppermute(a, "ctx", [(i, i ^ 1) for i in range(count)])


def in_hbm(a):
    return "h", pltpu.with_memory_space_constraint(a, pltpu.HBM)


def per_device(inputs, b_proj, c_proj, step_sizes, a_log, skip_gain, doc_lengths, grad_out):
    rows, columns = inputs.shape[1:]
    heads, width = a_log.shape[0], b_proj.shape[2]
    reach = max(lax.axis_size("ctx") // 4, 1)
    devices = lax.axis_size("ctx") * lax.axis_size("dp")
    alog, skip = a_log[None], skip_gain[None]
    bt, ct = jnp.swapaxes(b_proj, 1, 2), jnp.swapaxes(c_proj, 1, 2)
    blocks = columns // WIDE

    def v(shape, kind=F32):
        return "v", (shape, kind)

    dt, x, b, dy, c, *payloads = call(
        states_kernel,
        reach,
        [
            v((heads, rows)),
            v((rows, columns), BF16),
            v((width, rows), BF16),
            v((rows, columns), BF16),
            v((width, rows), BF16),
        ]
        + [v((columns // LANES * (width + 1) // part, LANES)) for part in (1, 2, 2)],
        [in_hbm(a) for a in (doc_lengths, alog, step_sizes, inputs, bt, grad_out, ct)],
        10**9,
        4 * 2**20,
        [
            pltpu.SMEM(doc_lengths.shape, jnp.int32),
            pltpu.VMEM(alog.shape, F32),
            pltpu.SemaphoreType.DMA((5,)),
            pltpu.SemaphoreType.DMA((2, PIECES)),
        ],
    )
    messages = {}
    for j, second, half in message_plan(reach):
        if (j, second) == (1, 1) and reach > 1:
            continue
        payload = payloads[1 + half if second else 0]
        messages[j, second, half] = send(payload, j, second)
    if reach > 1:
        for half in (0, 1):
            messages[1, 1, half] = hand_on(messages[2, 1, half])
    messages = [messages[one] for one in message_plan(reach)]
    whole = "h", ((rows, columns), F32)
    state = v((width, columns))
    stage = pltpu.VMEM((rows, columns), F32)
    transposed = v((width, rows))
    xs, ys, v_wide, dx, b_end, c_live, masks, db, dc, sums, fwd_logs, bwd_logs, ends, small = call(
        inside_kernel,
        reach,
        [v((2 * rows, columns), BF16)] * 2
        + [whole] * 2
        + [v((rows, 2 * width), BF16)] * 2
        + [v((8, rows)), transposed, transposed, v((2 * rows, heads))]
        + [state, state, v((8, columns)), v((1, LANES))],
        [("s", doc_lengths)] + [("v", a) for a in (alog, skip, dt, x, b, dy, c)]
        + [("any", messages[0])],
        4 * 10**9,
        12 * 2**20,
        [stage, stage, pltpu.SemaphoreType.DMA((2, blocks))],
    )
    partial, came, pull = call(
        functools.partial(rates_kernel, reach, columns // heads),
        reach,
        [v((devices, LANES)), state, state],
        [("v", a) for a in (*messages, ends, fwd_logs, bwd_logs, small)],
        10**8,
        4 * 2**20,
    )
    input_grads, b_gradient, c_gradient, step_grads = call(
        outputs_kernel,
        reach,
        [("h", ((1, rows, columns), BF16))]
        + [v((1, width, rows), BF16)] * 2
        + [v((1, heads, rows))],
        [("v", a) for a in (came, pull, ends, xs, ys)]
        + [in_hbm(v_wide), in_hbm(dx)]
        + [("v", a) for a in (b_end, c_live, masks, db, dc, sums, alog, dt)],
        2 * 10**9,
        12 * 2**20,
        [
            stage,
            stage,
            pltpu.VMEM((rows, columns), BF16),
            pltpu.SemaphoreType.DMA((2, blocks)),
            pltpu.SemaphoreType.DMA((blocks,)),
        ],
    )
    gathered = lax.all_to_all(partial, ("dp", "ctx"), 0, 0, tiled=True)
    totals = jnp.sum(gathered, axis=0)
    return (
        input_grads,
        jnp.swapaxes(b_gradient, 1, 2),
        jnp.swapaxes(c_gradient, 1, 2),
        step_grads,
        totals[:heads],
        totals[heads : 2 * heads],
    )


def solution(mesh):
    in_specs = (
        P("dp", "ctx", None),
        P("dp", "ctx", None),
        P("dp", "ctx", None),
        P("dp", None, "ctx"),
        P(),
        P(),
        P("dp", None),
        P("dp", "ctx", None),
    )
    out_specs = (
        P("dp", "ctx", None),
        P("dp", "ctx", None),
        P("dp", "ctx", None),
        P("dp", None, "ctx"),
        P(),
        P(),
    )
    return jax.shard_map(
        per_device, mesh=mesh, in_specs=in_specs, out_specs=out_specs, check_vma=False
    )
```

```python
import functools

import jax
import jax.numpy as jnp
from jax import lax
from jax.experimental import pallas as pl
from jax.experimental.pallas import tpu as pltpu
from jax.sharding import PartitionSpec as P

F32 = jnp.float32
BF16 = jnp.bfloat16
LANES = 128
WIDE = 256
PARTS = WIDE // LANES
FAR = 2**30
PIECES = 4


def dot(a, b, ca, cb):
    return lax.dot_general(a, b, (((ca,), (cb,)), ((), ())), preferred_element_type=F32)


def iota(shape, dim):
    return lax.broadcasted_iota(jnp.int32, shape, dim)


def split2(a):
    high = a.astype(BF16)
    return high, (a - high.astype(F32)).astype(BF16)


def split3(a):
    high = a.astype(BF16)
    rest = a - high.astype(F32)
    middle = rest.astype(BF16)
    return high, middle, (rest - middle.astype(F32)).astype(BF16)


def dot_pairs(a, b, ca, cb):
    return dot(a[0], b[0], ca, cb) + (dot(a[0], b[1], ca, cb) + dot(a[1], b[0], ca, cb))


def stack(parts, axis):
    return jnp.concatenate(parts, axis=axis)


def document_places(lens_ref, rows):
    offset = shard() * rows
    starts = [jnp.int32(0)]
    for d in range(lens_ref.shape[1] - 1):
        starts.append(starts[-1] + lens_ref[0, d])
    first = jnp.int32(FAR)
    last = jnp.int32(0)
    for start in starts:
        first = jnp.minimum(first, jnp.where(start >= offset, start, FAR))
        last = jnp.maximum(last, jnp.where(start < offset + rows, start, 0))
    return starts, offset, first, last


def rate_column(alog_ref):
    heads = alog_ref.shape[1]
    square = jnp.broadcast_to(alog_ref[...], (heads, heads))
    picked = jnp.where(iota((heads, heads), 0) == iota((heads, heads), 1), square, 0.0)
    return -jnp.exp(jnp.sum(picked, axis=1, keepdims=True))


def log2(size):
    assert size & (size - 1) == 0
    return size.bit_length() - 1


def head_distance(heads, head_width):
    shape = (3 * heads, WIDE)
    return (iota(shape, 0) & (heads - 1)) - lax.shift_right_logical(
        iota(shape, 1), log2(head_width)
    )


def head_rows(distance, head_width, block):
    return jnp.where(distance == block * (WIDE // head_width), 1.0, 0.0).astype(BF16)


def head_columns(heads, head_width, block):
    shape = (WIDE, heads)
    column = lax.shift_right_logical(iota(shape, 0), log2(head_width))
    return jnp.where(iota(shape, 1) - column == block * (WIDE // head_width), 1.0, 0.0).astype(BF16)


def shard():
    return lax.axis_index("ctx")


def message_block(ref, block, width):
    at = block * PARTS
    return stack([ref[(at + i) * width : (at + i + 1) * width, :] for i in range(PARTS)], 1)


def message_tail(ref, block, width):
    tail = ref.shape[0] // (width + 1) * width + block * PARTS
    return stack([ref[tail + i : tail + i + 1, :] for i in range(PARTS)], 1)


def message_plan(reach):
    near = [(1, 0, 0)]
    relayed = [(1, 1, 0), (1, 1, 1)]
    far = [(2, 1, 0), (2, 1, 1), (2, 0, 0)] if reach > 1 else []
    rest = [(j, *one) for j in range(3, reach + 1) for one in ((0, 0), (1, 0), (1, 1))]
    return near + far + relayed + rest


def received(messages, reach, block, blocks, width):
    came = pull = None
    half, inner = divmod(block, blocks // 2)
    for j in range(reach, 0, -1):
        one, two = messages[j, 0, 0], messages[j, 1, half]
        a, b = message_block(one, block, width), message_block(two, inner, width)
        first = jnp.broadcast_to(lax.rem(shard() + j, 2), a.shape) == 0
        near_came, near_pull = jnp.where(first, a, b), jnp.where(first, b, a)
        if came is None:
            came, pull = near_came, near_pull
        else:
            a, b = message_tail(one, block, width), message_tail(two, inner, width)
            first = jnp.broadcast_to(lax.rem(shard() + j, 2), a.shape) == 0
            came = near_came + jnp.where(first, a, b) * came
            pull = near_pull + jnp.where(first, b, a) * pull
    return came, pull


def states_kernel(
    lens_hbm,
    alog_hbm,
    skip_hbm,
    dt_hbm,
    x_hbm,
    b_hbm,
    dy_hbm,
    c_hbm,
    alog_ref,
    skip_ref,
    dt_ref,
    x_ref,
    b_ref,
    dy_ref,
    c_ref,
    one_ref,
    two_ref,
    three_ref,
    lens_ref,
    small_sems,
    sems,
):
    rows, columns = x_ref.shape
    heads, width = dt_ref.shape[0], b_ref.shape[0]
    head_width = columns // heads
    piece = columns // PIECES
    small = [
        pltpu.make_async_copy(source, target, small_sems.at[i])
        for i, (source, target) in enumerate(
            (
                (lens_hbm, lens_ref),
                (alog_hbm, alog_ref),
                (dt_hbm.at[0], dt_ref),
                (b_hbm.at[0], b_ref),
                (c_hbm.at[0], c_ref),
                (skip_hbm, skip_ref),
            )
        )
    ]
    for copy in small:
        copy.start()
    large = []
    for i in range(PIECES):
        at = slice(i * piece, (i + 1) * piece)
        for side, (source, target) in enumerate(((x_hbm, x_ref), (dy_hbm, dy_ref))):
            copy = pltpu.make_async_copy(
                source.at[0, :, at], target.at[:, at], sems.at[side, i]
            )
            copy.start()
            large.append(copy)
    square = (rows, rows)
    upper = jnp.where(iota(square, 0) <= iota(square, 1), 1.0, 0.0).astype(BF16)
    even = jnp.broadcast_to(lax.rem(shard(), 2), (width, LANES)) == 0
    left = iota((1, LANES), 1) < head_width
    for copy in small:
        copy.wait()
    _, offset, first, last = document_places(lens_ref, rows)
    through = jnp.where(first >= offset + rows, 1.0, 0.0)
    dt = dt_ref[...]
    logs = sum(dot(part, upper, 1, 0) for part in split3(dt * rate_column(alog_ref)))
    end_log = logs[:, rows - 1 : rows]
    place = iota((heads, rows), 1) + offset
    keeping = jnp.where(place >= last, jnp.exp(end_log - logs) * dt, 0.0)
    carried = jnp.where(place < first, jnp.exp(logs), 0.0)
    kept = jnp.broadcast_to(jnp.exp(end_log) * through, (heads, LANES))
    b, c = b_ref[...].astype(F32), c_ref[...].astype(F32)
    own = LANES // head_width

    def block_states(vectors, weights, values):
        rows_in = [stack(split2(vectors * weights[h : h + 1, :]), 1) for h in range(PARTS * own)]
        out = dot(stack(rows_in, 0), stack([values, values], 0), 1, 0)
        pairs = []
        for i in range(PARTS):
            lanes = slice(i * LANES, (i + 1) * LANES)
            sides = [
                out[h * width : (h + 1) * width, lanes] for h in range(i * own, (i + 1) * own)
            ]
            pairs.append(jnp.where(left, sides[0], sides[1]))
        return pairs

    pairs = columns // LANES
    for block in range(columns // WIDE):
        if block * WIDE % piece == 0:
            large[block * WIDE // piece * 2].wait()
            large[block * WIDE // piece * 2 + 1].wait()
        at = slice(block * WIDE, (block + 1) * WIDE)
        here = slice(block * PARTS * own, (block + 1) * PARTS * own)
        states = block_states(b, keeping[here], x_ref[:, at])
        pulls = block_states(c, carried[here], dy_ref[:, at])
        for i in range(PARTS):
            pair = block * PARTS + i
            kept_row = jnp.where(left, kept[pair * own : pair * own + 1], kept[pair * own + 1 :][:1])
            first = jnp.where(even, states[i], pulls[i])
            second = jnp.where(even, pulls[i], states[i])
            half, inner = divmod(pair, pairs // 2)
            for ref, place_in, whole, value in (
                (one_ref, pair, pairs, first),
                ((two_ref, three_ref)[half], inner, pairs // 2, second),
            ):
                ref[place_in * width : (place_in + 1) * width, :] = value
                ref[whole * width + place_in : whole * width + place_in + 1, :] = kept_row


def inside_kernel(
    lens_hbm,
    alog_ref,
    skip_ref,
    dt_ref,
    x_ref,
    b_ref,
    dy_ref,
    c_ref,
    _,
    xs_ref,
    ys_ref,
    v_wide_hbm,
    dx_hbm,
    b_end_ref,
    c_live_ref,
    masks_ref,
    db_ref,
    dc_ref,
    sums_ref,
    fwd_ref,
    bwd_ref,
    ends_ref,
    small_ref,
    v_stage,
    dx_stage,
    lens_ref,
    lens_sem,
    sems,
):
    rows, columns = x_ref.shape
    heads, width = dt_ref.shape[0], b_ref.shape[0]
    head_width = columns // heads
    lens_copy = pltpu.make_async_copy(lens_hbm, lens_ref, lens_sem)
    lens_copy.start()
    distance = head_distance(heads, head_width)
    bt, ct = b_ref[...], c_ref[...]
    raw_scores, raw_flipped = dot(ct, bt, 0, 0), dot(bt, ct, 0, 0)
    lens_copy.wait()
    starts, offset, first, last = document_places(lens_ref, rows)
    through = jnp.where(first >= offset + rows, 1.0, 0.0)
    square = (rows, rows)
    place0, place1 = iota(square, 0) + offset, iota(square, 1) + offset
    segment0, segment1 = jnp.zeros(square, jnp.int32), jnp.zeros(square, jnp.int32)
    for start in starts:
        segment0 += jnp.where(place0 >= start, 1, 0)
        segment1 += jnp.where(place1 >= start, 1, 0)
    same = segment0 == segment1
    down = same & (place0 >= place1)
    lower = jnp.where(place0 >= place1, 1.0, 0.0).astype(BF16)
    eye = jnp.where(place0 == place1, 1.0, 0.0).astype(BF16)
    dt = dt_ref[...]
    logs = sum(dot(lower, part, 1, 1) for part in split3(dt * rate_column(alog_ref)))
    steps = sum(dot(eye, part, 1, 1) for part in split3(dt))
    scores = split2(jnp.where(down, raw_scores, 0.0))
    flipped = split2(jnp.where(same & (place1 >= place0), raw_flipped, 0.0))
    place = iota((width, rows), 1) + offset
    bt_end = jnp.where(place >= last, bt.astype(F32), 0.0)
    ct_live = jnp.where(place < first, ct.astype(F32), 0.0)
    b_end, c_live = jnp.transpose(bt_end).astype(BF16), jnp.transpose(ct_live).astype(BF16)
    bt_end, ct_live = bt_end.astype(BF16), ct_live.astype(BF16)
    b_end_ref[...] = stack([b_end, b_end], 1)
    c_live_ref[...] = stack([c_live, c_live], 1)
    bt_end, ct_live = stack([bt_end, bt_end], 1), stack([ct_live, ct_live], 1)
    masks_ref[0:1] = jnp.where(place[:1] >= last, 1.0, 0.0)
    masks_ref[1:2] = jnp.where(place[:1] < first, 1.0, 0.0)
    tables = stack(
        [
            stack(split3(a), 1)
            for a in (
                jnp.exp(logs),
                jnp.exp(-logs) * steps,
                logs,
                jnp.broadcast_to(skip_ref[...], (16, heads)),
            )
        ],
        0,
    )
    d_scores = jnp.zeros((2 * rows, 2 * rows), F32)
    sums = jnp.zeros((2 * rows + 16, heads), F32)
    copies = []
    for block in range(columns // WIDE):
        at = slice(block * WIDE, (block + 1) * WIDE)
        wide = dot(tables, head_rows(distance, head_width, block), 1, 0)
        ones = head_columns(heads, head_width, block)
        u_wide, v_wide, l_wide = wide[:rows], wide[rows : 2 * rows], wide[2 * rows : 3 * rows]
        skip_wide = wide[3 * rows : 3 * rows + 1]
        x = x_ref[:, at].astype(F32)
        dy = dy_ref[:, at].astype(F32)
        xv = x * v_wide
        yu = dy * u_wide
        xs, ys = split2(xv), split2(yu)
        xs_ref[:, at] = stack(xs, 0)
        ys_ref[:, at] = stack(ys, 0)
        v_stage[:, at] = v_wide
        out = dot_pairs(scores, xs, 1, 0)
        back = dot_pairs(flipped, ys, 1, 0)
        d_scores += dot(stack(ys, 0), stack(xs, 0), 1, 1)
        dx_stage[:, at] = v_wide * back + skip_wide * dy
        for i, (stage, target) in enumerate(((v_stage, v_wide_hbm), (dx_stage, dx_hbm))):
            copy = pltpu.make_async_copy(stage.at[:, at], target.at[:, at], sems.at[i, block])
            copy.start()
            copies.append(copy)
        column_part = xv * back
        product = jnp.broadcast_to(jnp.sum(x * dy, axis=0, keepdims=True), (16, WIDE))
        for part in split3(stack([yu * out - column_part, column_part, product], 0)):
            sums += dot(part, ones, 1, 0)
        ending = u_wide[rows - 1 : rows]
        end_log = l_wide[rows - 1 : rows]
        gap = end_log - l_wide
        fwd_ref[:, at] = dot(bt_end, stack(split2(xv * gap), 0), 1, 0) * ending
        bwd_ref[:, at] = dot(ct_live, stack(split2(yu * l_wide), 0), 1, 0)
        ends_ref[0:1, at] = ending
        ends_ref[1:2, at] = ending * through
        ends_ref[2:3, at] = ending * through * end_log
    d_scores = (d_scores[:rows, :rows] + d_scores[:rows, rows:]) + d_scores[rows:, :rows]
    d_scores = split2(jnp.where(down, d_scores, 0.0))
    dc_ref[...] = sum(dot(bt, p, 1, 1) for p in d_scores)
    db_ref[...] = sum(dot(ct, p, 1, 0) for p in d_scores)
    sums_ref[...] = sums[: 2 * rows]
    rate_grads = jnp.sum(logs * sums[:rows], axis=0, keepdims=True)
    empty = jnp.zeros((1, LANES - 2 * heads), F32)
    small_ref[...] = stack([rate_grads, sums[2 * rows : 2 * rows + 1], empty], 1)
    for copy in copies:
        copy.wait()


def rates_kernel(reach, head_width, *refs):
    plan = message_plan(reach)
    messages = dict(zip(plan, refs))
    ends_ref, fwd_ref, bwd_ref, small_ref, out_ref, came_ref, pull_ref = refs[len(plan) :]
    width, columns = fwd_ref.shape
    blocks = columns // WIDE
    whole = []
    for block in range(blocks):
        at = slice(block * WIDE, (block + 1) * WIDE)
        came, pull = received(messages, reach, block, blocks, width)
        came_ref[:, at] = came
        pull_ref[:, at] = pull
        terms = came * bwd_ref[:, at] + pull * (fwd_ref[:, at] + ends_ref[2:3, at] * came)
        whole.append(jnp.sum(terms, axis=0, keepdims=True))
    own = WIDE // head_width
    shape = (WIDE, LANES)
    column = lax.shift_right_logical(iota(shape, 0), log2(head_width))
    ones = jnp.where(column == (iota(shape, 1) & (own - 1)), 1.0, 0.0).astype(BF16)
    sums = dot(stack(split3(stack(whole, 0)), 0), ones, 1, 0)
    sums = (sums[:blocks] + sums[blocks : 2 * blocks]) + sums[2 * blocks :]
    lane = iota(sums.shape, 1)
    mine = lax.shift_right_logical(lane, log2(own)) == iota(sums.shape, 0)
    total = small_ref[...] + jnp.sum(jnp.where(mine, sums, 0.0), axis=0, keepdims=True)
    out_ref[...] = jnp.broadcast_to(total, out_ref.shape)


def outputs_kernel(
    came_ref,
    pull_ref,
    ends_ref,
    xs_ref,
    ys_ref,
    v_wide_hbm,
    dx_hbm,
    b_end_ref,
    c_live_ref,
    masks_ref,
    db_ref,
    dc_ref,
    sums_ref,
    alog_ref,
    dt_ref,
    dx_out,
    db_out,
    dc_out,
    dt_out,
    v_stage,
    dx_stage,
    stage,
    in_sems,
    out_sems,
):
    rows, columns = dx_hbm.shape
    heads, width = dt_ref.shape[0], db_ref.shape[0]
    blocks = columns // WIDE
    copies = []
    for block in range(blocks):
        at = slice(block * WIDE, (block + 1) * WIDE)
        for i, (source, target) in enumerate(((v_wide_hbm, v_stage), (dx_hbm, dx_stage))):
            copy = pltpu.make_async_copy(
                source.at[:, at], target.at[:, at], in_sems.at[i, block]
            )
            copy.start()
            copies.append(copy)
    b_end, c_live = b_end_ref[...], c_live_ref[...]
    own_sums = sums_ref[...]
    sums = own_sums
    dc = jnp.zeros((2 * width, 2 * rows), F32)
    db = jnp.zeros((2 * width, 2 * rows), F32)
    at_last = iota((rows, WIDE), 0) == rows - 1
    sent = []
    for block in range(blocks):
        at = slice(block * WIDE, (block + 1) * WIDE)
        ones = head_columns(heads, columns // heads, block)
        came, pull = came_ref[:, at], pull_ref[:, at]
        meet = jnp.sum(came * pull, axis=0, keepdims=True) * ends_ref[1:2, at]
        cames = stack(split2(came), 0)
        pulls = stack(split2(pull * ends_ref[0:1, at]), 0)
        xs, ys = xs_ref[:, at], ys_ref[:, at]
        out = dot(c_live, cames, 1, 0)
        back = dot(b_end, pulls, 1, 0)
        column_part = (xs[:rows].astype(F32) + xs[rows:].astype(F32)) * back
        row_part = (ys[:rows].astype(F32) + ys[rows:].astype(F32)) * out
        row_part = jnp.where(at_last, row_part + meet, row_part)
        for part in split2(stack([row_part - column_part, column_part], 0)):
            sums += dot(part, ones, 1, 0)
        dc += dot(cames, ys, 1, 1)
        db += dot(pulls, xs, 1, 1)
        copies[2 * block].wait()
        copies[2 * block + 1].wait()
        stage[:, at] = (dx_stage[:, at] + v_stage[:, at] * back).astype(BF16)
        copy = pltpu.make_async_copy(stage.at[:, at], dx_out.at[0, :, at], out_sems.at[block])
        copy.start()
        sent.append(copy)
    dc = (dc[:width, :rows] + dc[:width, rows:]) + dc[width:, :rows]
    db = (db[:width, :rows] + db[:width, rows:]) + db[width:, :rows]
    db_out[0] = (db_ref[...] + masks_ref[0:1] * db).astype(BF16)
    dc_out[0] = (dc_ref[...] + masks_ref[1:2] * dc).astype(BF16)
    square = (rows, rows)
    upper = jnp.where(iota(square, 0) >= iota(square, 1), 1.0, 0.0).astype(BF16)
    eye = jnp.where(iota(square, 0) == iota(square, 1), 1.0, 0.0).astype(BF16)
    at_end = jnp.sum(sums[rows:] - own_sums[rows:], axis=0, keepdims=True)
    dl = sums[:rows] + jnp.where(iota((rows, heads), 0) == rows - 1, at_end, 0.0)
    d_decay = sum(dot(part, upper, 0, 0) for part in split3(dl))
    total = sum(dot(part, eye, 0, 0) for part in split3(sums[rows:]))
    dt_out[0] = total / dt_ref[...] + rate_column(alog_ref) * d_decay
    for copy in sent:
        copy.wait()


def call(kernel, reach, outs, ins, flops, moved, scratch=()):
    spaces = {"s": pltpu.SMEM, "v": pltpu.VMEM, "h": pltpu.HBM, "any": pl.ANY}
    return pl.pallas_call(
        kernel,
        out_shape=[
            pltpu.HBM(*out) if place == "h" else jax.ShapeDtypeStruct(*out) for place, out in outs
        ],
        in_specs=[pl.BlockSpec(memory_space=spaces[place]) for place, _ in ins],
        out_specs=[pl.BlockSpec(memory_space=spaces[place]) for place, _ in outs],
        scratch_shapes=scratch,
        compiler_params=pltpu.CompilerParams(vmem_limit_bytes=min(16 + 2 * reach, 56) * 2**20),
        cost_estimate=pl.CostEstimate(flops=flops, bytes_accessed=moved, transcendentals=0),
    )(*(a for _, a in ins))


def send(a, by, second):
    count = lax.axis_size("ctx")
    pairs = [(i, i + by if (i + second) % 2 == 0 else i - by) for i in range(count)]
    return lax.ppermute(a, "ctx", [(i, j) for i, j in pairs if 0 <= j < count])


def hand_on(a):
    count = lax.axis_size("ctx")
    return lax.ppermute(a, "ctx", [(i, i ^ 1) for i in range(count) if i not in (1, count - 2)])


def in_hbm(a):
    return "h", pltpu.with_memory_space_constraint(a, pltpu.HBM)


def per_device(inputs, b_proj, c_proj, step_sizes, a_log, skip_gain, doc_lengths, grad_out):
    rows, columns = inputs.shape[1:]
    heads, width = a_log.shape[0], b_proj.shape[2]
    reach = max(lax.axis_size("ctx") // 4, 1)
    devices = lax.axis_size("ctx") * lax.axis_size("dp")
    alog, skip = a_log[None], skip_gain[None]
    bt, ct = jnp.swapaxes(b_proj, 1, 2), jnp.swapaxes(c_proj, 1, 2)
    blocks = columns // WIDE

    def v(shape, kind=F32):
        return "v", (shape, kind)

    alog, skip, dt, x, b, dy, c, *payloads = call(
        states_kernel,
        reach,
        [
            v(alog.shape),
            v(skip.shape),
            v((heads, rows)),
            v((rows, columns), BF16),
            v((width, rows), BF16),
            v((rows, columns), BF16),
            v((width, rows), BF16),
        ]
        + [v((columns // LANES * (width + 1) // part, LANES)) for part in (1, 2, 2)],
        [in_hbm(a) for a in (doc_lengths, alog, skip, step_sizes, inputs, bt, grad_out, ct)],
        10**9,
        4 * 2**20,
        [
            pltpu.SMEM(doc_lengths.shape, jnp.int32),
            pltpu.SemaphoreType.DMA((6,)),
            pltpu.SemaphoreType.DMA((2, PIECES)),
        ],
    )
    messages = {}
    for j, second, half in message_plan(reach):
        if (j, second) == (1, 1) and reach > 1:
            continue
        payload = payloads[1 + half if second else 0]
        messages[j, second, half] = send(payload, j, second)
    if reach > 1:
        for half in (0, 1):
            messages[1, 1, half] = hand_on(messages[2, 1, half])
    messages = [messages[one] for one in message_plan(reach)]
    whole = "h", ((rows, columns), F32)
    state = v((width, columns))
    stage = pltpu.VMEM((rows, columns), F32)
    transposed = v((width, rows))
    xs, ys, v_wide, dx, b_end, c_live, masks, db, dc, sums, fwd_logs, bwd_logs, ends, small = call(
        inside_kernel,
        reach,
        [v((2 * rows, columns), BF16)] * 2
        + [whole] * 2
        + [v((rows, 2 * width), BF16)] * 2
        + [v((8, rows)), transposed, transposed, v((2 * rows, heads))]
        + [state, state, v((8, columns)), v((1, LANES))],
        [in_hbm(doc_lengths)]
        + [("v", a) for a in (alog, skip, dt, x, b, dy, c)]
        + [("any", messages[0])],
        4 * 10**9,
        12 * 2**20,
        [
            stage,
            stage,
            pltpu.SMEM(doc_lengths.shape, jnp.int32),
            pltpu.SemaphoreType.DMA,
            pltpu.SemaphoreType.DMA((2, blocks)),
        ],
    )
    partial, came, pull = call(
        functools.partial(rates_kernel, reach, columns // heads),
        reach,
        [v((devices, LANES)), state, state],
        [("v", a) for a in (*messages, ends, fwd_logs, bwd_logs, small)],
        10**8,
        4 * 2**20,
    )
    input_grads, b_gradient, c_gradient, step_grads = call(
        outputs_kernel,
        reach,
        [("h", ((1, rows, columns), BF16))]
        + [v((1, width, rows), BF16)] * 2
        + [v((1, heads, rows))],
        [("v", a) for a in (came, pull, ends, xs, ys)]
        + [in_hbm(v_wide), in_hbm(dx)]
        + [("v", a) for a in (b_end, c_live, masks, db, dc, sums, alog, dt)],
        2 * 10**9,
        12 * 2**20,
        [
            stage,
            stage,
            pltpu.VMEM((rows, columns), BF16),
            pltpu.SemaphoreType.DMA((2, blocks)),
            pltpu.SemaphoreType.DMA((blocks,)),
        ],
    )
    gathered = lax.all_to_all(partial, ("ctx", "dp"), 0, 0, tiled=True)
    totals = jnp.sum(gathered, axis=0)
    return (
        input_grads,
        jnp.swapaxes(b_gradient, 1, 2),
        jnp.swapaxes(c_gradient, 1, 2),
        step_grads,
        totals[:heads],
        totals[heads : 2 * heads],
    )


def solution(mesh):
    in_specs = (
        P("dp", "ctx", None),
        P("dp", "ctx", None),
        P("dp", "ctx", None),
        P("dp", None, "ctx"),
        P(),
        P(),
        P("dp", None),
        P("dp", "ctx", None),
    )
    out_specs = (
        P("dp", "ctx", None),
        P("dp", "ctx", None),
        P("dp", "ctx", None),
        P("dp", None, "ctx"),
        P(),
        P(),
    )
    return jax.shard_map(
        per_device, mesh=mesh, in_specs=in_specs, out_specs=out_specs, check_vma=False
    )
```

```python
import functools

import jax
import jax.numpy as jnp
from jax import lax
from jax.experimental import pallas as pl
from jax.experimental.pallas import tpu as pltpu
from jax.sharding import PartitionSpec as P

F32 = jnp.float32
BF16 = jnp.bfloat16
LANES = 128
WIDE = 256
PARTS = WIDE // LANES
FAR = 2**30
PIECES = 4


def dot(a, b, ca, cb):
    return lax.dot_general(a, b, (((ca,), (cb,)), ((), ())), preferred_element_type=F32)


def iota(shape, dim):
    return lax.broadcasted_iota(jnp.int32, shape, dim)


def split2(a):
    high = a.astype(BF16)
    return high, (a - high.astype(F32)).astype(BF16)


def split3(a):
    high = a.astype(BF16)
    rest = a - high.astype(F32)
    middle = rest.astype(BF16)
    return high, middle, (rest - middle.astype(F32)).astype(BF16)


def dot_pairs(a, b, ca, cb):
    return dot(a[0], b[0], ca, cb) + (dot(a[0], b[1], ca, cb) + dot(a[1], b[0], ca, cb))


def stack(parts, axis):
    return jnp.concatenate(parts, axis=axis)


def document_places(lens_ref, rows):
    offset = shard() * rows
    starts = [jnp.int32(0)]
    for d in range(lens_ref.shape[1] - 1):
        starts.append(starts[-1] + lens_ref[0, d])
    first = jnp.int32(FAR)
    last = jnp.int32(0)
    for start in starts:
        first = jnp.minimum(first, jnp.where(start >= offset, start, FAR))
        last = jnp.maximum(last, jnp.where(start < offset + rows, start, 0))
    return starts, offset, first, last


def rate_column(alog_ref):
    heads = alog_ref.shape[1]
    square = jnp.broadcast_to(alog_ref[...], (heads, heads))
    picked = jnp.where(iota((heads, heads), 0) == iota((heads, heads), 1), square, 0.0)
    return -jnp.exp(jnp.sum(picked, axis=1, keepdims=True))


def log2(size):
    assert size & (size - 1) == 0
    return size.bit_length() - 1


def head_distance(heads, head_width):
    shape = (3 * heads, WIDE)
    return (iota(shape, 0) & (heads - 1)) - lax.shift_right_logical(
        iota(shape, 1), log2(head_width)
    )


def head_rows(distance, head_width, block):
    return jnp.where(distance == block * (WIDE // head_width), 1.0, 0.0).astype(BF16)


def head_columns(heads, head_width, block):
    shape = (WIDE, heads)
    column = lax.shift_right_logical(iota(shape, 0), log2(head_width))
    return jnp.where(iota(shape, 1) - column == block * (WIDE // head_width), 1.0, 0.0).astype(BF16)


def shard():
    return lax.axis_index("ctx")


def message_block(ref, block, width):
    at = block * PARTS
    return stack([ref[(at + i) * width : (at + i + 1) * width, :] for i in range(PARTS)], 1)


def message_tail(ref, block, width):
    tail = ref.shape[0] // (width + 1) * width + block * PARTS
    return stack([ref[tail + i : tail + i + 1, :] for i in range(PARTS)], 1)


def message_plan(reach, only=None):
    near = [(1, 0, 0)]
    relayed = [(1, 1, 0), (1, 1, 1)]
    far = [(2, 1, 0), (2, 1, 1), (2, 0, 0)] if reach > 1 else []
    rest = [(j, *one) for j in range(3, reach + 1) for one in ((0, 0), (1, 0), (1, 1))]
    plan = near + far + relayed + rest
    return [one for one in plan if only is None or not one[1] or one[2] == only]


def received(messages, reach, block, blocks, width):
    came = pull = None
    half, inner = divmod(block, blocks // 2)
    for j in range(reach, 0, -1):
        one, two = messages[j, 0, 0], messages[j, 1, half]
        a, b = message_block(one, block, width), message_block(two, inner, width)
        first = jnp.broadcast_to(lax.rem(shard() + j, 2), a.shape) == 0
        near_came, near_pull = jnp.where(first, a, b), jnp.where(first, b, a)
        if came is None:
            came, pull = near_came, near_pull
        else:
            a, b = message_tail(one, block, width), message_tail(two, inner, width)
            first = jnp.broadcast_to(lax.rem(shard() + j, 2), a.shape) == 0
            came = near_came + jnp.where(first, a, b) * came
            pull = near_pull + jnp.where(first, b, a) * pull
    return came, pull


def states_kernel(
    lens_hbm,
    alog_hbm,
    skip_hbm,
    dt_hbm,
    x_hbm,
    b_hbm,
    dy_hbm,
    c_hbm,
    alog_ref,
    skip_ref,
    dt_ref,
    x_ref,
    b_ref,
    dy_ref,
    c_ref,
    one_ref,
    two_ref,
    three_ref,
    lens_ref,
    small_sems,
    sems,
):
    rows, columns = x_ref.shape
    heads, width = dt_ref.shape[0], b_ref.shape[0]
    head_width = columns // heads
    piece = columns // PIECES
    small = [
        pltpu.make_async_copy(source, target, small_sems.at[i])
        for i, (source, target) in enumerate(
            (
                (lens_hbm, lens_ref),
                (alog_hbm, alog_ref),
                (dt_hbm.at[0], dt_ref),
                (b_hbm.at[0], b_ref),
                (c_hbm.at[0], c_ref),
                (skip_hbm, skip_ref),
            )
        )
    ]
    for copy in small:
        copy.start()
    large = []
    for i in range(PIECES):
        at = slice(i * piece, (i + 1) * piece)
        for side, (source, target) in enumerate(((x_hbm, x_ref), (dy_hbm, dy_ref))):
            copy = pltpu.make_async_copy(
                source.at[0, :, at], target.at[:, at], sems.at[side, i]
            )
            copy.start()
            large.append(copy)
    square = (rows, rows)
    upper = jnp.where(iota(square, 0) <= iota(square, 1), 1.0, 0.0).astype(BF16)
    even = jnp.broadcast_to(lax.rem(shard(), 2), (width, LANES)) == 0
    left = iota((1, LANES), 1) < head_width
    for copy in small:
        copy.wait()
    _, offset, first, last = document_places(lens_ref, rows)
    through = jnp.where(first >= offset + rows, 1.0, 0.0)
    dt = dt_ref[...]
    logs = sum(dot(part, upper, 1, 0) for part in split3(dt * rate_column(alog_ref)))
    end_log = logs[:, rows - 1 : rows]
    place = iota((heads, rows), 1) + offset
    keeping = jnp.where(place >= last, jnp.exp(end_log - logs) * dt, 0.0)
    carried = jnp.where(place < first, jnp.exp(logs), 0.0)
    kept = jnp.broadcast_to(jnp.exp(end_log) * through, (heads, LANES))
    b, c = b_ref[...].astype(F32), c_ref[...].astype(F32)
    own = LANES // head_width

    def block_states(vectors, weights, values):
        rows_in = [stack(split2(vectors * weights[h : h + 1, :]), 1) for h in range(PARTS * own)]
        out = dot(stack(rows_in, 0), stack([values, values], 0), 1, 0)
        pairs = []
        for i in range(PARTS):
            lanes = slice(i * LANES, (i + 1) * LANES)
            sides = [
                out[h * width : (h + 1) * width, lanes] for h in range(i * own, (i + 1) * own)
            ]
            pairs.append(jnp.where(left, sides[0], sides[1]))
        return pairs

    pairs = columns // LANES
    for block in range(columns // WIDE):
        if block * WIDE % piece == 0:
            large[block * WIDE // piece * 2].wait()
            large[block * WIDE // piece * 2 + 1].wait()
        at = slice(block * WIDE, (block + 1) * WIDE)
        here = slice(block * PARTS * own, (block + 1) * PARTS * own)
        states = block_states(b, keeping[here], x_ref[:, at])
        pulls = block_states(c, carried[here], dy_ref[:, at])
        for i in range(PARTS):
            pair = block * PARTS + i
            kept_row = jnp.where(left, kept[pair * own : pair * own + 1], kept[pair * own + 1 :][:1])
            first = jnp.where(even, states[i], pulls[i])
            second = jnp.where(even, pulls[i], states[i])
            half, inner = divmod(pair, pairs // 2)
            for ref, place_in, whole, value in (
                (one_ref, pair, pairs, first),
                ((two_ref, three_ref)[half], inner, pairs // 2, second),
            ):
                ref[place_in * width : (place_in + 1) * width, :] = value
                ref[whole * width + place_in : whole * width + place_in + 1, :] = kept_row


def inside_kernel(
    lens_hbm,
    alog_ref,
    skip_ref,
    dt_ref,
    x_ref,
    b_ref,
    dy_ref,
    c_ref,
    _,
    xs_ref,
    ys_ref,
    v_wide_hbm,
    dx_hbm,
    b_end_ref,
    c_live_ref,
    masks_ref,
    db_ref,
    dc_ref,
    sums_ref,
    fwd_ref,
    bwd_ref,
    ends_ref,
    small_ref,
    v_stage,
    dx_stage,
    lens_ref,
    lens_sem,
    sems,
):
    rows, columns = x_ref.shape
    heads, width = dt_ref.shape[0], b_ref.shape[0]
    head_width = columns // heads
    lens_copy = pltpu.make_async_copy(lens_hbm, lens_ref, lens_sem)
    lens_copy.start()
    distance = head_distance(heads, head_width)
    bt, ct = b_ref[...], c_ref[...]
    raw_scores, raw_flipped = dot(ct, bt, 0, 0), dot(bt, ct, 0, 0)
    lens_copy.wait()
    starts, offset, first, last = document_places(lens_ref, rows)
    through = jnp.where(first >= offset + rows, 1.0, 0.0)
    square = (rows, rows)
    place0, place1 = iota(square, 0) + offset, iota(square, 1) + offset
    segment0, segment1 = jnp.zeros(square, jnp.int32), jnp.zeros(square, jnp.int32)
    for start in starts:
        segment0 += jnp.where(place0 >= start, 1, 0)
        segment1 += jnp.where(place1 >= start, 1, 0)
    same = segment0 == segment1
    down = same & (place0 >= place1)
    lower = jnp.where(place0 >= place1, 1.0, 0.0).astype(BF16)
    eye = jnp.where(place0 == place1, 1.0, 0.0).astype(BF16)
    dt = dt_ref[...]
    logs = sum(dot(lower, part, 1, 1) for part in split3(dt * rate_column(alog_ref)))
    steps = sum(dot(eye, part, 1, 1) for part in split3(dt))
    scores = split2(jnp.where(down, raw_scores, 0.0))
    flipped = split2(jnp.where(same & (place1 >= place0), raw_flipped, 0.0))
    place = iota((width, rows), 1) + offset
    bt_end = jnp.where(place >= last, bt.astype(F32), 0.0)
    ct_live = jnp.where(place < first, ct.astype(F32), 0.0)
    b_end, c_live = jnp.transpose(bt_end).astype(BF16), jnp.transpose(ct_live).astype(BF16)
    bt_end, ct_live = bt_end.astype(BF16), ct_live.astype(BF16)
    b_end_ref[...] = stack([b_end, b_end], 1)
    c_live_ref[...] = stack([c_live, c_live], 1)
    bt_end, ct_live = stack([bt_end, bt_end], 1), stack([ct_live, ct_live], 1)
    masks_ref[0:1] = jnp.where(place[:1] >= last, 1.0, 0.0)
    masks_ref[1:2] = jnp.where(place[:1] < first, 1.0, 0.0)
    tables = stack(
        [
            stack(split3(a), 1)
            for a in (
                jnp.exp(logs),
                jnp.exp(-logs) * steps,
                logs,
                jnp.broadcast_to(skip_ref[...], (16, heads)),
            )
        ],
        0,
    )
    d_scores = jnp.zeros((2 * rows, 2 * rows), F32)
    sums = jnp.zeros((2 * rows + 16, heads), F32)
    copies = []
    for block in range(columns // WIDE):
        at = slice(block * WIDE, (block + 1) * WIDE)
        wide = dot(tables, head_rows(distance, head_width, block), 1, 0)
        ones = head_columns(heads, head_width, block)
        u_wide, v_wide, l_wide = wide[:rows], wide[rows : 2 * rows], wide[2 * rows : 3 * rows]
        skip_wide = wide[3 * rows : 3 * rows + 1]
        x = x_ref[:, at].astype(F32)
        dy = dy_ref[:, at].astype(F32)
        xv = x * v_wide
        yu = dy * u_wide
        xs, ys = split2(xv), split2(yu)
        xs_ref[:, at] = stack(xs, 0)
        ys_ref[:, at] = stack(ys, 0)
        v_stage[:, at] = v_wide
        out = dot_pairs(scores, xs, 1, 0)
        back = dot_pairs(flipped, ys, 1, 0)
        d_scores += dot(stack(ys, 0), stack(xs, 0), 1, 1)
        dx_stage[:, at] = v_wide * back + skip_wide * dy
        for i, (stage, target) in enumerate(((v_stage, v_wide_hbm), (dx_stage, dx_hbm))):
            copy = pltpu.make_async_copy(stage.at[:, at], target.at[:, at], sems.at[i, block])
            copy.start()
            copies.append(copy)
        column_part = xv * back
        product = jnp.broadcast_to(jnp.sum(x * dy, axis=0, keepdims=True), (16, WIDE))
        for part in split3(stack([yu * out - column_part, column_part, product], 0)):
            sums += dot(part, ones, 1, 0)
        ending = u_wide[rows - 1 : rows]
        end_log = l_wide[rows - 1 : rows]
        gap = end_log - l_wide
        fwd_ref[:, at] = dot(bt_end, stack(split2(xv * gap), 0), 1, 0) * ending
        bwd_ref[:, at] = dot(ct_live, stack(split2(yu * l_wide), 0), 1, 0)
        ends_ref[0:1, at] = ending
        ends_ref[1:2, at] = ending * through
        ends_ref[2:3, at] = ending * through * end_log
    d_scores = (d_scores[:rows, :rows] + d_scores[:rows, rows:]) + d_scores[rows:, :rows]
    d_scores = split2(jnp.where(down, d_scores, 0.0))
    dc_ref[...] = sum(dot(bt, p, 1, 1) for p in d_scores)
    db_ref[...] = sum(dot(ct, p, 1, 0) for p in d_scores)
    sums_ref[...] = sums[: 2 * rows]
    rate_grads = jnp.sum(logs * sums[:rows], axis=0, keepdims=True)
    empty = jnp.zeros((1, LANES - 2 * heads), F32)
    small_ref[...] = stack([rate_grads, sums[2 * rows : 2 * rows + 1], empty], 1)
    for copy in copies:
        copy.wait()


def rates_kernel(reach, head_width, half, *refs):
    plan = message_plan(reach, half)
    messages = dict(zip(plan, refs))
    ends_ref, fwd_ref, bwd_ref, *refs = refs[len(plan) :]
    width, columns = fwd_ref.shape
    blocks = columns // WIDE
    own_blocks = blocks // 2
    came_ref, pull_ref, out_ref = refs[-3:]
    whole = []
    for i in range(own_blocks):
        block = half * own_blocks + i
        at = slice(block * WIDE, (block + 1) * WIDE)
        own = slice(i * WIDE, (i + 1) * WIDE)
        came, pull = received(messages, reach, block, blocks, width)
        came_ref[:, own] = came
        pull_ref[:, own] = pull
        terms = came * bwd_ref[:, at] + pull * (fwd_ref[:, at] + ends_ref[2:3, at] * came)
        whole.append(jnp.sum(terms, axis=0, keepdims=True))
    if not half:
        out_ref[...] = stack(whole, 0)
        return
    small_ref, first_ref = refs[:2]
    own = WIDE // head_width
    shape = (WIDE, LANES)
    column = lax.shift_right_logical(iota(shape, 0), log2(head_width))
    ones = jnp.where(column == (iota(shape, 1) & (own - 1)), 1.0, 0.0).astype(BF16)
    sums = dot(stack(split3(stack([first_ref[...], *whole], 0)), 0), ones, 1, 0)
    sums = (sums[:blocks] + sums[blocks : 2 * blocks]) + sums[2 * blocks :]
    lane = iota(sums.shape, 1)
    mine = lax.shift_right_logical(lane, log2(own)) == iota(sums.shape, 0)
    total = small_ref[...] + jnp.sum(jnp.where(mine, sums, 0.0), axis=0, keepdims=True)
    out_ref[...] = jnp.broadcast_to(total, out_ref.shape)


def outputs_kernel(
    came_one,
    came_two,
    pull_one,
    pull_two,
    ends_ref,
    xs_ref,
    ys_ref,
    v_wide_hbm,
    dx_hbm,
    b_end_ref,
    c_live_ref,
    masks_ref,
    db_ref,
    dc_ref,
    sums_ref,
    alog_ref,
    dt_ref,
    dx_out,
    db_out,
    dc_out,
    dt_out,
    v_stage,
    dx_stage,
    stage,
    in_sems,
    out_sems,
):
    rows, columns = dx_hbm.shape
    heads, width = dt_ref.shape[0], db_ref.shape[0]
    blocks = columns // WIDE
    copies = []
    for block in range(blocks):
        at = slice(block * WIDE, (block + 1) * WIDE)
        for i, (source, target) in enumerate(((v_wide_hbm, v_stage), (dx_hbm, dx_stage))):
            copy = pltpu.make_async_copy(
                source.at[:, at], target.at[:, at], in_sems.at[i, block]
            )
            copy.start()
            copies.append(copy)
    b_end, c_live = b_end_ref[...], c_live_ref[...]
    own_sums = sums_ref[...]
    sums = own_sums
    dc = jnp.zeros((2 * width, 2 * rows), F32)
    db = jnp.zeros((2 * width, 2 * rows), F32)
    at_last = iota((rows, WIDE), 0) == rows - 1
    sent = []
    for block in range(blocks):
        at = slice(block * WIDE, (block + 1) * WIDE)
        ones = head_columns(heads, columns // heads, block)
        half, inner = divmod(block, blocks // 2)
        own = slice(inner * WIDE, (inner + 1) * WIDE)
        came, pull = (came_one, came_two)[half][:, own], (pull_one, pull_two)[half][:, own]
        meet = jnp.sum(came * pull, axis=0, keepdims=True) * ends_ref[1:2, at]
        cames = stack(split2(came), 0)
        pulls = stack(split2(pull * ends_ref[0:1, at]), 0)
        xs, ys = xs_ref[:, at], ys_ref[:, at]
        out = dot(c_live, cames, 1, 0)
        back = dot(b_end, pulls, 1, 0)
        column_part = (xs[:rows].astype(F32) + xs[rows:].astype(F32)) * back
        row_part = (ys[:rows].astype(F32) + ys[rows:].astype(F32)) * out
        row_part = jnp.where(at_last, row_part + meet, row_part)
        for part in split2(stack([row_part - column_part, column_part], 0)):
            sums += dot(part, ones, 1, 0)
        dc += dot(cames, ys, 1, 1)
        db += dot(pulls, xs, 1, 1)
        copies[2 * block].wait()
        copies[2 * block + 1].wait()
        stage[:, at] = (dx_stage[:, at] + v_stage[:, at] * back).astype(BF16)
        copy = pltpu.make_async_copy(stage.at[:, at], dx_out.at[0, :, at], out_sems.at[block])
        copy.start()
        sent.append(copy)
    dc = (dc[:width, :rows] + dc[:width, rows:]) + dc[width:, :rows]
    db = (db[:width, :rows] + db[:width, rows:]) + db[width:, :rows]
    db_out[0] = (db_ref[...] + masks_ref[0:1] * db).astype(BF16)
    dc_out[0] = (dc_ref[...] + masks_ref[1:2] * dc).astype(BF16)
    square = (rows, rows)
    upper = jnp.where(iota(square, 0) >= iota(square, 1), 1.0, 0.0).astype(BF16)
    eye = jnp.where(iota(square, 0) == iota(square, 1), 1.0, 0.0).astype(BF16)
    at_end = jnp.sum(sums[rows:] - own_sums[rows:], axis=0, keepdims=True)
    dl = sums[:rows] + jnp.where(iota((rows, heads), 0) == rows - 1, at_end, 0.0)
    d_decay = sum(dot(part, upper, 0, 0) for part in split3(dl))
    total = sum(dot(part, eye, 0, 0) for part in split3(sums[rows:]))
    dt_out[0] = total / dt_ref[...] + rate_column(alog_ref) * d_decay
    for copy in sent:
        copy.wait()


def call(kernel, reach, outs, ins, flops, moved, scratch=()):
    spaces = {"s": pltpu.SMEM, "v": pltpu.VMEM, "h": pltpu.HBM, "any": pl.ANY}
    return pl.pallas_call(
        kernel,
        out_shape=[
            pltpu.HBM(*out) if place == "h" else jax.ShapeDtypeStruct(*out) for place, out in outs
        ],
        in_specs=[pl.BlockSpec(memory_space=spaces[place]) for place, _ in ins],
        out_specs=[pl.BlockSpec(memory_space=spaces[place]) for place, _ in outs],
        scratch_shapes=scratch,
        compiler_params=pltpu.CompilerParams(vmem_limit_bytes=min(16 + 2 * reach, 56) * 2**20),
        cost_estimate=pl.CostEstimate(flops=flops, bytes_accessed=moved, transcendentals=0),
    )(*(a for _, a in ins))


def send(a, by, second):
    count = lax.axis_size("ctx")
    pairs = [(i, i + by if (i + second) % 2 == 0 else i - by) for i in range(count)]
    return lax.ppermute(a, "ctx", [(i, j) for i, j in pairs if 0 <= j < count])


def hand_on(a):
    count = lax.axis_size("ctx")
    return lax.ppermute(a, "ctx", [(i, i ^ 1) for i in range(count)])


def in_hbm(a):
    return "h", pltpu.with_memory_space_constraint(a, pltpu.HBM)


def per_device(inputs, b_proj, c_proj, step_sizes, a_log, skip_gain, doc_lengths, grad_out):
    rows, columns = inputs.shape[1:]
    heads, width = a_log.shape[0], b_proj.shape[2]
    reach = max(lax.axis_size("ctx") // 4, 1)
    devices = lax.axis_size("ctx") * lax.axis_size("dp")
    alog, skip = a_log[None], skip_gain[None]
    bt, ct = jnp.swapaxes(b_proj, 1, 2), jnp.swapaxes(c_proj, 1, 2)
    blocks = columns // WIDE

    def v(shape, kind=F32):
        return "v", (shape, kind)

    alog, skip, dt, x, b, dy, c, *payloads = call(
        states_kernel,
        reach,
        [
            v(alog.shape),
            v(skip.shape),
            v((heads, rows)),
            v((rows, columns), BF16),
            v((width, rows), BF16),
            v((rows, columns), BF16),
            v((width, rows), BF16),
        ]
        + [v((columns // LANES * (width + 1) // part, LANES)) for part in (1, 2, 2)],
        [in_hbm(a) for a in (doc_lengths, alog, skip, step_sizes, inputs, bt, grad_out, ct)],
        10**9,
        4 * 2**20,
        [
            pltpu.SMEM(doc_lengths.shape, jnp.int32),
            pltpu.SemaphoreType.DMA((6,)),
            pltpu.SemaphoreType.DMA((2, PIECES)),
        ],
    )
    messages = {}
    for j, second, half in message_plan(reach):
        if (j, second) == (1, 1) and reach > 1:
            continue
        payload = payloads[1 + half if second else 0]
        messages[j, second, half] = send(payload, j, second)
    if reach > 1:
        for half in (0, 1):
            messages[1, 1, half] = hand_on(messages[2, 1, half])
    whole = "h", ((rows, columns), F32)
    state = v((width, columns))
    stage = pltpu.VMEM((rows, columns), F32)
    transposed = v((width, rows))
    xs, ys, v_wide, dx, b_end, c_live, masks, db, dc, sums, fwd_logs, bwd_logs, ends, small = call(
        inside_kernel,
        reach,
        [v((2 * rows, columns), BF16)] * 2
        + [whole] * 2
        + [v((rows, 2 * width), BF16)] * 2
        + [v((8, rows)), transposed, transposed, v((2 * rows, heads))]
        + [state, state, v((8, columns)), v((1, LANES))],
        [in_hbm(doc_lengths)]
        + [("v", a) for a in (alog, skip, dt, x, b, dy, c)]
        + [("any", messages[1, 0, 0])],
        4 * 10**9,
        12 * 2**20,
        [
            stage,
            stage,
            pltpu.SMEM(doc_lengths.shape, jnp.int32),
            pltpu.SemaphoreType.DMA,
            pltpu.SemaphoreType.DMA((2, blocks)),
        ],
    )
    half_state = v((width, columns // 2))
    joined, last = [], []
    for half in (0, 1):
        out = v((devices, LANES)) if half else v((blocks // 2, WIDE))
        came, pull, partial = call(
            functools.partial(rates_kernel, reach, columns // heads, half),
            reach,
            [half_state, half_state, out],
            [("v", messages[one]) for one in message_plan(reach, half)]
            + [("v", a) for a in (ends, fwd_logs, bwd_logs, *last)],
            10**8,
            4 * 2**20,
        )
        joined.append((came, pull))
        last = [small, partial]
    input_grads, b_gradient, c_gradient, step_grads = call(
        outputs_kernel,
        reach,
        [("h", ((1, rows, columns), BF16))]
        + [v((1, width, rows), BF16)] * 2
        + [v((1, heads, rows))],
        [("v", a) for side in zip(*joined) for a in side]
        + [("v", a) for a in (ends, xs, ys)]
        + [in_hbm(v_wide), in_hbm(dx)]
        + [("v", a) for a in (b_end, c_live, masks, db, dc, sums, alog, dt)],
        2 * 10**9,
        12 * 2**20,
        [
            stage,
            stage,
            pltpu.VMEM((rows, columns), BF16),
            pltpu.SemaphoreType.DMA((2, blocks)),
            pltpu.SemaphoreType.DMA((blocks,)),
        ],
    )
    gathered = lax.all_to_all(partial, ("ctx", "dp"), 0, 0, tiled=True)
    totals = jnp.sum(gathered, axis=0)
    return (
        input_grads,
        jnp.swapaxes(b_gradient, 1, 2),
        jnp.swapaxes(c_gradient, 1, 2),
        step_grads,
        totals[:heads],
        totals[heads : 2 * heads],
    )


def solution(mesh):
    in_specs = (
        P("dp", "ctx", None),
        P("dp", "ctx", None),
        P("dp", "ctx", None),
        P("dp", None, "ctx"),
        P(),
        P(),
        P("dp", None),
        P("dp", "ctx", None),
    )
    out_specs = (
        P("dp", "ctx", None),
        P("dp", "ctx", None),
        P("dp", "ctx", None),
        P("dp", None, "ctx"),
        P(),
        P(),
    )
    return jax.shard_map(
        per_device, mesh=mesh, in_specs=in_specs, out_specs=out_specs, check_vma=False
    )
```

```python
import functools

import jax
import jax.numpy as jnp
from jax import lax
from jax.experimental import pallas as pl
from jax.experimental.pallas import tpu as pltpu
from jax.sharding import PartitionSpec as P

F32 = jnp.float32
BF16 = jnp.bfloat16
LANES = 128
WIDE = 256
PARTS = WIDE // LANES
FAR = 2**30
PIECES = 4


def dot(a, b, ca, cb):
    return lax.dot_general(a, b, (((ca,), (cb,)), ((), ())), preferred_element_type=F32)


def iota(shape, dim):
    return lax.broadcasted_iota(jnp.int32, shape, dim)


def split2(a):
    high = a.astype(BF16)
    return high, (a - high.astype(F32)).astype(BF16)


def split3(a):
    high = a.astype(BF16)
    rest = a - high.astype(F32)
    middle = rest.astype(BF16)
    return high, middle, (rest - middle.astype(F32)).astype(BF16)


def dot_pairs(a, b, ca, cb):
    return dot(a[0], b[0], ca, cb) + (dot(a[0], b[1], ca, cb) + dot(a[1], b[0], ca, cb))


def stack(parts, axis):
    return jnp.concatenate(parts, axis=axis)


def document_places(lens_ref, rows):
    offset = shard() * rows
    starts = [jnp.int32(0)]
    for d in range(lens_ref.shape[1] - 1):
        starts.append(starts[-1] + lens_ref[0, d])
    first = jnp.int32(FAR)
    last = jnp.int32(0)
    for start in starts:
        first = jnp.minimum(first, jnp.where(start >= offset, start, FAR))
        last = jnp.maximum(last, jnp.where(start < offset + rows, start, 0))
    return starts, offset, first, last


def rate_column(alog_ref):
    heads = alog_ref.shape[1]
    square = jnp.broadcast_to(alog_ref[...], (heads, heads))
    picked = jnp.where(iota((heads, heads), 0) == iota((heads, heads), 1), square, 0.0)
    return -jnp.exp(jnp.sum(picked, axis=1, keepdims=True))


def log2(size):
    assert size & (size - 1) == 0
    return size.bit_length() - 1


def head_distance(heads, head_width):
    shape = (3 * heads, WIDE)
    return (iota(shape, 0) & (heads - 1)) - lax.shift_right_logical(
        iota(shape, 1), log2(head_width)
    )


def head_rows(distance, head_width, block):
    return jnp.where(distance == block * (WIDE // head_width), 1.0, 0.0).astype(BF16)


def head_columns(heads, head_width, block):
    shape = (WIDE, heads)
    column = lax.shift_right_logical(iota(shape, 0), log2(head_width))
    return jnp.where(iota(shape, 1) - column == block * (WIDE // head_width), 1.0, 0.0).astype(BF16)


def shard():
    return lax.axis_index("ctx")


def message_block(ref, block, width):
    at = block * PARTS
    return stack([ref[(at + i) * width : (at + i + 1) * width, :] for i in range(PARTS)], 1)


def message_tail(ref, block, width):
    tail = ref.shape[0] // (width + 1) * width + block * PARTS
    return stack([ref[tail + i : tail + i + 1, :] for i in range(PARTS)], 1)


def message_plan(reach, only=None):
    near = [(1, 0, 0)]
    relayed = [(1, 1, 0), (1, 1, 1)]
    far = [(2, 1, 0), (2, 1, 1), (2, 0, 0)] if reach > 1 else []
    rest = [(j, *one) for j in range(3, reach + 1) for one in ((0, 0), (1, 0), (1, 1))]
    plan = near + far + relayed + rest
    return [one for one in plan if only is None or not one[1] or one[2] == only]


def received(messages, reach, block, blocks, width):
    came = pull = None
    half, inner = divmod(block, blocks // 2)
    for j in range(reach, 0, -1):
        one, two = messages[j, 0, 0], messages[j, 1, half]
        a, b = message_block(one, block, width), message_block(two, inner, width)
        first = jnp.broadcast_to(lax.rem(shard() + j, 2), a.shape) == 0
        near_came, near_pull = jnp.where(first, a, b), jnp.where(first, b, a)
        if came is None:
            came, pull = near_came, near_pull
        else:
            a, b = message_tail(one, block, width), message_tail(two, inner, width)
            first = jnp.broadcast_to(lax.rem(shard() + j, 2), a.shape) == 0
            came = near_came + jnp.where(first, a, b) * came
            pull = near_pull + jnp.where(first, b, a) * pull
    return came, pull


def states_kernel(second, *refs):
    refs, sems = refs[:-PIECES], refs[-PIECES:]
    if second:
        lens_hbm, x_hbm, dy_hbm, alog_ref, dt_ref, b_ref, c_ref = refs[:7]
        x_ref, *messages = refs[7:10]
        lens_ref, small_sems = refs[10:]
        moves = [(lens_hbm, lens_ref)]
    else:
        lens_hbm, x_hbm, dy_hbm, alog_hbm, skip_hbm, dt_hbm, b_hbm, c_hbm = refs[:8]
        alog_ref, skip_ref, dt_ref, b_ref, c_ref, x_ref, *messages = refs[8:15]
        lens_ref, small_sems = refs[15:]
        moves = [
            (dt_hbm.at[0], dt_ref),
            (alog_hbm, alog_ref),
            (lens_hbm, lens_ref),
            (b_hbm.at[0], b_ref),
            (c_hbm.at[0], c_ref),
            (skip_hbm, skip_ref),
        ]
    rows, columns = x_ref.shape
    heads, width = dt_ref.shape[0], b_ref.shape[0]
    head_width = columns // heads
    piece = columns // PIECES
    small = [
        pltpu.make_async_copy(source, target, small_sems.at[i])
        for i, (source, target) in enumerate(moves)
    ]
    for copy in small:
        copy.start()

    def piece_copy(source, i):
        at = slice(i * piece, (i + 1) * piece)
        return pltpu.make_async_copy(source.at[0, :, at], x_ref.at[:, at], sems[i])

    forward = lax.rem(shard() + second, 2)

    @pl.when(forward == 0)
    def _():
        for i in range(PIECES):
            piece_copy(x_hbm, i).start()

    @pl.when(forward != 0)
    def _():
        for i in range(PIECES):
            piece_copy(dy_hbm, i).start()

    square = (rows, rows)
    upper = jnp.where(iota(square, 0) <= iota(square, 1), 1.0, 0.0).astype(BF16)
    left = iota((1, LANES), 1) < head_width
    for copy in small:
        copy.wait()
    _, offset, first, last = document_places(lens_ref, rows)
    through = jnp.where(first >= offset + rows, 1.0, 0.0)
    dt = dt_ref[...]
    logs = sum(dot(part, upper, 1, 0) for part in split3(dt * rate_column(alog_ref)))
    end_log = logs[:, rows - 1 : rows]
    place = iota((heads, rows), 1) + offset
    keeping = jnp.where(place >= last, jnp.exp(end_log - logs) * dt, 0.0)
    carried = jnp.where(place < first, jnp.exp(logs), 0.0)
    kept = jnp.broadcast_to(jnp.exp(end_log) * through, (heads, LANES))
    weights = jnp.where(jnp.broadcast_to(forward, (heads, rows)) == 0, keeping, carried)
    vectors = jnp.where(
        jnp.broadcast_to(forward, (width, rows)) == 0,
        b_ref[...].astype(F32),
        c_ref[...].astype(F32),
    )
    own = LANES // head_width
    pairs = columns // LANES // len(messages)
    for block in range(columns // WIDE):
        if block * WIDE % piece == 0:
            piece_copy(x_hbm, block * WIDE // piece).wait()
        values = x_ref[:, block * WIDE : (block + 1) * WIDE]
        here = range(block * PARTS * own, (block + 1) * PARTS * own)
        rows_in = [stack(split2(vectors * weights[h : h + 1, :]), 1) for h in here]
        out = dot(stack(rows_in, 0), stack([values, values], 0), 1, 0)
        for i in range(PARTS):
            lanes = slice(i * LANES, (i + 1) * LANES)
            sides = [
                out[h * width : (h + 1) * width, lanes] for h in range(i * own, (i + 1) * own)
            ]
            pair = block * PARTS + i
            part, inner = divmod(pair, pairs)
            kept_row = jnp.where(left, kept[pair * own :][:1], kept[pair * own + 1 :][:1])
            ref, tail = messages[part], pairs * width + inner
            ref[inner * width : (inner + 1) * width, :] = jnp.where(left, sides[0], sides[1])
            ref[tail : tail + 1, :] = kept_row


def inside_kernel(
    lens_hbm,
    alog_ref,
    skip_ref,
    dt_ref,
    b_ref,
    c_ref,
    one_ref,
    two_ref,
    _,
    xs_ref,
    ys_ref,
    v_wide_hbm,
    dx_hbm,
    b_end_ref,
    c_live_ref,
    masks_ref,
    db_ref,
    dc_ref,
    sums_ref,
    fwd_ref,
    bwd_ref,
    ends_ref,
    small_ref,
    v_stage,
    dx_stage,
    lens_ref,
    lens_sem,
    sems,
):
    rows, columns = one_ref.shape
    heads, width = dt_ref.shape[0], b_ref.shape[0]
    head_width = columns // heads
    lens_copy = pltpu.make_async_copy(lens_hbm, lens_ref, lens_sem)
    lens_copy.start()
    distance = head_distance(heads, head_width)
    bt, ct = b_ref[...], c_ref[...]
    raw_scores, raw_flipped = dot(ct, bt, 0, 0), dot(bt, ct, 0, 0)
    lens_copy.wait()
    starts, offset, first, last = document_places(lens_ref, rows)
    through = jnp.where(first >= offset + rows, 1.0, 0.0)
    square = (rows, rows)
    place0, place1 = iota(square, 0) + offset, iota(square, 1) + offset
    segment0, segment1 = jnp.zeros(square, jnp.int32), jnp.zeros(square, jnp.int32)
    for start in starts:
        segment0 += jnp.where(place0 >= start, 1, 0)
        segment1 += jnp.where(place1 >= start, 1, 0)
    same = segment0 == segment1
    down = same & (place0 >= place1)
    lower = jnp.where(place0 >= place1, 1.0, 0.0).astype(BF16)
    eye = jnp.where(place0 == place1, 1.0, 0.0).astype(BF16)
    dt = dt_ref[...]
    logs = sum(dot(lower, part, 1, 1) for part in split3(dt * rate_column(alog_ref)))
    steps = sum(dot(eye, part, 1, 1) for part in split3(dt))
    scores = split2(jnp.where(down, raw_scores, 0.0))
    flipped = split2(jnp.where(same & (place1 >= place0), raw_flipped, 0.0))
    place = iota((width, rows), 1) + offset
    bt_end = jnp.where(place >= last, bt.astype(F32), 0.0)
    ct_live = jnp.where(place < first, ct.astype(F32), 0.0)
    b_end, c_live = jnp.transpose(bt_end).astype(BF16), jnp.transpose(ct_live).astype(BF16)
    bt_end, ct_live = bt_end.astype(BF16), ct_live.astype(BF16)
    b_end_ref[...] = stack([b_end, b_end], 1)
    c_live_ref[...] = stack([c_live, c_live], 1)
    bt_end, ct_live = stack([bt_end, bt_end], 1), stack([ct_live, ct_live], 1)
    masks_ref[0:1] = jnp.where(place[:1] >= last, 1.0, 0.0)
    masks_ref[1:2] = jnp.where(place[:1] < first, 1.0, 0.0)
    tables = stack(
        [
            stack(split3(a), 1)
            for a in (
                jnp.exp(logs),
                jnp.exp(-logs) * steps,
                logs,
                jnp.broadcast_to(skip_ref[...], (16, heads)),
            )
        ],
        0,
    )
    d_scores = jnp.zeros((2 * rows, 2 * rows), F32)
    sums = jnp.zeros((2 * rows + 16, heads), F32)
    copies = []
    even = jnp.broadcast_to(lax.rem(shard(), 2), (rows, WIDE)) == 0
    for block in range(columns // WIDE):
        at = slice(block * WIDE, (block + 1) * WIDE)
        wide = dot(tables, head_rows(distance, head_width, block), 1, 0)
        ones = head_columns(heads, head_width, block)
        u_wide, v_wide, l_wide = wide[:rows], wide[rows : 2 * rows], wide[2 * rows : 3 * rows]
        skip_wide = wide[3 * rows : 3 * rows + 1]
        one, two = one_ref[:, at].astype(F32), two_ref[:, at].astype(F32)
        x, dy = jnp.where(even, one, two), jnp.where(even, two, one)
        xv = x * v_wide
        yu = dy * u_wide
        xs, ys = split2(xv), split2(yu)
        xs_ref[:, at] = stack(xs, 0)
        ys_ref[:, at] = stack(ys, 0)
        v_stage[:, at] = v_wide
        out = dot_pairs(scores, xs, 1, 0)
        back = dot_pairs(flipped, ys, 1, 0)
        d_scores += dot(stack(ys, 0), stack(xs, 0), 1, 1)
        dx_stage[:, at] = v_wide * back + skip_wide * dy
        for i, (stage, target) in enumerate(((v_stage, v_wide_hbm), (dx_stage, dx_hbm))):
            copy = pltpu.make_async_copy(stage.at[:, at], target.at[:, at], sems.at[i, block])
            copy.start()
            copies.append(copy)
        column_part = xv * back
        product = jnp.broadcast_to(jnp.sum(x * dy, axis=0, keepdims=True), (16, WIDE))
        for part in split3(stack([yu * out - column_part, column_part, product], 0)):
            sums += dot(part, ones, 1, 0)
        ending = u_wide[rows - 1 : rows]
        end_log = l_wide[rows - 1 : rows]
        gap = end_log - l_wide
        fwd_ref[:, at] = dot(bt_end, stack(split2(xv * gap), 0), 1, 0) * ending
        bwd_ref[:, at] = dot(ct_live, stack(split2(yu * l_wide), 0), 1, 0)
        ends_ref[0:1, at] = ending
        ends_ref[1:2, at] = ending * through
        ends_ref[2:3, at] = ending * through * end_log
    d_scores = (d_scores[:rows, :rows] + d_scores[:rows, rows:]) + d_scores[rows:, :rows]
    d_scores = split2(jnp.where(down, d_scores, 0.0))
    dc_ref[...] = sum(dot(bt, p, 1, 1) for p in d_scores)
    db_ref[...] = sum(dot(ct, p, 1, 0) for p in d_scores)
    sums_ref[...] = sums[: 2 * rows]
    rate_grads = jnp.sum(logs * sums[:rows], axis=0, keepdims=True)
    empty = jnp.zeros((1, LANES - 2 * heads), F32)
    small_ref[...] = stack([rate_grads, sums[2 * rows : 2 * rows + 1], empty], 1)
    for copy in copies:
        copy.wait()


def rates_kernel(reach, head_width, half, *refs):
    plan = message_plan(reach, half)
    messages = dict(zip(plan, refs))
    ends_ref, fwd_ref, bwd_ref, *refs = refs[len(plan) :]
    width, columns = fwd_ref.shape
    blocks = columns // WIDE
    own_blocks = blocks // 2
    came_ref, pull_ref, out_ref = refs[-3:]
    whole = []
    for i in range(own_blocks):
        block = half * own_blocks + i
        at = slice(block * WIDE, (block + 1) * WIDE)
        own = slice(i * WIDE, (i + 1) * WIDE)
        came, pull = received(messages, reach, block, blocks, width)
        came_ref[:, own] = came
        pull_ref[:, own] = pull
        terms = came * bwd_ref[:, at] + pull * (fwd_ref[:, at] + ends_ref[2:3, at] * came)
        whole.append(jnp.sum(terms, axis=0, keepdims=True))
    if not half:
        out_ref[...] = stack(whole, 0)
        return
    small_ref, first_ref = refs[:2]
    own = WIDE // head_width
    shape = (WIDE, LANES)
    column = lax.shift_right_logical(iota(shape, 0), log2(head_width))
    ones = jnp.where(column == (iota(shape, 1) & (own - 1)), 1.0, 0.0).astype(BF16)
    sums = dot(stack(split3(stack([first_ref[...], *whole], 0)), 0), ones, 1, 0)
    sums = (sums[:blocks] + sums[blocks : 2 * blocks]) + sums[2 * blocks :]
    lane = iota(sums.shape, 1)
    mine = lax.shift_right_logical(lane, log2(own)) == iota(sums.shape, 0)
    total = small_ref[...] + jnp.sum(jnp.where(mine, sums, 0.0), axis=0, keepdims=True)
    out_ref[...] = jnp.broadcast_to(total, out_ref.shape)


def outputs_kernel(
    came_one,
    came_two,
    pull_one,
    pull_two,
    ends_ref,
    xs_ref,
    ys_ref,
    v_wide_hbm,
    dx_hbm,
    b_end_ref,
    c_live_ref,
    masks_ref,
    db_ref,
    dc_ref,
    sums_ref,
    alog_ref,
    dt_ref,
    dx_out,
    db_out,
    dc_out,
    dt_out,
    v_stage,
    dx_stage,
    stage,
    in_sems,
    out_sems,
):
    rows, columns = dx_hbm.shape
    heads, width = dt_ref.shape[0], db_ref.shape[0]
    blocks = columns // WIDE
    copies = []
    for block in range(blocks):
        at = slice(block * WIDE, (block + 1) * WIDE)
        for i, (source, target) in enumerate(((v_wide_hbm, v_stage), (dx_hbm, dx_stage))):
            copy = pltpu.make_async_copy(
                source.at[:, at], target.at[:, at], in_sems.at[i, block]
            )
            copy.start()
            copies.append(copy)
    b_end, c_live = b_end_ref[...], c_live_ref[...]
    own_sums = sums_ref[...]
    sums = own_sums
    dc = jnp.zeros((2 * width, 2 * rows), F32)
    db = jnp.zeros((2 * width, 2 * rows), F32)
    at_last = iota((rows, WIDE), 0) == rows - 1
    sent = []
    for block in range(blocks):
        at = slice(block * WIDE, (block + 1) * WIDE)
        ones = head_columns(heads, columns // heads, block)
        half, inner = divmod(block, blocks // 2)
        own = slice(inner * WIDE, (inner + 1) * WIDE)
        came, pull = (came_one, came_two)[half][:, own], (pull_one, pull_two)[half][:, own]
        meet = jnp.sum(came * pull, axis=0, keepdims=True) * ends_ref[1:2, at]
        cames = stack(split2(came), 0)
        pulls = stack(split2(pull * ends_ref[0:1, at]), 0)
        xs, ys = xs_ref[:, at], ys_ref[:, at]
        out = dot(c_live, cames, 1, 0)
        back = dot(b_end, pulls, 1, 0)
        column_part = (xs[:rows].astype(F32) + xs[rows:].astype(F32)) * back
        row_part = (ys[:rows].astype(F32) + ys[rows:].astype(F32)) * out
        row_part = jnp.where(at_last, row_part + meet, row_part)
        for part in split2(stack([row_part - column_part, column_part], 0)):
            sums += dot(part, ones, 1, 0)
        dc += dot(cames, ys, 1, 1)
        db += dot(pulls, xs, 1, 1)
        copies[2 * block].wait()
        copies[2 * block + 1].wait()
        stage[:, at] = (dx_stage[:, at] + v_stage[:, at] * back).astype(BF16)
        copy = pltpu.make_async_copy(stage.at[:, at], dx_out.at[0, :, at], out_sems.at[block])
        copy.start()
        sent.append(copy)
    dc = (dc[:width, :rows] + dc[:width, rows:]) + dc[width:, :rows]
    db = (db[:width, :rows] + db[:width, rows:]) + db[width:, :rows]
    db_out[0] = (db_ref[...] + masks_ref[0:1] * db).astype(BF16)
    dc_out[0] = (dc_ref[...] + masks_ref[1:2] * dc).astype(BF16)
    square = (rows, rows)
    upper = jnp.where(iota(square, 0) >= iota(square, 1), 1.0, 0.0).astype(BF16)
    eye = jnp.where(iota(square, 0) == iota(square, 1), 1.0, 0.0).astype(BF16)
    at_end = jnp.sum(sums[rows:] - own_sums[rows:], axis=0, keepdims=True)
    dl = sums[:rows] + jnp.where(iota((rows, heads), 0) == rows - 1, at_end, 0.0)
    d_decay = sum(dot(part, upper, 0, 0) for part in split3(dl))
    total = sum(dot(part, eye, 0, 0) for part in split3(sums[rows:]))
    dt_out[0] = total / dt_ref[...] + rate_column(alog_ref) * d_decay
    for copy in sent:
        copy.wait()


def call(kernel, reach, outs, ins, flops, moved, scratch=()):
    spaces = {"s": pltpu.SMEM, "v": pltpu.VMEM, "h": pltpu.HBM, "any": pl.ANY}
    return pl.pallas_call(
        kernel,
        out_shape=[
            pltpu.HBM(*out) if place == "h" else jax.ShapeDtypeStruct(*out) for place, out in outs
        ],
        in_specs=[pl.BlockSpec(memory_space=spaces[place]) for place, _ in ins],
        out_specs=[pl.BlockSpec(memory_space=spaces[place]) for place, _ in outs],
        scratch_shapes=scratch,
        compiler_params=pltpu.CompilerParams(vmem_limit_bytes=min(16 + 2 * reach, 56) * 2**20),
        cost_estimate=pl.CostEstimate(flops=flops, bytes_accessed=moved, transcendentals=0),
    )(*(a for _, a in ins))


def send(a, by, second):
    count = lax.axis_size("ctx")
    pairs = [(i, i + by if (i + second) % 2 == 0 else i - by) for i in range(count)]
    return lax.ppermute(a, "ctx", [(i, j) for i, j in pairs if 0 <= j < count])


def hand_on(a):
    count = lax.axis_size("ctx")
    return lax.ppermute(a, "ctx", [(i, i ^ 1) for i in range(count)])


def in_hbm(a):
    return "h", pltpu.with_memory_space_constraint(a, pltpu.HBM)


def per_device(inputs, b_proj, c_proj, step_sizes, a_log, skip_gain, doc_lengths, grad_out):
    rows, columns = inputs.shape[1:]
    heads, width = a_log.shape[0], b_proj.shape[2]
    reach = max(lax.axis_size("ctx") // 4, 1)
    devices = lax.axis_size("ctx") * lax.axis_size("dp")
    alog, skip = a_log[None], skip_gain[None]
    bt, ct = jnp.swapaxes(b_proj, 1, 2), jnp.swapaxes(c_proj, 1, 2)
    blocks = columns // WIDE

    def v(shape, kind=F32):
        return "v", (shape, kind)

    large = v((rows, columns), BF16)
    lens_space = pltpu.SMEM(doc_lengths.shape, jnp.int32)
    first_in = [in_hbm(a) for a in (doc_lengths, inputs, grad_out)]
    alog, skip, dt, b, c, one, payload = call(
        functools.partial(states_kernel, 0),
        reach,
        [v(alog.shape), v(skip.shape), v((heads, rows))]
        + [v((width, rows), BF16)] * 2
        + [large, v((columns // LANES * (width + 1), LANES))],
        first_in + [in_hbm(a) for a in (alog, skip, step_sizes, bt, ct)],
        10**9,
        2 * 2**20,
        [lens_space, pltpu.SemaphoreType.DMA((6,))] + [pltpu.SemaphoreType.DMA] * PIECES,
    )
    two, *halves = call(
        functools.partial(states_kernel, 1),
        reach,
        [large] + [v((columns // LANES * (width + 1) // 2, LANES))] * 2,
        first_in + [("v", a) for a in (alog, dt, b, c)],
        10**9,
        2 * 2**20,
        [lens_space, pltpu.SemaphoreType.DMA((1,))] + [pltpu.SemaphoreType.DMA] * PIECES,
    )
    payloads = [payload, *halves]
    messages = {}
    for j, second, half in message_plan(reach):
        if (j, second) == (1, 1) and reach > 1:
            continue
        payload = payloads[1 + half if second else 0]
        messages[j, second, half] = send(payload, j, second)
    if reach > 1:
        for half in (0, 1):
            messages[1, 1, half] = hand_on(messages[2, 1, half])
    whole = "h", ((rows, columns), F32)
    state = v((width, columns))
    stage = pltpu.VMEM((rows, columns), F32)
    transposed = v((width, rows))
    xs, ys, v_wide, dx, b_end, c_live, masks, db, dc, sums, fwd_logs, bwd_logs, ends, small = call(
        inside_kernel,
        reach,
        [v((2 * rows, columns), BF16)] * 2
        + [whole] * 2
        + [v((rows, 2 * width), BF16)] * 2
        + [v((8, rows)), transposed, transposed, v((2 * rows, heads))]
        + [state, state, v((8, columns)), v((1, LANES))],
        [in_hbm(doc_lengths)]
        + [("v", a) for a in (alog, skip, dt, b, c, one, two)]
        + [("any", messages[1, 0, 0])],
        4 * 10**9,
        12 * 2**20,
        [
            stage,
            stage,
            pltpu.SMEM(doc_lengths.shape, jnp.int32),
            pltpu.SemaphoreType.DMA,
            pltpu.SemaphoreType.DMA((2, blocks)),
        ],
    )
    half_state = v((width, columns // 2))
    joined, last = [], []
    for half in (0, 1):
        out = v((devices, LANES)) if half else v((blocks // 2, WIDE))
        came, pull, partial = call(
            functools.partial(rates_kernel, reach, columns // heads, half),
            reach,
            [half_state, half_state, out],
            [("v", messages[one]) for one in message_plan(reach, half)]
            + [("v", a) for a in (ends, fwd_logs, bwd_logs, *last)],
            10**8,
            4 * 2**20,
        )
        joined.append((came, pull))
        last = [small, partial]
    input_grads, b_gradient, c_gradient, step_grads = call(
        outputs_kernel,
        reach,
        [("h", ((1, rows, columns), BF16))]
        + [v((1, width, rows), BF16)] * 2
        + [v((1, heads, rows))],
        [("v", a) for side in zip(*joined) for a in side]
        + [("v", a) for a in (ends, xs, ys)]
        + [in_hbm(v_wide), in_hbm(dx)]
        + [("v", a) for a in (b_end, c_live, masks, db, dc, sums, alog, dt)],
        2 * 10**9,
        12 * 2**20,
        [
            stage,
            stage,
            pltpu.VMEM((rows, columns), BF16),
            pltpu.SemaphoreType.DMA((2, blocks)),
            pltpu.SemaphoreType.DMA((blocks,)),
        ],
    )
    gathered = lax.all_to_all(partial, ("ctx", "dp"), 0, 0, tiled=True)
    totals = jnp.sum(gathered, axis=0)
    return (
        input_grads,
        jnp.swapaxes(b_gradient, 1, 2),
        jnp.swapaxes(c_gradient, 1, 2),
        step_grads,
        totals[:heads],
        totals[heads : 2 * heads],
    )


def solution(mesh):
    in_specs = (
        P("dp", "ctx", None),
        P("dp", "ctx", None),
        P("dp", "ctx", None),
        P("dp", None, "ctx"),
        P(),
        P(),
        P("dp", None),
        P("dp", "ctx", None),
    )
    out_specs = (
        P("dp", "ctx", None),
        P("dp", "ctx", None),
        P("dp", "ctx", None),
        P("dp", None, "ctx"),
        P(),
        P(),
    )
    return jax.shard_map(
        per_device, mesh=mesh, in_specs=in_specs, out_specs=out_specs, check_vma=False
    )
```

```python
import functools

import jax
import jax.numpy as jnp
from jax import lax
from jax.experimental import pallas as pl
from jax.experimental.pallas import tpu as pltpu
from jax.sharding import PartitionSpec as P

F32 = jnp.float32
BF16 = jnp.bfloat16
LANES = 128
WIDE = 256
PARTS = WIDE // LANES
FAR = 2**30
PIECES = 2


def dot(a, b, ca, cb):
    return lax.dot_general(a, b, (((ca,), (cb,)), ((), ())), preferred_element_type=F32)


def iota(shape, dim):
    return lax.broadcasted_iota(jnp.int32, shape, dim)


def split2(a):
    high = a.astype(BF16)
    return high, (a - high.astype(F32)).astype(BF16)


def split3(a):
    high = a.astype(BF16)
    rest = a - high.astype(F32)
    middle = rest.astype(BF16)
    return high, middle, (rest - middle.astype(F32)).astype(BF16)


def dot_pairs(a, b, ca, cb):
    return dot(a[0], b[0], ca, cb) + (dot(a[0], b[1], ca, cb) + dot(a[1], b[0], ca, cb))


def stack(parts, axis):
    return jnp.concatenate(parts, axis=axis)


def document_places(lens_ref, rows):
    offset = shard() * rows
    starts = [jnp.int32(0)]
    for d in range(lens_ref.shape[1] - 1):
        starts.append(starts[-1] + lens_ref[0, d])
    first = jnp.int32(FAR)
    last = jnp.int32(0)
    for start in starts:
        first = jnp.minimum(first, jnp.where(start >= offset, start, FAR))
        last = jnp.maximum(last, jnp.where(start < offset + rows, start, 0))
    return starts, offset, first, last


def rate_column(alog_ref):
    heads = alog_ref.shape[1]
    square = jnp.broadcast_to(alog_ref[...], (heads, heads))
    picked = jnp.where(iota((heads, heads), 0) == iota((heads, heads), 1), square, 0.0)
    return -jnp.exp(jnp.sum(picked, axis=1, keepdims=True))


def log2(size):
    assert size & (size - 1) == 0
    return size.bit_length() - 1


def head_distance(heads, head_width):
    shape = (3 * heads, WIDE)
    return (iota(shape, 0) & (heads - 1)) - lax.shift_right_logical(
        iota(shape, 1), log2(head_width)
    )


def head_rows(distance, head_width, block):
    return jnp.where(distance == block * (WIDE // head_width), 1.0, 0.0).astype(BF16)


def head_columns(heads, head_width, block):
    shape = (WIDE, heads)
    column = lax.shift_right_logical(iota(shape, 0), log2(head_width))
    return jnp.where(iota(shape, 1) - column == block * (WIDE // head_width), 1.0, 0.0).astype(BF16)


def shard():
    return lax.axis_index("ctx")


def message_block(ref, block, width):
    at = block * PARTS
    return stack([ref[(at + i) * width : (at + i + 1) * width, :] for i in range(PARTS)], 1)


def message_tail(ref, block, width):
    tail = ref.shape[0] // (width + 1) * width + block * PARTS
    return stack([ref[tail + i : tail + i + 1, :] for i in range(PARTS)], 1)


def message_plan(reach, only=None):
    near = [(1, 0, 0)]
    relayed = [(1, 1, 0), (1, 1, 1)]
    far = [(2, 1, 0), (2, 1, 1), (2, 0, 0)] if reach > 1 else []
    rest = [(j, *one) for j in range(3, reach + 1) for one in ((0, 0), (1, 0), (1, 1))]
    plan = near + far + relayed + rest
    return [one for one in plan if only is None or not one[1] or one[2] == only]


def received(messages, reach, block, blocks, width):
    came = pull = None
    half, inner = divmod(block, blocks // 2)
    for j in range(reach, 0, -1):
        one, two = messages[j, 0, 0], messages[j, 1, half]
        a, b = message_block(one, block, width), message_block(two, inner, width)
        first = jnp.broadcast_to(lax.rem(shard() + j, 2), a.shape) == 0
        near_came, near_pull = jnp.where(first, a, b), jnp.where(first, b, a)
        if came is None:
            came, pull = near_came, near_pull
        else:
            a, b = message_tail(one, block, width), message_tail(two, inner, width)
            first = jnp.broadcast_to(lax.rem(shard() + j, 2), a.shape) == 0
            came = near_came + jnp.where(first, a, b) * came
            pull = near_pull + jnp.where(first, b, a) * pull
    return came, pull


def states_kernel(
    lens_hbm,
    alog_hbm,
    skip_hbm,
    dt_hbm,
    x_hbm,
    b_hbm,
    dy_hbm,
    c_hbm,
    alog_ref,
    skip_ref,
    dt_ref,
    x_ref,
    b_ref,
    dy_ref,
    c_ref,
    one_ref,
    two_ref,
    three_ref,
    lens_ref,
    small_sems,
    sems,
):
    rows, columns = x_ref.shape
    heads, width = dt_ref.shape[0], b_ref.shape[0]
    head_width = columns // heads
    piece = columns // PIECES
    small = [
        pltpu.make_async_copy(source, target, small_sems.at[i])
        for i, (source, target) in enumerate(
            (
                (dt_hbm.at[0], dt_ref),
                (alog_hbm, alog_ref),
                (lens_hbm, lens_ref),
                (b_hbm.at[0], b_ref),
                (c_hbm.at[0], c_ref),
                (skip_hbm, skip_ref),
            )
        )
    ]
    for copy in small[:-1]:
        copy.start()
    large = []
    for i in range(PIECES):
        at = slice(i * piece, (i + 1) * piece)
        for side, (source, target) in enumerate(((x_hbm, x_ref), (dy_hbm, dy_ref))):
            copy = pltpu.make_async_copy(
                source.at[0, :, at], target.at[:, at], sems.at[side, i]
            )
            copy.start()
            large.append(copy)
    small[-1].start()
    square = (rows, rows)
    upper = jnp.where(iota(square, 0) <= iota(square, 1), 1.0, 0.0).astype(BF16)
    even = jnp.broadcast_to(lax.rem(shard(), 2), (width, LANES)) == 0
    left = iota((1, LANES), 1) < head_width
    for copy in small[:-1]:
        copy.wait()
    _, offset, first, last = document_places(lens_ref, rows)
    through = jnp.where(first >= offset + rows, 1.0, 0.0)
    dt = dt_ref[...]
    logs = sum(dot(part, upper, 1, 0) for part in split3(dt * rate_column(alog_ref)))
    end_log = logs[:, rows - 1 : rows]
    place = iota((heads, rows), 1) + offset
    keeping = jnp.where(place >= last, jnp.exp(end_log - logs) * dt, 0.0)
    carried = jnp.where(place < first, jnp.exp(logs), 0.0)
    kept = jnp.broadcast_to(jnp.exp(end_log) * through, (heads, LANES))
    b, c = b_ref[...].astype(F32), c_ref[...].astype(F32)
    own = LANES // head_width

    def block_states(vectors, weights, values):
        rows_in = [stack(split2(vectors * weights[h : h + 1, :]), 1) for h in range(PARTS * own)]
        out = dot(stack(rows_in, 0), stack([values, values], 0), 1, 0)
        pairs = []
        for i in range(PARTS):
            lanes = slice(i * LANES, (i + 1) * LANES)
            sides = [
                out[h * width : (h + 1) * width, lanes] for h in range(i * own, (i + 1) * own)
            ]
            pairs.append(jnp.where(left, sides[0], sides[1]))
        return pairs

    pairs = columns // LANES
    for block in range(columns // WIDE):
        if block * WIDE % piece == 0:
            large[block * WIDE // piece * 2].wait()
            large[block * WIDE // piece * 2 + 1].wait()
        at = slice(block * WIDE, (block + 1) * WIDE)
        here = slice(block * PARTS * own, (block + 1) * PARTS * own)
        states = block_states(b, keeping[here], x_ref[:, at])
        pulls = block_states(c, carried[here], dy_ref[:, at])
        for i in range(PARTS):
            pair = block * PARTS + i
            kept_row = jnp.where(left, kept[pair * own : pair * own + 1], kept[pair * own + 1 :][:1])
            first = jnp.where(even, states[i], pulls[i])
            second = jnp.where(even, pulls[i], states[i])
            half, inner = divmod(pair, pairs // 2)
            for ref, place_in, whole, value in (
                (one_ref, pair, pairs, first),
                ((two_ref, three_ref)[half], inner, pairs // 2, second),
            ):
                ref[place_in * width : (place_in + 1) * width, :] = value
                ref[whole * width + place_in : whole * width + place_in + 1, :] = kept_row
    small[-1].wait()


def inside_kernel(
    lens_hbm,
    alog_ref,
    skip_ref,
    dt_ref,
    x_ref,
    b_ref,
    dy_ref,
    c_ref,
    _,
    xs_ref,
    ys_ref,
    v_wide_hbm,
    dx_hbm,
    b_end_ref,
    c_live_ref,
    masks_ref,
    db_ref,
    dc_ref,
    sums_ref,
    fwd_ref,
    bwd_ref,
    ends_ref,
    small_ref,
    v_stage,
    dx_stage,
    lens_ref,
    lens_sem,
    sems,
):
    rows, columns = x_ref.shape
    heads, width = dt_ref.shape[0], b_ref.shape[0]
    head_width = columns // heads
    lens_copy = pltpu.make_async_copy(lens_hbm, lens_ref, lens_sem)
    lens_copy.start()
    distance = head_distance(heads, head_width)
    bt, ct = b_ref[...], c_ref[...]
    raw_scores, raw_flipped = dot(ct, bt, 0, 0), dot(bt, ct, 0, 0)
    lens_copy.wait()
    starts, offset, first, last = document_places(lens_ref, rows)
    through = jnp.where(first >= offset + rows, 1.0, 0.0)
    square = (rows, rows)
    place0, place1 = iota(square, 0) + offset, iota(square, 1) + offset
    segment0, segment1 = jnp.zeros(square, jnp.int32), jnp.zeros(square, jnp.int32)
    for start in starts:
        segment0 += jnp.where(place0 >= start, 1, 0)
        segment1 += jnp.where(place1 >= start, 1, 0)
    same = segment0 == segment1
    down = same & (place0 >= place1)
    lower = jnp.where(place0 >= place1, 1.0, 0.0).astype(BF16)
    eye = jnp.where(place0 == place1, 1.0, 0.0).astype(BF16)
    dt = dt_ref[...]
    logs = sum(dot(lower, part, 1, 1) for part in split3(dt * rate_column(alog_ref)))
    steps = sum(dot(eye, part, 1, 1) for part in split3(dt))
    scores = split2(jnp.where(down, raw_scores, 0.0))
    flipped = split2(jnp.where(same & (place1 >= place0), raw_flipped, 0.0))
    place = iota((width, rows), 1) + offset
    bt_end = jnp.where(place >= last, bt.astype(F32), 0.0)
    ct_live = jnp.where(place < first, ct.astype(F32), 0.0)
    b_end, c_live = jnp.transpose(bt_end).astype(BF16), jnp.transpose(ct_live).astype(BF16)
    bt_end, ct_live = bt_end.astype(BF16), ct_live.astype(BF16)
    b_end_ref[...] = stack([b_end, b_end], 1)
    c_live_ref[...] = stack([c_live, c_live], 1)
    bt_end, ct_live = stack([bt_end, bt_end], 1), stack([ct_live, ct_live], 1)
    masks_ref[0:1] = jnp.where(place[:1] >= last, 1.0, 0.0)
    masks_ref[1:2] = jnp.where(place[:1] < first, 1.0, 0.0)
    tables = stack(
        [
            stack(split3(a), 1)
            for a in (
                jnp.exp(logs),
                jnp.exp(-logs) * steps,
                logs,
                jnp.broadcast_to(skip_ref[...], (16, heads)),
            )
        ],
        0,
    )
    d_scores = jnp.zeros((2 * rows, 2 * rows), F32)
    sums = jnp.zeros((2 * rows + 16, heads), F32)
    copies = []
    for block in range(columns // WIDE):
        at = slice(block * WIDE, (block + 1) * WIDE)
        wide = dot(tables, head_rows(distance, head_width, block), 1, 0)
        ones = head_columns(heads, head_width, block)
        u_wide, v_wide, l_wide = wide[:rows], wide[rows : 2 * rows], wide[2 * rows : 3 * rows]
        skip_wide = wide[3 * rows : 3 * rows + 1]
        x = x_ref[:, at].astype(F32)
        dy = dy_ref[:, at].astype(F32)
        xv = x * v_wide
        yu = dy * u_wide
        xs, ys = split2(xv), split2(yu)
        xs_ref[:, at] = stack(xs, 0)
        ys_ref[:, at] = stack(ys, 0)
        v_stage[:, at] = v_wide
        out = dot_pairs(scores, xs, 1, 0)
        back = dot_pairs(flipped, ys, 1, 0)
        d_scores += dot(stack(ys, 0), stack(xs, 0), 1, 1)
        dx_stage[:, at] = v_wide * back + skip_wide * dy
        for i, (stage, target) in enumerate(((v_stage, v_wide_hbm), (dx_stage, dx_hbm))):
            copy = pltpu.make_async_copy(stage.at[:, at], target.at[:, at], sems.at[i, block])
            copy.start()
            copies.append(copy)
        column_part = xv * back
        product = jnp.broadcast_to(jnp.sum(x * dy, axis=0, keepdims=True), (16, WIDE))
        for part in split3(stack([yu * out - column_part, column_part, product], 0)):
            sums += dot(part, ones, 1, 0)
        ending = u_wide[rows - 1 : rows]
        end_log = l_wide[rows - 1 : rows]
        gap = end_log - l_wide
        fwd_ref[:, at] = dot(bt_end, stack(split2(xv * gap), 0), 1, 0) * ending
        bwd_ref[:, at] = dot(ct_live, stack(split2(yu * l_wide), 0), 1, 0)
        ends_ref[0:1, at] = ending
        ends_ref[1:2, at] = ending * through
        ends_ref[2:3, at] = ending * through * end_log
    d_scores = (d_scores[:rows, :rows] + d_scores[:rows, rows:]) + d_scores[rows:, :rows]
    d_scores = split2(jnp.where(down, d_scores, 0.0))
    dc_ref[...] = sum(dot(bt, p, 1, 1) for p in d_scores)
    db_ref[...] = sum(dot(ct, p, 1, 0) for p in d_scores)
    sums_ref[...] = sums[: 2 * rows]
    rate_grads = jnp.sum(logs * sums[:rows], axis=0, keepdims=True)
    empty = jnp.zeros((1, LANES - 2 * heads), F32)
    small_ref[...] = stack([rate_grads, sums[2 * rows : 2 * rows + 1], empty], 1)
    for copy in copies:
        copy.wait()


def rates_kernel(reach, head_width, half, *refs):
    plan = message_plan(reach, half)
    messages = dict(zip(plan, refs))
    ends_ref, fwd_ref, bwd_ref, *refs = refs[len(plan) :]
    width, columns = fwd_ref.shape
    blocks = columns // WIDE
    own_blocks = blocks // 2
    came_ref, pull_ref, out_ref = refs[-3:]
    whole = []
    for i in range(own_blocks):
        block = half * own_blocks + i
        at = slice(block * WIDE, (block + 1) * WIDE)
        own = slice(i * WIDE, (i + 1) * WIDE)
        came, pull = received(messages, reach, block, blocks, width)
        came_ref[:, own] = came
        pull_ref[:, own] = pull
        terms = came * bwd_ref[:, at] + pull * (fwd_ref[:, at] + ends_ref[2:3, at] * came)
        whole.append(jnp.sum(terms, axis=0, keepdims=True))
    if not half:
        out_ref[...] = stack(whole, 0)
        return
    small_ref, first_ref = refs[:2]
    own = WIDE // head_width
    shape = (WIDE, LANES)
    column = lax.shift_right_logical(iota(shape, 0), log2(head_width))
    ones = jnp.where(column == (iota(shape, 1) & (own - 1)), 1.0, 0.0).astype(BF16)
    sums = dot(stack(split3(stack([first_ref[...], *whole], 0)), 0), ones, 1, 0)
    sums = (sums[:blocks] + sums[blocks : 2 * blocks]) + sums[2 * blocks :]
    lane = iota(sums.shape, 1)
    mine = lax.shift_right_logical(lane, log2(own)) == iota(sums.shape, 0)
    total = small_ref[...] + jnp.sum(jnp.where(mine, sums, 0.0), axis=0, keepdims=True)
    out_ref[...] = jnp.broadcast_to(total, out_ref.shape)


def outputs_kernel(
    came_one,
    came_two,
    pull_one,
    pull_two,
    ends_ref,
    xs_ref,
    ys_ref,
    v_wide_hbm,
    dx_hbm,
    b_end_ref,
    c_live_ref,
    masks_ref,
    db_ref,
    dc_ref,
    sums_ref,
    alog_ref,
    dt_ref,
    dx_out,
    db_out,
    dc_out,
    dt_out,
    v_stage,
    dx_stage,
    stage,
    in_sems,
    out_sems,
):
    rows, columns = dx_hbm.shape
    heads, width = dt_ref.shape[0], db_ref.shape[0]
    blocks = columns // WIDE
    copies = []
    for block in range(blocks):
        at = slice(block * WIDE, (block + 1) * WIDE)
        for i, (source, target) in enumerate(((v_wide_hbm, v_stage), (dx_hbm, dx_stage))):
            copy = pltpu.make_async_copy(
                source.at[:, at], target.at[:, at], in_sems.at[i, block]
            )
            copy.start()
            copies.append(copy)
    b_end, c_live = b_end_ref[...], c_live_ref[...]
    own_sums = sums_ref[...]
    sums = own_sums
    dc = jnp.zeros((2 * width, 2 * rows), F32)
    db = jnp.zeros((2 * width, 2 * rows), F32)
    at_last = iota((rows, WIDE), 0) == rows - 1
    sent = []
    for block in range(blocks):
        at = slice(block * WIDE, (block + 1) * WIDE)
        ones = head_columns(heads, columns // heads, block)
        half, inner = divmod(block, blocks // 2)
        own = slice(inner * WIDE, (inner + 1) * WIDE)
        came, pull = (came_one, came_two)[half][:, own], (pull_one, pull_two)[half][:, own]
        meet = jnp.sum(came * pull, axis=0, keepdims=True) * ends_ref[1:2, at]
        cames = stack(split2(came), 0)
        pulls = stack(split2(pull * ends_ref[0:1, at]), 0)
        xs, ys = xs_ref[:, at], ys_ref[:, at]
        out = dot(c_live, cames, 1, 0)
        back = dot(b_end, pulls, 1, 0)
        column_part = (xs[:rows].astype(F32) + xs[rows:].astype(F32)) * back
        row_part = (ys[:rows].astype(F32) + ys[rows:].astype(F32)) * out
        row_part = jnp.where(at_last, row_part + meet, row_part)
        for part in split2(stack([row_part - column_part, column_part], 0)):
            sums += dot(part, ones, 1, 0)
        dc += dot(cames, ys, 1, 1)
        db += dot(pulls, xs, 1, 1)
        copies[2 * block].wait()
        copies[2 * block + 1].wait()
        stage[:, at] = (dx_stage[:, at] + v_stage[:, at] * back).astype(BF16)
        copy = pltpu.make_async_copy(stage.at[:, at], dx_out.at[0, :, at], out_sems.at[block])
        copy.start()
        sent.append(copy)
    dc = (dc[:width, :rows] + dc[:width, rows:]) + dc[width:, :rows]
    db = (db[:width, :rows] + db[:width, rows:]) + db[width:, :rows]
    db_out[0] = (db_ref[...] + masks_ref[0:1] * db).astype(BF16)
    dc_out[0] = (dc_ref[...] + masks_ref[1:2] * dc).astype(BF16)
    square = (rows, rows)
    upper = jnp.where(iota(square, 0) >= iota(square, 1), 1.0, 0.0).astype(BF16)
    eye = jnp.where(iota(square, 0) == iota(square, 1), 1.0, 0.0).astype(BF16)
    at_end = jnp.sum(sums[rows:] - own_sums[rows:], axis=0, keepdims=True)
    dl = sums[:rows] + jnp.where(iota((rows, heads), 0) == rows - 1, at_end, 0.0)
    d_decay = sum(dot(part, upper, 0, 0) for part in split3(dl))
    total = sum(dot(part, eye, 0, 0) for part in split3(sums[rows:]))
    dt_out[0] = total / dt_ref[...] + rate_column(alog_ref) * d_decay
    for copy in sent:
        copy.wait()


def call(kernel, reach, outs, ins, flops, moved, scratch=()):
    spaces = {"s": pltpu.SMEM, "v": pltpu.VMEM, "h": pltpu.HBM, "any": pl.ANY}
    return pl.pallas_call(
        kernel,
        out_shape=[
            pltpu.HBM(*out) if place == "h" else jax.ShapeDtypeStruct(*out) for place, out in outs
        ],
        in_specs=[pl.BlockSpec(memory_space=spaces[place]) for place, _ in ins],
        out_specs=[pl.BlockSpec(memory_space=spaces[place]) for place, _ in outs],
        scratch_shapes=scratch,
        compiler_params=pltpu.CompilerParams(vmem_limit_bytes=min(16 + 2 * reach, 56) * 2**20),
        cost_estimate=pl.CostEstimate(flops=flops, bytes_accessed=moved, transcendentals=0),
    )(*(a for _, a in ins))


def send(a, by, second):
    count = lax.axis_size("ctx")
    pairs = [(i, i + by if (i + second) % 2 == 0 else i - by) for i in range(count)]
    return lax.ppermute(a, "ctx", [(i, j) for i, j in pairs if 0 <= j < count])


def hand_on(a):
    count = lax.axis_size("ctx")
    return lax.ppermute(a, "ctx", [(i, i ^ 1) for i in range(count) if i not in (1, count - 2)])


def in_hbm(a):
    return "h", pltpu.with_memory_space_constraint(a, pltpu.HBM)


def per_device(inputs, b_proj, c_proj, step_sizes, a_log, skip_gain, doc_lengths, grad_out):
    rows, columns = inputs.shape[1:]
    heads, width = a_log.shape[0], b_proj.shape[2]
    reach = max(lax.axis_size("ctx") // 4, 1)
    devices = lax.axis_size("ctx") * lax.axis_size("dp")
    alog, skip = a_log[None], skip_gain[None]
    bt, ct = jnp.swapaxes(b_proj, 1, 2), jnp.swapaxes(c_proj, 1, 2)
    blocks = columns // WIDE

    def v(shape, kind=F32):
        return "v", (shape, kind)

    alog, skip, dt, x, b, dy, c, *payloads = call(
        states_kernel,
        reach,
        [
            v(alog.shape),
            v(skip.shape),
            v((heads, rows)),
            v((rows, columns), BF16),
            v((width, rows), BF16),
            v((rows, columns), BF16),
            v((width, rows), BF16),
        ]
        + [v((columns // LANES * (width + 1) // part, LANES)) for part in (1, 2, 2)],
        [in_hbm(a) for a in (doc_lengths, alog, skip, step_sizes, inputs, bt, grad_out, ct)],
        10**9,
        4 * 2**20,
        [
            pltpu.SMEM(doc_lengths.shape, jnp.int32),
            pltpu.SemaphoreType.DMA((6,)),
            pltpu.SemaphoreType.DMA((2, PIECES)),
        ],
    )
    messages = {}
    for j, second, half in message_plan(reach):
        if (j, second) == (1, 1) and reach > 1:
            continue
        payload = payloads[1 + half if second else 0]
        messages[j, second, half] = send(payload, j, second)
    if reach > 1:
        for half in (0, 1):
            messages[1, 1, half] = hand_on(messages[2, 1, half])
    whole = "h", ((rows, columns), F32)
    state = v((width, columns))
    stage = pltpu.VMEM((rows, columns), F32)
    transposed = v((width, rows))
    xs, ys, v_wide, dx, b_end, c_live, masks, db, dc, sums, fwd_logs, bwd_logs, ends, small = call(
        inside_kernel,
        reach,
        [v((2 * rows, columns), BF16)] * 2
        + [whole] * 2
        + [v((rows, 2 * width), BF16)] * 2
        + [v((8, rows)), transposed, transposed, v((2 * rows, heads))]
        + [state, state, v((8, columns)), v((1, LANES))],
        [in_hbm(doc_lengths)]
        + [("v", a) for a in (alog, skip, dt, x, b, dy, c)]
        + [("any", messages[1, 0, 0])],
        4 * 10**9,
        12 * 2**20,
        [
            stage,
            stage,
            pltpu.SMEM(doc_lengths.shape, jnp.int32),
            pltpu.SemaphoreType.DMA,
            pltpu.SemaphoreType.DMA((2, blocks)),
        ],
    )
    half_state = v((width, columns // 2))
    joined, last = [], []
    for half in (0, 1):
        out = v((devices, LANES)) if half else v((blocks // 2, WIDE))
        came, pull, partial = call(
            functools.partial(rates_kernel, reach, columns // heads, half),
            reach,
            [half_state, half_state, out],
            [("v", messages[one]) for one in message_plan(reach, half)]
            + [("v", a) for a in (ends, fwd_logs, bwd_logs, *last)],
            10**8,
            4 * 2**20,
        )
        joined.append((came, pull))
        last = [small, partial]
    input_grads, b_gradient, c_gradient, step_grads = call(
        outputs_kernel,
        reach,
        [("h", ((1, rows, columns), BF16))]
        + [v((1, width, rows), BF16)] * 2
        + [v((1, heads, rows))],
        [("v", a) for side in zip(*joined) for a in side]
        + [("v", a) for a in (ends, xs, ys)]
        + [in_hbm(v_wide), in_hbm(dx)]
        + [("v", a) for a in (b_end, c_live, masks, db, dc, sums, alog, dt)],
        2 * 10**9,
        12 * 2**20,
        [
            stage,
            stage,
            pltpu.VMEM((rows, columns), BF16),
            pltpu.SemaphoreType.DMA((2, blocks)),
            pltpu.SemaphoreType.DMA((blocks,)),
        ],
    )
    gathered = lax.all_to_all(partial, ("ctx", "dp"), 0, 0, tiled=True)
    totals = jnp.sum(gathered, axis=0)
    return (
        input_grads,
        jnp.swapaxes(b_gradient, 1, 2),
        jnp.swapaxes(c_gradient, 1, 2),
        step_grads,
        totals[:heads],
        totals[heads : 2 * heads],
    )


def solution(mesh):
    in_specs = (
        P("dp", "ctx", None),
        P("dp", "ctx", None),
        P("dp", "ctx", None),
        P("dp", None, "ctx"),
        P(),
        P(),
        P("dp", None),
        P("dp", "ctx", None),
    )
    out_specs = (
        P("dp", "ctx", None),
        P("dp", "ctx", None),
        P("dp", "ctx", None),
        P("dp", None, "ctx"),
        P(),
        P(),
    )
    return jax.shard_map(
        per_device, mesh=mesh, in_specs=in_specs, out_specs=out_specs, check_vma=False
    )
```

```python
import functools

import jax
import jax.numpy as jnp
from jax import lax
from jax.experimental import pallas as pl
from jax.experimental.pallas import tpu as pltpu
from jax.sharding import PartitionSpec as P

F32 = jnp.float32
BF16 = jnp.bfloat16
LANES = 128
WIDE = 256
PARTS = WIDE // LANES
FAR = 2**30
PIECES = 2


def dot(a, b, ca, cb):
    return lax.dot_general(a, b, (((ca,), (cb,)), ((), ())), preferred_element_type=F32)


def iota(shape, dim):
    return lax.broadcasted_iota(jnp.int32, shape, dim)


def split2(a):
    high = a.astype(BF16)
    return high, (a - high.astype(F32)).astype(BF16)


def split3(a):
    high = a.astype(BF16)
    rest = a - high.astype(F32)
    middle = rest.astype(BF16)
    return high, middle, (rest - middle.astype(F32)).astype(BF16)


def dot_pairs(a, b, ca, cb):
    return dot(a[0], b[0], ca, cb) + (dot(a[0], b[1], ca, cb) + dot(a[1], b[0], ca, cb))


def stack(parts, axis):
    return jnp.concatenate(parts, axis=axis)


def document_places(lens_ref, rows):
    offset = shard() * rows
    starts = [jnp.int32(0)]
    for d in range(lens_ref.shape[1] - 1):
        starts.append(starts[-1] + lens_ref[0, d])
    first = jnp.int32(FAR)
    last = jnp.int32(0)
    for start in starts:
        first = jnp.minimum(first, jnp.where(start >= offset, start, FAR))
        last = jnp.maximum(last, jnp.where(start < offset + rows, start, 0))
    return starts, offset, first, last


def rate_column(alog_ref):
    heads = alog_ref.shape[1]
    square = jnp.broadcast_to(alog_ref[...], (heads, heads))
    picked = jnp.where(iota((heads, heads), 0) == iota((heads, heads), 1), square, 0.0)
    return -jnp.exp(jnp.sum(picked, axis=1, keepdims=True))


def log2(size):
    assert size & (size - 1) == 0
    return size.bit_length() - 1


def head_distance(heads, head_width):
    shape = (3 * heads, WIDE)
    return (iota(shape, 0) & (heads - 1)) - lax.shift_right_logical(
        iota(shape, 1), log2(head_width)
    )


def head_rows(distance, head_width, block):
    return jnp.where(distance == block * (WIDE // head_width), 1.0, 0.0).astype(BF16)


def head_columns(heads, head_width, block):
    shape = (WIDE, heads)
    column = lax.shift_right_logical(iota(shape, 0), log2(head_width))
    return jnp.where(iota(shape, 1) - column == block * (WIDE // head_width), 1.0, 0.0).astype(BF16)


def shard():
    return lax.axis_index("ctx")


def message_block(ref, block, width):
    at = block * PARTS
    return stack([ref[(at + i) * width : (at + i + 1) * width, :] for i in range(PARTS)], 1)


def message_tail(ref, block, width):
    tail = ref.shape[0] // (width + 1) * width + block * PARTS
    return stack([ref[tail + i : tail + i + 1, :] for i in range(PARTS)], 1)


def message_plan(reach, only=None):
    near = [(1, 0, 0)]
    relayed = [(1, 1, 0), (1, 1, 1)]
    far = [(2, 1, 0), (2, 1, 1), (2, 0, 0)] if reach > 1 else []
    rest = [(j, *one) for j in range(3, reach + 1) for one in ((0, 0), (1, 0), (1, 1))]
    plan = near + far + relayed + rest
    return [one for one in plan if only is None or not one[1] or one[2] == only]


def received(messages, reach, block, blocks, width):
    came = pull = None
    half, inner = divmod(block, blocks // 2)
    for j in range(reach, 0, -1):
        one, two = messages[j, 0, 0], messages[j, 1, half]
        a, b = message_block(one, block, width), message_block(two, inner, width)
        first = jnp.broadcast_to(lax.rem(shard() + j, 2), a.shape) == 0
        near_came, near_pull = jnp.where(first, a, b), jnp.where(first, b, a)
        if came is None:
            came, pull = near_came, near_pull
        else:
            a, b = message_tail(one, block, width), message_tail(two, inner, width)
            first = jnp.broadcast_to(lax.rem(shard() + j, 2), a.shape) == 0
            came = near_came + jnp.where(first, a, b) * came
            pull = near_pull + jnp.where(first, b, a) * pull
    return came, pull


def states_kernel(
    lens_hbm,
    alog_hbm,
    dt_hbm,
    x_hbm,
    b_hbm,
    dy_hbm,
    c_hbm,
    alog_ref,
    dt_ref,
    x_ref,
    b_ref,
    dy_ref,
    c_ref,
    one_ref,
    two_ref,
    three_ref,
    lens_ref,
    small_sems,
    sems,
):
    rows, columns = x_ref.shape
    heads, width = dt_ref.shape[0], b_ref.shape[0]
    head_width = columns // heads
    piece = columns // PIECES
    small = [
        pltpu.make_async_copy(source, target, small_sems.at[i])
        for i, (source, target) in enumerate(
            (
                (dt_hbm.at[0], dt_ref),
                (alog_hbm, alog_ref),
                (lens_hbm, lens_ref),
                (b_hbm.at[0], b_ref),
                (c_hbm.at[0], c_ref),
            )
        )
    ]
    for copy in small:
        copy.start()
    large = []
    for i in range(PIECES):
        at = slice(i * piece, (i + 1) * piece)
        for side, (source, target) in enumerate(((x_hbm, x_ref), (dy_hbm, dy_ref))):
            copy = pltpu.make_async_copy(
                source.at[0, :, at], target.at[:, at], sems.at[side, i]
            )
            copy.start()
            large.append(copy)
    square = (rows, rows)
    upper = jnp.where(iota(square, 0) <= iota(square, 1), 1.0, 0.0).astype(BF16)
    even = jnp.broadcast_to(lax.rem(shard(), 2), (width, LANES)) == 0
    left = iota((1, LANES), 1) < head_width
    for copy in small:
        copy.wait()
    _, offset, first, last = document_places(lens_ref, rows)
    through = jnp.where(first >= offset + rows, 1.0, 0.0)
    dt = dt_ref[...]
    logs = sum(dot(part, upper, 1, 0) for part in split3(dt * rate_column(alog_ref)))
    end_log = logs[:, rows - 1 : rows]
    place = iota((heads, rows), 1) + offset
    keeping = jnp.where(place >= last, jnp.exp(end_log - logs) * dt, 0.0)
    carried = jnp.where(place < first, jnp.exp(logs), 0.0)
    kept = jnp.broadcast_to(jnp.exp(end_log) * through, (heads, LANES))
    b, c = b_ref[...].astype(F32), c_ref[...].astype(F32)
    own = LANES // head_width

    def block_states(vectors, weights, values):
        rows_in = [stack(split2(vectors * weights[h : h + 1, :]), 1) for h in range(PARTS * own)]
        out = dot(stack(rows_in, 0), stack([values, values], 0), 1, 0)
        pairs = []
        for i in range(PARTS):
            lanes = slice(i * LANES, (i + 1) * LANES)
            sides = [
                out[h * width : (h + 1) * width, lanes] for h in range(i * own, (i + 1) * own)
            ]
            pairs.append(jnp.where(left, sides[0], sides[1]))
        return pairs

    pairs = columns // LANES
    for block in range(columns // WIDE):
        if block * WIDE % piece == 0:
            large[block * WIDE // piece * 2].wait()
            large[block * WIDE // piece * 2 + 1].wait()
        at = slice(block * WIDE, (block + 1) * WIDE)
        here = slice(block * PARTS * own, (block + 1) * PARTS * own)
        states = block_states(b, keeping[here], x_ref[:, at])
        pulls = block_states(c, carried[here], dy_ref[:, at])
        for i in range(PARTS):
            pair = block * PARTS + i
            kept_row = jnp.where(left, kept[pair * own : pair * own + 1], kept[pair * own + 1 :][:1])
            first = jnp.where(even, states[i], pulls[i])
            second = jnp.where(even, pulls[i], states[i])
            half, inner = divmod(pair, pairs // 2)
            for ref, place_in, whole, value in (
                (one_ref, pair, pairs, first),
                ((two_ref, three_ref)[half], inner, pairs // 2, second),
            ):
                ref[place_in * width : (place_in + 1) * width, :] = value
                ref[whole * width + place_in : whole * width + place_in + 1, :] = kept_row


def inside_kernel(
    lens_hbm,
    skip_hbm,
    alog_ref,
    dt_ref,
    x_ref,
    b_ref,
    dy_ref,
    c_ref,
    _,
    xs_ref,
    ys_ref,
    v_wide_hbm,
    dx_hbm,
    b_end_ref,
    c_live_ref,
    masks_ref,
    db_ref,
    dc_ref,
    sums_ref,
    fwd_ref,
    bwd_ref,
    ends_ref,
    small_ref,
    v_stage,
    dx_stage,
    lens_ref,
    skip_ref,
    lens_sem,
    skip_sem,
    sems,
):
    rows, columns = x_ref.shape
    heads, width = dt_ref.shape[0], b_ref.shape[0]
    head_width = columns // heads
    lens_copy = pltpu.make_async_copy(lens_hbm, lens_ref, lens_sem)
    skip_copy = pltpu.make_async_copy(skip_hbm, skip_ref, skip_sem)
    lens_copy.start()
    skip_copy.start()
    distance = head_distance(heads, head_width)
    bt, ct = b_ref[...], c_ref[...]
    raw_scores, raw_flipped = dot(ct, bt, 0, 0), dot(bt, ct, 0, 0)
    lens_copy.wait()
    skip_copy.wait()
    starts, offset, first, last = document_places(lens_ref, rows)
    through = jnp.where(first >= offset + rows, 1.0, 0.0)
    square = (rows, rows)
    place0, place1 = iota(square, 0) + offset, iota(square, 1) + offset
    segment0, segment1 = jnp.zeros(square, jnp.int32), jnp.zeros(square, jnp.int32)
    for start in starts:
        segment0 += jnp.where(place0 >= start, 1, 0)
        segment1 += jnp.where(place1 >= start, 1, 0)
    same = segment0 == segment1
    down = same & (place0 >= place1)
    lower = jnp.where(place0 >= place1, 1.0, 0.0).astype(BF16)
    eye = jnp.where(place0 == place1, 1.0, 0.0).astype(BF16)
    dt = dt_ref[...]
    logs = sum(dot(lower, part, 1, 1) for part in split3(dt * rate_column(alog_ref)))
    steps = sum(dot(eye, part, 1, 1) for part in split3(dt))
    scores = split2(jnp.where(down, raw_scores, 0.0))
    flipped = split2(jnp.where(same & (place1 >= place0), raw_flipped, 0.0))
    place = iota((width, rows), 1) + offset
    bt_end = jnp.where(place >= last, bt.astype(F32), 0.0)
    ct_live = jnp.where(place < first, ct.astype(F32), 0.0)
    b_end, c_live = jnp.transpose(bt_end).astype(BF16), jnp.transpose(ct_live).astype(BF16)
    bt_end, ct_live = bt_end.astype(BF16), ct_live.astype(BF16)
    b_end_ref[...] = stack([b_end, b_end], 1)
    c_live_ref[...] = stack([c_live, c_live], 1)
    bt_end, ct_live = stack([bt_end, bt_end], 1), stack([ct_live, ct_live], 1)
    masks_ref[0:1] = jnp.where(place[:1] >= last, 1.0, 0.0)
    masks_ref[1:2] = jnp.where(place[:1] < first, 1.0, 0.0)
    tables = stack(
        [
            stack(split3(a), 1)
            for a in (
                jnp.exp(logs),
                jnp.exp(-logs) * steps,
                logs,
                jnp.broadcast_to(skip_ref[...], (16, heads)),
            )
        ],
        0,
    )
    d_scores = jnp.zeros((2 * rows, 2 * rows), F32)
    sums = jnp.zeros((2 * rows + 16, heads), F32)
    copies = []
    for block in range(columns // WIDE):
        at = slice(block * WIDE, (block + 1) * WIDE)
        wide = dot(tables, head_rows(distance, head_width, block), 1, 0)
        ones = head_columns(heads, head_width, block)
        u_wide, v_wide, l_wide = wide[:rows], wide[rows : 2 * rows], wide[2 * rows : 3 * rows]
        skip_wide = wide[3 * rows : 3 * rows + 1]
        x = x_ref[:, at].astype(F32)
        dy = dy_ref[:, at].astype(F32)
        xv = x * v_wide
        yu = dy * u_wide
        xs, ys = split2(xv), split2(yu)
        xs_ref[:, at] = stack(xs, 0)
        ys_ref[:, at] = stack(ys, 0)
        v_stage[:, at] = v_wide
        out = dot_pairs(scores, xs, 1, 0)
        back = dot_pairs(flipped, ys, 1, 0)
        d_scores += dot(stack(ys, 0), stack(xs, 0), 1, 1)
        dx_stage[:, at] = v_wide * back + skip_wide * dy
        if block % 2:
            both = slice((block - 1) * WIDE, (block + 1) * WIDE)
            for i, (stage, target) in enumerate(((v_stage, v_wide_hbm), (dx_stage, dx_hbm))):
                copy = pltpu.make_async_copy(
                    stage.at[:, both], target.at[:, both], sems.at[i, block]
                )
                copy.start()
                copies.append(copy)
        column_part = xv * back
        product = jnp.broadcast_to(jnp.sum(x * dy, axis=0, keepdims=True), (16, WIDE))
        for part in split3(stack([yu * out - column_part, column_part, product], 0)):
            sums += dot(part, ones, 1, 0)
        ending = u_wide[rows - 1 : rows]
        end_log = l_wide[rows - 1 : rows]
        gap = end_log - l_wide
        fwd_ref[:, at] = dot(bt_end, stack(split2(xv * gap), 0), 1, 0) * ending
        bwd_ref[:, at] = dot(ct_live, stack(split2(yu * l_wide), 0), 1, 0)
        ends_ref[0:1, at] = ending
        ends_ref[1:2, at] = ending * through
        ends_ref[2:3, at] = ending * through * end_log
    d_scores = (d_scores[:rows, :rows] + d_scores[:rows, rows:]) + d_scores[rows:, :rows]
    d_scores = split2(jnp.where(down, d_scores, 0.0))
    dc_ref[...] = sum(dot(bt, p, 1, 1) for p in d_scores)
    db_ref[...] = sum(dot(ct, p, 1, 0) for p in d_scores)
    sums_ref[...] = sums[: 2 * rows]
    rate_grads = jnp.sum(logs * sums[:rows], axis=0, keepdims=True)
    empty = jnp.zeros((1, LANES - 2 * heads), F32)
    small_ref[...] = stack([rate_grads, sums[2 * rows : 2 * rows + 1], empty], 1)
    for copy in copies:
        copy.wait()


def rates_kernel(reach, head_width, half, *refs):
    plan = message_plan(reach, half)
    messages = dict(zip(plan, refs))
    ends_ref, fwd_ref, bwd_ref, *refs = refs[len(plan) :]
    width, columns = fwd_ref.shape
    blocks = columns // WIDE
    own_blocks = blocks // 2
    came_ref, pull_ref, out_ref = refs[-3:]
    whole = []
    for i in range(own_blocks):
        block = half * own_blocks + i
        at = slice(block * WIDE, (block + 1) * WIDE)
        own = slice(i * WIDE, (i + 1) * WIDE)
        came, pull = received(messages, reach, block, blocks, width)
        came_ref[:, own] = came
        pull_ref[:, own] = pull
        terms = came * bwd_ref[:, at] + pull * (fwd_ref[:, at] + ends_ref[2:3, at] * came)
        whole.append(jnp.sum(terms, axis=0, keepdims=True))
    if not half:
        out_ref[...] = stack(whole, 0)
        return
    small_ref, first_ref = refs[:2]
    own = WIDE // head_width
    shape = (WIDE, LANES)
    column = lax.shift_right_logical(iota(shape, 0), log2(head_width))
    ones = jnp.where(column == (iota(shape, 1) & (own - 1)), 1.0, 0.0).astype(BF16)
    sums = dot(stack(split3(stack([first_ref[...], *whole], 0)), 0), ones, 1, 0)
    sums = (sums[:blocks] + sums[blocks : 2 * blocks]) + sums[2 * blocks :]
    lane = iota(sums.shape, 1)
    mine = lax.shift_right_logical(lane, log2(own)) == iota(sums.shape, 0)
    total = small_ref[...] + jnp.sum(jnp.where(mine, sums, 0.0), axis=0, keepdims=True)
    out_ref[...] = jnp.broadcast_to(total, out_ref.shape)


def outputs_kernel(
    came_one,
    came_two,
    pull_one,
    pull_two,
    ends_ref,
    xs_ref,
    ys_ref,
    v_wide_hbm,
    dx_hbm,
    b_end_ref,
    c_live_ref,
    masks_ref,
    db_ref,
    dc_ref,
    sums_ref,
    alog_ref,
    dt_ref,
    dx_out,
    db_out,
    dc_out,
    dt_out,
    v_stage,
    dx_stage,
    stage,
    in_sems,
    out_sems,
):
    rows, columns = dx_hbm.shape
    heads, width = dt_ref.shape[0], db_ref.shape[0]
    blocks = columns // WIDE
    copies = []
    for block in range(0, blocks, 2):
        at = slice(block * WIDE, (block + 2) * WIDE)
        for i, (source, target) in enumerate(((v_wide_hbm, v_stage), (dx_hbm, dx_stage))):
            copy = pltpu.make_async_copy(
                source.at[:, at], target.at[:, at], in_sems.at[i, block]
            )
            copy.start()
            copies.append(copy)
    b_end, c_live = b_end_ref[...], c_live_ref[...]
    own_sums = sums_ref[...]
    sums = own_sums
    dc = jnp.zeros((2 * width, 2 * rows), F32)
    db = jnp.zeros((2 * width, 2 * rows), F32)
    at_last = iota((rows, WIDE), 0) == rows - 1
    sent = []
    for block in range(blocks):
        at = slice(block * WIDE, (block + 1) * WIDE)
        ones = head_columns(heads, columns // heads, block)
        half, inner = divmod(block, blocks // 2)
        own = slice(inner * WIDE, (inner + 1) * WIDE)
        came, pull = (came_one, came_two)[half][:, own], (pull_one, pull_two)[half][:, own]
        meet = jnp.sum(came * pull, axis=0, keepdims=True) * ends_ref[1:2, at]
        cames = stack(split2(came), 0)
        pulls = stack(split2(pull * ends_ref[0:1, at]), 0)
        xs, ys = xs_ref[:, at], ys_ref[:, at]
        out = dot(c_live, cames, 1, 0)
        back = dot(b_end, pulls, 1, 0)
        column_part = (xs[:rows].astype(F32) + xs[rows:].astype(F32)) * back
        row_part = (ys[:rows].astype(F32) + ys[rows:].astype(F32)) * out
        row_part = jnp.where(at_last, row_part + meet, row_part)
        for part in split2(stack([row_part - column_part, column_part], 0)):
            sums += dot(part, ones, 1, 0)
        dc += dot(cames, ys, 1, 1)
        db += dot(pulls, xs, 1, 1)
        if block % 2 == 0:
            copies[block].wait()
            copies[block + 1].wait()
        stage[:, at] = (dx_stage[:, at] + v_stage[:, at] * back).astype(BF16)
        if block % 2:
            both = slice((block - 1) * WIDE, (block + 1) * WIDE)
            copy = pltpu.make_async_copy(
                stage.at[:, both], dx_out.at[0, :, both], out_sems.at[block]
            )
            copy.start()
            sent.append(copy)
    dc = (dc[:width, :rows] + dc[:width, rows:]) + dc[width:, :rows]
    db = (db[:width, :rows] + db[:width, rows:]) + db[width:, :rows]
    db_out[0] = (db_ref[...] + masks_ref[0:1] * db).astype(BF16)
    dc_out[0] = (dc_ref[...] + masks_ref[1:2] * dc).astype(BF16)
    square = (rows, rows)
    upper = jnp.where(iota(square, 0) >= iota(square, 1), 1.0, 0.0).astype(BF16)
    eye = jnp.where(iota(square, 0) == iota(square, 1), 1.0, 0.0).astype(BF16)
    at_end = jnp.sum(sums[rows:] - own_sums[rows:], axis=0, keepdims=True)
    dl = sums[:rows] + jnp.where(iota((rows, heads), 0) == rows - 1, at_end, 0.0)
    d_decay = sum(dot(part, upper, 0, 0) for part in split3(dl))
    total = sum(dot(part, eye, 0, 0) for part in split3(sums[rows:]))
    dt_out[0] = total / dt_ref[...] + rate_column(alog_ref) * d_decay
    for copy in sent:
        copy.wait()


def call(kernel, reach, outs, ins, flops, moved, scratch=()):
    spaces = {"s": pltpu.SMEM, "v": pltpu.VMEM, "h": pltpu.HBM, "any": pl.ANY}
    return pl.pallas_call(
        kernel,
        out_shape=[
            pltpu.HBM(*out) if place == "h" else jax.ShapeDtypeStruct(*out) for place, out in outs
        ],
        in_specs=[pl.BlockSpec(memory_space=spaces[place]) for place, _ in ins],
        out_specs=[pl.BlockSpec(memory_space=spaces[place]) for place, _ in outs],
        scratch_shapes=scratch,
        compiler_params=pltpu.CompilerParams(vmem_limit_bytes=min(16 + 2 * reach, 56) * 2**20),
        cost_estimate=pl.CostEstimate(flops=flops, bytes_accessed=moved, transcendentals=0),
    )(*(a for _, a in ins))


def send(a, by, second):
    count = lax.axis_size("ctx")
    pairs = [(i, i + by if (i + second) % 2 == 0 else i - by) for i in range(count)]
    return lax.ppermute(a, "ctx", [(i, j) for i, j in pairs if 0 <= j < count])


def hand_on(a):
    count = lax.axis_size("ctx")
    return lax.ppermute(a, "ctx", [(i, i ^ 1) for i in range(count) if i not in (1, count - 2)])


def in_hbm(a):
    return "h", pltpu.with_memory_space_constraint(a, pltpu.HBM)


def per_device(inputs, b_proj, c_proj, step_sizes, a_log, skip_gain, doc_lengths, grad_out):
    rows, columns = inputs.shape[1:]
    heads, width = a_log.shape[0], b_proj.shape[2]
    reach = max(lax.axis_size("ctx") // 4, 1)
    devices = lax.axis_size("ctx") * lax.axis_size("dp")
    alog, skip = a_log[None], skip_gain[None]
    bt, ct = jnp.swapaxes(b_proj, 1, 2), jnp.swapaxes(c_proj, 1, 2)
    blocks = columns // WIDE

    def v(shape, kind=F32):
        return "v", (shape, kind)

    alog, dt, x, b, dy, c, *payloads = call(
        states_kernel,
        reach,
        [
            v(alog.shape),
            v((heads, rows)),
            v((rows, columns), BF16),
            v((width, rows), BF16),
            v((rows, columns), BF16),
            v((width, rows), BF16),
        ]
        + [v((columns // LANES * (width + 1) // part, LANES)) for part in (1, 2, 2)],
        [in_hbm(a) for a in (doc_lengths, alog, step_sizes, inputs, bt, grad_out, ct)],
        10**9,
        4 * 2**20,
        [
            pltpu.SMEM(doc_lengths.shape, jnp.int32),
            pltpu.SemaphoreType.DMA((5,)),
            pltpu.SemaphoreType.DMA((2, PIECES)),
        ],
    )
    messages = {}
    for j, second, half in message_plan(reach):
        if (j, second) == (1, 1) and reach > 1:
            continue
        payload = payloads[1 + half if second else 0]
        messages[j, second, half] = send(payload, j, second)
    if reach > 1:
        for half in (0, 1):
            messages[1, 1, half] = hand_on(messages[2, 1, half])
    whole = "h", ((rows, columns), F32)
    state = v((width, columns))
    stage = pltpu.VMEM((rows, columns), F32)
    transposed = v((width, rows))
    xs, ys, v_wide, dx, b_end, c_live, masks, db, dc, sums, fwd_logs, bwd_logs, ends, small = call(
        inside_kernel,
        reach,
        [v((2 * rows, columns), BF16)] * 2
        + [whole] * 2
        + [v((rows, 2 * width), BF16)] * 2
        + [v((8, rows)), transposed, transposed, v((2 * rows, heads))]
        + [state, state, v((8, columns)), v((1, LANES))],
        [in_hbm(doc_lengths), in_hbm(skip)]
        + [("v", a) for a in (alog, dt, x, b, dy, c)]
        + [("any", messages[1, 0, 0])],
        4 * 10**9,
        12 * 2**20,
        [
            stage,
            stage,
            pltpu.SMEM(doc_lengths.shape, jnp.int32),
            pltpu.VMEM(skip.shape, F32),
            pltpu.SemaphoreType.DMA,
            pltpu.SemaphoreType.DMA,
            pltpu.SemaphoreType.DMA((2, blocks)),
        ],
    )
    half_state = v((width, columns // 2))
    joined, last = [], []
    for half in (0, 1):
        out = v((devices, LANES)) if half else v((blocks // 2, WIDE))
        came, pull, partial = call(
            functools.partial(rates_kernel, reach, columns // heads, half),
            reach,
            [half_state, half_state, out],
            [("v", messages[one]) for one in message_plan(reach, half)]
            + [("v", a) for a in (ends, fwd_logs, bwd_logs, *last)],
            10**8,
            4 * 2**20,
        )
        joined.append((came, pull))
        last = [small, partial]
    input_grads, b_gradient, c_gradient, step_grads = call(
        outputs_kernel,
        reach,
        [("h", ((1, rows, columns), BF16))]
        + [v((1, width, rows), BF16)] * 2
        + [v((1, heads, rows))],
        [("v", a) for side in zip(*joined) for a in side]
        + [("v", a) for a in (ends, xs, ys)]
        + [in_hbm(v_wide), in_hbm(dx)]
        + [("v", a) for a in (b_end, c_live, masks, db, dc, sums, alog, dt)],
        2 * 10**9,
        12 * 2**20,
        [
            stage,
            stage,
            pltpu.VMEM((rows, columns), BF16),
            pltpu.SemaphoreType.DMA((2, blocks)),
            pltpu.SemaphoreType.DMA((blocks,)),
        ],
    )
    gathered = lax.all_to_all(partial, ("ctx", "dp"), 0, 0, tiled=True)
    totals = jnp.sum(gathered, axis=0)
    return (
        input_grads,
        jnp.swapaxes(b_gradient, 1, 2),
        jnp.swapaxes(c_gradient, 1, 2),
        step_grads,
        totals[:heads],
        totals[heads : 2 * heads],
    )


def solution(mesh):
    in_specs = (
        P("dp", "ctx", None),
        P("dp", "ctx", None),
        P("dp", "ctx", None),
        P("dp", None, "ctx"),
        P(),
        P(),
        P("dp", None),
        P("dp", "ctx", None),
    )
    out_specs = (
        P("dp", "ctx", None),
        P("dp", "ctx", None),
        P("dp", "ctx", None),
        P("dp", None, "ctx"),
        P(),
        P(),
    )
    return jax.shard_map(
        per_device, mesh=mesh, in_specs=in_specs, out_specs=out_specs, check_vma=False
    )
```

```python
import functools

import jax
import jax.numpy as jnp
from jax import lax
from jax.experimental import pallas as pl
from jax.experimental.pallas import tpu as pltpu
from jax.sharding import PartitionSpec as P

F32 = jnp.float32
BF16 = jnp.bfloat16
LANES = 128
WIDE = 256
PARTS = WIDE // LANES
FAR = 2**30
PIECES = 2


def dot(a, b, ca, cb):
    return lax.dot_general(a, b, (((ca,), (cb,)), ((), ())), preferred_element_type=F32)


def iota(shape, dim):
    return lax.broadcasted_iota(jnp.int32, shape, dim)


def split2(a):
    high = a.astype(BF16)
    return high, (a - high.astype(F32)).astype(BF16)


def split3(a):
    high = a.astype(BF16)
    rest = a - high.astype(F32)
    middle = rest.astype(BF16)
    return high, middle, (rest - middle.astype(F32)).astype(BF16)


def dot_pairs(a, b, ca, cb):
    return dot(a[0], b[0], ca, cb) + (dot(a[0], b[1], ca, cb) + dot(a[1], b[0], ca, cb))


def stack(parts, axis):
    return jnp.concatenate(parts, axis=axis)


def document_places(lens_ref, rows):
    offset = shard() * rows
    starts = [jnp.int32(0)]
    for d in range(lens_ref.shape[1] - 1):
        starts.append(starts[-1] + lens_ref[0, d])
    first = jnp.int32(FAR)
    last = jnp.int32(0)
    for start in starts:
        first = jnp.minimum(first, jnp.where(start >= offset, start, FAR))
        last = jnp.maximum(last, jnp.where(start < offset + rows, start, 0))
    return starts, offset, first, last


def rate_column(alog_ref):
    heads = alog_ref.shape[1]
    square = jnp.broadcast_to(alog_ref[...], (heads, heads))
    picked = jnp.where(iota((heads, heads), 0) == iota((heads, heads), 1), square, 0.0)
    return -jnp.exp(jnp.sum(picked, axis=1, keepdims=True))


def log2(size):
    assert size & (size - 1) == 0
    return size.bit_length() - 1


def head_distance(heads, head_width):
    shape = (3 * heads, WIDE)
    return (iota(shape, 0) & (heads - 1)) - lax.shift_right_logical(
        iota(shape, 1), log2(head_width)
    )


def head_rows(distance, head_width, block):
    return jnp.where(distance == block * (WIDE // head_width), 1.0, 0.0).astype(BF16)


def head_columns(heads, head_width, block):
    shape = (WIDE, heads)
    column = lax.shift_right_logical(iota(shape, 0), log2(head_width))
    return jnp.where(iota(shape, 1) - column == block * (WIDE // head_width), 1.0, 0.0).astype(BF16)


def shard():
    return lax.axis_index("ctx")


def message_block(ref, block, width):
    at = block * PARTS
    return stack([ref[(at + i) * width : (at + i + 1) * width, :] for i in range(PARTS)], 1)


def message_tail(ref, block, width):
    tail = ref.shape[0] // (width + 1) * width + block * PARTS
    return stack([ref[tail + i : tail + i + 1, :] for i in range(PARTS)], 1)


def message_plan(reach, only=None):
    near = [(1, 0, 0)]
    relayed = [(1, 1, 0), (1, 1, 1)]
    far = [(2, 1, 0), (2, 1, 1), (2, 0, 0)] if reach > 1 else []
    rest = [(j, *one) for j in range(3, reach + 1) for one in ((0, 0), (1, 0), (1, 1))]
    plan = near + far + relayed + rest
    return [one for one in plan if only is None or not one[1] or one[2] == only]


def received(messages, reach, block, blocks, width):
    came = pull = None
    half, inner = divmod(block, blocks // 2)
    for j in range(reach, 0, -1):
        one, two = messages[j, 0, 0], messages[j, 1, half]
        a, b = message_block(one, block, width), message_block(two, inner, width)
        first = jnp.broadcast_to(lax.rem(shard() + j, 2), a.shape) == 0
        near_came, near_pull = jnp.where(first, a, b), jnp.where(first, b, a)
        if came is None:
            came, pull = near_came, near_pull
        else:
            a, b = message_tail(one, block, width), message_tail(two, inner, width)
            first = jnp.broadcast_to(lax.rem(shard() + j, 2), a.shape) == 0
            came = near_came + jnp.where(first, a, b) * came
            pull = near_pull + jnp.where(first, b, a) * pull
    return came, pull


def states_kernel(
    lens_hbm,
    alog_hbm,
    skip_hbm,
    dt_hbm,
    x_hbm,
    b_hbm,
    dy_hbm,
    c_hbm,
    alog_ref,
    skip_ref,
    dt_ref,
    x_ref,
    b_ref,
    dy_ref,
    c_ref,
    one_ref,
    two_ref,
    three_ref,
    lens_ref,
    small_sems,
    sems,
):
    rows, columns = x_ref.shape
    heads, width = dt_ref.shape[0], b_ref.shape[0]
    head_width = columns // heads
    piece = columns // PIECES
    small = [
        pltpu.make_async_copy(source, target, small_sems.at[i])
        for i, (source, target) in enumerate(
            (
                (dt_hbm.at[0], dt_ref),
                (alog_hbm, alog_ref),
                (lens_hbm, lens_ref),
                (b_hbm.at[0], b_ref),
                (c_hbm.at[0], c_ref),
                (skip_hbm, skip_ref),
            )
        )
    ]
    for copy in small[:-1]:
        copy.start()
    large = []
    for i in range(PIECES):
        at = slice(i * piece, (i + 1) * piece)
        for side, (source, target) in enumerate(((x_hbm, x_ref), (dy_hbm, dy_ref))):
            copy = pltpu.make_async_copy(
                source.at[0, :, at], target.at[:, at], sems.at[side, i]
            )
            copy.start()
            large.append(copy)
    small[-1].start()
    square = (rows, rows)
    upper = jnp.where(iota(square, 0) <= iota(square, 1), 1.0, 0.0).astype(BF16)
    even = jnp.broadcast_to(lax.rem(shard(), 2), (width, LANES)) == 0
    left = iota((1, LANES), 1) < head_width
    for copy in small[:-1]:
        copy.wait()
    _, offset, first, last = document_places(lens_ref, rows)
    through = jnp.where(first >= offset + rows, 1.0, 0.0)
    dt = dt_ref[...]
    logs = sum(dot(part, upper, 1, 0) for part in split3(dt * rate_column(alog_ref)))
    end_log = logs[:, rows - 1 : rows]
    place = iota((heads, rows), 1) + offset
    keeping = jnp.where(place >= last, jnp.exp(end_log - logs) * dt, 0.0)
    carried = jnp.where(place < first, jnp.exp(logs), 0.0)
    kept = jnp.broadcast_to(jnp.exp(end_log) * through, (heads, LANES))
    b, c = b_ref[...].astype(F32), c_ref[...].astype(F32)
    own = LANES // head_width

    def block_states(vectors, weights, values):
        rows_in = [stack(split2(vectors * weights[h : h + 1, :]), 1) for h in range(PARTS * own)]
        out = dot(stack(rows_in, 0), stack([values, values], 0), 1, 0)
        pairs = []
        for i in range(PARTS):
            lanes = slice(i * LANES, (i + 1) * LANES)
            sides = [
                out[h * width : (h + 1) * width, lanes] for h in range(i * own, (i + 1) * own)
            ]
            pairs.append(jnp.where(left, sides[0], sides[1]))
        return pairs

    pairs = columns // LANES
    for block in range(columns // WIDE):
        if block * WIDE % piece == 0:
            large[block * WIDE // piece * 2].wait()
            large[block * WIDE // piece * 2 + 1].wait()
        at = slice(block * WIDE, (block + 1) * WIDE)
        here = slice(block * PARTS * own, (block + 1) * PARTS * own)
        states = block_states(b, keeping[here], x_ref[:, at])
        pulls = block_states(c, carried[here], dy_ref[:, at])
        for i in range(PARTS):
            pair = block * PARTS + i
            kept_row = jnp.where(left, kept[pair * own : pair * own + 1], kept[pair * own + 1 :][:1])
            first = jnp.where(even, states[i], pulls[i])
            second = jnp.where(even, pulls[i], states[i])
            half, inner = divmod(pair, pairs // 2)
            for ref, place_in, whole, value in (
                (one_ref, pair, pairs, first),
                ((two_ref, three_ref)[half], inner, pairs // 2, second),
            ):
                ref[place_in * width : (place_in + 1) * width, :] = value
                ref[whole * width + place_in : whole * width + place_in + 1, :] = kept_row
    small[-1].wait()


def inside_kernel(
    lens_hbm,
    alog_ref,
    skip_ref,
    dt_ref,
    x_ref,
    b_ref,
    dy_ref,
    c_ref,
    _,
    xs_ref,
    ys_ref,
    v_wide_hbm,
    dx_hbm,
    b_end_ref,
    c_live_ref,
    masks_ref,
    db_ref,
    dc_ref,
    sums_ref,
    fwd_ref,
    bwd_ref,
    ends_ref,
    small_ref,
    v_stage,
    dx_stage,
    lens_ref,
    lens_sem,
    sems,
):
    rows, columns = x_ref.shape
    heads, width = dt_ref.shape[0], b_ref.shape[0]
    head_width = columns // heads
    lens_copy = pltpu.make_async_copy(lens_hbm, lens_ref, lens_sem)
    lens_copy.start()
    distance = head_distance(heads, head_width)
    bt, ct = b_ref[...], c_ref[...]
    raw_scores, raw_flipped = dot(ct, bt, 0, 0), dot(bt, ct, 0, 0)
    lens_copy.wait()
    starts, offset, first, last = document_places(lens_ref, rows)
    through = jnp.where(first >= offset + rows, 1.0, 0.0)
    square = (rows, rows)
    place0, place1 = iota(square, 0) + offset, iota(square, 1) + offset
    segment0, segment1 = jnp.zeros(square, jnp.int32), jnp.zeros(square, jnp.int32)
    for start in starts:
        segment0 += jnp.where(place0 >= start, 1, 0)
        segment1 += jnp.where(place1 >= start, 1, 0)
    same = segment0 == segment1
    down = same & (place0 >= place1)
    lower = jnp.where(place0 >= place1, 1.0, 0.0).astype(BF16)
    eye = jnp.where(place0 == place1, 1.0, 0.0).astype(BF16)
    dt = dt_ref[...]
    logs = sum(dot(lower, part, 1, 1) for part in split3(dt * rate_column(alog_ref)))
    steps = sum(dot(eye, part, 1, 1) for part in split3(dt))
    scores = split2(jnp.where(down, raw_scores, 0.0))
    flipped = split2(jnp.where(same & (place1 >= place0), raw_flipped, 0.0))
    place = iota((width, rows), 1) + offset
    bt_end = jnp.where(place >= last, bt.astype(F32), 0.0)
    ct_live = jnp.where(place < first, ct.astype(F32), 0.0)
    b_end, c_live = jnp.transpose(bt_end).astype(BF16), jnp.transpose(ct_live).astype(BF16)
    bt_end, ct_live = bt_end.astype(BF16), ct_live.astype(BF16)
    b_end_ref[...] = stack([b_end, b_end], 1)
    c_live_ref[...] = stack([c_live, c_live], 1)
    bt_end, ct_live = stack([bt_end, bt_end], 1), stack([ct_live, ct_live], 1)
    masks_ref[0:1] = jnp.where(place[:1] >= last, 1.0, 0.0)
    masks_ref[1:2] = jnp.where(place[:1] < first, 1.0, 0.0)
    tables = stack(
        [
            stack(split3(a), 1)
            for a in (
                jnp.exp(logs),
                jnp.exp(-logs) * steps,
                logs,
                jnp.broadcast_to(skip_ref[...], (16, heads)),
            )
        ],
        0,
    )
    d_scores = jnp.zeros((2 * rows, 2 * rows), F32)
    sums = jnp.zeros((2 * rows + 16, heads), F32)
    copies = []
    for block in range(columns // WIDE):
        at = slice(block * WIDE, (block + 1) * WIDE)
        wide = dot(tables, head_rows(distance, head_width, block), 1, 0)
        ones = head_columns(heads, head_width, block)
        u_wide, v_wide, l_wide = wide[:rows], wide[rows : 2 * rows], wide[2 * rows : 3 * rows]
        skip_wide = wide[3 * rows : 3 * rows + 1]
        x = x_ref[:, at].astype(F32)
        dy = dy_ref[:, at].astype(F32)
        xv = x * v_wide
        yu = dy * u_wide
        xs, ys = split2(xv), split2(yu)
        xs_ref[:, at] = stack(xs, 0)
        ys_ref[:, at] = stack(ys, 0)
        v_stage[:, at] = v_wide
        out = dot_pairs(scores, xs, 1, 0)
        back = dot_pairs(flipped, ys, 1, 0)
        d_scores += dot(stack(ys, 0), stack(xs, 0), 1, 1)
        dx_stage[:, at] = v_wide * back + skip_wide * dy
        for i, (stage, target) in enumerate(((v_stage, v_wide_hbm), (dx_stage, dx_hbm))):
            copy = pltpu.make_async_copy(stage.at[:, at], target.at[:, at], sems.at[i, block])
            copy.start()
            copies.append(copy)
        column_part = xv * back
        product = jnp.broadcast_to(jnp.sum(x * dy, axis=0, keepdims=True), (16, WIDE))
        for part in split3(stack([yu * out - column_part, column_part, product], 0)):
            sums += dot(part, ones, 1, 0)
        ending = u_wide[rows - 1 : rows]
        end_log = l_wide[rows - 1 : rows]
        gap = end_log - l_wide
        fwd_ref[:, at] = dot(bt_end, stack(split2(xv * gap), 0), 1, 0) * ending
        bwd_ref[:, at] = dot(ct_live, stack(split2(yu * l_wide), 0), 1, 0)
        ends_ref[0:1, at] = ending
        ends_ref[1:2, at] = ending * through
        ends_ref[2:3, at] = ending * through * end_log
    d_scores = (d_scores[:rows, :rows] + d_scores[:rows, rows:]) + d_scores[rows:, :rows]
    d_scores = split2(jnp.where(down, d_scores, 0.0))
    dc_ref[...] = sum(dot(bt, p, 1, 1) for p in d_scores)
    db_ref[...] = sum(dot(ct, p, 1, 0) for p in d_scores)
    sums_ref[...] = sums[: 2 * rows]
    rate_grads = jnp.sum(logs * sums[:rows], axis=0, keepdims=True)
    empty = jnp.zeros((1, LANES - 2 * heads), F32)
    small_ref[...] = stack([rate_grads, sums[2 * rows : 2 * rows + 1], empty], 1)
    for copy in copies:
        copy.wait()


def rates_kernel(reach, head_width, half, *refs):
    plan = message_plan(reach, half)
    messages = dict(zip(plan, refs))
    ends_ref, fwd_ref, bwd_ref, *refs = refs[len(plan) :]
    width, columns = fwd_ref.shape
    blocks = columns // WIDE
    own_blocks = blocks // 2
    came_ref, pull_ref, out_ref = refs[-3:]
    whole = []
    for i in range(own_blocks):
        block = half * own_blocks + i
        at = slice(block * WIDE, (block + 1) * WIDE)
        own = slice(i * WIDE, (i + 1) * WIDE)
        came, pull = received(messages, reach, block, blocks, width)
        came_ref[:, own] = came
        pull_ref[:, own] = pull
        terms = came * bwd_ref[:, at] + pull * (fwd_ref[:, at] + ends_ref[2:3, at] * came)
        whole.append(jnp.sum(terms, axis=0, keepdims=True))
    if not half:
        out_ref[...] = stack(whole, 0)
        return
    small_ref, first_ref = refs[:2]
    own = WIDE // head_width
    shape = (WIDE, LANES)
    column = lax.shift_right_logical(iota(shape, 0), log2(head_width))
    ones = jnp.where(column == (iota(shape, 1) & (own - 1)), 1.0, 0.0).astype(BF16)
    sums = dot(stack(split3(stack([first_ref[...], *whole], 0)), 0), ones, 1, 0)
    sums = (sums[:blocks] + sums[blocks : 2 * blocks]) + sums[2 * blocks :]
    lane = iota(sums.shape, 1)
    mine = lax.shift_right_logical(lane, log2(own)) == iota(sums.shape, 0)
    total = small_ref[...] + jnp.sum(jnp.where(mine, sums, 0.0), axis=0, keepdims=True)
    out_ref[...] = jnp.broadcast_to(total, out_ref.shape)


def outputs_kernel(
    came_one,
    came_two,
    pull_one,
    pull_two,
    ends_ref,
    xs_ref,
    ys_ref,
    v_wide_hbm,
    dx_hbm,
    b_end_ref,
    c_live_ref,
    masks_ref,
    db_ref,
    dc_ref,
    sums_ref,
    alog_ref,
    dt_ref,
    dx_out,
    db_out,
    dc_out,
    dt_out,
    v_stage,
    dx_stage,
    stage,
    in_sems,
    out_sems,
):
    rows, columns = dx_hbm.shape
    heads, width = dt_ref.shape[0], db_ref.shape[0]
    blocks = columns // WIDE
    copies = []
    for block in range(blocks):
        at = slice(block * WIDE, (block + 1) * WIDE)
        for i, (source, target) in enumerate(((v_wide_hbm, v_stage), (dx_hbm, dx_stage))):
            copy = pltpu.make_async_copy(
                source.at[:, at], target.at[:, at], in_sems.at[i, block]
            )
            copy.start()
            copies.append(copy)
    b_end, c_live = b_end_ref[...], c_live_ref[...]
    own_sums = sums_ref[...]
    sums = own_sums
    dc = jnp.zeros((2 * width, 2 * rows), F32)
    db = jnp.zeros((2 * width, 2 * rows), F32)
    at_last = iota((rows, WIDE), 0) == rows - 1
    sent = []
    for block in range(blocks):
        at = slice(block * WIDE, (block + 1) * WIDE)
        ones = head_columns(heads, columns // heads, block)
        half, inner = divmod(block, blocks // 2)
        own = slice(inner * WIDE, (inner + 1) * WIDE)
        came, pull = (came_one, came_two)[half][:, own], (pull_one, pull_two)[half][:, own]
        meet = jnp.sum(came * pull, axis=0, keepdims=True) * ends_ref[1:2, at]
        cames = stack(split2(came), 0)
        pulls = stack(split2(pull * ends_ref[0:1, at]), 0)
        xs, ys = xs_ref[:, at], ys_ref[:, at]
        out = dot(c_live, cames, 1, 0)
        back = dot(b_end, pulls, 1, 0)
        column_part = (xs[:rows].astype(F32) + xs[rows:].astype(F32)) * back
        row_part = (ys[:rows].astype(F32) + ys[rows:].astype(F32)) * out
        row_part = jnp.where(at_last, row_part + meet, row_part)
        for part in split2(stack([row_part - column_part, column_part], 0)):
            sums += dot(part, ones, 1, 0)
        dc += dot(cames, ys, 1, 1)
        db += dot(pulls, xs, 1, 1)
        copies[2 * block].wait()
        copies[2 * block + 1].wait()
        stage[:, at] = (dx_stage[:, at] + v_stage[:, at] * back).astype(BF16)
        copy = pltpu.make_async_copy(stage.at[:, at], dx_out.at[0, :, at], out_sems.at[block])
        copy.start()
        sent.append(copy)
    dc = (dc[:width, :rows] + dc[:width, rows:]) + dc[width:, :rows]
    db = (db[:width, :rows] + db[:width, rows:]) + db[width:, :rows]
    db_out[0] = (db_ref[...] + masks_ref[0:1] * db).astype(BF16)
    dc_out[0] = (dc_ref[...] + masks_ref[1:2] * dc).astype(BF16)
    square = (rows, rows)
    upper = jnp.where(iota(square, 0) >= iota(square, 1), 1.0, 0.0).astype(BF16)
    eye = jnp.where(iota(square, 0) == iota(square, 1), 1.0, 0.0).astype(BF16)
    at_end = jnp.sum(sums[rows:] - own_sums[rows:], axis=0, keepdims=True)
    dl = sums[:rows] + jnp.where(iota((rows, heads), 0) == rows - 1, at_end, 0.0)
    d_decay = sum(dot(part, upper, 0, 0) for part in split3(dl))
    total = sum(dot(part, eye, 0, 0) for part in split3(sums[rows:]))
    dt_out[0] = total / dt_ref[...] + rate_column(alog_ref) * d_decay
    for copy in sent:
        copy.wait()


def call(kernel, reach, outs, ins, flops, moved, scratch=()):
    spaces = {"s": pltpu.SMEM, "v": pltpu.VMEM, "h": pltpu.HBM, "any": pl.ANY}
    return pl.pallas_call(
        kernel,
        out_shape=[
            pltpu.HBM(*out) if place == "h" else jax.ShapeDtypeStruct(*out) for place, out in outs
        ],
        in_specs=[pl.BlockSpec(memory_space=spaces[place]) for place, _ in ins],
        out_specs=[pl.BlockSpec(memory_space=spaces[place]) for place, _ in outs],
        scratch_shapes=scratch,
        compiler_params=pltpu.CompilerParams(vmem_limit_bytes=min(16 + 2 * reach, 56) * 2**20),
        cost_estimate=pl.CostEstimate(flops=flops, bytes_accessed=moved, transcendentals=0),
    )(*(a for _, a in ins))


def send(a, by, second):
    count = lax.axis_size("ctx")
    pairs = [(i, i + by if (i + second) % 2 == 0 else i - by) for i in range(count)]
    return lax.ppermute(a, "ctx", [(i, j) for i, j in pairs if 0 <= j < count])


def hand_on(a, half):
    count = lax.axis_size("ctx")
    spared = (1, count - 2) if half else ()
    return lax.ppermute(a, "ctx", [(i, i ^ 1) for i in range(count) if i not in spared])


def in_hbm(a):
    return "h", pltpu.with_memory_space_constraint(a, pltpu.HBM)


def per_device(inputs, b_proj, c_proj, step_sizes, a_log, skip_gain, doc_lengths, grad_out):
    rows, columns = inputs.shape[1:]
    heads, width = a_log.shape[0], b_proj.shape[2]
    reach = max(lax.axis_size("ctx") // 4, 1)
    devices = lax.axis_size("ctx") * lax.axis_size("dp")
    alog, skip = a_log[None], skip_gain[None]
    bt, ct = jnp.swapaxes(b_proj, 1, 2), jnp.swapaxes(c_proj, 1, 2)
    blocks = columns // WIDE

    def v(shape, kind=F32):
        return "v", (shape, kind)

    alog, skip, dt, x, b, dy, c, *payloads = call(
        states_kernel,
        reach,
        [
            v(alog.shape),
            v(skip.shape),
            v((heads, rows)),
            v((rows, columns), BF16),
            v((width, rows), BF16),
            v((rows, columns), BF16),
            v((width, rows), BF16),
        ]
        + [v((columns // LANES * (width + 1) // part, LANES)) for part in (1, 2, 2)],
        [in_hbm(a) for a in (doc_lengths, alog, skip, step_sizes, inputs, bt, grad_out, ct)],
        10**9,
        4 * 2**20,
        [
            pltpu.SMEM(doc_lengths.shape, jnp.int32),
            pltpu.SemaphoreType.DMA((6,)),
            pltpu.SemaphoreType.DMA((2, PIECES)),
        ],
    )
    messages = {}
    for j, second, half in message_plan(reach):
        if (j, second) == (1, 1) and reach > 1:
            continue
        payload = payloads[1 + half if second else 0]
        messages[j, second, half] = send(payload, j, second)
    if reach > 1:
        for half in (0, 1):
            messages[1, 1, half] = hand_on(messages[2, 1, half], half)
    whole = "h", ((rows, columns), F32)
    state = v((width, columns))
    stage = pltpu.VMEM((rows, columns), F32)
    transposed = v((width, rows))
    xs, ys, v_wide, dx, b_end, c_live, masks, db, dc, sums, fwd_logs, bwd_logs, ends, small = call(
        inside_kernel,
        reach,
        [v((2 * rows, columns), BF16)] * 2
        + [whole] * 2
        + [v((rows, 2 * width), BF16)] * 2
        + [v((8, rows)), transposed, transposed, v((2 * rows, heads))]
        + [state, state, v((8, columns)), v((1, LANES))],
        [in_hbm(doc_lengths)]
        + [("v", a) for a in (alog, skip, dt, x, b, dy, c)]
        + [("any", messages[1, 0, 0])],
        4 * 10**9,
        12 * 2**20,
        [
            stage,
            stage,
            pltpu.SMEM(doc_lengths.shape, jnp.int32),
            pltpu.SemaphoreType.DMA,
            pltpu.SemaphoreType.DMA((2, blocks)),
        ],
    )
    half_state = v((width, columns // 2))
    joined, last = [], []
    for half in (0, 1):
        out = v((devices, LANES)) if half else v((blocks // 2, WIDE))
        came, pull, partial = call(
            functools.partial(rates_kernel, reach, columns // heads, half),
            reach,
            [half_state, half_state, out],
            [("v", messages[one]) for one in message_plan(reach, half)]
            + [("v", a) for a in (ends, fwd_logs, bwd_logs, *last)],
            10**8,
            4 * 2**20,
        )
        joined.append((came, pull))
        last = [small, partial]
    input_grads, b_gradient, c_gradient, step_grads = call(
        outputs_kernel,
        reach,
        [("h", ((1, rows, columns), BF16))]
        + [v((1, width, rows), BF16)] * 2
        + [v((1, heads, rows))],
        [("v", a) for side in zip(*joined) for a in side]
        + [("v", a) for a in (ends, xs, ys)]
        + [in_hbm(v_wide), in_hbm(dx)]
        + [("v", a) for a in (b_end, c_live, masks, db, dc, sums, alog, dt)],
        2 * 10**9,
        12 * 2**20,
        [
            stage,
            stage,
            pltpu.VMEM((rows, columns), BF16),
            pltpu.SemaphoreType.DMA((2, blocks)),
            pltpu.SemaphoreType.DMA((blocks,)),
        ],
    )
    gathered = lax.all_to_all(partial, ("ctx", "dp"), 0, 0, tiled=True)
    totals = jnp.sum(gathered, axis=0)
    return (
        input_grads,
        jnp.swapaxes(b_gradient, 1, 2),
        jnp.swapaxes(c_gradient, 1, 2),
        step_grads,
        totals[:heads],
        totals[heads : 2 * heads],
    )


def solution(mesh):
    in_specs = (
        P("dp", "ctx", None),
        P("dp", "ctx", None),
        P("dp", "ctx", None),
        P("dp", None, "ctx"),
        P(),
        P(),
        P("dp", None),
        P("dp", "ctx", None),
    )
    out_specs = (
        P("dp", "ctx", None),
        P("dp", "ctx", None),
        P("dp", "ctx", None),
        P("dp", None, "ctx"),
        P(),
        P(),
    )
    return jax.shard_map(
        per_device, mesh=mesh, in_specs=in_specs, out_specs=out_specs, check_vma=False
    )
```

```python
import functools

import jax
import jax.numpy as jnp
from jax import lax
from jax.experimental import pallas as pl
from jax.experimental.pallas import tpu as pltpu
from jax.sharding import PartitionSpec as P

F32 = jnp.float32
BF16 = jnp.bfloat16
LANES = 128
WIDE = 256
PARTS = WIDE // LANES
FAR = 2**30
PIECES = 2


def dot(a, b, ca, cb):
    return lax.dot_general(a, b, (((ca,), (cb,)), ((), ())), preferred_element_type=F32)


def iota(shape, dim):
    return lax.broadcasted_iota(jnp.int32, shape, dim)


def split2(a):
    high = a.astype(BF16)
    return high, (a - high.astype(F32)).astype(BF16)


def split3(a):
    high = a.astype(BF16)
    rest = a - high.astype(F32)
    middle = rest.astype(BF16)
    return high, middle, (rest - middle.astype(F32)).astype(BF16)


def dot_pairs(a, b, ca, cb):
    return dot(a[0], b[0], ca, cb) + (dot(a[0], b[1], ca, cb) + dot(a[1], b[0], ca, cb))


def stack(parts, axis):
    return jnp.concatenate(parts, axis=axis)


def document_places(lens_ref, rows):
    offset = shard() * rows
    starts = [jnp.int32(0)]
    for d in range(lens_ref.shape[1] - 1):
        starts.append(starts[-1] + lens_ref[0, d])
    first = jnp.int32(FAR)
    last = jnp.int32(0)
    for start in starts:
        first = jnp.minimum(first, jnp.where(start >= offset, start, FAR))
        last = jnp.maximum(last, jnp.where(start < offset + rows, start, 0))
    return starts, offset, first, last


def rate_column(alog_ref):
    heads = alog_ref.shape[1]
    square = jnp.broadcast_to(alog_ref[...], (heads, heads))
    picked = jnp.where(iota((heads, heads), 0) == iota((heads, heads), 1), square, 0.0)
    return -jnp.exp(jnp.sum(picked, axis=1, keepdims=True))


def log2(size):
    assert size & (size - 1) == 0
    return size.bit_length() - 1


def head_distance(heads, head_width):
    shape = (3 * heads, WIDE)
    return (iota(shape, 0) & (heads - 1)) - lax.shift_right_logical(
        iota(shape, 1), log2(head_width)
    )


def head_rows(distance, head_width, block):
    return jnp.where(distance == block * (WIDE // head_width), 1.0, 0.0).astype(BF16)


def head_columns(heads, head_width, block):
    shape = (WIDE, heads)
    column = lax.shift_right_logical(iota(shape, 0), log2(head_width))
    return jnp.where(iota(shape, 1) - column == block * (WIDE // head_width), 1.0, 0.0).astype(BF16)


def shard():
    return lax.axis_index("ctx")


def message_block(ref, block, width):
    at = block * PARTS
    return stack([ref[(at + i) * width : (at + i + 1) * width, :] for i in range(PARTS)], 1)


def message_tail(ref, block, width):
    tail = ref.shape[0] // (width + 1) * width + block * PARTS
    return stack([ref[tail + i : tail + i + 1, :] for i in range(PARTS)], 1)


def message_plan(reach, only=None):
    near = [(1, 0, 0)]
    relayed = [(1, 1, 0), (1, 1, 1)]
    far = [(2, 1, 0), (2, 1, 1), (2, 0, 0)] if reach > 1 else []
    rest = [(j, *one) for j in range(3, reach + 1) for one in ((0, 0), (1, 0), (1, 1))]
    plan = near + far + relayed + rest
    return [one for one in plan if only is None or not one[1] or one[2] == only]


def received(messages, reach, block, blocks, width):
    came = pull = None
    half, inner = divmod(block, blocks // 2)
    for j in range(reach, 0, -1):
        one, two = messages[j, 0, 0], messages[j, 1, half]
        a, b = message_block(one, block, width), message_block(two, inner, width)
        first = jnp.broadcast_to(lax.rem(shard() + j, 2), a.shape) == 0
        near_came, near_pull = jnp.where(first, a, b), jnp.where(first, b, a)
        if came is None:
            came, pull = near_came, near_pull
        else:
            a, b = message_tail(one, block, width), message_tail(two, inner, width)
            first = jnp.broadcast_to(lax.rem(shard() + j, 2), a.shape) == 0
            came = near_came + jnp.where(first, a, b) * came
            pull = near_pull + jnp.where(first, b, a) * pull
    return came, pull


def states_kernel(
    lens_hbm,
    alog_hbm,
    skip_hbm,
    dt_hbm,
    x_hbm,
    b_hbm,
    dy_hbm,
    c_hbm,
    alog_ref,
    skip_ref,
    dt_ref,
    x_ref,
    b_ref,
    dy_ref,
    c_ref,
    one_ref,
    two_ref,
    three_ref,
    lens_ref,
    small_sems,
    sems,
):
    rows, columns = x_ref.shape
    heads, width = dt_ref.shape[0], b_ref.shape[0]
    head_width = columns // heads
    piece = columns // PIECES
    small = [
        pltpu.make_async_copy(source, target, small_sems.at[i])
        for i, (source, target) in enumerate(
            (
                (dt_hbm.at[0], dt_ref),
                (alog_hbm, alog_ref),
                (lens_hbm, lens_ref),
                (b_hbm.at[0], b_ref),
                (c_hbm.at[0], c_ref),
                (skip_hbm, skip_ref),
            )
        )
    ]
    large = []
    for i in range(PIECES):
        at = slice(i * piece, (i + 1) * piece)
        for side, (source, target) in enumerate(((x_hbm, x_ref), (dy_hbm, dy_ref))):
            copy = pltpu.make_async_copy(
                source.at[0, :, at], target.at[:, at], sems.at[side, i]
            )
            large.append(copy)
    for copy in (*small[:3], *large[:2], *small[3:5], *large[2:], *small[5:]):
        copy.start()
    square = (rows, rows)
    upper = jnp.where(iota(square, 0) <= iota(square, 1), 1.0, 0.0).astype(BF16)
    even = jnp.broadcast_to(lax.rem(shard(), 2), (width, LANES)) == 0
    left = iota((1, LANES), 1) < head_width
    for copy in small[:3]:
        copy.wait()
    _, offset, first, last = document_places(lens_ref, rows)
    through = jnp.where(first >= offset + rows, 1.0, 0.0)
    dt = dt_ref[...]
    logs = sum(dot(part, upper, 1, 0) for part in split3(dt * rate_column(alog_ref)))
    end_log = logs[:, rows - 1 : rows]
    place = iota((heads, rows), 1) + offset
    keeping = jnp.where(place >= last, jnp.exp(end_log - logs) * dt, 0.0)
    carried = jnp.where(place < first, jnp.exp(logs), 0.0)
    kept = jnp.broadcast_to(jnp.exp(end_log) * through, (heads, LANES))
    for copy in small[3:5]:
        copy.wait()
    b, c = b_ref[...].astype(F32), c_ref[...].astype(F32)
    own = LANES // head_width

    def block_states(vectors, weights, values):
        rows_in = [stack(split2(vectors * weights[h : h + 1, :]), 1) for h in range(PARTS * own)]
        out = dot(stack(rows_in, 0), stack([values, values], 0), 1, 0)
        pairs = []
        for i in range(PARTS):
            lanes = slice(i * LANES, (i + 1) * LANES)
            sides = [
                out[h * width : (h + 1) * width, lanes] for h in range(i * own, (i + 1) * own)
            ]
            pairs.append(jnp.where(left, sides[0], sides[1]))
        return pairs

    pairs = columns // LANES
    for block in range(columns // WIDE):
        if block * WIDE % piece == 0:
            large[block * WIDE // piece * 2].wait()
            large[block * WIDE // piece * 2 + 1].wait()
        at = slice(block * WIDE, (block + 1) * WIDE)
        here = slice(block * PARTS * own, (block + 1) * PARTS * own)
        states = block_states(b, keeping[here], x_ref[:, at])
        pulls = block_states(c, carried[here], dy_ref[:, at])
        for i in range(PARTS):
            pair = block * PARTS + i
            kept_row = jnp.where(left, kept[pair * own : pair * own + 1], kept[pair * own + 1 :][:1])
            first = jnp.where(even, states[i], pulls[i])
            second = jnp.where(even, pulls[i], states[i])
            half, inner = divmod(pair, pairs // 2)
            for ref, place_in, whole, value in (
                (one_ref, pair, pairs, first),
                ((two_ref, three_ref)[half], inner, pairs // 2, second),
            ):
                ref[place_in * width : (place_in + 1) * width, :] = value
                ref[whole * width + place_in : whole * width + place_in + 1, :] = kept_row
    small[-1].wait()


def inside_kernel(
    lens_hbm,
    alog_ref,
    skip_ref,
    dt_ref,
    x_ref,
    b_ref,
    dy_ref,
    c_ref,
    _,
    xs_ref,
    ys_ref,
    v_wide_hbm,
    dx_hbm,
    b_end_ref,
    c_live_ref,
    masks_ref,
    db_ref,
    dc_ref,
    sums_ref,
    fwd_ref,
    bwd_ref,
    ends_ref,
    small_ref,
    v_stage,
    dx_stage,
    lens_ref,
    lens_sem,
    sems,
):
    rows, columns = x_ref.shape
    heads, width = dt_ref.shape[0], b_ref.shape[0]
    head_width = columns // heads
    lens_copy = pltpu.make_async_copy(lens_hbm, lens_ref, lens_sem)
    lens_copy.start()
    distance = head_distance(heads, head_width)
    bt, ct = b_ref[...], c_ref[...]
    raw_scores, raw_flipped = dot(ct, bt, 0, 0), dot(bt, ct, 0, 0)
    lens_copy.wait()
    starts, offset, first, last = document_places(lens_ref, rows)
    through = jnp.where(first >= offset + rows, 1.0, 0.0)
    square = (rows, rows)
    place0, place1 = iota(square, 0) + offset, iota(square, 1) + offset
    segment0, segment1 = jnp.zeros(square, jnp.int32), jnp.zeros(square, jnp.int32)
    for start in starts:
        segment0 += jnp.where(place0 >= start, 1, 0)
        segment1 += jnp.where(place1 >= start, 1, 0)
    same = segment0 == segment1
    down = same & (place0 >= place1)
    lower = jnp.where(place0 >= place1, 1.0, 0.0).astype(BF16)
    eye = jnp.where(place0 == place1, 1.0, 0.0).astype(BF16)
    dt = dt_ref[...]
    logs = sum(dot(lower, part, 1, 1) for part in split3(dt * rate_column(alog_ref)))
    steps = sum(dot(eye, part, 1, 1) for part in split3(dt))
    scores = split2(jnp.where(down, raw_scores, 0.0))
    flipped = split2(jnp.where(same & (place1 >= place0), raw_flipped, 0.0))
    place = iota((width, rows), 1) + offset
    bt_end = jnp.where(place >= last, bt.astype(F32), 0.0)
    ct_live = jnp.where(place < first, ct.astype(F32), 0.0)
    b_end, c_live = jnp.transpose(bt_end).astype(BF16), jnp.transpose(ct_live).astype(BF16)
    bt_end, ct_live = bt_end.astype(BF16), ct_live.astype(BF16)
    b_end_ref[...] = stack([b_end, b_end], 1)
    c_live_ref[...] = stack([c_live, c_live], 1)
    bt_end, ct_live = stack([bt_end, bt_end], 1), stack([ct_live, ct_live], 1)
    masks_ref[0:1] = jnp.where(place[:1] >= last, 1.0, 0.0)
    masks_ref[1:2] = jnp.where(place[:1] < first, 1.0, 0.0)
    tables = stack(
        [
            stack(split3(a), 1)
            for a in (
                jnp.exp(logs),
                jnp.exp(-logs) * steps,
                logs,
                jnp.broadcast_to(skip_ref[...], (16, heads)),
            )
        ],
        0,
    )
    d_scores = jnp.zeros((2 * rows, 2 * rows), F32)
    sums = jnp.zeros((2 * rows + 16, heads), F32)
    copies = []
    for block in range(columns // WIDE):
        at = slice(block * WIDE, (block + 1) * WIDE)
        wide = dot(tables, head_rows(distance, head_width, block), 1, 0)
        ones = head_columns(heads, head_width, block)
        u_wide, v_wide, l_wide = wide[:rows], wide[rows : 2 * rows], wide[2 * rows : 3 * rows]
        skip_wide = wide[3 * rows : 3 * rows + 1]
        x = x_ref[:, at].astype(F32)
        dy = dy_ref[:, at].astype(F32)
        xv = x * v_wide
        yu = dy * u_wide
        xs, ys = split2(xv), split2(yu)
        xs_ref[:, at] = stack(xs, 0)
        ys_ref[:, at] = stack(ys, 0)
        v_stage[:, at] = v_wide
        out = dot_pairs(scores, xs, 1, 0)
        back = dot_pairs(flipped, ys, 1, 0)
        d_scores += dot(stack(ys, 0), stack(xs, 0), 1, 1)
        dx_stage[:, at] = v_wide * back + skip_wide * dy
        for i, (stage, target) in enumerate(((v_stage, v_wide_hbm), (dx_stage, dx_hbm))):
            copy = pltpu.make_async_copy(stage.at[:, at], target.at[:, at], sems.at[i, block])
            copy.start()
            copies.append(copy)
        column_part = xv * back
        product = jnp.broadcast_to(jnp.sum(x * dy, axis=0, keepdims=True), (16, WIDE))
        for part in split3(stack([yu * out - column_part, column_part, product], 0)):
            sums += dot(part, ones, 1, 0)
        ending = u_wide[rows - 1 : rows]
        end_log = l_wide[rows - 1 : rows]
        gap = end_log - l_wide
        fwd_ref[:, at] = dot(bt_end, stack(split2(xv * gap), 0), 1, 0) * ending
        bwd_ref[:, at] = dot(ct_live, stack(split2(yu * l_wide), 0), 1, 0)
        ends_ref[0:1, at] = ending
        ends_ref[1:2, at] = ending * through
        ends_ref[2:3, at] = ending * through * end_log
    d_scores = (d_scores[:rows, :rows] + d_scores[:rows, rows:]) + d_scores[rows:, :rows]
    d_scores = split2(jnp.where(down, d_scores, 0.0))
    dc_ref[...] = sum(dot(bt, p, 1, 1) for p in d_scores)
    db_ref[...] = sum(dot(ct, p, 1, 0) for p in d_scores)
    sums_ref[...] = sums[: 2 * rows]
    rate_grads = jnp.sum(logs * sums[:rows], axis=0, keepdims=True)
    empty = jnp.zeros((1, LANES - 2 * heads), F32)
    small_ref[...] = stack([rate_grads, sums[2 * rows : 2 * rows + 1], empty], 1)
    for copy in copies:
        copy.wait()


def rates_kernel(reach, head_width, half, *refs):
    plan = message_plan(reach, half)
    messages = dict(zip(plan, refs))
    ends_ref, fwd_ref, bwd_ref, *refs = refs[len(plan) :]
    width, columns = fwd_ref.shape
    blocks = columns // WIDE
    own_blocks = blocks // 2
    came_ref, pull_ref, out_ref = refs[-3:]
    whole = []
    for i in range(own_blocks):
        block = half * own_blocks + i
        at = slice(block * WIDE, (block + 1) * WIDE)
        own = slice(i * WIDE, (i + 1) * WIDE)
        came, pull = received(messages, reach, block, blocks, width)
        came_ref[:, own] = came
        pull_ref[:, own] = pull
        terms = came * bwd_ref[:, at] + pull * (fwd_ref[:, at] + ends_ref[2:3, at] * came)
        whole.append(jnp.sum(terms, axis=0, keepdims=True))
    if not half:
        out_ref[...] = stack(whole, 0)
        return
    small_ref, first_ref = refs[:2]
    own = WIDE // head_width
    shape = (WIDE, LANES)
    column = lax.shift_right_logical(iota(shape, 0), log2(head_width))
    ones = jnp.where(column == (iota(shape, 1) & (own - 1)), 1.0, 0.0).astype(BF16)
    sums = dot(stack(split3(stack([first_ref[...], *whole], 0)), 0), ones, 1, 0)
    sums = (sums[:blocks] + sums[blocks : 2 * blocks]) + sums[2 * blocks :]
    lane = iota(sums.shape, 1)
    mine = lax.shift_right_logical(lane, log2(own)) == iota(sums.shape, 0)
    total = small_ref[...] + jnp.sum(jnp.where(mine, sums, 0.0), axis=0, keepdims=True)
    out_ref[...] = jnp.broadcast_to(total, out_ref.shape)


def outputs_kernel(
    came_one,
    came_two,
    pull_one,
    pull_two,
    ends_ref,
    xs_ref,
    ys_ref,
    v_wide_hbm,
    dx_hbm,
    b_end_ref,
    c_live_ref,
    masks_ref,
    db_ref,
    dc_ref,
    sums_ref,
    alog_ref,
    dt_ref,
    dx_out,
    db_out,
    dc_out,
    dt_out,
    v_stage,
    dx_stage,
    stage,
    in_sems,
    out_sems,
):
    rows, columns = dx_hbm.shape
    heads, width = dt_ref.shape[0], db_ref.shape[0]
    blocks = columns // WIDE
    copies = []
    for block in range(blocks):
        at = slice(block * WIDE, (block + 1) * WIDE)
        for i, (source, target) in enumerate(((v_wide_hbm, v_stage), (dx_hbm, dx_stage))):
            copy = pltpu.make_async_copy(
                source.at[:, at], target.at[:, at], in_sems.at[i, block]
            )
            copy.start()
            copies.append(copy)
    b_end, c_live = b_end_ref[...], c_live_ref[...]
    own_sums = sums_ref[...]
    sums = own_sums
    dc = jnp.zeros((2 * width, 2 * rows), F32)
    db = jnp.zeros((2 * width, 2 * rows), F32)
    at_last = iota((rows, WIDE), 0) == rows - 1
    sent = []
    for block in range(blocks):
        at = slice(block * WIDE, (block + 1) * WIDE)
        ones = head_columns(heads, columns // heads, block)
        half, inner = divmod(block, blocks // 2)
        own = slice(inner * WIDE, (inner + 1) * WIDE)
        came, pull = (came_one, came_two)[half][:, own], (pull_one, pull_two)[half][:, own]
        meet = jnp.sum(came * pull, axis=0, keepdims=True) * ends_ref[1:2, at]
        cames = stack(split2(came), 0)
        pulls = stack(split2(pull * ends_ref[0:1, at]), 0)
        xs, ys = xs_ref[:, at], ys_ref[:, at]
        out = dot(c_live, cames, 1, 0)
        back = dot(b_end, pulls, 1, 0)
        column_part = (xs[:rows].astype(F32) + xs[rows:].astype(F32)) * back
        row_part = (ys[:rows].astype(F32) + ys[rows:].astype(F32)) * out
        row_part = jnp.where(at_last, row_part + meet, row_part)
        for part in split2(stack([row_part - column_part, column_part], 0)):
            sums += dot(part, ones, 1, 0)
        dc += dot(cames, ys, 1, 1)
        db += dot(pulls, xs, 1, 1)
        copies[2 * block].wait()
        copies[2 * block + 1].wait()
        stage[:, at] = (dx_stage[:, at] + v_stage[:, at] * back).astype(BF16)
        copy = pltpu.make_async_copy(stage.at[:, at], dx_out.at[0, :, at], out_sems.at[block])
        copy.start()
        sent.append(copy)
    dc = (dc[:width, :rows] + dc[:width, rows:]) + dc[width:, :rows]
    db = (db[:width, :rows] + db[:width, rows:]) + db[width:, :rows]
    db_out[0] = (db_ref[...] + masks_ref[0:1] * db).astype(BF16)
    dc_out[0] = (dc_ref[...] + masks_ref[1:2] * dc).astype(BF16)
    square = (rows, rows)
    upper = jnp.where(iota(square, 0) >= iota(square, 1), 1.0, 0.0).astype(BF16)
    eye = jnp.where(iota(square, 0) == iota(square, 1), 1.0, 0.0).astype(BF16)
    at_end = jnp.sum(sums[rows:] - own_sums[rows:], axis=0, keepdims=True)
    dl = sums[:rows] + jnp.where(iota((rows, heads), 0) == rows - 1, at_end, 0.0)
    d_decay = sum(dot(part, upper, 0, 0) for part in split3(dl))
    total = sum(dot(part, eye, 0, 0) for part in split3(sums[rows:]))
    dt_out[0] = total / dt_ref[...] + rate_column(alog_ref) * d_decay
    for copy in sent:
        copy.wait()


def call(kernel, reach, outs, ins, flops, moved, scratch=()):
    spaces = {"s": pltpu.SMEM, "v": pltpu.VMEM, "h": pltpu.HBM, "any": pl.ANY}
    return pl.pallas_call(
        kernel,
        out_shape=[
            pltpu.HBM(*out) if place == "h" else jax.ShapeDtypeStruct(*out) for place, out in outs
        ],
        in_specs=[pl.BlockSpec(memory_space=spaces[place]) for place, _ in ins],
        out_specs=[pl.BlockSpec(memory_space=spaces[place]) for place, _ in outs],
        scratch_shapes=scratch,
        compiler_params=pltpu.CompilerParams(vmem_limit_bytes=min(16 + 2 * reach, 56) * 2**20),
        cost_estimate=pl.CostEstimate(flops=flops, bytes_accessed=moved, transcendentals=0),
    )(*(a for _, a in ins))


def send(a, by, second):
    count = lax.axis_size("ctx")
    pairs = [(i, i + by if (i + second) % 2 == 0 else i - by) for i in range(count)]
    return lax.ppermute(a, "ctx", [(i, j) for i, j in pairs if 0 <= j < count])


def hand_on(a, half):
    count = lax.axis_size("ctx")
    spared = (1, count - 2) if half else ()
    return lax.ppermute(a, "ctx", [(i, i ^ 1) for i in range(count) if i not in spared])


def in_hbm(a):
    return "h", pltpu.with_memory_space_constraint(a, pltpu.HBM)


def per_device(inputs, b_proj, c_proj, step_sizes, a_log, skip_gain, doc_lengths, grad_out):
    rows, columns = inputs.shape[1:]
    heads, width = a_log.shape[0], b_proj.shape[2]
    reach = max(lax.axis_size("ctx") // 4, 1)
    devices = lax.axis_size("ctx") * lax.axis_size("dp")
    alog, skip = a_log[None], skip_gain[None]
    bt, ct = jnp.swapaxes(b_proj, 1, 2), jnp.swapaxes(c_proj, 1, 2)
    blocks = columns // WIDE

    def v(shape, kind=F32):
        return "v", (shape, kind)

    alog, skip, dt, x, b, dy, c, *payloads = call(
        states_kernel,
        reach,
        [
            v(alog.shape),
            v(skip.shape),
            v((heads, rows)),
            v((rows, columns), BF16),
            v((width, rows), BF16),
            v((rows, columns), BF16),
            v((width, rows), BF16),
        ]
        + [v((columns // LANES * (width + 1) // part, LANES)) for part in (1, 2, 2)],
        [in_hbm(a) for a in (doc_lengths, alog, skip, step_sizes, inputs, bt, grad_out, ct)],
        10**9,
        4 * 2**20,
        [
            pltpu.SMEM(doc_lengths.shape, jnp.int32),
            pltpu.SemaphoreType.DMA((6,)),
            pltpu.SemaphoreType.DMA((2, PIECES)),
        ],
    )
    messages = {}
    for j, second, half in message_plan(reach):
        if (j, second) == (1, 1) and reach > 1:
            continue
        payload = payloads[1 + half if second else 0]
        messages[j, second, half] = send(payload, j, second)
    if reach > 1:
        for half in (0, 1):
            messages[1, 1, half] = hand_on(messages[2, 1, half], half)
    whole = "h", ((rows, columns), F32)
    state = v((width, columns))
    stage = pltpu.VMEM((rows, columns), F32)
    transposed = v((width, rows))
    xs, ys, v_wide, dx, b_end, c_live, masks, db, dc, sums, fwd_logs, bwd_logs, ends, small = call(
        inside_kernel,
        reach,
        [v((2 * rows, columns), BF16)] * 2
        + [whole] * 2
        + [v((rows, 2 * width), BF16)] * 2
        + [v((8, rows)), transposed, transposed, v((2 * rows, heads))]
        + [state, state, v((8, columns)), v((1, LANES))],
        [in_hbm(doc_lengths)]
        + [("v", a) for a in (alog, skip, dt, x, b, dy, c)]
        + [("any", messages[1, 0, 0])],
        4 * 10**9,
        12 * 2**20,
        [
            stage,
            stage,
            pltpu.SMEM(doc_lengths.shape, jnp.int32),
            pltpu.SemaphoreType.DMA,
            pltpu.SemaphoreType.DMA((2, blocks)),
        ],
    )
    half_state = v((width, columns // 2))
    joined, last = [], []
    for half in (0, 1):
        out = v((devices, LANES)) if half else v((blocks // 2, WIDE))
        came, pull, partial = call(
            functools.partial(rates_kernel, reach, columns // heads, half),
            reach,
            [half_state, half_state, out],
            [("v", messages[one]) for one in message_plan(reach, half)]
            + [("v", a) for a in (ends, fwd_logs, bwd_logs, *last)],
            10**8,
            4 * 2**20,
        )
        joined.append((came, pull))
        last = [small, partial]
    input_grads, b_gradient, c_gradient, step_grads = call(
        outputs_kernel,
        reach,
        [("h", ((1, rows, columns), BF16))]
        + [v((1, width, rows), BF16)] * 2
        + [v((1, heads, rows))],
        [("v", a) for side in zip(*joined) for a in side]
        + [("v", a) for a in (ends, xs, ys)]
        + [in_hbm(v_wide), in_hbm(dx)]
        + [("v", a) for a in (b_end, c_live, masks, db, dc, sums, alog, dt)],
        2 * 10**9,
        12 * 2**20,
        [
            stage,
            stage,
            pltpu.VMEM((rows, columns), BF16),
            pltpu.SemaphoreType.DMA((2, blocks)),
            pltpu.SemaphoreType.DMA((blocks,)),
        ],
    )
    gathered = lax.all_to_all(partial, ("ctx", "dp"), 0, 0, tiled=True)
    totals = jnp.sum(gathered, axis=0)
    return (
        input_grads,
        jnp.swapaxes(b_gradient, 1, 2),
        jnp.swapaxes(c_gradient, 1, 2),
        step_grads,
        totals[:heads],
        totals[heads : 2 * heads],
    )


def solution(mesh):
    in_specs = (
        P("dp", "ctx", None),
        P("dp", "ctx", None),
        P("dp", "ctx", None),
        P("dp", None, "ctx"),
        P(),
        P(),
        P("dp", None),
        P("dp", "ctx", None),
    )
    out_specs = (
        P("dp", "ctx", None),
        P("dp", "ctx", None),
        P("dp", "ctx", None),
        P("dp", None, "ctx"),
        P(),
        P(),
    )
    return jax.shard_map(
        per_device, mesh=mesh, in_specs=in_specs, out_specs=out_specs, check_vma=False
    )
```

```python
import functools

import jax
import jax.numpy as jnp
from jax import lax
from jax.experimental import pallas as pl
from jax.experimental.pallas import tpu as pltpu
from jax.sharding import PartitionSpec as P

F32 = jnp.float32
BF16 = jnp.bfloat16
LANES = 128
WIDE = 256
PARTS = WIDE // LANES
FAR = 2**30
PIECES = 1


def dot(a, b, ca, cb):
    return lax.dot_general(a, b, (((ca,), (cb,)), ((), ())), preferred_element_type=F32)


def iota(shape, dim):
    return lax.broadcasted_iota(jnp.int32, shape, dim)


def split2(a):
    high = a.astype(BF16)
    return high, (a - high.astype(F32)).astype(BF16)


def split3(a):
    high = a.astype(BF16)
    rest = a - high.astype(F32)
    middle = rest.astype(BF16)
    return high, middle, (rest - middle.astype(F32)).astype(BF16)


def dot_pairs(a, b, ca, cb):
    return dot(a[0], b[0], ca, cb) + (dot(a[0], b[1], ca, cb) + dot(a[1], b[0], ca, cb))


def stack(parts, axis):
    return jnp.concatenate(parts, axis=axis)


def document_places(lens_ref, rows):
    offset = shard() * rows
    starts = [jnp.int32(0)]
    for d in range(lens_ref.shape[1] - 1):
        starts.append(starts[-1] + lens_ref[0, d])
    first = jnp.int32(FAR)
    last = jnp.int32(0)
    for start in starts:
        first = jnp.minimum(first, jnp.where(start >= offset, start, FAR))
        last = jnp.maximum(last, jnp.where(start < offset + rows, start, 0))
    return starts, offset, first, last


def rate_column(alog_ref):
    heads = alog_ref.shape[1]
    square = jnp.broadcast_to(alog_ref[...], (heads, heads))
    picked = jnp.where(iota((heads, heads), 0) == iota((heads, heads), 1), square, 0.0)
    return -jnp.exp(jnp.sum(picked, axis=1, keepdims=True))


def log2(size):
    assert size & (size - 1) == 0
    return size.bit_length() - 1


def head_distance(heads, head_width):
    shape = (3 * heads, WIDE)
    return (iota(shape, 0) & (heads - 1)) - lax.shift_right_logical(
        iota(shape, 1), log2(head_width)
    )


def head_rows(distance, head_width, block):
    return jnp.where(distance == block * (WIDE // head_width), 1.0, 0.0).astype(BF16)


def head_columns(heads, head_width, block):
    shape = (WIDE, heads)
    column = lax.shift_right_logical(iota(shape, 0), log2(head_width))
    return jnp.where(iota(shape, 1) - column == block * (WIDE // head_width), 1.0, 0.0).astype(BF16)


def shard():
    return lax.axis_index("ctx")


def message_block(ref, block, width):
    at = block * PARTS
    return stack([ref[(at + i) * width : (at + i + 1) * width, :] for i in range(PARTS)], 1)


def message_tail(ref, block, width):
    tail = ref.shape[0] // (width + 1) * width + block * PARTS
    return stack([ref[tail + i : tail + i + 1, :] for i in range(PARTS)], 1)


def message_plan(reach, only=None):
    near = [(1, 0, 0)]
    relayed = [(1, 1, 0), (1, 1, 1)]
    far = [(2, 1, 0), (2, 1, 1), (2, 0, 0)] if reach > 1 else []
    rest = [(j, *one) for j in range(3, reach + 1) for one in ((0, 0), (1, 0), (1, 1))]
    plan = near + far + relayed + rest
    return [one for one in plan if only is None or not one[1] or one[2] == only]


def received(messages, reach, block, blocks, width):
    came = pull = None
    half, inner = divmod(block, blocks // 2)
    for j in range(reach, 0, -1):
        one, two = messages[j, 0, 0], messages[j, 1, half]
        a, b = message_block(one, block, width), message_block(two, inner, width)
        first = jnp.broadcast_to(lax.rem(shard() + j, 2), a.shape) == 0
        near_came, near_pull = jnp.where(first, a, b), jnp.where(first, b, a)
        if came is None:
            came, pull = near_came, near_pull
        else:
            a, b = message_tail(one, block, width), message_tail(two, inner, width)
            first = jnp.broadcast_to(lax.rem(shard() + j, 2), a.shape) == 0
            came = near_came + jnp.where(first, a, b) * came
            pull = near_pull + jnp.where(first, b, a) * pull
    return came, pull


def states_kernel(
    lens_hbm,
    alog_hbm,
    skip_hbm,
    dt_hbm,
    x_hbm,
    b_hbm,
    dy_hbm,
    c_hbm,
    alog_ref,
    skip_ref,
    dt_ref,
    x_ref,
    b_ref,
    dy_ref,
    c_ref,
    one_ref,
    two_ref,
    three_ref,
    lens_ref,
    small_sems,
    sems,
):
    rows, columns = x_ref.shape
    heads, width = dt_ref.shape[0], b_ref.shape[0]
    head_width = columns // heads
    piece = columns // PIECES
    small = [
        pltpu.make_async_copy(source, target, small_sems.at[i])
        for i, (source, target) in enumerate(
            (
                (dt_hbm.at[0], dt_ref),
                (alog_hbm, alog_ref),
                (lens_hbm, lens_ref),
                (b_hbm.at[0], b_ref),
                (c_hbm.at[0], c_ref),
                (skip_hbm, skip_ref),
            )
        )
    ]
    large = []
    for i in range(PIECES):
        at = slice(i * piece, (i + 1) * piece)
        for side, (source, target) in enumerate(((x_hbm, x_ref), (dy_hbm, dy_ref))):
            copy = pltpu.make_async_copy(
                source.at[0, :, at], target.at[:, at], sems.at[side, i]
            )
            large.append(copy)
    for copy in (*small[:3], *large[:2], *small[3:5], *large[2:], *small[5:]):
        copy.start()
    square = (rows, rows)
    upper = jnp.where(iota(square, 0) <= iota(square, 1), 1.0, 0.0).astype(BF16)
    even = jnp.broadcast_to(lax.rem(shard(), 2), (width, LANES)) == 0
    left = iota((1, LANES), 1) < head_width
    for copy in small[:3]:
        copy.wait()
    _, offset, first, last = document_places(lens_ref, rows)
    through = jnp.where(first >= offset + rows, 1.0, 0.0)
    dt = dt_ref[...]
    logs = sum(dot(part, upper, 1, 0) for part in split3(dt * rate_column(alog_ref)))
    end_log = logs[:, rows - 1 : rows]
    place = iota((heads, rows), 1) + offset
    keeping = jnp.where(place >= last, jnp.exp(end_log - logs) * dt, 0.0)
    carried = jnp.where(place < first, jnp.exp(logs), 0.0)
    kept = jnp.broadcast_to(jnp.exp(end_log) * through, (heads, LANES))
    for copy in small[3:5]:
        copy.wait()
    b, c = b_ref[...].astype(F32), c_ref[...].astype(F32)
    own = LANES // head_width

    def block_states(vectors, weights, values):
        rows_in = [stack(split2(vectors * weights[h : h + 1, :]), 1) for h in range(PARTS * own)]
        out = dot(stack(rows_in, 0), stack([values, values], 0), 1, 0)
        pairs = []
        for i in range(PARTS):
            lanes = slice(i * LANES, (i + 1) * LANES)
            sides = [
                out[h * width : (h + 1) * width, lanes] for h in range(i * own, (i + 1) * own)
            ]
            pairs.append(jnp.where(left, sides[0], sides[1]))
        return pairs

    pairs = columns // LANES
    for block in range(columns // WIDE):
        if block * WIDE % piece == 0:
            large[block * WIDE // piece * 2].wait()
            large[block * WIDE // piece * 2 + 1].wait()
        at = slice(block * WIDE, (block + 1) * WIDE)
        here = slice(block * PARTS * own, (block + 1) * PARTS * own)
        states = block_states(b, keeping[here], x_ref[:, at])
        pulls = block_states(c, carried[here], dy_ref[:, at])
        for i in range(PARTS):
            pair = block * PARTS + i
            kept_row = jnp.where(left, kept[pair * own : pair * own + 1], kept[pair * own + 1 :][:1])
            first = jnp.where(even, states[i], pulls[i])
            second = jnp.where(even, pulls[i], states[i])
            half, inner = divmod(pair, pairs // 2)
            for ref, place_in, whole, value in (
                (one_ref, pair, pairs, first),
                ((two_ref, three_ref)[half], inner, pairs // 2, second),
            ):
                ref[place_in * width : (place_in + 1) * width, :] = value
                ref[whole * width + place_in : whole * width + place_in + 1, :] = kept_row
    small[-1].wait()


def inside_kernel(
    lens_hbm,
    alog_ref,
    skip_ref,
    dt_ref,
    x_ref,
    b_ref,
    dy_ref,
    c_ref,
    _,
    xs_ref,
    ys_ref,
    v_wide_hbm,
    dx_hbm,
    b_end_ref,
    c_live_ref,
    masks_ref,
    db_ref,
    dc_ref,
    sums_ref,
    fwd_ref,
    bwd_ref,
    ends_ref,
    small_ref,
    v_stage,
    dx_stage,
    lens_ref,
    lens_sem,
    sems,
):
    rows, columns = x_ref.shape
    heads, width = dt_ref.shape[0], b_ref.shape[0]
    head_width = columns // heads
    lens_copy = pltpu.make_async_copy(lens_hbm, lens_ref, lens_sem)
    lens_copy.start()
    distance = head_distance(heads, head_width)
    bt, ct = b_ref[...], c_ref[...]
    raw_scores, raw_flipped = dot(ct, bt, 0, 0), dot(bt, ct, 0, 0)
    lens_copy.wait()
    starts, offset, first, last = document_places(lens_ref, rows)
    through = jnp.where(first >= offset + rows, 1.0, 0.0)
    square = (rows, rows)
    place0, place1 = iota(square, 0) + offset, iota(square, 1) + offset
    segment0, segment1 = jnp.zeros(square, jnp.int32), jnp.zeros(square, jnp.int32)
    for start in starts:
        segment0 += jnp.where(place0 >= start, 1, 0)
        segment1 += jnp.where(place1 >= start, 1, 0)
    same = segment0 == segment1
    down = same & (place0 >= place1)
    lower = jnp.where(place0 >= place1, 1.0, 0.0).astype(BF16)
    eye = jnp.where(place0 == place1, 1.0, 0.0).astype(BF16)
    dt = dt_ref[...]
    logs = sum(dot(lower, part, 1, 1) for part in split3(dt * rate_column(alog_ref)))
    steps = sum(dot(eye, part, 1, 1) for part in split3(dt))
    scores = split2(jnp.where(down, raw_scores, 0.0))
    flipped = split2(jnp.where(same & (place1 >= place0), raw_flipped, 0.0))
    place = iota((width, rows), 1) + offset
    bt_end = jnp.where(place >= last, bt.astype(F32), 0.0)
    ct_live = jnp.where(place < first, ct.astype(F32), 0.0)
    b_end, c_live = jnp.transpose(bt_end).astype(BF16), jnp.transpose(ct_live).astype(BF16)
    bt_end, ct_live = bt_end.astype(BF16), ct_live.astype(BF16)
    b_end_ref[...] = stack([b_end, b_end], 1)
    c_live_ref[...] = stack([c_live, c_live], 1)
    bt_end, ct_live = stack([bt_end, bt_end], 1), stack([ct_live, ct_live], 1)
    masks_ref[0:1] = jnp.where(place[:1] >= last, 1.0, 0.0)
    masks_ref[1:2] = jnp.where(place[:1] < first, 1.0, 0.0)
    tables = stack(
        [
            stack(split3(a), 1)
            for a in (
                jnp.exp(logs),
                jnp.exp(-logs) * steps,
                logs,
                jnp.broadcast_to(skip_ref[...], (16, heads)),
            )
        ],
        0,
    )
    d_scores = jnp.zeros((2 * rows, 2 * rows), F32)
    sums = jnp.zeros((2 * rows + 16, heads), F32)
    copies = []
    for block in range(columns // WIDE):
        at = slice(block * WIDE, (block + 1) * WIDE)
        wide = dot(tables, head_rows(distance, head_width, block), 1, 0)
        ones = head_columns(heads, head_width, block)
        u_wide, v_wide, l_wide = wide[:rows], wide[rows : 2 * rows], wide[2 * rows : 3 * rows]
        skip_wide = wide[3 * rows : 3 * rows + 1]
        x = x_ref[:, at].astype(F32)
        dy = dy_ref[:, at].astype(F32)
        xv = x * v_wide
        yu = dy * u_wide
        xs, ys = split2(xv), split2(yu)
        xs_ref[:, at] = stack(xs, 0)
        ys_ref[:, at] = stack(ys, 0)
        v_stage[:, at] = v_wide
        out = dot_pairs(scores, xs, 1, 0)
        back = dot_pairs(flipped, ys, 1, 0)
        d_scores += dot(stack(ys, 0), stack(xs, 0), 1, 1)
        dx_stage[:, at] = v_wide * back + skip_wide * dy
        for i, (stage, target) in enumerate(((v_stage, v_wide_hbm), (dx_stage, dx_hbm))):
            copy = pltpu.make_async_copy(stage.at[:, at], target.at[:, at], sems.at[i, block])
            copy.start()
            copies.append(copy)
        column_part = xv * back
        product = jnp.broadcast_to(jnp.sum(x * dy, axis=0, keepdims=True), (16, WIDE))
        for part in split3(stack([yu * out - column_part, column_part, product], 0)):
            sums += dot(part, ones, 1, 0)
        ending = u_wide[rows - 1 : rows]
        end_log = l_wide[rows - 1 : rows]
        gap = end_log - l_wide
        fwd_ref[:, at] = dot(bt_end, stack(split2(xv * gap), 0), 1, 0) * ending
        bwd_ref[:, at] = dot(ct_live, stack(split2(yu * l_wide), 0), 1, 0)
        ends_ref[0:1, at] = ending
        ends_ref[1:2, at] = ending * through
        ends_ref[2:3, at] = ending * through * end_log
    d_scores = (d_scores[:rows, :rows] + d_scores[:rows, rows:]) + d_scores[rows:, :rows]
    d_scores = split2(jnp.where(down, d_scores, 0.0))
    dc_ref[...] = sum(dot(bt, p, 1, 1) for p in d_scores)
    db_ref[...] = sum(dot(ct, p, 1, 0) for p in d_scores)
    sums_ref[...] = sums[: 2 * rows]
    rate_grads = jnp.sum(logs * sums[:rows], axis=0, keepdims=True)
    empty = jnp.zeros((1, LANES - 2 * heads), F32)
    small_ref[...] = stack([rate_grads, sums[2 * rows : 2 * rows + 1], empty], 1)
    for copy in copies:
        copy.wait()


def rates_kernel(reach, head_width, half, *refs):
    plan = message_plan(reach, half)
    messages = dict(zip(plan, refs))
    ends_ref, fwd_ref, bwd_ref, *refs = refs[len(plan) :]
    width, columns = fwd_ref.shape
    blocks = columns // WIDE
    own_blocks = blocks // 2
    came_ref, pull_ref, out_ref = refs[-3:]
    whole = []
    for i in range(own_blocks):
        block = half * own_blocks + i
        at = slice(block * WIDE, (block + 1) * WIDE)
        own = slice(i * WIDE, (i + 1) * WIDE)
        came, pull = received(messages, reach, block, blocks, width)
        came_ref[:, own] = came
        pull_ref[:, own] = pull
        terms = came * bwd_ref[:, at] + pull * (fwd_ref[:, at] + ends_ref[2:3, at] * came)
        whole.append(jnp.sum(terms, axis=0, keepdims=True))
    if not half:
        out_ref[...] = stack(whole, 0)
        return
    small_ref, first_ref = refs[:2]
    own = WIDE // head_width
    shape = (WIDE, LANES)
    column = lax.shift_right_logical(iota(shape, 0), log2(head_width))
    ones = jnp.where(column == (iota(shape, 1) & (own - 1)), 1.0, 0.0).astype(BF16)
    sums = dot(stack(split3(stack([first_ref[...], *whole], 0)), 0), ones, 1, 0)
    sums = (sums[:blocks] + sums[blocks : 2 * blocks]) + sums[2 * blocks :]
    lane = iota(sums.shape, 1)
    mine = lax.shift_right_logical(lane, log2(own)) == iota(sums.shape, 0)
    total = small_ref[...] + jnp.sum(jnp.where(mine, sums, 0.0), axis=0, keepdims=True)
    out_ref[...] = jnp.broadcast_to(total, out_ref.shape)


def outputs_kernel(
    came_one,
    came_two,
    pull_one,
    pull_two,
    ends_ref,
    xs_ref,
    ys_ref,
    v_wide_hbm,
    dx_hbm,
    b_end_ref,
    c_live_ref,
    masks_ref,
    db_ref,
    dc_ref,
    sums_ref,
    alog_ref,
    dt_ref,
    dx_out,
    db_out,
    dc_out,
    dt_out,
    v_stage,
    dx_stage,
    stage,
    in_sems,
    out_sems,
):
    rows, columns = dx_hbm.shape
    heads, width = dt_ref.shape[0], db_ref.shape[0]
    blocks = columns // WIDE
    copies = []
    for block in range(blocks):
        at = slice(block * WIDE, (block + 1) * WIDE)
        for i, (source, target) in enumerate(((v_wide_hbm, v_stage), (dx_hbm, dx_stage))):
            copy = pltpu.make_async_copy(
                source.at[:, at], target.at[:, at], in_sems.at[i, block]
            )
            copy.start()
            copies.append(copy)
    b_end, c_live = b_end_ref[...], c_live_ref[...]
    own_sums = sums_ref[...]
    sums = own_sums
    dc = jnp.zeros((2 * width, 2 * rows), F32)
    db = jnp.zeros((2 * width, 2 * rows), F32)
    at_last = iota((rows, WIDE), 0) == rows - 1
    sent = []
    for block in range(blocks):
        at = slice(block * WIDE, (block + 1) * WIDE)
        ones = head_columns(heads, columns // heads, block)
        half, inner = divmod(block, blocks // 2)
        own = slice(inner * WIDE, (inner + 1) * WIDE)
        came, pull = (came_one, came_two)[half][:, own], (pull_one, pull_two)[half][:, own]
        meet = jnp.sum(came * pull, axis=0, keepdims=True) * ends_ref[1:2, at]
        cames = stack(split2(came), 0)
        pulls = stack(split2(pull * ends_ref[0:1, at]), 0)
        xs, ys = xs_ref[:, at], ys_ref[:, at]
        out = dot(c_live, cames, 1, 0)
        back = dot(b_end, pulls, 1, 0)
        column_part = (xs[:rows].astype(F32) + xs[rows:].astype(F32)) * back
        row_part = (ys[:rows].astype(F32) + ys[rows:].astype(F32)) * out
        row_part = jnp.where(at_last, row_part + meet, row_part)
        for part in split2(stack([row_part - column_part, column_part], 0)):
            sums += dot(part, ones, 1, 0)
        dc += dot(cames, ys, 1, 1)
        db += dot(pulls, xs, 1, 1)
        copies[2 * block].wait()
        copies[2 * block + 1].wait()
        stage[:, at] = (dx_stage[:, at] + v_stage[:, at] * back).astype(BF16)
        copy = pltpu.make_async_copy(stage.at[:, at], dx_out.at[0, :, at], out_sems.at[block])
        copy.start()
        sent.append(copy)
    dc = (dc[:width, :rows] + dc[:width, rows:]) + dc[width:, :rows]
    db = (db[:width, :rows] + db[:width, rows:]) + db[width:, :rows]
    db_out[0] = (db_ref[...] + masks_ref[0:1] * db).astype(BF16)
    dc_out[0] = (dc_ref[...] + masks_ref[1:2] * dc).astype(BF16)
    square = (rows, rows)
    upper = jnp.where(iota(square, 0) >= iota(square, 1), 1.0, 0.0).astype(BF16)
    eye = jnp.where(iota(square, 0) == iota(square, 1), 1.0, 0.0).astype(BF16)
    at_end = jnp.sum(sums[rows:] - own_sums[rows:], axis=0, keepdims=True)
    dl = sums[:rows] + jnp.where(iota((rows, heads), 0) == rows - 1, at_end, 0.0)
    d_decay = sum(dot(part, upper, 0, 0) for part in split3(dl))
    total = sum(dot(part, eye, 0, 0) for part in split3(sums[rows:]))
    dt_out[0] = total / dt_ref[...] + rate_column(alog_ref) * d_decay
    for copy in sent:
        copy.wait()


def call(kernel, reach, outs, ins, flops, moved, scratch=()):
    spaces = {"s": pltpu.SMEM, "v": pltpu.VMEM, "h": pltpu.HBM, "any": pl.ANY}
    return pl.pallas_call(
        kernel,
        out_shape=[
            pltpu.HBM(*out) if place == "h" else jax.ShapeDtypeStruct(*out) for place, out in outs
        ],
        in_specs=[pl.BlockSpec(memory_space=spaces[place]) for place, _ in ins],
        out_specs=[pl.BlockSpec(memory_space=spaces[place]) for place, _ in outs],
        scratch_shapes=scratch,
        compiler_params=pltpu.CompilerParams(vmem_limit_bytes=min(16 + 2 * reach, 56) * 2**20),
        cost_estimate=pl.CostEstimate(flops=flops, bytes_accessed=moved, transcendentals=0),
    )(*(a for _, a in ins))


def send(a, by, second):
    count = lax.axis_size("ctx")
    pairs = [(i, i + by if (i + second) % 2 == 0 else i - by) for i in range(count)]
    return lax.ppermute(a, "ctx", [(i, j) for i, j in pairs if 0 <= j < count])


def hand_on(a, half):
    count = lax.axis_size("ctx")
    spared = (1, count - 2) if half else ()
    return lax.ppermute(a, "ctx", [(i, i ^ 1) for i in range(count) if i not in spared])


def in_hbm(a):
    return "h", pltpu.with_memory_space_constraint(a, pltpu.HBM)


def per_device(inputs, b_proj, c_proj, step_sizes, a_log, skip_gain, doc_lengths, grad_out):
    rows, columns = inputs.shape[1:]
    heads, width = a_log.shape[0], b_proj.shape[2]
    reach = max(lax.axis_size("ctx") // 4, 1)
    devices = lax.axis_size("ctx") * lax.axis_size("dp")
    alog, skip = a_log[None], skip_gain[None]
    bt, ct = jnp.swapaxes(b_proj, 1, 2), jnp.swapaxes(c_proj, 1, 2)
    blocks = columns // WIDE

    def v(shape, kind=F32):
        return "v", (shape, kind)

    alog, skip, dt, x, b, dy, c, *payloads = call(
        states_kernel,
        reach,
        [
            v(alog.shape),
            v(skip.shape),
            v((heads, rows)),
            v((rows, columns), BF16),
            v((width, rows), BF16),
            v((rows, columns), BF16),
            v((width, rows), BF16),
        ]
        + [v((columns // LANES * (width + 1) // part, LANES)) for part in (1, 2, 2)],
        [in_hbm(a) for a in (doc_lengths, alog, skip, step_sizes, inputs, bt, grad_out, ct)],
        10**9,
        4 * 2**20,
        [
            pltpu.SMEM(doc_lengths.shape, jnp.int32),
            pltpu.SemaphoreType.DMA((6,)),
            pltpu.SemaphoreType.DMA((2, PIECES)),
        ],
    )
    messages = {}
    for j, second, half in message_plan(reach):
        if (j, second) == (1, 1) and reach > 1:
            continue
        payload = payloads[1 + half if second else 0]
        messages[j, second, half] = send(payload, j, second)
    if reach > 1:
        for half in (0, 1):
            messages[1, 1, half] = hand_on(messages[2, 1, half], half)
    whole = "h", ((rows, columns), F32)
    state = v((width, columns))
    stage = pltpu.VMEM((rows, columns), F32)
    transposed = v((width, rows))
    xs, ys, v_wide, dx, b_end, c_live, masks, db, dc, sums, fwd_logs, bwd_logs, ends, small = call(
        inside_kernel,
        reach,
        [v((2 * rows, columns), BF16)] * 2
        + [whole] * 2
        + [v((rows, 2 * width), BF16)] * 2
        + [v((8, rows)), transposed, transposed, v((2 * rows, heads))]
        + [state, state, v((8, columns)), v((1, LANES))],
        [in_hbm(doc_lengths)]
        + [("v", a) for a in (alog, skip, dt, x, b, dy, c)]
        + [("any", messages[1, 0, 0])],
        4 * 10**9,
        12 * 2**20,
        [
            stage,
            stage,
            pltpu.SMEM(doc_lengths.shape, jnp.int32),
            pltpu.SemaphoreType.DMA,
            pltpu.SemaphoreType.DMA((2, blocks)),
        ],
    )
    half_state = v((width, columns // 2))
    joined, last = [], []
    for half in (0, 1):
        out = v((devices, LANES)) if half else v((blocks // 2, WIDE))
        came, pull, partial = call(
            functools.partial(rates_kernel, reach, columns // heads, half),
            reach,
            [half_state, half_state, out],
            [("v", messages[one]) for one in message_plan(reach, half)]
            + [("v", a) for a in (ends, fwd_logs, bwd_logs, *last)],
            10**8,
            4 * 2**20,
        )
        joined.append((came, pull))
        last = [small, partial]
    input_grads, b_gradient, c_gradient, step_grads = call(
        outputs_kernel,
        reach,
        [("h", ((1, rows, columns), BF16))]
        + [v((1, width, rows), BF16)] * 2
        + [v((1, heads, rows))],
        [("v", a) for side in zip(*joined) for a in side]
        + [("v", a) for a in (ends, xs, ys)]
        + [in_hbm(v_wide), in_hbm(dx)]
        + [("v", a) for a in (b_end, c_live, masks, db, dc, sums, alog, dt)],
        2 * 10**9,
        12 * 2**20,
        [
            stage,
            stage,
            pltpu.VMEM((rows, columns), BF16),
            pltpu.SemaphoreType.DMA((2, blocks)),
            pltpu.SemaphoreType.DMA((blocks,)),
        ],
    )
    gathered = lax.all_to_all(partial, ("ctx", "dp"), 0, 0, tiled=True)
    totals = jnp.sum(gathered, axis=0)
    return (
        input_grads,
        jnp.swapaxes(b_gradient, 1, 2),
        jnp.swapaxes(c_gradient, 1, 2),
        step_grads,
        totals[:heads],
        totals[heads : 2 * heads],
    )


def solution(mesh):
    in_specs = (
        P("dp", "ctx", None),
        P("dp", "ctx", None),
        P("dp", "ctx", None),
        P("dp", None, "ctx"),
        P(),
        P(),
        P("dp", None),
        P("dp", "ctx", None),
    )
    out_specs = (
        P("dp", "ctx", None),
        P("dp", "ctx", None),
        P("dp", "ctx", None),
        P("dp", None, "ctx"),
        P(),
        P(),
    )
    return jax.shard_map(
        per_device, mesh=mesh, in_specs=in_specs, out_specs=out_specs, check_vma=False
    )
```
